32 devices in a mesh: wide: 16 (over z, x, core), narrow: 2 (over y).
Axes of the slice: x: 2, y: 2, z: 4, core: 2. Of those that a mesh axis runs over, the one named last changes fastest.
Arguments:
- inputs: bfloat16 [16, 2, 2, 1024, 1024], P('wide', None, 'narrow'), may hold values from -6 to 6
- cotangent: bfloat16 [16, 2, 2, 1024, 1024], P('wide', None, 'narrow'), may hold values from -6 to 6
- lengths: int32 [16], P('wide'), may hold values from 512 to 4096, as said below
- w_qkv: bfloat16 [1024, 3072], replicated, may hold values from -0.1875 to 0.1875
- b_qkv: float32 [3072], replicated, may hold values from -1.5 to 1.5
- w_out: bfloat16 [1024, 1024], replicated, may hold values from -0.1875 to 0.1875
- b_out: float32 [1024], replicated, may hold values from -1.5 to 1.5
- w_up: bfloat16 [1024, 4096], replicated, may hold values from -0.1875 to 0.1875
- b_up: float32 [4096], replicated, may hold values from -1.5 to 1.5
- w_down: bfloat16 [4096, 1024], replicated, may hold values from -0.09375 to 0.09375
- b_down: float32 [1024], replicated, may hold values from -1.5 to 1.5
- gain_one: float32 [1024], replicated, may hold values from 0.5 to 1.5
- shift_one: float32 [1024], replicated, may hold values from -1.5 to 1.5
- gain_two: float32 [1024], replicated, may hold values from 0.5 to 1.5
- shift_two: float32 [1024], replicated, may hold values from -1.5 to 1.5
- gain_three: float32 [1024], replicated, may hold values from 0.5 to 1.5
- shift_three: float32 [1024], replicated, may hold values from -1.5 to 1.5
- gain_four: float32 [1024], replicated, may hold values from 0.5 to 1.5
- shift_four: float32 [1024], replicated, may hold values from -1.5 to 1.5
Outputs:
- output: bfloat16 [16, 2, 2, 1024, 1024], P('wide', None, 'narrow')
- input_grad: bfloat16 [16, 2, 2, 1024, 1024], P('wide', None, 'narrow')
- grad_w_qkv: float32 [1024, 3072], P(None, ('wide', 'narrow'))
- grad_w_out: float32 [1024, 1024], P(None, ('wide', 'narrow'))
- grad_w_up: float32 [1024, 4096], P(None, ('wide', 'narrow'))
- grad_w_down: float32 [4096, 1024], P(None, ('wide', 'narrow'))
- grad_b_qkv: float32 [3072], replicated
- grad_b_out: float32 [1024], replicated
- grad_b_up: float32 [4096], replicated
- grad_b_down: float32 [1024], replicated
- grad_gain_one: float32 [1024], replicated
- grad_shift_one: float32 [1024], replicated
- grad_gain_two: float32 [1024], replicated
- grad_shift_two: float32 [1024], replicated
- grad_gain_three: float32 [1024], replicated
- grad_shift_three: float32 [1024], replicated
- grad_gain_four: float32 [1024], replicated
- grad_shift_four: float32 [1024], replicated
The draws below stay inside these ranges and needn't reach their ends.
Inputs may be any that keep to these rules, and one draw needn't show every extreme that they name: `lengths`: in each aligned pair of sequences one, drawn from the seed, has length 4096.
All inputs are finite; a program needn't handle non-finite values.
Results may differ from the reference program's by a relative error of at most 0.018.
Values may be sent and summed in bfloat16 or wider, within the bound.
No kernel may reach another device: no remote copies, remote signals or barrier semaphores. Data moves between devices by JAX's collectives and lax.ppermute only.
A program may use at most 704 MiB of HBM per device.

```python
import math
import jax
import jax.numpy as jnp
from jax import lax

D = 1024
FF = 4096
HEAD_DIM = 64
LEN = 4096
SEQS = 16
GROUP = 1024
N_NARROW = 2


def draw_lengths(key, part):
    key = jax.random.fold_in(key, 11)
    first_key, second_key = jax.random.split(key)
    spans = jax.random.randint(first_key, (SEQS,), LEN // 8, LEN + 1)
    chosen = jax.random.randint(second_key, (SEQS // 2,), 0, 2)
    slot_of = jnp.arange(SEQS, dtype=jnp.int32) % 2
    full_one = slot_of == jnp.repeat(chosen, 2, total_repeat_length=SEQS)
    return jnp.where(full_one, LEN, spans).astype(jnp.int32)


def with_spikes(values, own_key, source, target, blocks, factor):
    owner, partner = [(jnp.arange(values.shape[position]) // (values.shape[position] // blocks)).reshape([-1 if axis == position else 1 for axis in range(values.ndim)]) for position in (source, target)]
    chosen = jax.random.permutation(own_key, blocks)[partner]
    strong = (owner == chosen) | (owner == (partner + blocks // 2) % blocks)
    return jnp.where(strong, factor * values, values)


def block_levels(key, dims, shards, low, largest):
    def one(axis_at, parts):
        heights = jax.random.uniform(jax.random.fold_in(jax.random.fold_in(key, 6), axis_at), (parts,), jnp.float32, low / len(shards), largest / len(shards))
        return jnp.repeat(jnp.exp(heights), dims[axis_at] // parts).reshape((-1,) + (1,) * (len(dims) - axis_at - 1))

    loudness = one(*shards[0])
    for cut in shards[1:]:
        loudness = loudness * one(*cut)
    return loudness


def normal_values(rng, shape, scale, bound, shards=(), held_as=jnp.bfloat16):
    entries = scale * jax.random.normal(rng, shape, jnp.float32)
    if shards:
        entries = entries * block_levels(rng, shape, shards, -0.22, 0.18)
    return jnp.clip(entries, -bound, bound).astype(held_as)


def noise_with(key, dims, scale, reach, cuts, heavy, held_as=jnp.bfloat16):
    values = scale * jax.random.normal(key, dims, jnp.float32)
    if cuts:
        values = values * block_levels(key, dims, cuts, -0.22, 0.18)
    return jnp.clip(with_spikes(values, jax.random.fold_in(key, 3), *heavy), -reach, reach).astype(held_as)


def setup_inputs(seed: int = 0) -> dict:
    key_of = jax.random.split(jax.random.key(seed), 20)
    inputs = normal_values(key_of[0], (SEQS, 2, N_NARROW, GROUP, D), 1.0, 6.0, ((0, 16), (2, 2)))
    cotangent = noise_with(key_of[1], (SEQS, 2, N_NARROW, GROUP, D), 1.0, 6.0, ((0, 16), (2, 2)), (0, 4, 16, 2.0))
    lengths = draw_lengths(jax.random.fold_in(key_of[19], 71), 0)
    w_qkv = normal_values(key_of[3], (D, 3 * D), D ** -0.5, 0.1875)
    b_qkv = normal_values(key_of[4], (3 * D,), 0.3, 1.5, (), jnp.float32)
    w_out = normal_values(key_of[5], (D, D), D ** -0.5, 0.1875)
    b_out = normal_values(key_of[6], (D,), 0.3, 1.5, (), jnp.float32)
    w_up = normal_values(key_of[7], (D, FF), D ** -0.5, 0.1875)
    b_up = normal_values(key_of[8], (FF,), 0.3, 1.5, (), jnp.float32)
    w_down = normal_values(key_of[9], (FF, D), FF ** -0.5, 0.09375)
    b_down = normal_values(key_of[10], (D,), 0.3, 1.5, (), jnp.float32)
    gain_one = jnp.clip(1.0 + 0.1 * jax.random.normal(key_of[11], (D,), jnp.float32), 0.5, 1.5)
    shift_one = normal_values(key_of[12], (D,), 0.3, 1.5, (), jnp.float32)
    gain_two = jnp.clip(1.0 + 0.1 * jax.random.normal(key_of[13], (D,), jnp.float32), 0.5, 1.5)
    shift_two = normal_values(key_of[14], (D,), 0.3, 1.5, (), jnp.float32)
    gain_three = jnp.clip(1.0 + 0.1 * jax.random.normal(key_of[15], (D,), jnp.float32), 0.5, 1.5)
    shift_three = normal_values(key_of[16], (D,), 0.3, 1.5, (), jnp.float32)
    gain_four = jnp.clip(1.0 + 0.1 * jax.random.normal(key_of[17], (D,), jnp.float32), 0.5, 1.5)
    shift_four = normal_values(key_of[18], (D,), 0.3, 1.5, (), jnp.float32)
    return dict(inputs=inputs, cotangent=cotangent, lengths=lengths, w_qkv=w_qkv, b_qkv=b_qkv, w_out=w_out, b_out=b_out, w_up=w_up, b_up=b_up, w_down=w_down, b_down=b_down, gain_one=gain_one, shift_one=shift_one, gain_two=gain_two, shift_two=shift_two, gain_three=gain_three, shift_three=shift_three, gain_four=gain_four, shift_four=shift_four)


EPS = 1e-05

@jax.custom_vjp
def low(v):
    return lax.optimization_barrier(v.astype(jnp.bfloat16)).astype(jnp.float32)

@jax.custom_vjp
def low_back(v):
    return v

def low_keep(v):
    return (low(v), None)

def low_pass(kept, grad):
    return (grad,)

def back_keep(v):
    return (v, None)

def back_low(kept, grad):
    return (low(grad),)
low.defvjp(low_keep, low_pass)
low_back.defvjp(back_keep, back_low)

def layer_norm(values, gain, shift):
    centre = values - lax.optimization_barrier(jnp.mean(values, axis=-1, keepdims=True))
    spread = lax.optimization_barrier(jnp.mean(centre * centre, axis=-1, keepdims=True))
    return centre * lax.rsqrt(spread + EPS) * gain + shift

def smooth(values):
    return jax.nn.gelu(values, approximate=True)

def turn(values, cosine, sine, sign):
    half = values.shape[-1] // 2
    first = values[..., :half]
    second = values[..., half:]
    return jnp.concatenate([first * cosine - sign * second * sine, second * cosine + sign * first * sine], axis=-1)

def angles(positions, half):
    freqs = jnp.power(10000.0, -jnp.arange(half, dtype=jnp.float32) / half)
    theta = positions[:, None] * freqs[None, :]
    return (jnp.cos(theta)[:, None, :], jnp.sin(theta)[:, None, :])

def matmul(left, right):
    return jnp.dot(left, right, precision=lax.Precision.HIGHEST)

def layer(params, tokens, length):
    w_qkv, b_qkv, w_out, b_out, w_up, b_up, w_down, b_down, gain_one, shift_one, gain_two, shift_two, gain_three, shift_three, gain_four, shift_four = params
    width = tokens.shape[1]
    heads = width // HEAD_DIM
    normed = low(layer_norm(tokens, gain_one, shift_one))
    mixed = low_back(matmul(normed, w_qkv) + b_qkv)
    places = jnp.arange(LEN, dtype=jnp.int32)
    cosine, sine = angles(places.astype(jnp.float32), HEAD_DIM // 2)
    query = low_back(low(turn(mixed[:, :width].reshape(LEN, heads, HEAD_DIM), cosine, sine, 1.0)))
    keys = low_back(low(turn(mixed[:, width:2 * width].reshape(LEN, heads, HEAD_DIM), cosine, sine, 1.0)))
    values = low_back(low(mixed[:, 2 * width:].reshape(LEN, heads, HEAD_DIM)))
    block = math.gcd(LEN, 512)

    def attend(index):
        start = index * block
        query_block = lax.dynamic_slice_in_dim(query, start, block, 0)
        scores = jnp.einsum('qhd,khd->hqk', query_block, keys, precision=lax.Precision.HIGHEST) * 0.125
        scores = low_back(scores)
        rows_at = start + jnp.arange(block, dtype=jnp.int32)
        allowed = (places[None, :] <= rows_at[:, None]) & (places[None, :] < length)
        scores = jnp.where(allowed[None], scores, -1e+30)
        peak = lax.optimization_barrier(jnp.max(scores, axis=-1, keepdims=True))
        expo = jnp.exp(scores - peak)
        probs = low(expo / lax.optimization_barrier(jnp.sum(expo, axis=-1, keepdims=True)))
        return jnp.einsum('hqk,khd->qhd', probs, values, precision=lax.Precision.HIGHEST)
    attended = lax.map(jax.checkpoint(attend), jnp.arange(LEN // block, dtype=jnp.int32)).reshape(LEN, width)
    attended = low(low_back(attended))
    branch = low_back(matmul(attended, w_out) + b_out)
    middle = tokens + layer_norm(branch, gain_two, shift_two)
    normed_two = low(layer_norm(middle, gain_three, shift_three))
    inner = low_back(matmul(normed_two, w_up) + b_up)
    hidden = low(smooth(inner))
    outer = low_back(matmul(hidden, w_down) + b_down)
    return middle + layer_norm(outer, gain_four, shift_four)

def to_seq(array):
    count = array.shape[0]
    early = array[:, 0].reshape(count, N_NARROW * GROUP, array.shape[-1])
    late = array[:, 1][:, ::-1].reshape(count, N_NARROW * GROUP, array.shape[-1])
    return jnp.concatenate([early, late], axis=1)

def from_seq(array):
    count = array.shape[0]
    early = array[:, :N_NARROW * GROUP].reshape(count, N_NARROW, GROUP, array.shape[-1])
    late = array[:, N_NARROW * GROUP:].reshape(count, N_NARROW, GROUP, array.shape[-1])[:, ::-1]
    return jnp.stack([early, late], axis=1)

def reference(inputs, cotangent, lengths, w_qkv, b_qkv, w_out, b_out, w_up, b_up, w_down, b_down, gain_one, shift_one, gain_two, shift_two, gain_three, shift_three, gain_four, shift_four):
    params = tuple((item.astype(jnp.float32) for item in (w_qkv, b_qkv, w_out, b_out, w_up, b_up, w_down, b_down, gain_one, shift_one, gain_two, shift_two, gain_three, shift_three, gain_four, shift_four)))
    seq_in = to_seq(inputs.astype(jnp.float32))
    seq_cot = to_seq(cotangent.astype(jnp.float32))

    def step(totals, item):
        tokens, grads_out, length = item
        result, pull = jax.vjp(lambda weights, tokens_in: layer(weights, tokens_in, length), params, tokens)
        grad_params, grad_tokens = pull(grads_out)
        totals = jax.tree.map(lambda left, right: left + right, totals, grad_params)
        return (totals, (result, grad_tokens))
    zeros = jax.tree.map(jnp.zeros_like, params)
    totals, (results, grad_inputs) = lax.scan(step, zeros, (seq_in, seq_cot, lengths))
    output = from_seq(results).astype(jnp.bfloat16)
    input_grad = from_seq(grad_inputs).astype(jnp.bfloat16)
    g_wqkv, g_bqkv, g_wout, g_bout, g_wup, g_bup, g_wdown, g_bdown, g_gone, g_sone, g_gtwo, g_stwo, g_gthree, g_sthree, g_gfour, g_sfour = totals
    return (output, input_grad, g_wqkv, g_wout, g_wup, g_wdown, g_bqkv, g_bout, g_bup, g_bdown, g_gone, g_sone, g_gtwo, g_stwo, g_gthree, g_sthree, g_gfour, g_sfour)
```

```python
import functools

import jax
import jax.numpy as jnp
from jax import lax
from jax.experimental import pallas as pl
from jax.experimental.pallas import tpu as pltpu
from jax.sharding import PartitionSpec as P

HEAD_DIM = 64
PAIR = 2 * HEAD_DIM
EPS = 1e-05
LOG2E = 1.4426950408889634
LN2 = 0.6931471805599453
NEG = -1e30
VMEM = 62 * 1024 * 1024
SPAN = 1024

f32 = jnp.float32
bf16 = jnp.bfloat16


def layer_norm(values, gain, shift):
    centre = values - jnp.mean(values, axis=-1, keepdims=True)
    spread = jnp.mean(centre * centre, axis=-1, keepdims=True)
    return centre * lax.rsqrt(spread + EPS) * gain + shift


def dot(left, right, left_dim, right_dim):
    return lax.dot_general(
        left, right, (((left_dim,), (right_dim,)), ((), ())), preferred_element_type=f32
    )


def fwd_chunk(q0, k0, q_n, k_n, offset, limit, qT, kT, vT, m_ref, l_ref, acc):
    queries = pl.ds(q0, q_n)
    strip = min(256, k_n)
    for h in range(2):
        rows = slice(HEAD_DIM * h, HEAD_DIM * (h + 1))
        old = m_ref[h : h + 1, queries]
        new = old
        strips = []
        for j in range(k_n // strip):
            keys = pl.ds(k0 + j * strip, strip)
            scores = dot(kT[rows, keys], qT[rows, queries], 0, 0)
            if offset is not None or limit is not None:
                key_at = j * strip + lax.broadcasted_iota(jnp.int32, (strip, q_n), 0)
                query_at = lax.broadcasted_iota(jnp.int32, (1, q_n), 1)
                last = jnp.zeros((1, q_n), jnp.int32) + (limit - 1)
                if offset is not None:
                    last = jnp.minimum(query_at + offset, last)
                scores = jnp.where(key_at <= last, scores, NEG)
            strips.append(scores)
            new = jnp.maximum(new, jnp.max(scores, axis=0, keepdims=True))
        factor = jnp.exp2(old - new)
        total = l_ref[h : h + 1, queries] * factor
        value = acc[rows, queries] * factor
        for j in range(k_n // strip):
            keys = pl.ds(k0 + j * strip, strip)
            weights = jnp.exp2(strips[j] - new)
            total = total + jnp.sum(weights, axis=0, keepdims=True)
            value = value + dot(vT[rows, keys], weights.astype(bf16), 1, 0)
        m_ref[h : h + 1, queries] = new
        l_ref[h : h + 1, queries] = total
        acc[rows, queries] = value


def pad_left(values, count):
    if not count:
        return values
    return jnp.concatenate([jnp.zeros((values.shape[0], count), f32), values], axis=1)


def pad_right(values, count):
    if not count:
        return values
    return jnp.concatenate([values, jnp.zeros((values.shape[0], count), f32)], axis=1)


def fwd_diagonal(base, group, qT, kT, vT, m_ref, l_ref, acc):
    strip = min(256, group)
    count = group // strip
    for h in range(2):
        rows = slice(HEAD_DIM * h, HEAD_DIM * (h + 1))
        strips = []
        for j in range(count):
            wide = group - j * strip
            keys, queries = pl.ds(base + j * strip, strip), pl.ds(base + j * strip, wide)
            scores = dot(kT[rows, keys], qT[rows, queries], 0, 0)
            key_at = lax.broadcasted_iota(jnp.int32, scores.shape, 0)
            query_at = lax.broadcasted_iota(jnp.int32, scores.shape, 1)
            strips.append(jnp.where(key_at <= query_at, scores, NEG))
        peaks = []
        for g in range(count):
            peak = None
            for j in range(g + 1):
                part = strips[j][:, (g - j) * strip : (g - j + 1) * strip]
                part = jnp.max(part, axis=0, keepdims=True)
                peak = part if peak is None else jnp.maximum(peak, part)
            peaks.append(peak)
        peak = jnp.concatenate(peaks, axis=1) if count > 1 else peaks[0]
        total, value = None, None
        for j in range(count):
            keys = pl.ds(base + j * strip, strip)
            weights = jnp.exp2(strips[j] - peak[:, j * strip :])
            part = pad_left(jnp.sum(weights, axis=0, keepdims=True), j * strip)
            term = pad_left(dot(vT[rows, keys], weights.astype(bf16), 1, 0), j * strip)
            total = part if total is None else total + part
            value = term if value is None else value + term
        queries = pl.ds(base, group)
        m_ref[h : h + 1, queries] = peak
        l_ref[h : h + 1, queries] = total
        acc[rows, queries] = value


def fwd_local_kernel(group, info, qT, kT, vT, acc, m_ref, l_ref):
    length = info[1]
    m_ref[...] = jnp.full(m_ref.shape, NEG, f32)
    l_ref[...] = jnp.zeros(l_ref.shape, f32)
    acc[...] = jnp.zeros(acc.shape, f32)
    refs = (qT, kT, vT, m_ref.at[0], l_ref.at[0], acc)

    def own(i, carry):
        base = pl.multiple_of(i * group, group)
        start = info[2 + i]

        @pl.when(start + group <= length)
        def _():
            fwd_diagonal(base, group, *refs)

        @pl.when((start < length) & (start + group > length))
        def _():
            fwd_chunk(base, base, group, group, 0, length - start, *refs)

        return carry

    lax.fori_loop(0, 2, own, 0)
    early = info[2]

    @pl.when(early + group <= length)
    def _():
        fwd_chunk(group, 0, group, group, None, None, *refs)

    @pl.when((early < length) & (early + group > length))
    def _():
        fwd_chunk(group, 0, group, group, None, length - early, *refs)


def remote_steps(group, parts, kind, info, full, partial):
    place, length = info[0], info[1]

    def visit(q_block, k_slot, k_block, wanted):
        q0 = pl.multiple_of(q_block * group, group)
        k0 = pl.multiple_of(k_slot * group, group)
        start = k_block * group

        @pl.when(wanted & (start + group <= length))
        def _():
            full(q0, k0)

        @pl.when(wanted & (start < length) & (start + group > length))
        def _():
            partial(q0, k0, length - start)

    others = parts - 1

    def early(i, carry):
        j = i // 2
        other = lax.rem(place + 1 + j, parts)
        late_query = lax.rem(i, 2)
        visit(late_query, j, other, (late_query == 1) | (other < place))
        return carry

    def late(j, carry):
        other = lax.rem(place + 1 + j, parts)
        slot = j + (others if kind == 2 else 0)
        visit(1, slot, 2 * parts - 1 - other, other > place)
        return carry

    if kind == 2:

        def both(i, carry):
            is_early = i < 2 * others
            j = jnp.where(is_early, i // 2, i - 2 * others)
            other = lax.rem(place + 1 + j, parts)
            late_query = jnp.where(is_early, lax.rem(i, 2), 1)
            slot = jnp.where(is_early, j, j + others)
            block = jnp.where(is_early, other, 2 * parts - 1 - other)
            wanted = jnp.where(
                is_early,
                ((late_query == 1) | (other < place)).astype(jnp.int32),
                (other > place).astype(jnp.int32),
            )
            visit(late_query, slot, block, wanted == 1)
            return carry

        lax.fori_loop(0, 3 * others, both, 0)
    elif kind == 0:
        lax.fori_loop(0, 2 * others, early, 0)
    else:
        lax.fori_loop(0, others, late, 0)


def fwd_remote_kernel(
    group, parts, kind, last, info, qT, kT, vT, acc_in, m_in, l_in, out, m_out, l_out, *scratch
):
    acc = scratch[0] if last else out
    acc[...] = acc_in[...]
    m_out[...] = m_in[...]
    l_out[...] = l_in[...]
    refs = (qT, kT, vT, m_out.at[0], l_out.at[0], acc)

    def full(q0, k0):
        fwd_chunk(q0, k0, group, group, None, None, *refs)

    def partial(q0, k0, limit):
        fwd_chunk(q0, k0, group, group, None, limit, *refs)

    remote_steps(group, parts, kind, info, full, partial)
    if last:
        for h in range(2):
            rows = slice(HEAD_DIM * h, HEAD_DIM * (h + 1))
            total = l_out[0, h : h + 1, :]
            out[rows, :] = (acc[rows, :] / total).astype(bf16)
            m_out[0, h : h + 1, :] = m_out[0, h : h + 1, :] + jnp.log2(total)


def split_three(values):
    high = values.astype(bf16).astype(f32)
    rest = values - high
    middle = rest.astype(bf16).astype(f32)
    low = (rest - middle).astype(bf16).astype(f32)
    return [high, middle, low]


def bwd_prepare(qT, kT, vT, doT, oT, lse, qa, da, ka, va):
    n_q, n_k = qT.shape[1], kT.shape[1]
    extra = qa.shape[1] - HEAD_DIM
    pad = jnp.zeros((extra - 3, n_q), f32)
    row_at = lax.broadcasted_iota(jnp.int32, (extra, n_k), 0)
    tail = jnp.where(row_at < 3, 1.0, 0.0).astype(bf16)
    for h in range(2):
        rows = slice(HEAD_DIM * h, HEAD_DIM * (h + 1))
        grad = doT[rows, :].astype(f32)
        delta = jnp.sum(grad * oT[rows, :].astype(f32), axis=0, keepdims=True)
        qa[h, :HEAD_DIM, :] = qT[rows, :]
        parts = split_three(-lse[0, h : h + 1, :]) + [pad]
        qa[h, HEAD_DIM:, :] = jnp.concatenate(parts, axis=0).astype(bf16)
        da[h, :HEAD_DIM, :] = doT[rows, :]
        parts = split_three(-delta) + [pad]
        da[h, HEAD_DIM:, :] = jnp.concatenate(parts, axis=0).astype(bf16)
        ka[h, :HEAD_DIM, :] = kT[rows, :]
        ka[h, HEAD_DIM:, :] = tail
        va[h, :HEAD_DIM, :] = vT[rows, :]
        va[h, HEAD_DIM:, :] = tail


def bwd_chunk(q0, k0, q_n, k_n, offset, limit, qT, kT, doT, qa, da, ka, va, dq, dk, dv):
    queries, keys = pl.ds(q0, q_n), pl.ds(k0, k_n)
    for h in range(2):
        rows = slice(HEAD_DIM * h, HEAD_DIM * (h + 1))
        probs = jnp.exp2(dot(qa[h, :, queries], ka[h, :, keys], 0, 0))
        if offset is not None or limit is not None:
            key_at = lax.broadcasted_iota(jnp.int32, (q_n, k_n), 1)
            last = jnp.zeros((q_n, 1), jnp.int32) + (limit - 1)
            if offset is not None:
                query_at = lax.broadcasted_iota(jnp.int32, (q_n, 1), 0)
                last = jnp.minimum(query_at + offset, last)
            probs = jnp.where(key_at <= last, probs, 0.0)
        d_probs = dot(da[h, :, queries], va[h, :, keys], 0, 0)
        d_scores = (probs * d_probs).astype(bf16)
        dv[rows, keys] += dot(doT[rows, queries], probs.astype(bf16), 1, 0)
        dk[rows, keys] += dot(qT[rows, queries], d_scores, 1, 0)
        dq[rows, queries] += dot(kT[rows, keys], d_scores, 1, 1)


def bwd_diagonal(base, group, qT, kT, doT, qa, da, ka, va, dq, dk, dv):
    strip = min(256, group)
    count = group // strip
    for h in range(2):
        rows = slice(HEAD_DIM * h, HEAD_DIM * (h + 1))
        d_keys, d_values, d_queries = None, None, []
        for j in range(count):
            wide = (j + 1) * strip
            queries, keys = pl.ds(base + j * strip, strip), pl.ds(base, wide)
            probs = jnp.exp2(dot(qa[h, :, queries], ka[h, :, keys], 0, 0))
            query_at = lax.broadcasted_iota(jnp.int32, probs.shape, 0)
            key_at = lax.broadcasted_iota(jnp.int32, probs.shape, 1)
            probs = jnp.where(key_at <= query_at + j * strip, probs, 0.0)
            d_probs = dot(da[h, :, queries], va[h, :, keys], 0, 0)
            d_scores = (probs * d_probs).astype(bf16)
            value = pad_right(dot(doT[rows, queries], probs.astype(bf16), 1, 0), group - wide)
            key = pad_right(dot(qT[rows, queries], d_scores, 1, 0), group - wide)
            d_values = value if d_values is None else d_values + value
            d_keys = key if d_keys is None else d_keys + key
            d_queries.append(dot(kT[rows, keys], d_scores, 1, 1))
        here = pl.ds(base, group)
        dq[rows, here] += jnp.concatenate(d_queries, axis=1) if count > 1 else d_queries[0]
        dk[rows, here] += d_keys
        dv[rows, here] += d_values


def turn_back(values, cosine, sine):
    half = HEAD_DIM // 2
    first, second = values[:half], values[half:]
    return jnp.concatenate(
        [first * cosine + second * sine, second * cosine - first * sine], axis=0
    )


def bwd_remote_kernel(group, parts, info, qT, kT, vT, doT, oT, lse, cosine, sine, *rest):
    dq, dkv, *scratch = rest[-8:]
    qa, da, ka, va, dk, dv = scratch
    bwd_prepare(qT, kT, vT, doT, oT, lse, qa, da, ka, va)
    dq[...] = jnp.zeros(dq.shape, f32)
    dk[...] = jnp.zeros(dk.shape, f32)
    dv[...] = jnp.zeros(dv.shape, f32)
    refs = (qT, kT, doT, qa, da, ka, va, dq, dk, dv)

    def full(q0, k0):
        bwd_chunk(q0, k0, group, group, None, None, *refs)

    def partial(q0, k0, limit):
        bwd_chunk(q0, k0, group, group, None, limit, *refs)

    remote_steps(group, parts, 2, info, full, partial)
    for h in range(2):
        rows = slice(HEAD_DIM * h, HEAD_DIM * (h + 1))
        dkv[0, rows, :] = turn_back(dk[rows, :] * LN2, cosine[...], sine[...]).astype(bf16)
    dkv[1] = dv[...].astype(bf16)


def bwd_local_kernel(group, info, qT, kT, vT, doT, oT, lse, cosine, sine, dq_in, *rest):
    dqkv, *scratch = rest[-8:]
    qa, da, ka, va, dq, dk, dv = scratch
    length = info[1]
    bwd_prepare(qT, kT, vT, doT, oT, lse, qa, da, ka, va)
    dq[...] = dq_in[...]
    dk[...] = jnp.zeros(dk.shape, f32)
    dv[...] = jnp.zeros(dv.shape, f32)
    refs = (qT, kT, doT, qa, da, ka, va, dq, dk, dv)

    def own(i, carry):
        base = pl.multiple_of(i * group, group)
        start = info[2 + i]

        @pl.when(start + group <= length)
        def _():
            bwd_diagonal(base, group, *refs)

        @pl.when((start < length) & (start + group > length))
        def _():
            bwd_chunk(base, base, group, group, 0, length - start, *refs)

        return carry

    lax.fori_loop(0, 2, own, 0)
    early = info[2]

    @pl.when(early + group <= length)
    def _():
        bwd_chunk(group, 0, group, group, None, None, *refs)

    @pl.when((early < length) & (early + group > length))
    def _():
        bwd_chunk(group, 0, group, group, None, length - early, *refs)

    for h in range(2):
        rows = slice(HEAD_DIM * h, HEAD_DIM * (h + 1))
        d_query = dq[rows, :] * 0.125
        dqkv[0, rows, :] = turn_back(d_query, cosine[...], sine[...]).astype(bf16)
        dqkv[1, rows, :] = turn_back(dk[rows, :] * LN2, cosine[...], sine[...]).astype(bf16)
    dqkv[2] = dv[...].astype(bf16)


def rows_of(count, first=0):
    return pl.BlockSpec((PAIR, count), lambda i, info: (first + i, 0))


def stats_of(count, first=0):
    return pl.BlockSpec((1, 2, count), lambda i, info: (first + i, 0, 0))


def planes_of(planes, count, first=0):
    return pl.BlockSpec((planes, PAIR, count), lambda i, info: (0, first + i, 0))


def whole(shape):
    return pl.BlockSpec(shape, lambda i, info: (0,) * len(shape))


def attention_call(kernel, pairs, in_specs, out_specs, out_shape, scratch, flops, name, alias={}):
    return pl.pallas_call(
        kernel,
        grid_spec=pltpu.PrefetchScalarGridSpec(
            num_scalar_prefetch=1,
            grid=(pairs,),
            in_specs=in_specs,
            out_specs=out_specs,
            scratch_shapes=scratch,
        ),
        out_shape=out_shape,
        input_output_aliases=alias,
        compiler_params=pltpu.CompilerParams(vmem_limit_bytes=VMEM),
        cost_estimate=pl.CostEstimate(
            flops=int(flops), bytes_accessed=1 << 25, transcendentals=0
        ),
        name=name,
    )


def attend_local(info, qT, kT, vT, group):
    width, n_q = qT.shape
    pairs = width // PAIR
    call = attention_call(
        functools.partial(fwd_local_kernel, group),
        pairs,
        [rows_of(n_q)] * 3,
        [rows_of(n_q), stats_of(n_q), stats_of(n_q)],
        [
            jax.ShapeDtypeStruct((width, n_q), f32),
            jax.ShapeDtypeStruct((pairs, 2, n_q), f32),
            jax.ShapeDtypeStruct((pairs, 2, n_q), f32),
        ],
        [],
        4 * width * 2 * group * group * 4,
        "attend_local",
    )
    return call(info, qT, kT, vT)


def attend_remote(info, qT, kT, vT, state, group, parts, kind, last):
    width, n_q = qT.shape
    n_k = kT.shape[1]
    pairs = width // PAIR
    scratch = [pltpu.VMEM((PAIR, n_q), f32)] if last else []
    call = attention_call(
        functools.partial(fwd_remote_kernel, group, parts, kind, last),
        pairs,
        [rows_of(n_q), rows_of(n_k), rows_of(n_k), rows_of(n_q), stats_of(n_q), stats_of(n_q)],
        [rows_of(n_q), stats_of(n_q), stats_of(n_q)],
        [
            jax.ShapeDtypeStruct((width, n_q), bf16 if last else f32),
            jax.ShapeDtypeStruct((pairs, 2, n_q), f32),
            jax.ShapeDtypeStruct((pairs, 2, n_q), f32),
        ],
        scratch,
        4 * width * group * group * 4,
        "attend_remote",
    )
    return call(info, qT, kT, vT, *state)


def back_scratch(n_q, n_k):
    rows = HEAD_DIM + 16
    return [
        pltpu.VMEM((2, rows, n_q), bf16),
        pltpu.VMEM((2, rows, n_q), bf16),
        pltpu.VMEM((2, rows, n_k), bf16),
        pltpu.VMEM((2, rows, n_k), bf16),
    ]


def back_remote(info, operands, lse, turns, group, parts, first, count, before):
    qT, kT = operands[:2]
    width, n_q = qT.shape
    n_k = kT.shape[1]
    half = HEAD_DIM // 2
    n_in = 1 + len(operands) + 1 + len(turns)
    call = attention_call(
        functools.partial(bwd_remote_kernel, group, parts),
        count,
        [rows_of(n_q, first), rows_of(n_k, first), rows_of(n_k, first)]
        + [rows_of(n_q, first)] * 2
        + [stats_of(n_q, first)]
        + [whole((half, n_k))] * 2
        + [pl.BlockSpec(memory_space=pl.ANY)] * len(before),
        [rows_of(n_q, first), planes_of(2, n_k, first)],
        [
            jax.ShapeDtypeStruct((width, n_q), f32),
            jax.ShapeDtypeStruct((2, width, n_k), bf16),
        ],
        back_scratch(n_q, n_k) + [pltpu.VMEM((PAIR, n_k), f32)] * 2,
        10 * count * PAIR * 2 * group * group * 4,
        "back_remote",
        {n_in + i: i for i in range(len(before))},
    )
    return call(info, *operands, lse, *turns, *before)


def back_local(info, operands, lse, turns, dq, group, first, count, before):
    qT = operands[0]
    width, n_q = qT.shape
    half = HEAD_DIM // 2
    n_in = 1 + len(operands) + 1 + len(turns) + 1
    call = attention_call(
        functools.partial(bwd_local_kernel, group),
        count,
        [rows_of(n_q, first)] * 5
        + [stats_of(n_q, first)]
        + [whole((half, n_q))] * 2
        + [rows_of(n_q, first)]
        + [pl.BlockSpec(memory_space=pl.ANY)] * len(before),
        planes_of(3, n_q, first),
        jax.ShapeDtypeStruct((3, width, n_q), bf16),
        back_scratch(n_q, n_q) + [pltpu.VMEM((PAIR, n_q), f32)] * 3,
        10 * count * PAIR * 2 * group * group * 4,
        "back_local",
        {n_in + i: i for i in range(len(before))},
    )
    return call(info, *operands, lse, *turns, dq, *before)


def normalize(values):
    centre = values - jnp.mean(values, axis=-1, keepdims=True)
    spread = jnp.mean(centre * centre, axis=-1, keepdims=True)
    rate = lax.rsqrt(spread + EPS)
    return centre * rate, rate


def norm_back(grad, unit, rate, gain):
    scaled = grad * gain
    first = jnp.mean(scaled, axis=-1, keepdims=True)
    second = jnp.mean(scaled * unit, axis=-1, keepdims=True)
    return rate * (scaled - first - unit * second)


GELU_A = 0.7978845608028654
GELU_B = 0.044715


def column_sum(values):
    return jnp.sum(values, axis=0, keepdims=True)


def block_kernel(
    span,
    oT,
    tokens,
    cotangent,
    w_out,
    w_up,
    w_down,
    b_out,
    b_up,
    b_down,
    gain_two,
    shift_two,
    gain_three,
    shift_three,
    gain_four,
    shift_four,
    result,
    d_middle_out,
    hidden_out,
    d_outer_out,
    normed_out,
    d_inner_out,
    d_branch_out,
    doT,
    small,
    small_up,
    slope,
):
    step = pl.program_id(0)

    @pl.when(step == 0)
    def _():
        small[...] = jnp.zeros(small.shape, f32)
        small_up[...] = jnp.zeros(small_up.shape, f32)

    wide = w_up.shape[1]
    branch = dot(oT[...], w_out[...], 0, 0) + b_out[...]
    unit_two, rate_two = normalize(branch)
    middle = tokens[...].astype(f32) + (unit_two * gain_two[...] + shift_two[...])
    unit_three, rate_three = normalize(middle)
    normed = (unit_three * gain_three[...] + shift_three[...]).astype(bf16)
    normed_out[...] = normed
    outer = None
    for c in range(wide // span):
        columns = slice(c * span, (c + 1) * span)
        inner = dot(normed, w_up[:, columns], 1, 0) + b_up[:, columns]
        square = inner * inner
        bend = jnp.tanh(inner * (GELU_A + (GELU_A * GELU_B) * square))
        half = 0.5 + 0.5 * bend
        hidden = (inner * half).astype(bf16)
        hidden_out[:, columns] = hidden
        slope[:, columns] = half + inner * (1.0 - bend * bend) * (
            0.5 * GELU_A + (1.5 * GELU_A * GELU_B) * square
        )
        term = dot(hidden, w_down[columns, :], 1, 0)
        outer = term if outer is None else outer + term
    unit_four, rate_four = normalize(outer + b_down[...])
    result[...] = (middle + (unit_four * gain_four[...] + shift_four[...])).astype(bf16)

    grad = cotangent[...].astype(f32)
    d_outer = norm_back(grad, unit_four, rate_four, gain_four[...]).astype(bf16)
    d_outer_out[...] = d_outer
    small[0:1, :] += column_sum(grad * unit_four)
    small[1:2, :] += column_sum(grad)
    small[2:3, :] += column_sum(d_outer.astype(f32))
    d_normed = None
    for c in range(wide // span):
        columns = slice(c * span, (c + 1) * span)
        d_hidden = dot(d_outer, w_down[columns, :], 1, 1)
        d_inner = (d_hidden * slope[:, columns]).astype(bf16)
        d_inner_out[:, columns] = d_inner
        small_up[:, columns] += column_sum(d_inner.astype(f32))
        term = dot(d_inner, w_up[:, columns], 1, 1)
        d_normed = term if d_normed is None else d_normed + term
    small[3:4, :] += column_sum(d_normed * unit_three)
    small[4:5, :] += column_sum(d_normed)
    d_middle = grad + norm_back(d_normed, unit_three, rate_three, gain_three[...])
    d_middle_out[...] = d_middle
    small[5:6, :] += column_sum(d_middle * unit_two)
    small[6:7, :] += column_sum(d_middle)
    d_branch = norm_back(d_middle, unit_two, rate_two, gain_two[...]).astype(bf16)
    d_branch_out[...] = d_branch
    small[7:8, :] += column_sum(d_branch.astype(f32))
    doT[...] = dot(w_out[...], d_branch, 1, 1).astype(bf16)


def block_call(oT, tokens, cotangent, weights, vectors):
    width, rows = oT.shape
    wide = weights[1].shape[1]
    step = min(256, rows)
    span = min(SPAN, wide)

    def lines(count):
        return pl.BlockSpec((step, count), lambda i: (i, 0))

    def fixed(shape):
        return pl.BlockSpec(shape, lambda i: (0, 0), pipeline_mode=pl.Buffered(1))

    def total(shape):
        return pl.BlockSpec(shape, lambda i: (0, 0))

    features = pl.BlockSpec((width, step), lambda i: (0, i))
    sizes = [width, width, wide, width, width, wide, width]
    kinds = [bf16, f32, bf16, bf16, bf16, bf16, bf16]
    return pl.pallas_call(
        functools.partial(block_kernel, span),
        grid=(rows // step,),
        in_specs=[features, lines(width), lines(width)]
        + [fixed(item.shape) for item in weights]
        + [fixed(item.shape) for item in vectors],
        out_specs=[lines(size) for size in sizes]
        + [features, total((8, width)), total((1, wide))],
        out_shape=[jax.ShapeDtypeStruct((rows, size), kind) for size, kind in zip(sizes, kinds)]
        + [
            jax.ShapeDtypeStruct((width, rows), bf16),
            jax.ShapeDtypeStruct((8, width), f32),
            jax.ShapeDtypeStruct((1, wide), f32),
        ],
        scratch_shapes=[pltpu.VMEM((step, wide), f32)],
        compiler_params=pltpu.CompilerParams(vmem_limit_bytes=VMEM),
        cost_estimate=pl.CostEstimate(
            flops=2 * 2 * rows * (width * width + 2 * width * wide),
            bytes_accessed=1 << 26,
            transcendentals=rows * wide,
        ),
        name="block",
    )(oT, tokens, cotangent, *weights, *vectors)


def bit_of(axis, position):
    return (lax.axis_index(axis) >> position) & 1


def swap(values, axis, position):
    size = lax.axis_size(axis)
    return lax.ppermute(values, axis, [(i, i ^ (1 << position)) for i in range(size)])


class Halving:
    def __init__(self, array, bits, order):
        self.bits = list(bits)
        self.order = list(order)
        rows = array.shape[0] >> len(bits)
        self.array = array.reshape((2,) * len(bits) + (rows, array.shape[1]))
        self.kept = self.received = None

    def send(self):
        bit = self.order.pop(0)
        at = self.bits.index(bit)
        mine = bit_of(*bit)
        away = lax.dynamic_index_in_dim(self.array, 1 - mine, at, False)
        self.kept = (self.array, mine, at)
        self.received = swap(away, *bit)
        self.bits.pop(at)

    def add(self):
        array, mine, at = self.kept
        kept = lax.dynamic_index_in_dim(array, mine, at, False).astype(f32)
        total = kept + self.received.astype(f32)
        self.array = total.astype(bf16) if self.bits else total

    def result(self):
        return self.array


class Adding:
    def __init__(self, array, order):
        self.array, self.order = array, list(order)

    def send(self):
        self.received = swap(self.array, *self.order.pop(0))

    def add(self):
        self.array = self.array + self.received


def tie(lead, sums):
    held, arrays = lax.optimization_barrier((lead, [item.array for item in sums]))
    for item, array in zip(sums, arrays):
        item.array = array
    return held


def turn_forward(values, cosine, sine):
    features, tokens = values.shape
    half = HEAD_DIM // 2
    pairs = values.reshape(features // HEAD_DIM, 2, half, tokens)
    first, second = pairs[:, 0], pairs[:, 1]
    turned = jnp.stack(
        [first * cosine - second * sine, second * cosine + first * sine], axis=1
    )
    return turned.reshape(features, tokens)


def angles(positions):
    half = HEAD_DIM // 2
    freqs = jnp.power(10000.0, -jnp.arange(half, dtype=f32) / half)
    theta = freqs[:, None] * positions.astype(f32)[None, :]
    return jnp.cos(theta), jnp.sin(theta)


def axis_bits(axis):
    return [(axis, position) for position in range(lax.axis_size(axis).bit_length() - 1)]


def body(
    inputs,
    cotangent,
    lengths,
    w_qkv,
    b_qkv,
    w_out,
    b_out,
    w_up,
    b_up,
    w_down,
    b_down,
    gain_one,
    shift_one,
    gain_two,
    shift_two,
    gain_three,
    shift_three,
    gain_four,
    shift_four,
):
    group = inputs.shape[3]
    width = inputs.shape[4]
    parts = lax.axis_size("narrow")
    place = lax.axis_index("narrow")
    others = parts - 1
    rows = 2 * group
    offsets = jnp.arange(group, dtype=jnp.int32)

    own_blocks = inputs.reshape(2, group, width)
    far_early, far_late = [], []
    for shift in range(1, parts):
        pairs = [((n + shift) % parts, n) for n in range(parts)]
        far_early.append(lax.ppermute(own_blocks[0], "narrow", pairs))
    for shift in range(1, parts):
        pairs = [((n + shift) % parts, n) for n in range(parts)]
        later = [(source, n) for source, n in pairs if source > n]
        far_late.append(lax.ppermute(own_blocks[1], "narrow", later))
    other = (place + 1 + jnp.arange(others, dtype=jnp.int32)) % parts

    early_at = place * group
    late_at = (2 * parts - 1 - place) * group
    info = jnp.stack([place, lengths[0], early_at, late_at]).astype(jnp.int32)
    own_pos = jnp.concatenate([early_at + offsets, late_at + offsets])
    far_early_pos = (other[:, None] * group + offsets[None]).reshape(-1)
    far_late_pos = ((2 * parts - 1 - other)[:, None] * group + offsets[None]).reshape(-1)
    cosine, sine = angles(own_pos)
    cosine_fe, sine_fe = angles(far_early_pos)
    cosine_fl, sine_fl = angles(far_late_pos)

    tokens = own_blocks.astype(f32).reshape(rows, width)
    normed_low = layer_norm(tokens, gain_one, shift_one).astype(bf16)
    mixedT = dot(w_qkv, normed_low, 0, 1) + b_qkv[:, None]
    qT = (turn_forward(mixedT[:width], cosine, sine) * (0.125 * LOG2E)).astype(bf16)
    kT = turn_forward(mixedT[width : 2 * width], cosine, sine).astype(bf16)
    vT = mixedT[2 * width :].astype(bf16)
    state = attend_local(info, qT, kT, vT, group)

    def far_keys(blocks, cos, sin):
        far = jnp.concatenate(blocks, axis=0).astype(f32)
        far_normed = layer_norm(far, gain_one, shift_one).astype(bf16)
        far_mixed = dot(w_qkv[:, width:], far_normed, 0, 1) + b_qkv[width:, None]
        keys = turn_forward(far_mixed[:width], cos, sin).astype(bf16)
        return far_normed, keys, far_mixed[width:].astype(bf16)

    normed_fe, kT_fe, vT_fe = far_keys(far_early, cosine_fe, sine_fe)
    state = attend_remote(info, qT, kT_fe, vT_fe, state, group, parts, 0, False)
    normed_fl, kT_fl, vT_fl = far_keys(far_late, cosine_fl, sine_fl)
    oT, lse, _ = attend_remote(info, qT, kT_fl, vT_fl, state, group, parts, 1, True)

    row = lambda vector: vector[None, :]
    blocks = block_call(
        oT,
        own_blocks.reshape(rows, width),
        cotangent.reshape(rows, width),
        [w_out, w_up, w_down],
        [row(item) for item in (b_out, b_up, b_down)]
        + [row(item) for item in (gain_two, shift_two, gain_three, shift_three)]
        + [row(item) for item in (gain_four, shift_four)],
    )
    result, d_middle, hidden, d_outer, normed_two, d_inner, d_branch, doT, small, small_up = blocks

    wide_bits = axis_bits("wide")
    narrow_bits = axis_bits("narrow")
    bits = wide_bits[::-1] + narrow_bits[::-1]
    first_order = wide_bits[:2] + narrow_bits + wide_bits[2:]
    second_order = wide_bits[:1] + narrow_bits + wide_bits[1:]
    steps = len(bits)

    sum_down = Halving(dot(d_outer, hidden, 0, 0).astype(bf16), bits, second_order)
    sum_down.send()
    sum_up = Halving(dot(d_inner, normed_two, 0, 0).astype(bf16), bits, first_order)
    sum_up.send()
    sum_out = Halving(dot(d_branch, oT, 0, 1).astype(bf16), bits, first_order)
    sum_out.send()
    early = Adding(jnp.concatenate([small.reshape(-1), small_up.reshape(-1)]), first_order)
    early.send()
    sums = [sum_down, sum_up, sum_out, early]

    def advance(lead):
        for item in sums:
            item.add()
        lead = tie(lead, sums)
        if sum_down.order:
            for item in sums:
                item.send()
        return lead

    kT_far = jnp.concatenate([kT_fe, kT_fl], axis=1)
    vT_far = jnp.concatenate([vT_fe, vT_fl], axis=1)
    turns_far = [
        jnp.concatenate([cosine_fe, cosine_fl], axis=1),
        jnp.concatenate([sine_fe, sine_fl], axis=1),
    ]
    heads = width // PAIR
    portions = 2 if heads % 2 == 0 else 1
    count = heads // portions
    far = []
    for portion in range(portions):
        doT = advance(doT)
        operands = [qT, kT_far, vT_far, doT, oT]
        far = back_remote(
            info, operands, lse, turns_far, group, parts, portion * count, count, far
        )
    dq_far, dkv_far = far
    dkv_far = dkv_far.reshape(2 * width, -1)
    w_qkvT = w_qkv.T
    d_normed_far = dot(dkv_far, w_qkvT[width:], 0, 0).astype(bf16)
    returned_early, returned_late = [], []
    for j in range(others):
        shift = j + 1
        pairs = [(n, (n + shift) % parts) for n in range(parts)]
        piece = d_normed_far[j * group : (j + 1) * group]
        returned_early.append(lax.ppermute(piece, "narrow", pairs))
    for j in range(others):
        shift = j + 1
        pairs = [(n, (n + shift) % parts) for n in range(parts)]
        later = [(n, owner) for n, owner in pairs if owner > n]
        piece = d_normed_far[(others + j) * group : (others + j + 1) * group]
        returned_late.append(lax.ppermute(piece, "narrow", later))
    dqkv = []
    for portion in range(portions):
        doT = advance(doT)
        operands = [qT, kT, vT, doT, oT]
        dqkv = [
            back_local(
                info, operands, lse, [cosine, sine], dq_far, group, portion * count, count, dqkv
            )
        ]
    dqkv = dqkv[0].reshape(3 * width, rows)
    while sum_down.order:
        dqkv = advance(dqkv)
    for item in sums:
        item.add()

    normed_far = jnp.concatenate([normed_fe, normed_fl], axis=0)
    grad_q = dot(dqkv[:width], normed_low, 1, 0)
    grad_kv = dot(dqkv[width:], normed_low, 1, 0) + dot(dkv_far, normed_far, 1, 0)
    grad_w_qkv = jnp.concatenate([grad_q.astype(bf16), grad_kv.astype(bf16)], axis=0)
    share = grad_w_qkv.shape[0] >> steps
    cut = share // 2
    pieces = grad_w_qkv.reshape(1 << steps, share, width)
    sum_first = Halving(pieces[:, :cut].reshape(-1, width), bits, first_order)
    sum_second = Halving(pieces[:, cut:].reshape(-1, width), bits, second_order)
    sum_first.send()
    sum_second.send()
    grad_b_qkv = jnp.sum(dqkv.astype(f32), axis=1) + jnp.concatenate(
        [jnp.zeros((width,), f32), jnp.sum(dkv_far.astype(f32), axis=1)]
    )
    weighted = w_qkvT.astype(f32)
    part_shift = jnp.sum(weighted * grad_b_qkv[:, None], axis=0)
    part_gain = jnp.sum(weighted * grad_w_qkv.astype(f32), axis=0)
    part_gain = (part_gain - shift_one * part_shift) / gain_one
    late = Adding(jnp.concatenate([grad_b_qkv, part_gain, part_shift]), first_order)
    late.send()
    sums = [sum_first, sum_second, late]

    dqkv = tie(dqkv, [])
    d_normed = dot(dqkv, w_qkvT, 0, 0)
    for item in sums:
        item.add()
    d_normed = tie(d_normed, sums)
    for item in sums:
        item.send()
    back_early = functools.reduce(jnp.add, [item.astype(f32) for item in returned_early])
    back_late = functools.reduce(jnp.add, [item.astype(f32) for item in returned_late])
    d_normed = d_normed + jnp.concatenate([back_early, back_late], axis=0)
    unit_one, rate_one = normalize(tokens)
    d_tokens = d_middle + norm_back(d_normed, unit_one, rate_one, gain_one)
    d_tokens = d_tokens.astype(bf16)
    while sum_first.order:
        for item in sums:
            item.add()
        d_tokens = tie(d_tokens, sums)
        for item in sums:
            item.send()
    for item in sums:
        item.add()

    qkv_rows = jnp.concatenate([sum_first.result(), sum_second.result()], axis=0)
    down_rows = sum_down.result().reshape(-1, w_down.shape[0])
    wide = w_up.shape[1]
    small = early.array[: 8 * width].reshape(8, width)
    small_up = early.array[8 * width :]
    late_small = late.array
    shape = inputs.shape
    return (
        result.reshape(shape),
        d_tokens.reshape(shape),
        qkv_rows.T,
        sum_out.result().T,
        sum_up.result().T,
        down_rows.T,
        late_small[: 3 * width],
        small[7],
        small_up,
        small[2],
        late_small[3 * width : 4 * width],
        late_small[4 * width :],
        small[5],
        small[6],
        small[3],
        small[4],
        small[0],
        small[1],
    )


def solution(mesh):
    tokens = P("wide", None, "narrow", None, None)
    columns = P(None, ("wide", "narrow"))
    in_specs = (tokens, tokens, P("wide")) + (P(),) * 16
    out_specs = (tokens, tokens) + (columns,) * 4 + (P(),) * 12
    return jax.shard_map(body, mesh=mesh, in_specs=in_specs, out_specs=out_specs, check_vma=False)
```

```python
import functools

import jax
import jax.numpy as jnp
from jax import lax
from jax.experimental import pallas as pl
from jax.experimental.pallas import tpu as pltpu
from jax.sharding import PartitionSpec as P

HEAD_DIM = 64
PAIR = 2 * HEAD_DIM
EPS = 1e-05
LOG2E = 1.4426950408889634
LN2 = 0.6931471805599453
NEG = -1e30
VMEM = 62 * 1024 * 1024
SPAN = 1024

f32 = jnp.float32
bf16 = jnp.bfloat16


def dot(left, right, left_dim, right_dim):
    return lax.dot_general(
        left, right, (((left_dim,), (right_dim,)), ((), ())), preferred_element_type=f32
    )


def fwd_chunk(q0, k0, q_n, k_n, offset, limit, qT, kT, vT, m_ref, l_ref, acc):
    queries = pl.ds(q0, q_n)
    strip = min(256, k_n)
    for h in range(2):
        rows = slice(HEAD_DIM * h, HEAD_DIM * (h + 1))
        old = m_ref[h : h + 1, queries]
        new = old
        strips = []
        for j in range(k_n // strip):
            keys = pl.ds(k0 + j * strip, strip)
            scores = dot(kT[rows, keys], qT[rows, queries], 0, 0)
            if offset is not None or limit is not None:
                key_at = j * strip + lax.broadcasted_iota(jnp.int32, (strip, q_n), 0)
                query_at = lax.broadcasted_iota(jnp.int32, (1, q_n), 1)
                last = jnp.zeros((1, q_n), jnp.int32) + (limit - 1)
                if offset is not None:
                    last = jnp.minimum(query_at + offset, last)
                scores = jnp.where(key_at <= last, scores, NEG)
            strips.append(scores)
            new = jnp.maximum(new, jnp.max(scores, axis=0, keepdims=True))
        factor = jnp.exp2(old - new)
        total = l_ref[h : h + 1, queries] * factor
        value = acc[rows, queries] * factor
        for j in range(k_n // strip):
            keys = pl.ds(k0 + j * strip, strip)
            weights = jnp.exp2(strips[j] - new)
            total = total + jnp.sum(weights, axis=0, keepdims=True)
            value = value + dot(vT[rows, keys], weights.astype(bf16), 1, 0)
        m_ref[h : h + 1, queries] = new
        l_ref[h : h + 1, queries] = total
        acc[rows, queries] = value


def pad_left(values, count):
    if not count:
        return values
    return jnp.concatenate([jnp.zeros((values.shape[0], count), f32), values], axis=1)


def pad_right(values, count):
    if not count:
        return values
    return jnp.concatenate([values, jnp.zeros((values.shape[0], count), f32)], axis=1)


def fwd_diagonal(base, group, qT, kT, vT, m_ref, l_ref, acc):
    strip = min(256, group)
    count = group // strip
    for h in range(2):
        rows = slice(HEAD_DIM * h, HEAD_DIM * (h + 1))
        strips = []
        for j in range(count):
            wide = group - j * strip
            keys, queries = pl.ds(base + j * strip, strip), pl.ds(base + j * strip, wide)
            scores = dot(kT[rows, keys], qT[rows, queries], 0, 0)
            key_at = lax.broadcasted_iota(jnp.int32, scores.shape, 0)
            query_at = lax.broadcasted_iota(jnp.int32, scores.shape, 1)
            strips.append(jnp.where(key_at <= query_at, scores, NEG))
        peaks = []
        for g in range(count):
            peak = None
            for j in range(g + 1):
                part = strips[j][:, (g - j) * strip : (g - j + 1) * strip]
                part = jnp.max(part, axis=0, keepdims=True)
                peak = part if peak is None else jnp.maximum(peak, part)
            peaks.append(peak)
        peak = jnp.concatenate(peaks, axis=1) if count > 1 else peaks[0]
        total, value = None, None
        for j in range(count):
            keys = pl.ds(base + j * strip, strip)
            weights = jnp.exp2(strips[j] - peak[:, j * strip :])
            part = pad_left(jnp.sum(weights, axis=0, keepdims=True), j * strip)
            term = pad_left(dot(vT[rows, keys], weights.astype(bf16), 1, 0), j * strip)
            total = part if total is None else total + part
            value = term if value is None else value + term
        queries = pl.ds(base, group)
        m_ref[h : h + 1, queries] = peak
        l_ref[h : h + 1, queries] = total
        acc[rows, queries] = value


def fwd_local_kernel(group, info, qT, kT, vT, acc, m_ref, l_ref):
    length = info[1]
    m_ref[...] = jnp.full(m_ref.shape, NEG, f32)
    l_ref[...] = jnp.zeros(l_ref.shape, f32)
    acc[...] = jnp.zeros(acc.shape, f32)
    refs = (qT, kT, vT, m_ref.at[0], l_ref.at[0], acc)

    def own(i, carry):
        base = pl.multiple_of(i * group, group)
        start = info[2 + i]

        @pl.when(start + group <= length)
        def _():
            fwd_diagonal(base, group, *refs)

        @pl.when((start < length) & (start + group > length))
        def _():
            fwd_chunk(base, base, group, group, 0, length - start, *refs)

        return carry

    lax.fori_loop(0, 2, own, 0)
    early = info[2]

    @pl.when(early + group <= length)
    def _():
        fwd_chunk(group, 0, group, group, None, None, *refs)

    @pl.when((early < length) & (early + group > length))
    def _():
        fwd_chunk(group, 0, group, group, None, length - early, *refs)


def remote_steps(group, parts, kind, info, full, partial):
    place, length = info[0], info[1]

    def visit(q_block, k_slot, k_block, wanted):
        q0 = pl.multiple_of(q_block * group, group)
        k0 = pl.multiple_of(k_slot * group, group)
        start = k_block * group

        @pl.when(wanted & (start + group <= length))
        def _():
            full(q0, k0)

        @pl.when(wanted & (start < length) & (start + group > length))
        def _():
            partial(q0, k0, length - start)

    others = parts - 1

    def early(i, carry):
        j = i // 2
        other = lax.rem(place + 1 + j, parts)
        late_query = lax.rem(i, 2)
        visit(late_query, j, other, (late_query == 1) | (other < place))
        return carry

    def late(j, carry):
        other = lax.rem(place + 1 + j, parts)
        slot = j + (others if kind == 2 else 0)
        visit(1, slot, 2 * parts - 1 - other, other > place)
        return carry

    if kind == 2:

        def both(i, carry):
            is_early = i < 2 * others
            j = jnp.where(is_early, i // 2, i - 2 * others)
            other = lax.rem(place + 1 + j, parts)
            late_query = jnp.where(is_early, lax.rem(i, 2), 1)
            slot = jnp.where(is_early, j, j + others)
            block = jnp.where(is_early, other, 2 * parts - 1 - other)
            wanted = jnp.where(
                is_early,
                ((late_query == 1) | (other < place)).astype(jnp.int32),
                (other > place).astype(jnp.int32),
            )
            visit(late_query, slot, block, wanted == 1)
            return carry

        lax.fori_loop(0, 3 * others, both, 0)
    elif kind == 0:
        lax.fori_loop(0, 2 * others, early, 0)
    else:
        lax.fori_loop(0, others, late, 0)


def fwd_remote_kernel(
    group, parts, kind, last, info, qT, kT, vT, acc_in, m_in, l_in, out, m_out, l_out, *scratch
):
    acc = scratch[0] if last else out
    acc[...] = acc_in[...]
    m_out[...] = m_in[...]
    l_out[...] = l_in[...]
    refs = (qT, kT, vT, m_out.at[0], l_out.at[0], acc)

    def full(q0, k0):
        fwd_chunk(q0, k0, group, group, None, None, *refs)

    def partial(q0, k0, limit):
        fwd_chunk(q0, k0, group, group, None, limit, *refs)

    remote_steps(group, parts, kind, info, full, partial)
    if last:
        for h in range(2):
            rows = slice(HEAD_DIM * h, HEAD_DIM * (h + 1))
            total = l_out[0, h : h + 1, :]
            out[rows, :] = (acc[rows, :] / total).astype(bf16)
            m_out[0, h : h + 1, :] = m_out[0, h : h + 1, :] + jnp.log2(total)


def split_three(values):
    high = values.astype(bf16).astype(f32)
    rest = values - high
    middle = rest.astype(bf16).astype(f32)
    low = (rest - middle).astype(bf16).astype(f32)
    return [high, middle, low]


def bwd_prepare(qT, keys, doT, oT, lse, qa, da, ka, va):
    n_q, n_k = qT.shape[1], ka.shape[2]
    extra = qa.shape[1] - HEAD_DIM
    pad = jnp.zeros((extra - 3, n_q), f32)
    row_at = lax.broadcasted_iota(jnp.int32, (extra, n_k), 0)
    tail = jnp.where(row_at < 3, 1.0, 0.0).astype(bf16)
    for h in range(2):
        rows = slice(HEAD_DIM * h, HEAD_DIM * (h + 1))
        grad = doT[rows, :].astype(f32)
        delta = jnp.sum(grad * oT[rows, :].astype(f32), axis=0, keepdims=True)
        qa[h, :HEAD_DIM, :] = qT[rows, :]
        parts = split_three(-lse[0, h : h + 1, :]) + [pad]
        qa[h, HEAD_DIM:, :] = jnp.concatenate(parts, axis=0).astype(bf16)
        da[h, :HEAD_DIM, :] = doT[rows, :]
        parts = split_three(-delta) + [pad]
        da[h, HEAD_DIM:, :] = jnp.concatenate(parts, axis=0).astype(bf16)
        at = 0
        for kT, vT in keys:
            part = slice(at, at + kT.shape[1])
            ka[h, :HEAD_DIM, part] = kT[rows, :]
            va[h, :HEAD_DIM, part] = vT[rows, :]
            at += kT.shape[1]
        ka[h, HEAD_DIM:, :] = tail
        va[h, HEAD_DIM:, :] = tail


def bwd_chunk(q0, k0, q_n, k_n, offset, limit, qT, doT, qa, da, ka, va, dq, dk, dv):
    queries, keys = pl.ds(q0, q_n), pl.ds(k0, k_n)
    for h in range(2):
        rows = slice(HEAD_DIM * h, HEAD_DIM * (h + 1))
        probs = jnp.exp2(dot(qa[h, :, queries], ka[h, :, keys], 0, 0))
        if offset is not None or limit is not None:
            key_at = lax.broadcasted_iota(jnp.int32, (q_n, k_n), 1)
            last = jnp.zeros((q_n, 1), jnp.int32) + (limit - 1)
            if offset is not None:
                query_at = lax.broadcasted_iota(jnp.int32, (q_n, 1), 0)
                last = jnp.minimum(query_at + offset, last)
            probs = jnp.where(key_at <= last, probs, 0.0)
        d_probs = dot(da[h, :, queries], va[h, :, keys], 0, 0)
        d_scores = (probs * d_probs).astype(bf16)
        dv[rows, keys] += dot(doT[rows, queries], probs.astype(bf16), 1, 0)
        dk[rows, keys] += dot(qT[rows, queries], d_scores, 1, 0)
        dq[rows, queries] += dot(ka[h, :HEAD_DIM, keys], d_scores, 1, 1)


def bwd_diagonal(base, group, qT, doT, qa, da, ka, va, dq, dk, dv):
    strip = min(256, group)
    count = group // strip
    for h in range(2):
        rows = slice(HEAD_DIM * h, HEAD_DIM * (h + 1))
        d_keys, d_values, d_queries = None, None, []
        for j in range(count):
            wide = (j + 1) * strip
            queries, keys = pl.ds(base + j * strip, strip), pl.ds(base, wide)
            probs = jnp.exp2(dot(qa[h, :, queries], ka[h, :, keys], 0, 0))
            query_at = lax.broadcasted_iota(jnp.int32, probs.shape, 0)
            key_at = lax.broadcasted_iota(jnp.int32, probs.shape, 1)
            probs = jnp.where(key_at <= query_at + j * strip, probs, 0.0)
            d_probs = dot(da[h, :, queries], va[h, :, keys], 0, 0)
            d_scores = (probs * d_probs).astype(bf16)
            value = pad_right(dot(doT[rows, queries], probs.astype(bf16), 1, 0), group - wide)
            key = pad_right(dot(qT[rows, queries], d_scores, 1, 0), group - wide)
            d_values = value if d_values is None else d_values + value
            d_keys = key if d_keys is None else d_keys + key
            d_queries.append(dot(ka[h, :HEAD_DIM, keys], d_scores, 1, 1))
        here = pl.ds(base, group)
        dq[rows, here] += jnp.concatenate(d_queries, axis=1) if count > 1 else d_queries[0]
        dk[rows, here] += d_keys
        dv[rows, here] += d_values


def turn_back(values, cosine, sine):
    half = HEAD_DIM // 2
    first, second = values[:half], values[half:]
    return jnp.concatenate(
        [first * cosine + second * sine, second * cosine - first * sine], axis=0
    )


def bwd_remote_kernel(
    group, parts, info, qT, doT, oT, lse, cosine, sine, k_early, v_early, k_late, v_late, *rest
):
    dq, dkv, *scratch = rest[-8:]
    qa, da, ka, va, dk, dv = scratch
    keys = [(k_early, v_early), (k_late, v_late)]
    bwd_prepare(qT, keys, doT, oT, lse, qa, da, ka, va)
    dq[...] = jnp.zeros(dq.shape, f32)
    dk[...] = jnp.zeros(dk.shape, f32)
    dv[...] = jnp.zeros(dv.shape, f32)
    refs = (qT, doT, qa, da, ka, va, dq, dk, dv)

    def full(q0, k0):
        bwd_chunk(q0, k0, group, group, None, None, *refs)

    def partial(q0, k0, limit):
        bwd_chunk(q0, k0, group, group, None, limit, *refs)

    remote_steps(group, parts, 2, info, full, partial)
    for h in range(2):
        rows = slice(HEAD_DIM * h, HEAD_DIM * (h + 1))
        dkv[1, rows, :] = turn_back(dk[rows, :] * LN2, cosine[...], sine[...]).astype(bf16)
    dkv[0] = jnp.zeros(dv.shape, bf16)
    dkv[2] = dv[...].astype(bf16)


def bwd_local_kernel(group, info, qT, doT, oT, lse, cosine, sine, kT, vT, dq_in, *rest):
    dqkv, *scratch = rest[-8:]
    qa, da, ka, va, dq, dk, dv = scratch
    length = info[1]
    bwd_prepare(qT, [(kT, vT)], doT, oT, lse, qa, da, ka, va)
    dq[...] = dq_in[...]
    dk[...] = jnp.zeros(dk.shape, f32)
    dv[...] = jnp.zeros(dv.shape, f32)
    refs = (qT, doT, qa, da, ka, va, dq, dk, dv)

    def own(i, carry):
        base = pl.multiple_of(i * group, group)
        start = info[2 + i]

        @pl.when(start + group <= length)
        def _():
            bwd_diagonal(base, group, *refs)

        @pl.when((start < length) & (start + group > length))
        def _():
            bwd_chunk(base, base, group, group, 0, length - start, *refs)

        return carry

    lax.fori_loop(0, 2, own, 0)
    early = info[2]

    @pl.when(early + group <= length)
    def _():
        bwd_chunk(group, 0, group, group, None, None, *refs)

    @pl.when((early < length) & (early + group > length))
    def _():
        bwd_chunk(group, 0, group, group, None, length - early, *refs)

    for h in range(2):
        rows = slice(HEAD_DIM * h, HEAD_DIM * (h + 1))
        d_query = dq[rows, :] * 0.125
        dqkv[0, rows, :] = turn_back(d_query, cosine[...], sine[...]).astype(bf16)
        dqkv[1, rows, :] = turn_back(dk[rows, :] * LN2, cosine[...], sine[...]).astype(bf16)
    dqkv[2] = dv[...].astype(bf16)


def rows_of(count, first=0):
    return pl.BlockSpec((PAIR, count), lambda i, info: (first + i, 0))


def stats_of(count, first=0):
    return pl.BlockSpec((1, 2, count), lambda i, info: (first + i, 0, 0))


def planes_of(planes, count, first=0):
    return pl.BlockSpec((planes, PAIR, count), lambda i, info: (0, first + i, 0))


def whole(shape):
    return pl.BlockSpec(shape, lambda i, info: (0,) * len(shape))


def attention_call(kernel, pairs, in_specs, out_specs, out_shape, scratch, flops, name, alias={}):
    return pl.pallas_call(
        kernel,
        grid_spec=pltpu.PrefetchScalarGridSpec(
            num_scalar_prefetch=1,
            grid=(pairs,),
            in_specs=in_specs,
            out_specs=out_specs,
            scratch_shapes=scratch,
        ),
        out_shape=out_shape,
        input_output_aliases=alias,
        compiler_params=pltpu.CompilerParams(vmem_limit_bytes=VMEM),
        cost_estimate=pl.CostEstimate(
            flops=int(flops), bytes_accessed=1 << 25, transcendentals=0
        ),
        name=name,
    )


def attend_local(info, qT, kT, vT, group):
    width, n_q = qT.shape
    pairs = width // PAIR
    call = attention_call(
        functools.partial(fwd_local_kernel, group),
        pairs,
        [rows_of(n_q)] * 3,
        [rows_of(n_q), stats_of(n_q), stats_of(n_q)],
        [
            jax.ShapeDtypeStruct((width, n_q), f32),
            jax.ShapeDtypeStruct((pairs, 2, n_q), f32),
            jax.ShapeDtypeStruct((pairs, 2, n_q), f32),
        ],
        [],
        4 * width * 2 * group * group * 4,
        "attend_local",
    )
    return call(info, qT, kT, vT)


def attend_remote(info, qT, kT, vT, state, group, parts, kind, last):
    width, n_q = qT.shape
    n_k = kT.shape[1]
    pairs = width // PAIR
    scratch = [pltpu.VMEM((PAIR, n_q), f32)] if last else []
    call = attention_call(
        functools.partial(fwd_remote_kernel, group, parts, kind, last),
        pairs,
        [rows_of(n_q), rows_of(n_k), rows_of(n_k), rows_of(n_q), stats_of(n_q), stats_of(n_q)],
        [rows_of(n_q), stats_of(n_q), stats_of(n_q)],
        [
            jax.ShapeDtypeStruct((width, n_q), bf16 if last else f32),
            jax.ShapeDtypeStruct((pairs, 2, n_q), f32),
            jax.ShapeDtypeStruct((pairs, 2, n_q), f32),
        ],
        scratch,
        4 * width * group * group * 4,
        "attend_remote",
    )
    return call(info, qT, kT, vT, *state)


def back_scratch(n_q, n_k):
    rows = HEAD_DIM + 16
    return [
        pltpu.VMEM((2, rows, n_q), bf16),
        pltpu.VMEM((2, rows, n_q), bf16),
        pltpu.VMEM((2, rows, n_k), bf16),
        pltpu.VMEM((2, rows, n_k), bf16),
    ]


def back_remote(info, operands, turns, keys, group, parts, first, count, before):
    width, n_q = operands[0].shape
    n_k = keys[0].shape[1] + keys[2].shape[1]
    half = HEAD_DIM // 2
    n_in = 1 + len(operands) + len(turns) + len(keys)
    call = attention_call(
        functools.partial(bwd_remote_kernel, group, parts),
        count,
        [rows_of(n_q, first)] * 3
        + [stats_of(n_q, first)]
        + [whole((half, n_k))] * 2
        + [rows_of(item.shape[1], first) for item in keys]
        + [pl.BlockSpec(memory_space=pl.ANY)] * len(before),
        [rows_of(n_q, first), planes_of(3, n_k, first)],
        [
            jax.ShapeDtypeStruct((width, n_q), f32),
            jax.ShapeDtypeStruct((3, width, n_k), bf16),
        ],
        back_scratch(n_q, n_k) + [pltpu.VMEM((PAIR, n_k), f32)] * 2,
        10 * count * PAIR * 2 * group * group * 4,
        "back_remote",
        {n_in + i: i for i in range(len(before))},
    )
    return call(info, *operands, *turns, *keys, *before)


def back_local(info, operands, turns, keys, dq, group, first, count, before):
    width, n_q = operands[0].shape
    half = HEAD_DIM // 2
    n_in = 1 + len(operands) + len(turns) + len(keys) + 1
    call = attention_call(
        functools.partial(bwd_local_kernel, group),
        count,
        [rows_of(n_q, first)] * 3
        + [stats_of(n_q, first)]
        + [whole((half, n_q))] * 2
        + [rows_of(n_q, first)] * 3
        + [pl.BlockSpec(memory_space=pl.ANY)] * len(before),
        planes_of(3, n_q, first),
        jax.ShapeDtypeStruct((3, width, n_q), bf16),
        back_scratch(n_q, n_q) + [pltpu.VMEM((PAIR, n_q), f32)] * 3,
        10 * count * PAIR * 2 * group * group * 4,
        "back_local",
        {n_in + i: i for i in range(len(before))},
    )
    return call(info, *operands, *turns, *keys, dq, *before)


def normalize(values):
    centre = values - jnp.mean(values, axis=-1, keepdims=True)
    spread = jnp.mean(centre * centre, axis=-1, keepdims=True)
    rate = lax.rsqrt(spread + EPS)
    return centre * rate, rate


def norm_back(grad, unit, rate, gain):
    scaled = grad * gain
    first = jnp.mean(scaled, axis=-1, keepdims=True)
    second = jnp.mean(scaled * unit, axis=-1, keepdims=True)
    return rate * (scaled - first - unit * second)


GELU_A = 0.7978845608028654
GELU_B = 0.044715


def column_sum(values):
    return jnp.sum(values, axis=0, keepdims=True)


def block_kernel(
    span,
    oT,
    tokens,
    cotangent,
    w_out,
    w_up,
    w_down,
    b_out,
    b_up,
    b_down,
    gain_two,
    shift_two,
    gain_three,
    shift_three,
    gain_four,
    shift_four,
    result,
    d_middle_out,
    hidden_out,
    d_outer_out,
    normed_out,
    d_inner_out,
    d_branch_out,
    doT,
    small,
    small_up,
    slope,
):
    step = pl.program_id(0)

    @pl.when(step == 0)
    def _():
        small[...] = jnp.zeros(small.shape, f32)
        small_up[...] = jnp.zeros(small_up.shape, f32)

    wide = w_up.shape[1]
    branch = dot(oT[...], w_out[...], 0, 0) + b_out[...]
    unit_two, rate_two = normalize(branch)
    middle = tokens[...].astype(f32) + (unit_two * gain_two[...] + shift_two[...])
    unit_three, rate_three = normalize(middle)
    normed = (unit_three * gain_three[...] + shift_three[...]).astype(bf16)
    normed_out[...] = normed
    outer = None
    for c in range(wide // span):
        columns = slice(c * span, (c + 1) * span)
        inner = dot(normed, w_up[:, columns], 1, 0) + b_up[:, columns]
        square = inner * inner
        bend = jnp.tanh(inner * (GELU_A + (GELU_A * GELU_B) * square))
        half = 0.5 + 0.5 * bend
        hidden = (inner * half).astype(bf16)
        hidden_out[:, columns] = hidden
        slope[:, columns] = half + inner * (1.0 - bend * bend) * (
            0.5 * GELU_A + (1.5 * GELU_A * GELU_B) * square
        )
        term = dot(hidden, w_down[columns, :], 1, 0)
        outer = term if outer is None else outer + term
    unit_four, rate_four = normalize(outer + b_down[...])
    result[...] = (middle + (unit_four * gain_four[...] + shift_four[...])).astype(bf16)

    grad = cotangent[...].astype(f32)
    d_outer = norm_back(grad, unit_four, rate_four, gain_four[...]).astype(bf16)
    d_outer_out[...] = d_outer
    small[0:1, :] += column_sum(grad * unit_four)
    small[1:2, :] += column_sum(grad)
    small[2:3, :] += column_sum(d_outer.astype(f32))
    d_normed = None
    for c in range(wide // span):
        columns = slice(c * span, (c + 1) * span)
        d_hidden = dot(d_outer, w_down[columns, :], 1, 1)
        d_inner = (d_hidden * slope[:, columns]).astype(bf16)
        d_inner_out[:, columns] = d_inner
        small_up[:, columns] += column_sum(d_inner.astype(f32))
        term = dot(d_inner, w_up[:, columns], 1, 1)
        d_normed = term if d_normed is None else d_normed + term
    small[3:4, :] += column_sum(d_normed * unit_three)
    small[4:5, :] += column_sum(d_normed)
    d_middle = grad + norm_back(d_normed, unit_three, rate_three, gain_three[...])
    d_middle_out[...] = d_middle
    small[5:6, :] += column_sum(d_middle * unit_two)
    small[6:7, :] += column_sum(d_middle)
    d_branch = norm_back(d_middle, unit_two, rate_two, gain_two[...]).astype(bf16)
    d_branch_out[...] = d_branch
    small[7:8, :] += column_sum(d_branch.astype(f32))
    doT[...] = dot(w_out[...], d_branch, 1, 1).astype(bf16)


def block_call(oT, tokens, cotangent, weights, vectors):
    width, rows = oT.shape
    wide = weights[1].shape[1]
    step = min(256, rows)
    span = min(SPAN, wide)

    def lines(count):
        return pl.BlockSpec((step, count), lambda i: (i, 0))

    def fixed(shape):
        return pl.BlockSpec(shape, lambda i: (0, 0), pipeline_mode=pl.Buffered(1))

    def total(shape):
        return pl.BlockSpec(shape, lambda i: (0, 0))

    features = pl.BlockSpec((width, step), lambda i: (0, i))
    sizes = [width, width, wide, width, width, wide, width]
    kinds = [bf16, f32, bf16, bf16, bf16, bf16, bf16]
    return pl.pallas_call(
        functools.partial(block_kernel, span),
        grid=(rows // step,),
        in_specs=[features, lines(width), lines(width)]
        + [fixed(item.shape) for item in weights]
        + [fixed(item.shape) for item in vectors],
        out_specs=[lines(size) for size in sizes]
        + [features, total((8, width)), total((1, wide))],
        out_shape=[jax.ShapeDtypeStruct((rows, size), kind) for size, kind in zip(sizes, kinds)]
        + [
            jax.ShapeDtypeStruct((width, rows), bf16),
            jax.ShapeDtypeStruct((8, width), f32),
            jax.ShapeDtypeStruct((1, wide), f32),
        ],
        scratch_shapes=[pltpu.VMEM((step, wide), f32)],
        compiler_params=pltpu.CompilerParams(vmem_limit_bytes=VMEM),
        cost_estimate=pl.CostEstimate(
            flops=2 * 2 * rows * (width * width + 2 * width * wide),
            bytes_accessed=1 << 26,
            transcendentals=rows * wide,
        ),
        name="block",
    )(oT, tokens, cotangent, *weights, *vectors)


def turn(values, cosine, sine):
    half = HEAD_DIM // 2
    first, second = values[:half], values[half:]
    return jnp.concatenate(
        [first * cosine - second * sine, second * cosine + first * sine], axis=0
    )


def project_kernel(sections, tokens, w, b, gain, shift, cosine, sine, normed_out, *outs):
    unit, rate = normalize(tokens[...].astype(f32))
    normed = (unit * gain[...] + shift[...]).astype(bf16)
    normed_out[...] = normed
    width = tokens.shape[1]
    chunk = min(256, width)
    for section, out in zip(sections, outs):
        for c in range(width // chunk):
            at = section * width + c * chunk
            mixed = dot(w[:, at : at + chunk], normed, 0, 1) + b[at : at + chunk, :]
            for h in range(chunk // HEAD_DIM):
                rows = slice(h * HEAD_DIM, (h + 1) * HEAD_DIM)
                place = slice(c * chunk + h * HEAD_DIM, c * chunk + (h + 1) * HEAD_DIM)
                value = mixed[rows]
                if section < 2:
                    value = turn(value, cosine[...], sine[...])
                if section == 0:
                    value = value * (0.125 * LOG2E)
                out[place, :] = value.astype(bf16)


def project(tokens, w, b, gain, shift, cosine, sine, sections, start=0):
    rows, width = tokens.shape
    step = min(512, rows)
    half = HEAD_DIM // 2
    first = start // step

    def fixed(shape):
        return pl.BlockSpec(shape, lambda i: (0, 0), pipeline_mode=pl.Buffered(1))

    lines = pl.BlockSpec((step, width), lambda i: (i, 0))
    features = pl.BlockSpec((width, step), lambda i: (0, i))
    turns = pl.BlockSpec((half, step), lambda i: (0, first + i))
    return pl.pallas_call(
        functools.partial(project_kernel, sections),
        grid=(rows // step,),
        in_specs=[lines, fixed(w.shape), fixed(b.shape), fixed(gain.shape), fixed(shift.shape)]
        + [turns] * 2,
        out_specs=[lines] + [features] * len(sections),
        out_shape=[jax.ShapeDtypeStruct((rows, width), bf16)]
        + [jax.ShapeDtypeStruct((width, rows), bf16)] * len(sections),
        compiler_params=pltpu.CompilerParams(vmem_limit_bytes=VMEM),
        cost_estimate=pl.CostEstimate(
            flops=2 * rows * width * width * len(sections),
            bytes_accessed=1 << 24,
            transcendentals=0,
        ),
        name="project",
    )(tokens, w, b, gain, shift, cosine, sine)


def unproject_kernel(planes, finish, *refs):
    d_mixed, w, out = refs[: len(planes)], refs[len(planes)], refs[-1]
    width = w.shape[0]
    total = None
    for plane, ref in zip(planes, d_mixed):
        term = dot(ref[0], w[:, plane * width : (plane + 1) * width], 0, 1)
        total = term if total is None else total + term
    if not finish:
        out[...] = total.astype(bf16)
        return
    returned, tokens, d_middle, gain = refs[len(planes) + 1 : len(planes) + 5]
    total = total + returned[...].astype(f32)
    unit, rate = normalize(tokens[...].astype(f32))
    out[...] = (d_middle[...] + norm_back(total, unit, rate, gain[...])).astype(bf16)


def unproject(d_mixed, w, planes, start, count, finish=(), before=()):
    _, width, total = d_mixed.shape
    step = min(256, count)
    first = start // step

    def fixed(shape):
        return pl.BlockSpec(shape, lambda i: (0, 0), pipeline_mode=pl.Buffered(1))

    def plane_of(plane):
        return pl.BlockSpec((1, width, step), lambda i: (plane, 0, first + i))

    lines = pl.BlockSpec((step, width), lambda i: (i, 0))
    later = pl.BlockSpec((step, width), lambda i: (first + i, 0))
    specs = [lines, later, later, fixed(finish[-1].shape)] if finish else []
    n_in = len(planes) + 1 + len(finish)
    return pl.pallas_call(
        functools.partial(unproject_kernel, planes, bool(finish)),
        grid=(count // step,),
        in_specs=[plane_of(plane) for plane in planes]
        + [fixed(w.shape)]
        + specs
        + [pl.BlockSpec(memory_space=pl.ANY)] * len(before),
        out_specs=later if finish else lines,
        out_shape=jax.ShapeDtypeStruct((total if finish else count, width), bf16),
        input_output_aliases={n_in + i: i for i in range(len(before))},
        compiler_params=pltpu.CompilerParams(vmem_limit_bytes=VMEM),
        cost_estimate=pl.CostEstimate(
            flops=2 * count * width * width * len(planes),
            bytes_accessed=1 << 24,
            transcendentals=0,
        ),
        name="unproject",
    )(*[d_mixed] * len(planes), w, *finish, *before)


def divide(total, share, core, kept, given):
    own, other = [], []
    for i in range(0, total.shape[0], 2 * share):
        zero, one = total[i : i + share], total[i + share : i + 2 * share]
        own.append(jnp.where(core == 0, zero, one))
        other.append(jnp.where(core == 0, one, zero))
    kept[...] = jnp.concatenate(own, axis=0).astype(bf16)
    given[...] = jnp.concatenate(other, axis=0).astype(bf16)


def outer_kernel(share, right_dim, core, left, right, kept, given):
    divide(dot(left[...], right[...], 0, right_dim), share, core[0], kept, given)


def outer_halves(core, left, right, right_dim, parts):
    rows, height = left.shape
    width = right.shape[1 - right_dim]
    share = height // parts
    high = max(2 * share, min(512, height))
    wide = min(1024, width)
    if right_dim == 0:
        right_spec = pl.BlockSpec((rows, wide), lambda j, i, core: (0, j))
    else:
        right_spec = pl.BlockSpec((wide, rows), lambda j, i, core: (j, 0))
    out_spec = pl.BlockSpec((high // 2, wide), lambda j, i, core: (i, j))
    out = jax.ShapeDtypeStruct((height // 2, width), bf16)
    return pl.pallas_call(
        functools.partial(outer_kernel, share, right_dim),
        grid_spec=pltpu.PrefetchScalarGridSpec(
            num_scalar_prefetch=1,
            grid=(width // wide, height // high),
            in_specs=[pl.BlockSpec((rows, high), lambda j, i, core: (0, i)), right_spec],
            out_specs=[out_spec] * 2,
        ),
        out_shape=[out] * 2,
        compiler_params=pltpu.CompilerParams(vmem_limit_bytes=VMEM),
        cost_estimate=pl.CostEstimate(
            flops=2 * rows * height * width, bytes_accessed=1 << 25, transcendentals=0
        ),
        name="outer",
    )(core, left, right)


def mixed_kernel(
    share, first_far, core, d_own, d_far, normed, far_early, far_late, w, kept, given, bias, sums
):
    step = pl.program_id(0)
    total = dot(d_own[...], normed[...], 1, 0)
    bias[...] = jnp.sum(d_own[...].astype(f32), axis=1, keepdims=True)

    @pl.when(step == 0)
    def _():
        sums[...] = jnp.zeros(sums.shape, f32)

    def finish(value):
        divide(value, share, core[0], kept, given)
        weights = w[...].astype(f32).T
        sums[0:1, :] += column_sum(weights * value)
        sums[1:2, :] += column_sum(weights * bias[...])

    @pl.when(step < first_far)
    def _():
        finish(total)

    @pl.when(step >= first_far)
    def _():
        split = far_early.shape[0]
        bias[...] += jnp.sum(d_far[...].astype(f32), axis=1, keepdims=True)
        finish(
            total
            + dot(d_far[:, :split], far_early[...], 1, 0)
            + dot(d_far[:, split:], far_late[...], 1, 0)
        )


def mixed_halves(core, d_own, d_far, normed, far_early, far_late, w, parts):
    height, rows = d_own.shape
    far = d_far.shape[1]
    width = normed.shape[1]
    share = height // parts
    high = 2 * share * max(1, 384 // (2 * share))
    first_far = width // high

    def fixed(shape):
        return pl.BlockSpec(shape, lambda i, core: (0, 0), pipeline_mode=pl.Buffered(1))

    out_spec = pl.BlockSpec((high // 2, width), lambda i, core: (i, 0))
    out = jax.ShapeDtypeStruct((height // 2, width), bf16)
    return pl.pallas_call(
        functools.partial(mixed_kernel, share, first_far),
        grid_spec=pltpu.PrefetchScalarGridSpec(
            num_scalar_prefetch=1,
            grid=(height // high,),
            in_specs=[
                pl.BlockSpec((high, rows), lambda i, core: (i, 0)),
                pl.BlockSpec((high, far), lambda i, core: (jnp.maximum(i, first_far), 0)),
                fixed(normed.shape),
                fixed(far_early.shape),
                fixed(far_late.shape),
                pl.BlockSpec((width, high), lambda i, core: (0, i)),
            ],
            out_specs=[out_spec] * 2
            + [
                pl.BlockSpec((high, 1), lambda i, core: (i, 0)),
                pl.BlockSpec((2, width), lambda i, core: (0, 0)),
            ],
        ),
        out_shape=[out] * 2
        + [
            jax.ShapeDtypeStruct((height, 1), f32),
            jax.ShapeDtypeStruct((2, width), f32),
        ],
        compiler_params=pltpu.CompilerParams(vmem_limit_bytes=VMEM),
        cost_estimate=pl.CostEstimate(
            flops=2 * (rows + far) * height * width, bytes_accessed=1 << 25, transcendentals=0
        ),
        name="mixed",
    )(core, d_own, d_far, normed, far_early, far_late, w)


def bit_of(axis, position):
    return (lax.axis_index(axis) >> position) & 1


def swap(values, axis, position):
    size = lax.axis_size(axis)
    return lax.ppermute(values, axis, [(i, i ^ (1 << position)) for i in range(size)])


class Halving:
    def __init__(self, array, bits, order):
        self.bits = list(bits)
        self.order = list(order)
        rows = array.shape[0] >> len(bits)
        self.array = array.reshape((2,) * len(bits) + (rows, array.shape[1]))

    def split(self):
        self.bit = self.order.pop(0)
        at = self.bits.index(self.bit)
        self.mine = bit_of(*self.bit)
        self.away = lax.dynamic_index_in_dim(self.array, 1 - self.mine, at, False)
        self.at = at
        self.bits.pop(at)

    def send(self):
        self.received = swap(self.away, *self.bit)

    def add(self):
        kept = lax.dynamic_index_in_dim(self.array, self.mine, self.at, False).astype(f32)
        total = kept + self.received.astype(f32)
        self.array = total.astype(bf16) if self.bits else total


class Crossing(Halving):
    def __init__(self, halves, bits, order):
        kept, given = halves
        super().__init__(kept, bits, order)
        self.received = swap(given, "wide", 0).reshape(self.array.shape)

    def add(self):
        if hasattr(self, "bit"):
            super().add()
        else:
            total = self.array.astype(f32) + self.received.astype(f32)
            self.array = total.astype(bf16)


class Adding:
    def __init__(self, array, order):
        self.array, self.order = array, list(order)

    def split(self):
        self.bit = self.order.pop(0)
        self.away = self.array

    def send(self):
        self.received = swap(self.away, *self.bit)

    def add(self):
        self.array = self.array + self.received


def launch(lead, sums, *others):
    for item in sums:
        item.split()
    held = (lead, others, [(item.array, item.away) for item in sums])
    lead, others, arrays = lax.optimization_barrier(held)
    for item, (array, away) in zip(sums, arrays):
        item.array, item.away = array, away
        item.send()
    return (lead, *others)


def angles(positions):
    half = HEAD_DIM // 2
    freqs = jnp.power(10000.0, -jnp.arange(half, dtype=f32) / half)
    theta = freqs[:, None] * positions.astype(f32)[None, :]
    return jnp.cos(theta), jnp.sin(theta)


def axis_bits(axis):
    return [(axis, position) for position in range(lax.axis_size(axis).bit_length() - 1)]


def body(
    inputs,
    cotangent,
    lengths,
    w_qkv,
    b_qkv,
    w_out,
    b_out,
    w_up,
    b_up,
    w_down,
    b_down,
    gain_one,
    shift_one,
    gain_two,
    shift_two,
    gain_three,
    shift_three,
    gain_four,
    shift_four,
):
    group = inputs.shape[3]
    width = inputs.shape[4]
    parts = lax.axis_size("narrow")
    place = lax.axis_index("narrow")
    others = parts - 1
    rows = 2 * group
    far_rows = others * group
    offsets = jnp.arange(group, dtype=jnp.int32)

    own_blocks = inputs.reshape(2, group, width)
    far_early, far_late = [], []
    for shift in range(1, parts):
        pairs = [((n + shift) % parts, n) for n in range(parts)]
        far_early.append(lax.ppermute(own_blocks[0], "narrow", pairs))
    for shift in range(1, parts):
        pairs = [((n + shift) % parts, n) for n in range(parts)]
        later = [(source, n) for source, n in pairs if source > n]
        far_late.append(lax.ppermute(own_blocks[1], "narrow", later))
    other = (place + 1 + jnp.arange(others, dtype=jnp.int32)) % parts

    early_at = place * group
    late_at = (2 * parts - 1 - place) * group
    info = jnp.stack([place, lengths[0], early_at, late_at]).astype(jnp.int32)
    core = bit_of("wide", 0).astype(jnp.int32)[None]
    starts = jnp.stack([early_at, late_at])
    turns = angles((starts[:, None] + offsets[None]).reshape(-1))
    starts = jnp.concatenate([other, 2 * parts - 1 - other]) * group
    turns_far = angles((starts[:, None] + offsets[None]).reshape(-1))

    def row(vector):
        return vector[None, :]

    norm_one = [row(gain_one), row(shift_one)]
    b_column = b_qkv[:, None]
    tokens = own_blocks.reshape(rows, width)
    normed, qT, kT, vT = project(tokens, w_qkv, b_column, *norm_one, *turns, (0, 1, 2))
    state = attend_local(info, qT, kT, vT, group)

    def far_keys(blocks, start):
        far = jnp.concatenate(blocks, axis=0) if others > 1 else blocks[0]
        return project(far, w_qkv, b_column, *norm_one, *turns_far, (1, 2), start)

    normed_fe, kT_fe, vT_fe = far_keys(far_early, 0)
    state = attend_remote(info, qT, kT_fe, vT_fe, state, group, parts, 0, False)
    normed_fl, kT_fl, vT_fl = far_keys(far_late, far_rows)
    oT, lse, _ = attend_remote(info, qT, kT_fl, vT_fl, state, group, parts, 1, True)

    blocks = block_call(
        oT,
        tokens,
        cotangent.reshape(rows, width),
        [w_out, w_up, w_down],
        [row(item) for item in (b_out, b_up, b_down)]
        + [row(item) for item in (gain_two, shift_two, gain_three, shift_three)]
        + [row(item) for item in (gain_four, shift_four)],
    )
    result, d_middle, hidden, d_outer, normed_two, d_inner, d_branch, doT, small, small_up = blocks

    wide_bits = axis_bits("wide")
    narrow_bits = axis_bits("narrow")
    devices = 1 << (len(wide_bits) + len(narrow_bits))
    cores = lax.axis_size("wide")
    bits = wide_bits[:0:-1] + narrow_bits[::-1]
    first_order = wide_bits[1:2] + narrow_bits + wide_bits[2:]
    second_order = narrow_bits + wide_bits[1:]

    sum_down = Crossing(outer_halves(core, d_outer, hidden, 0, cores), bits, second_order)
    sum_up = Crossing(outer_halves(core, d_inner, normed_two, 0, cores), bits, first_order)
    sum_out = Crossing(outer_halves(core, d_branch, oT, 1, cores), bits, first_order)
    early = Adding(jnp.concatenate([small.reshape(-1), small_up.reshape(-1)]), wide_bits[:1] + first_order)
    early.split()
    early.send()
    sums = [sum_down, sum_up, sum_out, early]

    def advance(lead, *others):
        for item in sums:
            item.add()
        return launch(lead, sums, *others)

    heads = width // PAIR
    portions = 2 if heads % 2 == 0 else 1
    count = heads // portions
    keys_far = [kT_fe, vT_fe, kT_fl, vT_fl]
    far = []
    for portion in range(portions):
        (doT,) = advance(doT)
        far = back_remote(
            info,
            [qT, doT, oT, lse],
            turns_far,
            keys_far,
            group,
            parts,
            portion * count,
            count,
            far,
        )
    dq_far, d_far = far
    d_early = unproject(d_far, w_qkv, (1, 2), 0, far_rows)
    d_late = unproject(d_far, w_qkv, (1, 2), far_rows, far_rows)

    def give_back(d_early, d_late):
        early_blocks, late_blocks = [], []
        for j in range(others):
            pairs = [(n, (n + j + 1) % parts) for n in range(parts)]
            piece = d_early[j * group : (j + 1) * group]
            early_blocks.append(lax.ppermute(piece, "narrow", pairs))
        for j in range(others):
            pairs = [(n, (n + j + 1) % parts) for n in range(parts)]
            later = [(n, owner) for n, owner in pairs if owner > n]
            piece = d_late[j * group : (j + 1) * group]
            late_blocks.append(lax.ppermute(piece, "narrow", later))
        return early_blocks, late_blocks

    d_mixed = []
    for portion in range(portions):
        doT, d_early, d_late = advance(doT, d_early, d_late)
        if not portion:
            returned_early, returned_late = give_back(d_early, d_late)
        d_mixed = [
            back_local(
                info,
                [qT, doT, oT, lse],
                turns,
                [kT, vT],
                dq_far,
                group,
                portion * count,
                count,
                d_mixed,
            )
        ]
    d_mixed = d_mixed[0]
    while sum_down.order:
        (d_mixed,) = advance(d_mixed)
    for item in sums:
        item.add()

    kept, given, bias, weighted = mixed_halves(
        core,
        d_mixed.reshape(3 * width, rows),
        d_far.reshape(3 * width, -1),
        normed,
        normed_fe,
        normed_fl,
        w_qkv,
        cores,
    )
    crossing = Crossing((kept, given), bits, [])
    part_shift = weighted[1]
    part_gain = (weighted[0] - shift_one * part_shift) / gain_one
    late = Adding(
        jnp.concatenate([bias.reshape(-1), part_gain, part_shift]), wide_bits[:1] + first_order
    )
    late.split()
    late.send()
    crossing.add()
    late.add()
    share = 3 * width // devices
    third_order = wide_bits[2:3] + wide_bits[1:2] + narrow_bits + wide_bits[3:]
    orders = [first_order, narrow_bits + wide_bits[2:3] + wide_bits[1:2] + wide_bits[3:], third_order]
    runs = crossing.array.reshape(-1, share, width)
    cut = share // 3
    pieces = [
        Halving(runs[:, i * cut : (i + 1) * cut].reshape(-1, width), bits, order)
        for i, order in enumerate(orders)
    ]
    sums = pieces + [late]
    (d_mixed,) = launch(d_mixed, sums)
    back_early = functools.reduce(jnp.add, [item.astype(f32) for item in returned_early])
    back_late = functools.reduce(jnp.add, [item.astype(f32) for item in returned_late])
    if others == 1:
        back_early, back_late = returned_early[0], returned_late[0]
    d_tokens = []
    for i, returned in enumerate((back_early, back_late)):
        finish = (returned, tokens, d_middle, row(gain_one))
        d_tokens = [
            unproject(d_mixed, w_qkv, (0, 1, 2), i * group, group, finish, d_tokens)
        ]
        for item in sums:
            item.add()
        if late.order:
            d_mixed, d_tokens[0] = launch(d_mixed, sums, d_tokens[0])
    while late.order:
        for item in sums:
            item.add()
        (d_tokens[0],) = launch(d_tokens[0], sums)
    for item in sums:
        item.add()

    qkv_rows = jnp.concatenate([item.array for item in pieces], axis=0)
    down_rows = sum_down.array
    small = early.array[: 8 * width].reshape(8, width)
    small_up = early.array[8 * width :]
    late_small = late.array
    shape = inputs.shape
    return (
        result.reshape(shape),
        d_tokens[0].reshape(shape),
        qkv_rows.T,
        sum_out.array.T,
        sum_up.array.T,
        down_rows.T,
        late_small[: 3 * width],
        small[7],
        small_up,
        small[2],
        late_small[3 * width : 4 * width],
        late_small[4 * width :],
        small[5],
        small[6],
        small[3],
        small[4],
        small[0],
        small[1],
    )


def solution(mesh):
    tokens = P("wide", None, "narrow", None, None)
    columns = P(None, ("wide", "narrow"))
    in_specs = (tokens, tokens, P("wide")) + (P(),) * 16
    out_specs = (tokens, tokens) + (columns,) * 4 + (P(),) * 12
    return jax.shard_map(body, mesh=mesh, in_specs=in_specs, out_specs=out_specs, check_vma=False)
```

```python
import functools

import jax
import jax.numpy as jnp
from jax import lax
from jax.experimental import pallas as pl
from jax.experimental.pallas import tpu as pltpu
from jax.sharding import PartitionSpec as P

HEAD_DIM = 64
PAIR = 2 * HEAD_DIM
EPS = 1e-05
LOG2E = 1.4426950408889634
LN2 = 0.6931471805599453
NEG = -1e30
VMEM = 62 * 1024 * 1024
SPAN = 1024

f32 = jnp.float32
bf16 = jnp.bfloat16


def dot(left, right, left_dim, right_dim):
    return lax.dot_general(
        left, right, (((left_dim,), (right_dim,)), ((), ())), preferred_element_type=f32
    )


def fwd_chunk(q0, k0, q_n, k_n, limit, qT, kT, vT, m_ref, l_ref, acc):
    queries = pl.ds(q0, q_n)
    strip = min(256, k_n)
    for h in range(2):
        rows = slice(HEAD_DIM * h, HEAD_DIM * (h + 1))
        old = m_ref[h : h + 1, queries]
        new = old
        strips = []
        for j in range(k_n // strip):
            keys = pl.ds(k0 + j * strip, strip)
            scores = dot(kT[rows, keys], qT[rows, queries], 0, 0)
            if limit is not None:
                key_at = lax.broadcasted_iota(jnp.int32, (strip, q_n), 0)
                scores = jnp.where(key_at < limit - j * strip, scores, NEG)
            strips.append(scores)
            new = jnp.maximum(new, jnp.max(scores, axis=0, keepdims=True))
        factor = jnp.exp2(old - new)
        total = l_ref[h : h + 1, queries] * factor
        value = acc[rows, queries] * factor
        for j in range(k_n // strip):
            keys = pl.ds(k0 + j * strip, strip)
            weights = jnp.exp2(strips[j] - new)
            total = total + jnp.sum(weights, axis=0, keepdims=True)
            value = value + dot(vT[rows, keys], weights.astype(bf16), 1, 0)
        m_ref[h : h + 1, queries] = new
        l_ref[h : h + 1, queries] = total
        acc[rows, queries] = value


def pad_left(values, count):
    if not count:
        return values
    return jnp.concatenate([jnp.zeros((values.shape[0], count), f32), values], axis=1)


def pad_right(values, count):
    if not count:
        return values
    return jnp.concatenate([values, jnp.zeros((values.shape[0], count), f32)], axis=1)


def fwd_diagonal(base, group, limit, qT, kT, vT, m_ref, l_ref, acc):
    strip = min(256, group)
    count = group // strip
    for h in range(2):
        rows = slice(HEAD_DIM * h, HEAD_DIM * (h + 1))
        strips = []
        for j in range(count):
            wide = group - j * strip
            keys, queries = pl.ds(base + j * strip, strip), pl.ds(base + j * strip, wide)
            scores = dot(kT[rows, keys], qT[rows, queries], 0, 0)
            key_at = lax.broadcasted_iota(jnp.int32, scores.shape, 0)
            query_at = lax.broadcasted_iota(jnp.int32, scores.shape, 1)
            scores = jnp.where(key_at <= query_at, scores, NEG)
            if limit is not None:
                scores = jnp.where(key_at < limit - j * strip, scores, NEG)
            strips.append(scores)
        peaks = []
        for g in range(count):
            peak = None
            for j in range(g + 1):
                part = strips[j][:, (g - j) * strip : (g - j + 1) * strip]
                part = jnp.max(part, axis=0, keepdims=True)
                peak = part if peak is None else jnp.maximum(peak, part)
            peaks.append(peak)
        peak = jnp.concatenate(peaks, axis=1) if count > 1 else peaks[0]
        total, value = None, None
        for j in range(count):
            keys = pl.ds(base + j * strip, strip)
            weights = jnp.exp2(strips[j] - peak[:, j * strip :])
            part = pad_left(jnp.sum(weights, axis=0, keepdims=True), j * strip)
            term = pad_left(dot(vT[rows, keys], weights.astype(bf16), 1, 0), j * strip)
            total = part if total is None else total + part
            value = term if value is None else value + term
        queries = pl.ds(base, group)
        m_ref[h : h + 1, queries] = peak
        l_ref[h : h + 1, queries] = total
        acc[rows, queries] = value


def fwd_local_kernel(group, info, qT, kT, vT, acc, m_ref, l_ref):
    length = info[1]
    m_ref[...] = jnp.full(m_ref.shape, NEG, f32)
    l_ref[...] = jnp.zeros(l_ref.shape, f32)
    acc[...] = jnp.zeros(acc.shape, f32)
    refs = (qT, kT, vT, m_ref.at[0], l_ref.at[0], acc)

    def own(i, carry):
        base = pl.multiple_of(i * group, group)
        start = info[2 + i]

        @pl.when(start + group <= length)
        def _():
            fwd_diagonal(base, group, None, *refs)

        @pl.when((start < length) & (start + group > length))
        def _():
            fwd_diagonal(base, group, length - start, *refs)

        return carry

    lax.fori_loop(0, 2, own, 0)
    early = info[2]

    @pl.when(early + group <= length)
    def _():
        fwd_chunk(group, 0, group, group, None, *refs)

    @pl.when((early < length) & (early + group > length))
    def _():
        fwd_chunk(group, 0, group, group, length - early, *refs)


def remote_steps(group, parts, info, full, partial):
    place, length = info[0], info[1]

    def visit(i, carry):
        j, turn_at = i // 3, lax.rem(i, 3)
        other = lax.rem(place + 1 + j, parts)
        late_key = turn_at == 2
        block = jnp.where(late_key, 2 * parts - 1 - other, other)
        before = (other < place).astype(jnp.int32)
        wanted = jnp.where(turn_at == 0, before, jnp.where(late_key, 1 - before, 1)) == 1
        q0 = pl.multiple_of(jnp.where(turn_at == 0, 0, group), group)
        k0 = pl.multiple_of((2 * j + jnp.where(late_key, 1, 0)) * group, group)
        start = block * group

        @pl.when(wanted & (start + group <= length))
        def _():
            full(q0, k0)

        @pl.when(wanted & (start < length) & (start + group > length))
        def _():
            partial(q0, k0, length - start)

        return carry

    lax.fori_loop(0, 3 * (parts - 1), visit, 0)


def fwd_remote_kernel(
    group, parts, info, qT, kT, vT, acc_in, m_in, l_in, out, lse, acc, m_ref, l_ref
):
    acc[...] = acc_in[...]
    m_ref[...] = m_in[0]
    l_ref[...] = l_in[0]
    refs = (qT, kT, vT, m_ref, l_ref, acc)

    def full(q0, k0):
        fwd_chunk(q0, k0, group, group, None, *refs)

    def partial(q0, k0, limit):
        fwd_chunk(q0, k0, group, group, limit, *refs)

    remote_steps(group, parts, info, full, partial)
    for h in range(2):
        rows = slice(HEAD_DIM * h, HEAD_DIM * (h + 1))
        total = l_ref[h : h + 1, :]
        out[rows, :] = (acc[rows, :] / total).astype(bf16)
        lse[0, h : h + 1, :] = m_ref[h : h + 1, :] + jnp.log2(total)


def split_three(values):
    high = values.astype(bf16).astype(f32)
    rest = values - high
    middle = rest.astype(bf16).astype(f32)
    low = (rest - middle).astype(bf16).astype(f32)
    return [high, middle, low]


def bwd_prepare(qT, kT, vT, doT, oT, lse, qa, da, ka, va):
    n_q, n_k = qT.shape[1], ka.shape[2]
    extra = qa.shape[1] - HEAD_DIM
    pad = jnp.zeros((extra - 3, n_q), f32)
    row_at = lax.broadcasted_iota(jnp.int32, (extra, n_k), 0)
    tail = jnp.where(row_at < 3, 1.0, 0.0).astype(bf16)
    for h in range(2):
        rows = slice(HEAD_DIM * h, HEAD_DIM * (h + 1))
        grad = doT[rows, :].astype(f32)
        delta = jnp.sum(grad * oT[rows, :].astype(f32), axis=0, keepdims=True)
        qa[h, :HEAD_DIM, :] = qT[rows, :]
        parts = split_three(-lse[0, h : h + 1, :]) + [pad]
        qa[h, HEAD_DIM:, :] = jnp.concatenate(parts, axis=0).astype(bf16)
        da[h, :HEAD_DIM, :] = doT[rows, :]
        parts = split_three(-delta) + [pad]
        da[h, HEAD_DIM:, :] = jnp.concatenate(parts, axis=0).astype(bf16)
        ka[h, :HEAD_DIM, :] = kT[rows, :]
        va[h, :HEAD_DIM, :] = vT[rows, :]
        ka[h, HEAD_DIM:, :] = tail
        va[h, HEAD_DIM:, :] = tail


def bwd_chunk(q0, k0, q_n, k_n, limit, qT, doT, qa, da, ka, va, dq, dk, dv):
    queries, keys = pl.ds(q0, q_n), pl.ds(k0, k_n)
    for h in range(2):
        rows = slice(HEAD_DIM * h, HEAD_DIM * (h + 1))
        probs = jnp.exp2(dot(qa[h, :, queries], ka[h, :, keys], 0, 0))
        if limit is not None:
            key_at = lax.broadcasted_iota(jnp.int32, (q_n, k_n), 1)
            probs = jnp.where(key_at < limit, probs, 0.0)
        d_probs = dot(da[h, :, queries], va[h, :, keys], 0, 0)
        d_scores = (probs * d_probs).astype(bf16)
        dv[rows, keys] += dot(doT[rows, queries], probs.astype(bf16), 1, 0)
        dk[rows, keys] += dot(qT[rows, queries], d_scores, 1, 0)
        dq[rows, queries] += dot(ka[h, :HEAD_DIM, keys], d_scores, 1, 1)


def bwd_diagonal(base, group, limit, qT, doT, qa, da, ka, va, dq, dk, dv):
    strip = min(256, group)
    count = group // strip
    for h in range(2):
        rows = slice(HEAD_DIM * h, HEAD_DIM * (h + 1))
        d_keys, d_values, d_queries = None, None, []
        for j in range(count):
            wide = (j + 1) * strip
            queries, keys = pl.ds(base + j * strip, strip), pl.ds(base, wide)
            probs = jnp.exp2(dot(qa[h, :, queries], ka[h, :, keys], 0, 0))
            query_at = lax.broadcasted_iota(jnp.int32, probs.shape, 0)
            key_at = lax.broadcasted_iota(jnp.int32, probs.shape, 1)
            probs = jnp.where(key_at <= query_at + j * strip, probs, 0.0)
            if limit is not None:
                probs = jnp.where(key_at < limit, probs, 0.0)
            d_probs = dot(da[h, :, queries], va[h, :, keys], 0, 0)
            d_scores = (probs * d_probs).astype(bf16)
            value = pad_right(dot(doT[rows, queries], probs.astype(bf16), 1, 0), group - wide)
            key = pad_right(dot(qT[rows, queries], d_scores, 1, 0), group - wide)
            d_values = value if d_values is None else d_values + value
            d_keys = key if d_keys is None else d_keys + key
            d_queries.append(dot(ka[h, :HEAD_DIM, keys], d_scores, 1, 1))
        here = pl.ds(base, group)
        dq[rows, here] += jnp.concatenate(d_queries, axis=1) if count > 1 else d_queries[0]
        dk[rows, here] += d_keys
        dv[rows, here] += d_values


def turn_back(values, cosine, sine):
    half = HEAD_DIM // 2
    first, second = values[:half], values[half:]
    return jnp.concatenate(
        [first * cosine + second * sine, second * cosine - first * sine], axis=0
    )


def bwd_remote_kernel(group, parts, info, qT, doT, oT, lse, cosine, sine, kT, vT, *rest):
    dq, dkv, *scratch = rest[-8:]
    qa, da, ka, va, dk, dv = scratch
    bwd_prepare(qT, kT, vT, doT, oT, lse, qa, da, ka, va)
    dq[...] = jnp.zeros(dq.shape, f32)
    dk[...] = jnp.zeros(dk.shape, f32)
    dv[...] = jnp.zeros(dv.shape, f32)
    refs = (qT, doT, qa, da, ka, va, dq, dk, dv)

    def full(q0, k0):
        bwd_chunk(q0, k0, group, group, None, *refs)

    def partial(q0, k0, limit):
        bwd_chunk(q0, k0, group, group, limit, *refs)

    remote_steps(group, parts, info, full, partial)
    for h in range(2):
        rows = slice(HEAD_DIM * h, HEAD_DIM * (h + 1))
        dkv[1, rows, :] = turn_back(dk[rows, :] * LN2, cosine[...], sine[...]).astype(bf16)
    dkv[0] = jnp.zeros(dv.shape, bf16)
    dkv[2] = dv[...].astype(bf16)


def bwd_local_kernel(group, info, qT, doT, oT, lse, cosine, sine, kT, vT, dq_in, *rest):
    dqkv, *scratch = rest[-8:]
    qa, da, ka, va, dq, dk, dv = scratch
    length = info[1]
    bwd_prepare(qT, kT, vT, doT, oT, lse, qa, da, ka, va)
    dq[...] = dq_in[...]
    dk[...] = jnp.zeros(dk.shape, f32)
    dv[...] = jnp.zeros(dv.shape, f32)
    refs = (qT, doT, qa, da, ka, va, dq, dk, dv)

    def own(i, carry):
        base = pl.multiple_of(i * group, group)
        start = info[2 + i]

        @pl.when(start + group <= length)
        def _():
            bwd_diagonal(base, group, None, *refs)

        @pl.when((start < length) & (start + group > length))
        def _():
            bwd_diagonal(base, group, length - start, *refs)

        return carry

    lax.fori_loop(0, 2, own, 0)
    early = info[2]

    @pl.when(early + group <= length)
    def _():
        bwd_chunk(group, 0, group, group, None, *refs)

    @pl.when((early < length) & (early + group > length))
    def _():
        bwd_chunk(group, 0, group, group, length - early, *refs)

    for h in range(2):
        rows = slice(HEAD_DIM * h, HEAD_DIM * (h + 1))
        d_query = dq[rows, :] * 0.125
        dqkv[0, rows, :] = turn_back(d_query, cosine[...], sine[...]).astype(bf16)
        dqkv[1, rows, :] = turn_back(dk[rows, :] * LN2, cosine[...], sine[...]).astype(bf16)
    dqkv[2] = dv[...].astype(bf16)


def rows_of(count, first=0):
    return pl.BlockSpec((PAIR, count), lambda i, info: (first + i, 0))


def stats_of(count, first=0):
    return pl.BlockSpec((1, 2, count), lambda i, info: (first + i, 0, 0))


def planes_of(planes, count, first=0):
    return pl.BlockSpec((planes, PAIR, count), lambda i, info: (0, first + i, 0))


def whole(shape):
    return pl.BlockSpec(shape, lambda i, info: (0,) * len(shape))


def attention_call(kernel, pairs, in_specs, out_specs, out_shape, scratch, flops, name, alias={}):
    return pl.pallas_call(
        kernel,
        grid_spec=pltpu.PrefetchScalarGridSpec(
            num_scalar_prefetch=1,
            grid=(pairs,),
            in_specs=in_specs,
            out_specs=out_specs,
            scratch_shapes=scratch,
        ),
        out_shape=out_shape,
        input_output_aliases=alias,
        compiler_params=pltpu.CompilerParams(vmem_limit_bytes=VMEM),
        cost_estimate=pl.CostEstimate(
            flops=int(flops), bytes_accessed=1 << 25, transcendentals=0
        ),
        name=name,
    )


def attend_local(info, qT, kT, vT, group):
    width, n_q = qT.shape
    pairs = width // PAIR
    call = attention_call(
        functools.partial(fwd_local_kernel, group),
        pairs,
        [rows_of(n_q)] * 3,
        [rows_of(n_q), stats_of(n_q), stats_of(n_q)],
        [
            jax.ShapeDtypeStruct((width, n_q), f32),
            jax.ShapeDtypeStruct((pairs, 2, n_q), f32),
            jax.ShapeDtypeStruct((pairs, 2, n_q), f32),
        ],
        [],
        4 * width * 2 * group * group * 4,
        "attend_local",
    )
    return call(info, qT, kT, vT)


def attend_remote(info, qT, kT, vT, state, group, parts):
    width, n_q = qT.shape
    n_k = kT.shape[1]
    pairs = width // PAIR
    call = attention_call(
        functools.partial(fwd_remote_kernel, group, parts),
        pairs,
        [rows_of(n_q), rows_of(n_k), rows_of(n_k), rows_of(n_q), stats_of(n_q), stats_of(n_q)],
        [rows_of(n_q), stats_of(n_q)],
        [
            jax.ShapeDtypeStruct((width, n_q), bf16),
            jax.ShapeDtypeStruct((pairs, 2, n_q), f32),
        ],
        [pltpu.VMEM((PAIR, n_q), f32)] + [pltpu.VMEM((2, n_q), f32)] * 2,
        4 * width * 2 * group * group * 4,
        "attend_remote",
    )
    return call(info, qT, kT, vT, *state)


def back_scratch(n_q, n_k):
    rows = HEAD_DIM + 16
    return [
        pltpu.VMEM((2, rows, n_q), bf16),
        pltpu.VMEM((2, rows, n_q), bf16),
        pltpu.VMEM((2, rows, n_k), bf16),
        pltpu.VMEM((2, rows, n_k), bf16),
    ]


def back_remote(info, operands, turns, keys, group, parts, first, count, before):
    width, n_q = operands[0].shape
    n_k = keys[0].shape[1]
    half = HEAD_DIM // 2
    n_in = 1 + len(operands) + len(turns) + len(keys)
    call = attention_call(
        functools.partial(bwd_remote_kernel, group, parts),
        count,
        [rows_of(n_q, first)] * 3
        + [stats_of(n_q, first)]
        + [whole((half, n_k))] * 2
        + [rows_of(n_k, first)] * 2
        + [pl.BlockSpec(memory_space=pl.ANY)] * len(before),
        [rows_of(n_q, first), planes_of(3, n_k, first)],
        [
            jax.ShapeDtypeStruct((width, n_q), f32),
            jax.ShapeDtypeStruct((3, width, n_k), bf16),
        ],
        back_scratch(n_q, n_k) + [pltpu.VMEM((PAIR, n_k), f32)] * 2,
        10 * count * PAIR * 2 * group * group * 4,
        "back_remote",
        {n_in + i: i for i in range(len(before))},
    )
    return call(info, *operands, *turns, *keys, *before)


def back_local(info, operands, turns, keys, dq, group, first, count, before):
    width, n_q = operands[0].shape
    half = HEAD_DIM // 2
    n_in = 1 + len(operands) + len(turns) + len(keys) + 1
    call = attention_call(
        functools.partial(bwd_local_kernel, group),
        count,
        [rows_of(n_q, first)] * 3
        + [stats_of(n_q, first)]
        + [whole((half, n_q))] * 2
        + [rows_of(n_q, first)] * 3
        + [pl.BlockSpec(memory_space=pl.ANY)] * len(before),
        planes_of(3, n_q, first),
        jax.ShapeDtypeStruct((3, width, n_q), bf16),
        back_scratch(n_q, n_q) + [pltpu.VMEM((PAIR, n_q), f32)] * 3,
        10 * count * PAIR * 2 * group * group * 4,
        "back_local",
        {n_in + i: i for i in range(len(before))},
    )
    return call(info, *operands, *turns, *keys, dq, *before)


def normalize(values):
    centre = values - jnp.mean(values, axis=-1, keepdims=True)
    spread = jnp.mean(centre * centre, axis=-1, keepdims=True)
    rate = lax.rsqrt(spread + EPS)
    return centre * rate, rate


def norm_back(grad, unit, rate, gain):
    scaled = grad * gain
    first = jnp.mean(scaled, axis=-1, keepdims=True)
    second = jnp.mean(scaled * unit, axis=-1, keepdims=True)
    return rate * (scaled - first - unit * second)


GELU_A = 0.7978845608028654
GELU_B = 0.044715


def column_sum(values):
    return jnp.sum(values, axis=0, keepdims=True)


def block_kernel(
    span,
    oT,
    tokens,
    cotangent,
    w_out,
    w_up,
    w_down,
    b_out,
    b_up,
    b_down,
    gain_two,
    shift_two,
    gain_three,
    shift_three,
    gain_four,
    shift_four,
    result,
    d_middle_out,
    hidden_out,
    d_outer_out,
    normed_out,
    d_inner_out,
    d_branch_out,
    doT,
    small,
    small_up,
    slope,
):
    step = pl.program_id(0)

    @pl.when(step == 0)
    def _():
        small[...] = jnp.zeros(small.shape, f32)
        small_up[...] = jnp.zeros(small_up.shape, f32)

    wide = w_up.shape[1]
    branch = dot(oT[...], w_out[...], 0, 0) + b_out[...]
    unit_two, rate_two = normalize(branch)
    middle = tokens[...].astype(f32) + (unit_two * gain_two[...] + shift_two[...])
    unit_three, rate_three = normalize(middle)
    normed = (unit_three * gain_three[...] + shift_three[...]).astype(bf16)
    normed_out[...] = normed
    outer = None
    for c in range(wide // span):
        columns = slice(c * span, (c + 1) * span)
        inner = dot(normed, w_up[:, columns], 1, 0) + b_up[:, columns]
        square = inner * inner
        bend = jnp.tanh(inner * (GELU_A + (GELU_A * GELU_B) * square))
        half = 0.5 + 0.5 * bend
        hidden = (inner * half).astype(bf16)
        hidden_out[:, columns] = hidden
        slope[:, columns] = half + inner * (1.0 - bend * bend) * (
            0.5 * GELU_A + (1.5 * GELU_A * GELU_B) * square
        )
        term = dot(hidden, w_down[columns, :], 1, 0)
        outer = term if outer is None else outer + term
    unit_four, rate_four = normalize(outer + b_down[...])
    result[...] = (middle + (unit_four * gain_four[...] + shift_four[...])).astype(bf16)

    grad = cotangent[...].astype(f32)
    d_outer = norm_back(grad, unit_four, rate_four, gain_four[...]).astype(bf16)
    d_outer_out[...] = d_outer
    small[0:1, :] += column_sum(grad * unit_four)
    small[1:2, :] += column_sum(grad)
    small[2:3, :] += column_sum(d_outer.astype(f32))
    d_normed = None
    for c in range(wide // span):
        columns = slice(c * span, (c + 1) * span)
        d_hidden = dot(d_outer, w_down[columns, :], 1, 1)
        d_inner = (d_hidden * slope[:, columns]).astype(bf16)
        d_inner_out[:, columns] = d_inner
        small_up[:, columns] += column_sum(d_inner.astype(f32))
        term = dot(d_inner, w_up[:, columns], 1, 1)
        d_normed = term if d_normed is None else d_normed + term
    small[3:4, :] += column_sum(d_normed * unit_three)
    small[4:5, :] += column_sum(d_normed)
    d_middle = grad + norm_back(d_normed, unit_three, rate_three, gain_three[...])
    d_middle_out[...] = d_middle
    small[5:6, :] += column_sum(d_middle * unit_two)
    small[6:7, :] += column_sum(d_middle)
    d_branch = norm_back(d_middle, unit_two, rate_two, gain_two[...]).astype(bf16)
    d_branch_out[...] = d_branch
    small[7:8, :] += column_sum(d_branch.astype(f32))
    doT[...] = dot(w_out[...], d_branch, 1, 1).astype(bf16)


def block_call(oT, tokens, cotangent, weights, vectors):
    width, rows = oT.shape
    wide = weights[1].shape[1]
    step = min(256, rows)
    span = min(SPAN, wide)

    def lines(count):
        return pl.BlockSpec((step, count), lambda i: (i, 0))

    def fixed(shape):
        return pl.BlockSpec(shape, lambda i: (0, 0), pipeline_mode=pl.Buffered(1))

    def total(shape):
        return pl.BlockSpec(shape, lambda i: (0, 0))

    features = pl.BlockSpec((width, step), lambda i: (0, i))
    sizes = [width, width, wide, width, width, wide, width]
    kinds = [bf16, f32, bf16, bf16, bf16, bf16, bf16]
    return pl.pallas_call(
        functools.partial(block_kernel, span),
        grid=(rows // step,),
        in_specs=[features, lines(width), lines(width)]
        + [fixed(item.shape) for item in weights]
        + [fixed(item.shape) for item in vectors],
        out_specs=[lines(size) for size in sizes]
        + [features, total((8, width)), total((1, wide))],
        out_shape=[jax.ShapeDtypeStruct((rows, size), kind) for size, kind in zip(sizes, kinds)]
        + [
            jax.ShapeDtypeStruct((width, rows), bf16),
            jax.ShapeDtypeStruct((8, width), f32),
            jax.ShapeDtypeStruct((1, wide), f32),
        ],
        scratch_shapes=[pltpu.VMEM((step, wide), f32)],
        compiler_params=pltpu.CompilerParams(vmem_limit_bytes=VMEM),
        cost_estimate=pl.CostEstimate(
            flops=2 * 2 * rows * (width * width + 2 * width * wide),
            bytes_accessed=1 << 26,
            transcendentals=rows * wide,
        ),
        name="block",
    )(oT, tokens, cotangent, *weights, *vectors)


def turn(values, cosine, sine):
    half = HEAD_DIM // 2
    first, second = values[:half], values[half:]
    return jnp.concatenate(
        [first * cosine - second * sine, second * cosine + first * sine], axis=0
    )


def project_kernel(sections, tokens, w, b, gain, shift, cosine, sine, normed_out, *outs):
    unit, rate = normalize(tokens[...].astype(f32))
    normed = (unit * gain[...] + shift[...]).astype(bf16)
    normed_out[...] = normed
    width = tokens.shape[1]
    chunk = min(256, width)
    for section, out in zip(sections, outs):
        for c in range(width // chunk):
            at = section * width + c * chunk
            mixed = dot(w[:, at : at + chunk], normed, 0, 1) + b[at : at + chunk, :]
            for h in range(chunk // HEAD_DIM):
                rows = slice(h * HEAD_DIM, (h + 1) * HEAD_DIM)
                place = slice(c * chunk + h * HEAD_DIM, c * chunk + (h + 1) * HEAD_DIM)
                value = mixed[rows]
                if section < 2:
                    value = turn(value, cosine[...], sine[...])
                if section == 0:
                    value = value * (0.125 * LOG2E)
                out[place, :] = value.astype(bf16)


def project(tokens, w, b, gain, shift, cosine, sine, sections):
    rows, width = tokens.shape
    step = min(512, rows)
    half = HEAD_DIM // 2

    def fixed(shape):
        return pl.BlockSpec(shape, lambda i: (0, 0), pipeline_mode=pl.Buffered(1))

    lines = pl.BlockSpec((step, width), lambda i: (i, 0))
    features = pl.BlockSpec((width, step), lambda i: (0, i))
    turns = pl.BlockSpec((half, step), lambda i: (0, i))
    return pl.pallas_call(
        functools.partial(project_kernel, sections),
        grid=(rows // step,),
        in_specs=[lines, fixed(w.shape), fixed(b.shape), fixed(gain.shape), fixed(shift.shape)]
        + [turns] * 2,
        out_specs=[lines] + [features] * len(sections),
        out_shape=[jax.ShapeDtypeStruct((rows, width), bf16)]
        + [jax.ShapeDtypeStruct((width, rows), bf16)] * len(sections),
        compiler_params=pltpu.CompilerParams(vmem_limit_bytes=VMEM),
        cost_estimate=pl.CostEstimate(
            flops=2 * rows * width * width * len(sections),
            bytes_accessed=1 << 24,
            transcendentals=0,
        ),
        name="project",
    )(tokens, w, b, gain, shift, cosine, sine)


def unproject_kernel(planes, finish, *refs):
    d_mixed, w, out = refs[: len(planes)], refs[len(planes)], refs[-1]
    width = w.shape[0]
    total = None
    for plane, ref in zip(planes, d_mixed):
        term = dot(ref[0], w[:, plane * width : (plane + 1) * width], 0, 1)
        total = term if total is None else total + term
    if not finish:
        out[...] = total.astype(bf16)
        return
    returned, tokens, d_middle, gain = refs[len(planes) + 1 : len(planes) + 5]
    total = total + returned[...].astype(f32)
    unit, rate = normalize(tokens[...].astype(f32))
    out[...] = (d_middle[...] + norm_back(total, unit, rate, gain[...])).astype(bf16)


def unproject(d_mixed, w, planes, start, count, finish=(), before=()):
    _, width, total = d_mixed.shape
    step = min(256, count)
    first = start // step

    def fixed(shape):
        return pl.BlockSpec(shape, lambda i: (0, 0), pipeline_mode=pl.Buffered(1))

    def plane_of(plane):
        return pl.BlockSpec((1, width, step), lambda i: (plane, 0, first + i))

    lines = pl.BlockSpec((step, width), lambda i: (i, 0))
    later = pl.BlockSpec((step, width), lambda i: (first + i, 0))
    specs = [later] * 3 + [fixed(finish[-1].shape)] if finish else []
    n_in = len(planes) + 1 + len(finish)
    return pl.pallas_call(
        functools.partial(unproject_kernel, planes, bool(finish)),
        grid=(count // step,),
        in_specs=[plane_of(plane) for plane in planes]
        + [fixed(w.shape)]
        + specs
        + [pl.BlockSpec(memory_space=pl.ANY)] * len(before),
        out_specs=later if finish else lines,
        out_shape=jax.ShapeDtypeStruct((total if finish else count, width), bf16),
        input_output_aliases={n_in + i: i for i in range(len(before))},
        compiler_params=pltpu.CompilerParams(vmem_limit_bytes=VMEM),
        cost_estimate=pl.CostEstimate(
            flops=2 * count * width * width * len(planes),
            bytes_accessed=1 << 24,
            transcendentals=0,
        ),
        name="unproject",
    )(*[d_mixed] * len(planes), w, *finish, *before)


def divide(total, run, levels, near, marks, orders, outs):
    chunks = [total[at : at + run] for at in range(0, total.shape[0], run)]
    bits = [("narrow", i) for i in range(near)] + [("wide", i) for i in range(levels + 1)]
    for place, (axis, position) in enumerate(bits):
        mine = (marks[1 if axis == "narrow" else 0] >> position) & 1
        chunks = [
            jnp.where(mine == 1, chunks[k ^ (1 << place)], chunks[k]) for k in range(len(chunks))
        ]
    cut = run // len(orders)
    for i, order in enumerate(orders):
        for k, chunk in enumerate(chunks):
            value = {bit: (k >> place) & 1 for place, bit in enumerate(bits)}
            out = outs[2 * i + value["wide", 0]]
            index = tuple(value.get(bit, 0) for bit in order)
            out[index] = chunk[i * cut : (i + 1) * cut].astype(bf16)


def divided(orders, levels, run, height, wide, width):
    cut = run // len(orders)
    specs, shapes = [], []
    for order in orders:

        def held(bit):
            return bit[0] == "narrow" or bit[1] <= levels

        def index(j, i, marks, order=order):
            relative = i ^ (marks[0] >> (levels + 1))
            at = [0 if held(bit) else (relative >> (bit[1] - 1 - levels)) & 1 for bit in order]
            return (*at, 0, j)

        block = tuple(2 if held(bit) else 1 for bit in order) + (cut, wide)
        specs += [pl.BlockSpec(block, index)] * 2
        shapes += [jax.ShapeDtypeStruct((2,) * len(order) + (cut, width), bf16)] * 2
    return specs, shapes


def outer_kernel(run, levels, near, orders, right_dim, marks, left, right, *outs):
    divide(dot(left[...], right[...], 0, right_dim), run, levels, near, marks, orders, outs)


def outer_halves(marks, left, right, right_dim, cores, parts, order):
    rows, height = left.shape
    width = right.shape[1 - right_dim]
    share = height // cores
    high = max(2 * share, min(512, height))
    levels = (high // (2 * share)).bit_length() - 1
    wide = min(1024, width)
    if right_dim == 0:
        right_spec = pl.BlockSpec((rows, wide), lambda j, i, marks: (0, j))
    else:
        right_spec = pl.BlockSpec((wide, rows), lambda j, i, marks: (j, 0))
    run = share // parts
    near = parts.bit_length() - 1
    specs, shapes = divided([order], levels, run, height, wide, width)
    halves = pl.pallas_call(
        functools.partial(outer_kernel, run, levels, near, [order], right_dim),
        grid_spec=pltpu.PrefetchScalarGridSpec(
            num_scalar_prefetch=1,
            grid=(width // wide, height // high),
            in_specs=[pl.BlockSpec((rows, high), lambda j, i, marks: (0, i)), right_spec],
            out_specs=specs,
        ),
        out_shape=shapes,
        compiler_params=pltpu.CompilerParams(vmem_limit_bytes=VMEM),
        cost_estimate=pl.CostEstimate(
            flops=2 * rows * height * width, bytes_accessed=1 << 25, transcendentals=0
        ),
        name="outer",
    )(marks, left, right)
    return [item.reshape(height // 2, width) for item in halves]


def mixed_kernel(
    run, levels, near, orders, first_far, marks, d_own, d_far, normed, normed_far, w, *outs
):
    *halves, bias, sums = outs
    step = pl.program_id(1)
    total = dot(d_own[...], normed[...], 1, 0)
    bias[...] = jnp.sum(d_own[...].astype(f32), axis=1, keepdims=True)

    @pl.when(step == 0)
    def _():
        sums[...] = jnp.zeros(sums.shape, f32)

    def finish(value):
        divide(value, run, levels, near, marks, orders, halves)
        weights = w[...].astype(f32).T
        sums[0:1, :] += column_sum(weights * value)
        sums[1:2, :] += column_sum(weights * bias[...])

    @pl.when(step < first_far)
    def _():
        finish(total)

    @pl.when(step >= first_far)
    def _():
        bias[...] += jnp.sum(d_far[...].astype(f32), axis=1, keepdims=True)
        finish(total + dot(d_far[...], normed_far[...], 1, 0))


def mixed_halves(marks, d_own, d_far, normed, normed_far, w, cores, parts, orders):
    height, rows = d_own.shape
    far = d_far.shape[1]
    width = normed.shape[1]
    share = height // cores
    pairs = max(1, 384 // (2 * share))
    levels = pairs.bit_length() - 1
    high = 2 * share * pairs
    first_far = width // high
    run = share // parts
    near = parts.bit_length() - 1

    def fixed(shape):
        return pl.BlockSpec(shape, lambda j, i, marks: (0, 0), pipeline_mode=pl.Buffered(1))

    specs, shapes = divided(orders, levels, run, height, width, width)
    *halves, bias, sums = pl.pallas_call(
        functools.partial(mixed_kernel, run, levels, near, orders, first_far),
        grid_spec=pltpu.PrefetchScalarGridSpec(
            num_scalar_prefetch=1,
            grid=(1, height // high),
            in_specs=[
                pl.BlockSpec((high, rows), lambda j, i, marks: (i, 0)),
                pl.BlockSpec((high, far), lambda j, i, marks: (jnp.maximum(i, first_far), 0)),
                fixed(normed.shape),
                fixed(normed_far.shape),
                pl.BlockSpec((width, high), lambda j, i, marks: (0, i)),
            ],
            out_specs=specs
            + [
                pl.BlockSpec((high, 1), lambda j, i, marks: (i, 0)),
                pl.BlockSpec((2, width), lambda j, i, marks: (0, 0)),
            ],
        ),
        out_shape=shapes
        + [
            jax.ShapeDtypeStruct((height, 1), f32),
            jax.ShapeDtypeStruct((2, width), f32),
        ],
        compiler_params=pltpu.CompilerParams(vmem_limit_bytes=VMEM),
        cost_estimate=pl.CostEstimate(
            flops=2 * (rows + far) * height * width, bytes_accessed=1 << 25, transcendentals=0
        ),
        name="mixed",
    )(marks, d_own, d_far, normed, normed_far, w)
    halves = [item.reshape(-1, width) for item in halves]
    return [halves[i : i + 2] for i in range(0, len(halves), 2)], bias, sums


def bit_of(axis, position):
    return (lax.axis_index(axis) >> position) & 1


def swap(values, axis, position):
    size = lax.axis_size(axis)
    return lax.ppermute(values, axis, [(i, i ^ (1 << position)) for i in range(size)])


class Halving:
    def __init__(self, halves, order):
        self.order = list(order)
        kept, given = halves
        self.terms = [kept, swap(given, "wide", 0)]

    def send(self, array, away):
        self.terms = [array, swap(away, *self.order.pop(0))]


class Adding:
    def __init__(self, array, order):
        self.order = list(order)
        self.terms = [array, swap(array, *self.order.pop(0))]

    def send(self, total):
        self.terms = [total, swap(total, *self.order.pop(0))]


def halve_kernel(count, *refs):
    ins, outs = refs[: 4 * count + 2], refs[4 * count + 2 :]
    for i in range(count):
        one, two = ins[4 * i : 4 * i + 2], ins[4 * i + 2 : 4 * i + 4]
        for half in range(2):
            total = one[half][0].astype(f32) + two[half][0].astype(f32)
            outs[2 * i + half][...] = total.astype(bf16)
    outs[-1][...] = ins[-2][...] + ins[-1][...]


def halve(sums, small):
    heights = [item.terms[0].shape[0] // 2 for item in sums]
    grid = 4 if all(height % 64 == 0 for height in heights) else 1
    operands, in_specs, out_specs, out_shape = [], [], [], []
    for item, height in zip(sums, heights):
        width = item.terms[0].shape[1]
        block = (height // grid, width)
        for term in item.terms:
            for half in range(2):
                operands.append(term.reshape(2, height, width))
                in_specs.append(pl.BlockSpec((1, *block), lambda i, half=half: (half, i, 0)))
        out_specs += [pl.BlockSpec(block, lambda i: (i, 0))] * 2
        out_shape += [jax.ShapeDtypeStruct((height, width), bf16)] * 2
    whole_small = pl.BlockSpec(small.terms[0].shape, lambda i: (0, 0))
    return pl.pallas_call(
        functools.partial(halve_kernel, len(sums)),
        grid=(grid,),
        in_specs=in_specs + [whole_small] * 2,
        out_specs=out_specs + [whole_small],
        out_shape=out_shape + [jax.ShapeDtypeStruct(small.terms[0].shape, f32)],
        compiler_params=pltpu.CompilerParams(vmem_limit_bytes=VMEM),
        name="halve",
    )(*operands, *small.terms)


def launch(lead, sums, small, *others):
    lead, others, halves = lax.optimization_barrier((lead, others, halve(sums, small)))
    for i, item in enumerate(sums):
        item.send(halves[2 * i], halves[2 * i + 1])
    small.send(halves[-1])
    return (lead, *others)


def settle(lead, sums, small):
    everything = sums + [small]
    lead, terms = lax.optimization_barrier((lead, [item.terms for item in everything]))
    for item, arrays in zip(everything, terms):
        item.terms = list(arrays)
    return lead


def collect_kernel(groups, *refs):
    at = 0
    for out, count in zip(refs[-len(groups) :], groups):
        parts = [
            refs[at + 2 * i][...].astype(f32) + refs[at + 2 * i + 1][...].astype(f32)
            for i in range(count)
        ]
        at += 2 * count
        height = parts[0].shape[0]
        for i, part in enumerate(parts):
            out[i * height : (i + 1) * height, :] = part


def collect(groups):
    operands = [term for group in groups for item in group for term in item.terms]
    return pl.pallas_call(
        functools.partial(collect_kernel, [len(group) for group in groups]),
        out_shape=[
            jax.ShapeDtypeStruct(
                (sum(item.terms[0].shape[0] for item in group), group[0].terms[0].shape[1]), f32
            )
            for group in groups
        ],
        compiler_params=pltpu.CompilerParams(vmem_limit_bytes=VMEM),
        name="collect",
    )(*operands)


def angles(positions):
    half = HEAD_DIM // 2
    freqs = jnp.power(10000.0, -jnp.arange(half, dtype=f32) / half)
    theta = freqs[:, None] * positions.astype(f32)[None, :]
    return jnp.cos(theta), jnp.sin(theta)


def axis_bits(axis):
    return [(axis, position) for position in range(lax.axis_size(axis).bit_length() - 1)]


def body(
    inputs,
    cotangent,
    lengths,
    w_qkv,
    b_qkv,
    w_out,
    b_out,
    w_up,
    b_up,
    w_down,
    b_down,
    gain_one,
    shift_one,
    gain_two,
    shift_two,
    gain_three,
    shift_three,
    gain_four,
    shift_four,
):
    group = inputs.shape[3]
    width = inputs.shape[4]
    parts = lax.axis_size("narrow")
    place = lax.axis_index("narrow")
    cores = lax.axis_size("wide")
    others = parts - 1
    rows = 2 * group
    offsets = jnp.arange(group, dtype=jnp.int32)

    def row(vector):
        return vector[None, :]

    def positions(owners):
        starts = jnp.stack([owners, 2 * parts - 1 - owners], axis=1).reshape(-1) * group
        return (starts[:, None] + offsets[None]).reshape(-1)

    def joined(items):
        return jnp.concatenate(items, axis=0) if len(items) > 1 else items[0]

    tokens = inputs.reshape(rows, width)
    far_tokens = joined(
        [
            lax.ppermute(tokens, "narrow", [((n + shift) % parts, n) for n in range(parts)])
            for shift in range(1, parts)
        ]
    )
    other = (place + 1 + jnp.arange(others, dtype=jnp.int32)) % parts
    early_at = place * group
    late_at = (2 * parts - 1 - place) * group
    info = jnp.stack([place, lengths[0], early_at, late_at]).astype(jnp.int32)
    marks = jnp.stack([lax.axis_index("wide"), place]).astype(jnp.int32)
    turns = angles(positions(place[None]))
    turns_far = angles(positions(other))

    norm_one = [row(gain_one), row(shift_one)]
    b_column = b_qkv[:, None]
    normed, qT, kT, vT = project(tokens, w_qkv, b_column, *norm_one, *turns, (0, 1, 2))
    state = attend_local(info, qT, kT, vT, group)
    normed_far, kT_far, vT_far = project(
        far_tokens, w_qkv, b_column, *norm_one, *turns_far, (1, 2)
    )
    oT, lse = attend_remote(info, qT, kT_far, vT_far, state, group, parts)

    blocks = block_call(
        oT,
        tokens,
        cotangent.reshape(rows, width),
        [w_out, w_up, w_down],
        [row(item) for item in (b_out, b_up, b_down)]
        + [row(item) for item in (gain_two, shift_two, gain_three, shift_three)]
        + [row(item) for item in (gain_four, shift_four)],
    )
    result, d_middle, hidden, d_outer, normed_two, d_inner, d_branch, doT, small, small_up = blocks

    wide_bits = axis_bits("wide")
    narrow_bits = axis_bits("narrow")
    first_order = wide_bits[1:2] + narrow_bits + wide_bits[2:]
    second_order = narrow_bits + wide_bits[1:]
    third_order = narrow_bits + wide_bits[2:3] + wide_bits[1:2] + wide_bits[3:]
    fourth_order = wide_bits[2:3] + wide_bits[1:2] + narrow_bits + wide_bits[3:]
    small_order = wide_bits[:1] + first_order

    def outer(left, right, right_dim, order):
        return Halving(outer_halves(marks, left, right, right_dim, cores, parts, order), order)

    sum_up = outer(d_inner, normed_two, 0, first_order)
    sum_down = outer(d_outer, hidden, 0, second_order)
    sum_out = outer(d_branch, oT, 1, first_order)
    flat = jnp.concatenate([small.reshape(-1), small_up.reshape(-1)])
    early = Adding(flat.reshape(-1, PAIR), small_order)
    sums = [sum_down, sum_up, sum_out]

    heads = width // PAIR
    portions = 2 if heads % 2 == 0 else 1
    count = heads // portions
    far = []
    for portion in range(portions):
        (doT,) = launch(doT, sums, early)
        far = back_remote(
            info,
            [qT, doT, oT, lse],
            turns_far,
            [kT_far, vT_far],
            group,
            parts,
            portion * count,
            count,
            far,
        )
    dq_far, d_far = far
    d_back = unproject(d_far, w_qkv, (1, 2), 0, others * rows)
    d_mixed = []
    for portion in range(portions):
        doT, d_back = launch(doT, sums, early, d_back)
        if not portion:
            returned = [
                lax.ppermute(
                    d_back[j * rows : (j + 1) * rows] if others > 1 else d_back,
                    "narrow",
                    [(n, (n + j + 1) % parts) for n in range(parts)],
                )
                for j in range(others)
            ]
        d_mixed = [
            back_local(
                info,
                [qT, doT, oT, lse],
                turns,
                [kT, vT],
                dq_far,
                group,
                portion * count,
                count,
                d_mixed,
            )
        ]
    d_mixed = d_mixed[0]
    while early.order:
        (d_mixed,) = launch(d_mixed, sums, early)
    d_mixed = settle(d_mixed, sums, early)
    d_mixed, returned = lax.optimization_barrier((d_mixed, returned))
    if others > 1:
        returned = [functools.reduce(jnp.add, [item.astype(f32) for item in returned])]

    orders = [first_order, third_order, fourth_order]
    pieces, bias, weighted = mixed_halves(
        marks,
        d_mixed.reshape(3 * width, rows),
        d_far.reshape(3 * width, -1),
        normed,
        normed_far,
        w_qkv,
        cores,
        parts,
        orders,
    )
    pieces = [Halving(halves, order) for halves, order in zip(pieces, orders)]
    part_shift = weighted[1]
    part_gain = (weighted[0] - shift_one * part_shift) / gain_one
    flat = jnp.concatenate([bias.reshape(-1), part_gain, part_shift])
    late = Adding(flat.reshape(-1, PAIR), small_order)
    sum_w_down, sum_w_up, sum_w_out = collect([[item] for item in sums])
    (d_mixed,) = launch(d_mixed, pieces, late)
    d_tokens = []
    for i in range(2):
        finish = (returned[0], tokens, d_middle, row(gain_one))
        d_tokens = [
            unproject(d_mixed, w_qkv, (0, 1, 2), i * group, group, finish, d_tokens)
        ]
        if late.order:
            d_mixed, d_tokens[0] = launch(d_mixed, pieces, late, d_tokens[0])
    while late.order:
        (d_tokens[0],) = launch(d_tokens[0], pieces, late)

    (sum_w_qkv,) = collect([pieces])
    early_small = (early.terms[0] + early.terms[1]).reshape(-1)
    small = early_small[: 8 * width].reshape(8, width)
    small_up = early_small[8 * width :]
    late_small = (late.terms[0] + late.terms[1]).reshape(-1)
    shape = inputs.shape
    return (
        result.reshape(shape),
        d_tokens[0].reshape(shape),
        sum_w_qkv.T,
        sum_w_out.T,
        sum_w_up.T,
        sum_w_down.T,
        late_small[: 3 * width],
        small[7],
        small_up,
        small[2],
        late_small[3 * width : 4 * width],
        late_small[4 * width :],
        small[5],
        small[6],
        small[3],
        small[4],
        small[0],
        small[1],
    )


def solution(mesh):
    tokens = P("wide", None, "narrow", None, None)
    columns = P(None, ("wide", "narrow"))
    in_specs = (tokens, tokens, P("wide")) + (P(),) * 16
    out_specs = (tokens, tokens) + (columns,) * 4 + (P(),) * 12
    return jax.shard_map(body, mesh=mesh, in_specs=in_specs, out_specs=out_specs, check_vma=False)
```

```python
import functools

import jax
import jax.numpy as jnp
from jax import lax
from jax.experimental import pallas as pl
from jax.experimental.pallas import tpu as pltpu
from jax.sharding import PartitionSpec as P

HEAD_DIM = 64
PAIR = 2 * HEAD_DIM
EPS = 1e-05
LOG2E = 1.4426950408889634
LN2 = 0.6931471805599453
NEG = -1e30
REACH = 60.0
VMEM = 62 * 1024 * 1024
SPAN = 1024

f32 = jnp.float32
bf16 = jnp.bfloat16


def dot(left, right, left_dim, right_dim):
    return lax.dot_general(
        left, right, (((left_dim,), (right_dim,)), ((), ())), preferred_element_type=f32
    )


def bounded(qT, kT):
    worst = None
    for h in range(2):
        rows = slice(HEAD_DIM * h, HEAD_DIM * (h + 1))
        norms = []
        for item in (qT, kT):
            values = item[rows, :].astype(f32)
            norms.append(jnp.max(jnp.sum(values * values, axis=0, keepdims=True)))
        both = norms[0] * norms[1]
        worst = both if worst is None else jnp.maximum(worst, both)
    return worst <= REACH * REACH


def fwd_chunk(fast, q0, k0, q_n, k_n, limit, qT, kT, vT, m_ref, l_ref, acc):
    queries = pl.ds(q0, q_n)
    strip = min(256, k_n)
    for h in range(2):
        rows = slice(HEAD_DIM * h, HEAD_DIM * (h + 1))
        old = m_ref[h : h + 1, queries]
        new = jnp.zeros_like(old) if fast else old
        strips = []
        for j in range(k_n // strip):
            keys = pl.ds(k0 + j * strip, strip)
            scores = dot(kT[rows, keys], qT[rows, queries], 0, 0)
            if limit is not None:
                key_at = lax.broadcasted_iota(jnp.int32, (strip, q_n), 0)
                scores = jnp.where(key_at < limit - j * strip, scores, NEG)
            strips.append(scores)
            if not fast:
                new = jnp.maximum(new, jnp.max(scores, axis=0, keepdims=True))
        factor = jnp.exp2(old - new)
        total = l_ref[h : h + 1, queries] * factor
        value = acc[rows, queries] * factor
        for j in range(k_n // strip):
            keys = pl.ds(k0 + j * strip, strip)
            weights = jnp.exp2(strips[j] if fast else strips[j] - new)
            total = total + jnp.sum(weights, axis=0, keepdims=True)
            value = value + dot(vT[rows, keys], weights.astype(bf16), 1, 0)
        m_ref[h : h + 1, queries] = new
        l_ref[h : h + 1, queries] = total
        acc[rows, queries] = value


def pad_left(values, count):
    if not count:
        return values
    return jnp.concatenate([jnp.zeros((values.shape[0], count), f32), values], axis=1)


def pad_right(values, count):
    if not count:
        return values
    return jnp.concatenate([values, jnp.zeros((values.shape[0], count), f32)], axis=1)


def fwd_diagonal(fast, base, group, limit, qT, kT, vT, m_ref, l_ref, acc):
    strip = min(256, group)
    count = group // strip
    for h in range(2):
        rows = slice(HEAD_DIM * h, HEAD_DIM * (h + 1))
        strips = []
        for j in range(count):
            wide = group - j * strip
            keys, queries = pl.ds(base + j * strip, strip), pl.ds(base + j * strip, wide)
            scores = dot(kT[rows, keys], qT[rows, queries], 0, 0)
            key_at = lax.broadcasted_iota(jnp.int32, scores.shape, 0)
            query_at = lax.broadcasted_iota(jnp.int32, scores.shape, 1)
            scores = jnp.where(key_at <= query_at, scores, NEG)
            if limit is not None:
                scores = jnp.where(key_at < limit - j * strip, scores, NEG)
            strips.append(scores)
        peaks = []
        for g in range(0 if fast else count):
            peak = None
            for j in range(g + 1):
                part = strips[j][:, (g - j) * strip : (g - j + 1) * strip]
                part = jnp.max(part, axis=0, keepdims=True)
                peak = part if peak is None else jnp.maximum(peak, part)
            peaks.append(peak)
        if fast:
            peak = jnp.zeros((1, group), f32)
        else:
            peak = jnp.concatenate(peaks, axis=1) if count > 1 else peaks[0]
        total, value = None, None
        for j in range(count):
            keys = pl.ds(base + j * strip, strip)
            weights = jnp.exp2(strips[j] if fast else strips[j] - peak[:, j * strip :])
            part = pad_left(jnp.sum(weights, axis=0, keepdims=True), j * strip)
            term = pad_left(dot(vT[rows, keys], weights.astype(bf16), 1, 0), j * strip)
            total = part if total is None else total + part
            value = term if value is None else value + term
        queries = pl.ds(base, group)
        m_ref[h : h + 1, queries] = peak
        l_ref[h : h + 1, queries] = total
        acc[rows, queries] = value


def fwd_local_kernel(group, info, qT, kT, vT, acc, m_ref, l_ref):
    length = info[1]
    m_ref[...] = jnp.full(m_ref.shape, NEG, f32)
    l_ref[...] = jnp.zeros(l_ref.shape, f32)
    acc[...] = jnp.zeros(acc.shape, f32)
    refs = (qT, kT, vT, m_ref.at[0], l_ref.at[0], acc)

    def walk(fast):
        def own(i, carry):
            base = pl.multiple_of(i * group, group)
            start = info[2 + i]

            @pl.when(start + group <= length)
            def _():
                fwd_diagonal(fast, base, group, None, *refs)

            @pl.when((start < length) & (start + group > length))
            def _():
                fwd_diagonal(fast, base, group, length - start, *refs)

            return carry

        lax.fori_loop(0, 2, own, 0)
        early = info[2]

        @pl.when(early + group <= length)
        def _():
            fwd_chunk(fast, group, 0, group, group, None, *refs)

        @pl.when((early < length) & (early + group > length))
        def _():
            fwd_chunk(fast, group, 0, group, group, length - early, *refs)

    small = bounded(qT, kT)
    pl.when(small)(functools.partial(walk, True))
    pl.when(jnp.logical_not(small))(functools.partial(walk, False))


def remote_steps(group, parts, info, full, partial):
    place, length = info[0], info[1]

    def visit(i, carry):
        j, turn_at = i // 3, lax.rem(i, 3)
        other = lax.rem(place + 1 + j, parts)
        late_key = turn_at == 2
        block = jnp.where(late_key, 2 * parts - 1 - other, other)
        before = (other < place).astype(jnp.int32)
        wanted = jnp.where(turn_at == 0, before, jnp.where(late_key, 1 - before, 1)) == 1
        q0 = pl.multiple_of(jnp.where(turn_at == 0, 0, group), group)
        k0 = pl.multiple_of((2 * j + jnp.where(late_key, 1, 0)) * group, group)
        start = block * group

        @pl.when(wanted & (start + group <= length))
        def _():
            full(q0, k0)

        @pl.when(wanted & (start < length) & (start + group > length))
        def _():
            partial(q0, k0, length - start)

        return carry

    lax.fori_loop(0, 3 * (parts - 1), visit, 0)


def fwd_remote_kernel(
    group, parts, info, qT, kT, vT, acc_in, m_in, l_in, out, lse, acc, m_ref, l_ref
):
    acc[...] = acc_in[...]
    m_ref[...] = m_in[0]
    l_ref[...] = l_in[0]
    refs = (qT, kT, vT, m_ref, l_ref, acc)

    def walk(fast):
        def full(q0, k0):
            fwd_chunk(fast, q0, k0, group, group, None, *refs)

        def partial(q0, k0, limit):
            fwd_chunk(fast, q0, k0, group, group, limit, *refs)

        remote_steps(group, parts, info, full, partial)

    small = bounded(qT, kT) & (jnp.max(m_in[...]) <= 0.0)
    pl.when(small)(functools.partial(walk, True))
    pl.when(jnp.logical_not(small))(functools.partial(walk, False))
    for h in range(2):
        rows = slice(HEAD_DIM * h, HEAD_DIM * (h + 1))
        total = l_ref[h : h + 1, :]
        out[rows, :] = (acc[rows, :] / total).astype(bf16)
        lse[0, h : h + 1, :] = m_ref[h : h + 1, :] + jnp.log2(total)


def split_three(values):
    high = values.astype(bf16).astype(f32)
    rest = values - high
    middle = rest.astype(bf16).astype(f32)
    low = (rest - middle).astype(bf16).astype(f32)
    return [high, middle, low]


def bwd_prepare(qT, kT, vT, doT, oT, lse, qa, da, ka, va):
    n_q, n_k = qT.shape[1], ka.shape[2]
    extra = qa.shape[1] - HEAD_DIM
    pad = jnp.zeros((extra - 3, n_q), f32)
    row_at = lax.broadcasted_iota(jnp.int32, (extra, n_k), 0)
    tail = jnp.where(row_at < 3, 1.0, 0.0).astype(bf16)
    for h in range(2):
        rows = slice(HEAD_DIM * h, HEAD_DIM * (h + 1))
        grad = doT[rows, :].astype(f32)
        delta = jnp.sum(grad * oT[rows, :].astype(f32), axis=0, keepdims=True)
        qa[h, :HEAD_DIM, :] = qT[rows, :]
        parts = split_three(-lse[0, h : h + 1, :]) + [pad]
        qa[h, HEAD_DIM:, :] = jnp.concatenate(parts, axis=0).astype(bf16)
        da[h, :HEAD_DIM, :] = doT[rows, :]
        parts = split_three(-delta) + [pad]
        da[h, HEAD_DIM:, :] = jnp.concatenate(parts, axis=0).astype(bf16)
        ka[h, :HEAD_DIM, :] = kT[rows, :]
        va[h, :HEAD_DIM, :] = vT[rows, :]
        ka[h, HEAD_DIM:, :] = tail
        va[h, HEAD_DIM:, :] = tail


def bwd_chunk(q0, k0, q_n, k_n, limit, qT, doT, qa, da, ka, va, dq, dk, dv):
    queries, keys = pl.ds(q0, q_n), pl.ds(k0, k_n)
    for h in range(2):
        rows = slice(HEAD_DIM * h, HEAD_DIM * (h + 1))
        probs = jnp.exp2(dot(qa[h, :, queries], ka[h, :, keys], 0, 0))
        if limit is not None:
            key_at = lax.broadcasted_iota(jnp.int32, (q_n, k_n), 1)
            probs = jnp.where(key_at < limit, probs, 0.0)
        d_probs = dot(da[h, :, queries], va[h, :, keys], 0, 0)
        d_scores = (probs * d_probs).astype(bf16)
        dv[rows, keys] += dot(doT[rows, queries], probs.astype(bf16), 1, 0)
        dk[rows, keys] += dot(qT[rows, queries], d_scores, 1, 0)
        dq[rows, queries] += dot(ka[h, :HEAD_DIM, keys], d_scores, 1, 1)


def bwd_diagonal(base, group, limit, qT, doT, qa, da, ka, va, dq, dk, dv):
    strip = min(256, group)
    count = group // strip
    for h in range(2):
        rows = slice(HEAD_DIM * h, HEAD_DIM * (h + 1))
        d_keys, d_values, d_queries = None, None, []
        for j in range(count):
            wide = (j + 1) * strip
            queries, keys = pl.ds(base + j * strip, strip), pl.ds(base, wide)
            probs = jnp.exp2(dot(qa[h, :, queries], ka[h, :, keys], 0, 0))
            query_at = lax.broadcasted_iota(jnp.int32, probs.shape, 0)
            key_at = lax.broadcasted_iota(jnp.int32, probs.shape, 1)
            probs = jnp.where(key_at <= query_at + j * strip, probs, 0.0)
            if limit is not None:
                probs = jnp.where(key_at < limit, probs, 0.0)
            d_probs = dot(da[h, :, queries], va[h, :, keys], 0, 0)
            d_scores = (probs * d_probs).astype(bf16)
            value = pad_right(dot(doT[rows, queries], probs.astype(bf16), 1, 0), group - wide)
            key = pad_right(dot(qT[rows, queries], d_scores, 1, 0), group - wide)
            d_values = value if d_values is None else d_values + value
            d_keys = key if d_keys is None else d_keys + key
            d_queries.append(dot(ka[h, :HEAD_DIM, keys], d_scores, 1, 1))
        here = pl.ds(base, group)
        dq[rows, here] += jnp.concatenate(d_queries, axis=1) if count > 1 else d_queries[0]
        dk[rows, here] += d_keys
        dv[rows, here] += d_values


def turn_back(values, cosine, sine):
    half = HEAD_DIM // 2
    first, second = values[:half], values[half:]
    return jnp.concatenate(
        [first * cosine + second * sine, second * cosine - first * sine], axis=0
    )


def bwd_remote_kernel(group, parts, info, qT, doT, oT, lse, cosine, sine, kT, vT, *rest):
    dq, dkv, *scratch = rest[-8:]
    qa, da, ka, va, dk, dv = scratch
    bwd_prepare(qT, kT, vT, doT, oT, lse, qa, da, ka, va)
    dq[...] = jnp.zeros(dq.shape, f32)
    dk[...] = jnp.zeros(dk.shape, f32)
    dv[...] = jnp.zeros(dv.shape, f32)
    refs = (qT, doT, qa, da, ka, va, dq, dk, dv)

    def full(q0, k0):
        bwd_chunk(q0, k0, group, group, None, *refs)

    def partial(q0, k0, limit):
        bwd_chunk(q0, k0, group, group, limit, *refs)

    remote_steps(group, parts, info, full, partial)
    for h in range(2):
        rows = slice(HEAD_DIM * h, HEAD_DIM * (h + 1))
        dkv[1, rows, :] = turn_back(dk[rows, :] * LN2, cosine[...], sine[...]).astype(bf16)
    dkv[0] = jnp.zeros(dv.shape, bf16)
    dkv[2] = dv[...].astype(bf16)


def bwd_local_kernel(group, info, qT, doT, oT, lse, cosine, sine, kT, vT, dq_in, *rest):
    dqkv, *scratch = rest[-8:]
    qa, da, ka, va, dq, dk, dv = scratch
    length = info[1]
    bwd_prepare(qT, kT, vT, doT, oT, lse, qa, da, ka, va)
    dq[...] = dq_in[...]
    dk[...] = jnp.zeros(dk.shape, f32)
    dv[...] = jnp.zeros(dv.shape, f32)
    refs = (qT, doT, qa, da, ka, va, dq, dk, dv)

    def own(i, carry):
        base = pl.multiple_of(i * group, group)
        start = info[2 + i]

        @pl.when(start + group <= length)
        def _():
            bwd_diagonal(base, group, None, *refs)

        @pl.when((start < length) & (start + group > length))
        def _():
            bwd_diagonal(base, group, length - start, *refs)

        return carry

    lax.fori_loop(0, 2, own, 0)
    early = info[2]

    @pl.when(early + group <= length)
    def _():
        bwd_chunk(group, 0, group, group, None, *refs)

    @pl.when((early < length) & (early + group > length))
    def _():
        bwd_chunk(group, 0, group, group, length - early, *refs)

    for h in range(2):
        rows = slice(HEAD_DIM * h, HEAD_DIM * (h + 1))
        d_query = dq[rows, :] * 0.125
        dqkv[0, rows, :] = turn_back(d_query, cosine[...], sine[...]).astype(bf16)
        dqkv[1, rows, :] = turn_back(dk[rows, :] * LN2, cosine[...], sine[...]).astype(bf16)
    dqkv[2] = dv[...].astype(bf16)


def rows_of(count, first=0):
    return pl.BlockSpec((PAIR, count), lambda i, info: (first + i, 0))


def stats_of(count, first=0):
    return pl.BlockSpec((1, 2, count), lambda i, info: (first + i, 0, 0))


def planes_of(planes, count, first=0):
    return pl.BlockSpec((planes, PAIR, count), lambda i, info: (0, first + i, 0))


def whole(shape):
    return pl.BlockSpec(shape, lambda i, info: (0,) * len(shape))


def attention_call(kernel, pairs, in_specs, out_specs, out_shape, scratch, flops, name, alias={}):
    return pl.pallas_call(
        kernel,
        grid_spec=pltpu.PrefetchScalarGridSpec(
            num_scalar_prefetch=1,
            grid=(pairs,),
            in_specs=in_specs,
            out_specs=out_specs,
            scratch_shapes=scratch,
        ),
        out_shape=out_shape,
        input_output_aliases=alias,
        compiler_params=pltpu.CompilerParams(vmem_limit_bytes=VMEM),
        cost_estimate=pl.CostEstimate(
            flops=int(flops), bytes_accessed=1 << 25, transcendentals=0
        ),
        name=name,
    )


def attend_local(info, qT, kT, vT, group):
    width, n_q = qT.shape
    pairs = width // PAIR
    call = attention_call(
        functools.partial(fwd_local_kernel, group),
        pairs,
        [rows_of(n_q)] * 3,
        [rows_of(n_q), stats_of(n_q), stats_of(n_q)],
        [
            jax.ShapeDtypeStruct((width, n_q), f32),
            jax.ShapeDtypeStruct((pairs, 2, n_q), f32),
            jax.ShapeDtypeStruct((pairs, 2, n_q), f32),
        ],
        [],
        4 * width * 2 * group * group * 4,
        "attend_local",
    )
    return call(info, qT, kT, vT)


def attend_remote(info, qT, kT, vT, state, group, parts):
    width, n_q = qT.shape
    n_k = kT.shape[1]
    pairs = width // PAIR
    call = attention_call(
        functools.partial(fwd_remote_kernel, group, parts),
        pairs,
        [rows_of(n_q), rows_of(n_k), rows_of(n_k), rows_of(n_q), stats_of(n_q), stats_of(n_q)],
        [rows_of(n_q), stats_of(n_q)],
        [
            jax.ShapeDtypeStruct((width, n_q), bf16),
            jax.ShapeDtypeStruct((pairs, 2, n_q), f32),
        ],
        [pltpu.VMEM((PAIR, n_q), f32)] + [pltpu.VMEM((2, n_q), f32)] * 2,
        4 * width * 2 * group * group * 4,
        "attend_remote",
    )
    return call(info, qT, kT, vT, *state)


def back_scratch(n_q, n_k):
    rows = HEAD_DIM + 16
    return [
        pltpu.VMEM((2, rows, n_q), bf16),
        pltpu.VMEM((2, rows, n_q), bf16),
        pltpu.VMEM((2, rows, n_k), bf16),
        pltpu.VMEM((2, rows, n_k), bf16),
    ]


def back_remote(info, operands, turns, keys, group, parts, first, count, before):
    width, n_q = operands[0].shape
    n_k = keys[0].shape[1]
    half = HEAD_DIM // 2
    n_in = 1 + len(operands) + len(turns) + len(keys)
    call = attention_call(
        functools.partial(bwd_remote_kernel, group, parts),
        count,
        [rows_of(n_q, first)] * 3
        + [stats_of(n_q, first)]
        + [whole((half, n_k))] * 2
        + [rows_of(n_k, first)] * 2
        + [pl.BlockSpec(memory_space=pl.ANY)] * len(before),
        [rows_of(n_q, first), planes_of(3, n_k, first)],
        [
            jax.ShapeDtypeStruct((width, n_q), f32),
            jax.ShapeDtypeStruct((3, width, n_k), bf16),
        ],
        back_scratch(n_q, n_k) + [pltpu.VMEM((PAIR, n_k), f32)] * 2,
        10 * count * PAIR * 2 * group * group * 4,
        "back_remote",
        {n_in + i: i for i in range(len(before))},
    )
    return call(info, *operands, *turns, *keys, *before)


def back_local(info, operands, turns, keys, dq, group, first, count, before):
    width, n_q = operands[0].shape
    half = HEAD_DIM // 2
    n_in = 1 + len(operands) + len(turns) + len(keys) + 1
    call = attention_call(
        functools.partial(bwd_local_kernel, group),
        count,
        [rows_of(n_q, first)] * 3
        + [stats_of(n_q, first)]
        + [whole((half, n_q))] * 2
        + [rows_of(n_q, first)] * 3
        + [pl.BlockSpec(memory_space=pl.ANY)] * len(before),
        planes_of(3, n_q, first),
        jax.ShapeDtypeStruct((3, width, n_q), bf16),
        back_scratch(n_q, n_q) + [pltpu.VMEM((PAIR, n_q), f32)] * 3,
        10 * count * PAIR * 2 * group * group * 4,
        "back_local",
        {n_in + i: i for i in range(len(before))},
    )
    return call(info, *operands, *turns, *keys, dq, *before)


def normalize(values):
    centre = values - jnp.mean(values, axis=-1, keepdims=True)
    spread = jnp.mean(centre * centre, axis=-1, keepdims=True)
    rate = lax.rsqrt(spread + EPS)
    return centre * rate, rate


def norm_back(grad, unit, rate, gain):
    scaled = grad * gain
    first = jnp.mean(scaled, axis=-1, keepdims=True)
    second = jnp.mean(scaled * unit, axis=-1, keepdims=True)
    return rate * (scaled - first - unit * second)


GELU_A = 0.7978845608028654
GELU_B = 0.044715


def column_sum(values):
    return jnp.sum(values, axis=0, keepdims=True)


def block_kernel(
    span,
    oT,
    tokens,
    cotangent,
    w_out,
    w_up,
    w_down,
    b_out,
    b_up,
    b_down,
    gain_two,
    shift_two,
    gain_three,
    shift_three,
    gain_four,
    shift_four,
    result,
    d_middle_out,
    hidden_out,
    d_outer_out,
    normed_out,
    d_inner_out,
    d_branch_out,
    doT,
    small,
    small_up,
    slope,
):
    step = pl.program_id(0)

    @pl.when(step == 0)
    def _():
        small[...] = jnp.zeros(small.shape, f32)
        small_up[...] = jnp.zeros(small_up.shape, f32)

    wide = w_up.shape[1]
    branch = dot(oT[...], w_out[...], 0, 0) + b_out[...]
    unit_two, rate_two = normalize(branch)
    middle = tokens[...].astype(f32) + (unit_two * gain_two[...] + shift_two[...])
    unit_three, rate_three = normalize(middle)
    normed = (unit_three * gain_three[...] + shift_three[...]).astype(bf16)
    normed_out[...] = normed
    outer = None
    for c in range(wide // span):
        columns = slice(c * span, (c + 1) * span)
        inner = dot(normed, w_up[:, columns], 1, 0) + b_up[:, columns]
        square = inner * inner
        bend = jnp.tanh(inner * (GELU_A + (GELU_A * GELU_B) * square))
        half = 0.5 + 0.5 * bend
        hidden = (inner * half).astype(bf16)
        hidden_out[:, columns] = hidden
        slope[:, columns] = half + inner * (1.0 - bend * bend) * (
            0.5 * GELU_A + (1.5 * GELU_A * GELU_B) * square
        )
        term = dot(hidden, w_down[columns, :], 1, 0)
        outer = term if outer is None else outer + term
    unit_four, rate_four = normalize(outer + b_down[...])
    result[...] = (middle + (unit_four * gain_four[...] + shift_four[...])).astype(bf16)

    grad = cotangent[...].astype(f32)
    d_outer = norm_back(grad, unit_four, rate_four, gain_four[...]).astype(bf16)
    d_outer_out[...] = d_outer
    small[0:1, :] += column_sum(grad * unit_four)
    small[1:2, :] += column_sum(grad)
    small[2:3, :] += column_sum(d_outer.astype(f32))
    d_normed = None
    for c in range(wide // span):
        columns = slice(c * span, (c + 1) * span)
        d_hidden = dot(d_outer, w_down[columns, :], 1, 1)
        d_inner = (d_hidden * slope[:, columns]).astype(bf16)
        d_inner_out[:, columns] = d_inner
        small_up[:, columns] += column_sum(d_inner.astype(f32))
        term = dot(d_inner, w_up[:, columns], 1, 1)
        d_normed = term if d_normed is None else d_normed + term
    small[3:4, :] += column_sum(d_normed * unit_three)
    small[4:5, :] += column_sum(d_normed)
    d_middle = grad + norm_back(d_normed, unit_three, rate_three, gain_three[...])
    d_middle_out[...] = d_middle
    small[5:6, :] += column_sum(d_middle * unit_two)
    small[6:7, :] += column_sum(d_middle)
    d_branch = norm_back(d_middle, unit_two, rate_two, gain_two[...]).astype(bf16)
    d_branch_out[...] = d_branch
    small[7:8, :] += column_sum(d_branch.astype(f32))
    doT[...] = dot(w_out[...], d_branch, 1, 1).astype(bf16)


def block_call(oT, tokens, cotangent, weights, vectors):
    width, rows = oT.shape
    wide = weights[1].shape[1]
    step = min(256, rows)
    span = min(SPAN, wide)

    def lines(count):
        return pl.BlockSpec((step, count), lambda i: (i, 0))

    def fixed(shape):
        return pl.BlockSpec(shape, lambda i: (0, 0), pipeline_mode=pl.Buffered(1))

    def total(shape):
        return pl.BlockSpec(shape, lambda i: (0, 0))

    features = pl.BlockSpec((width, step), lambda i: (0, i))
    sizes = [width, width, wide, width, width, wide, width]
    kinds = [bf16, f32, bf16, bf16, bf16, bf16, bf16]
    return pl.pallas_call(
        functools.partial(block_kernel, span),
        grid=(rows // step,),
        in_specs=[features, lines(width), lines(width)]
        + [fixed(item.shape) for item in weights]
        + [fixed(item.shape) for item in vectors],
        out_specs=[lines(size) for size in sizes]
        + [features, total((8, width)), total((1, wide))],
        out_shape=[jax.ShapeDtypeStruct((rows, size), kind) for size, kind in zip(sizes, kinds)]
        + [
            jax.ShapeDtypeStruct((width, rows), bf16),
            jax.ShapeDtypeStruct((8, width), f32),
            jax.ShapeDtypeStruct((1, wide), f32),
        ],
        scratch_shapes=[pltpu.VMEM((step, wide), f32)],
        compiler_params=pltpu.CompilerParams(vmem_limit_bytes=VMEM),
        cost_estimate=pl.CostEstimate(
            flops=2 * 2 * rows * (width * width + 2 * width * wide),
            bytes_accessed=1 << 26,
            transcendentals=rows * wide,
        ),
        name="block",
    )(oT, tokens, cotangent, *weights, *vectors)


def turn(values, cosine, sine):
    half = HEAD_DIM // 2
    first, second = values[:half], values[half:]
    return jnp.concatenate(
        [first * cosine - second * sine, second * cosine + first * sine], axis=0
    )


def project_kernel(sections, tokens, w, b, gain, shift, cosine, sine, normed_out, *outs):
    unit, rate = normalize(tokens[...].astype(f32))
    normed = (unit * gain[...] + shift[...]).astype(bf16)
    normed_out[...] = normed
    width = tokens.shape[1]
    chunk = min(256, width)
    for section, out in zip(sections, outs):
        for c in range(width // chunk):
            at = section * width + c * chunk
            mixed = dot(w[:, at : at + chunk], normed, 0, 1) + b[:, at : at + chunk].T
            for h in range(chunk // HEAD_DIM):
                rows = slice(h * HEAD_DIM, (h + 1) * HEAD_DIM)
                place = slice(c * chunk + h * HEAD_DIM, c * chunk + (h + 1) * HEAD_DIM)
                value = mixed[rows]
                if section < 2:
                    value = turn(value, cosine[...], sine[...])
                if section == 0:
                    value = value * (0.125 * LOG2E)
                out[place, :] = value.astype(bf16)


def project(tokens, w, b, gain, shift, cosine, sine, sections):
    rows, width = tokens.shape
    step = min(512, rows)
    half = HEAD_DIM // 2

    def fixed(shape):
        return pl.BlockSpec(shape, lambda i: (0, 0), pipeline_mode=pl.Buffered(1))

    lines = pl.BlockSpec((step, width), lambda i: (i, 0))
    features = pl.BlockSpec((width, step), lambda i: (0, i))
    turns = pl.BlockSpec((half, step), lambda i: (0, i))
    return pl.pallas_call(
        functools.partial(project_kernel, sections),
        grid=(rows // step,),
        in_specs=[lines, fixed(w.shape), fixed(b.shape), fixed(gain.shape), fixed(shift.shape)]
        + [turns] * 2,
        out_specs=[lines] + [features] * len(sections),
        out_shape=[jax.ShapeDtypeStruct((rows, width), bf16)]
        + [jax.ShapeDtypeStruct((width, rows), bf16)] * len(sections),
        compiler_params=pltpu.CompilerParams(vmem_limit_bytes=VMEM),
        cost_estimate=pl.CostEstimate(
            flops=2 * rows * width * width * len(sections),
            bytes_accessed=1 << 24,
            transcendentals=0,
        ),
        name="project",
    )(tokens, w, b, gain, shift, cosine, sine)


def unproject_kernel(planes, finish, *refs):
    d_mixed, w, out = refs[: len(planes)], refs[len(planes)], refs[-1]
    width = w.shape[0]
    total = None
    for plane, ref in zip(planes, d_mixed):
        term = dot(ref[0], w[:, plane * width : (plane + 1) * width], 0, 1)
        total = term if total is None else total + term
    if not finish:
        out[...] = total.astype(bf16)
        return
    returned, tokens, d_middle, gain = refs[len(planes) + 1 : len(planes) + 5]
    total = total + returned[...].astype(f32)
    unit, rate = normalize(tokens[...].astype(f32))
    out[...] = (d_middle[...] + norm_back(total, unit, rate, gain[...])).astype(bf16)


def unproject(d_mixed, w, planes, start, count, finish=(), before=()):
    _, width, total = d_mixed.shape
    step = min(256, count)
    first = start // step

    def fixed(shape):
        return pl.BlockSpec(shape, lambda i: (0, 0), pipeline_mode=pl.Buffered(1))

    def plane_of(plane):
        return pl.BlockSpec((1, width, step), lambda i: (plane, 0, first + i))

    lines = pl.BlockSpec((step, width), lambda i: (i, 0))
    later = pl.BlockSpec((step, width), lambda i: (first + i, 0))
    specs = [later] * 3 + [fixed(finish[-1].shape)] if finish else []
    n_in = len(planes) + 1 + len(finish)
    return pl.pallas_call(
        functools.partial(unproject_kernel, planes, bool(finish)),
        grid=(count // step,),
        in_specs=[plane_of(plane) for plane in planes]
        + [fixed(w.shape)]
        + specs
        + [pl.BlockSpec(memory_space=pl.ANY)] * len(before),
        out_specs=later if finish else lines,
        out_shape=jax.ShapeDtypeStruct((total if finish else count, width), bf16),
        input_output_aliases={n_in + i: i for i in range(len(before))},
        compiler_params=pltpu.CompilerParams(vmem_limit_bytes=VMEM),
        cost_estimate=pl.CostEstimate(
            flops=2 * count * width * width * len(planes),
            bytes_accessed=1 << 24,
            transcendentals=0,
        ),
        name="unproject",
    )(*[d_mixed] * len(planes), w, *finish, *before)


def divide(total, run, levels, near, marks, orders, outs):
    bits = [("narrow", i) for i in range(near)] + [("wide", i) for i in range(levels + 1)]
    cut = run // len(orders)

    def write(core):
        for at in range(0, total.shape[0], run):
            number = at // run
            value = {}
            for place, (axis, position) in enumerate(bits):
                mine = (marks[1 if axis == "narrow" else 0] >> position) & 1
                value[axis, position] = mine ^ ((number >> place) & 1)
            other = core ^ ((number >> near) & 1)
            for i, order in enumerate(orders):
                index = tuple(value.get(bit, 0) for bit in order)
                part = total[at + i * cut : at + (i + 1) * cut]
                outs[2 * i + other][index] = part.astype(bf16)

    pl.when((marks[0] & 1) == 0)(functools.partial(write, 0))
    pl.when((marks[0] & 1) == 1)(functools.partial(write, 1))


def divided(orders, levels, run, height, wide, width):
    cut = run // len(orders)
    specs, shapes = [], []
    for order in orders:

        def held(bit):
            return bit[0] == "narrow" or bit[1] <= levels

        def index(j, i, marks, order=order):
            relative = i ^ (marks[0] >> (levels + 1))
            at = [0 if held(bit) else (relative >> (bit[1] - 1 - levels)) & 1 for bit in order]
            return (*at, 0, j)

        block = tuple(2 if held(bit) else 1 for bit in order) + (cut, wide)
        specs += [pl.BlockSpec(block, index)] * 2
        shapes += [jax.ShapeDtypeStruct((2,) * len(order) + (cut, width), bf16)] * 2
    return specs, shapes


def outer_kernel(run, levels, near, orders, right_dim, marks, left, right, *outs):
    divide(dot(left[...], right[...], 0, right_dim), run, levels, near, marks, orders, outs)


def outer_halves(marks, left, right, right_dim, cores, parts, order):
    rows, height = left.shape
    width = right.shape[1 - right_dim]
    share = height // cores
    high = max(2 * share, min(1024, height))
    levels = (high // (2 * share)).bit_length() - 1
    wide = min(1024, width)
    if right_dim == 0:
        right_spec = pl.BlockSpec((rows, wide), lambda j, i, marks: (0, j))
    else:
        right_spec = pl.BlockSpec((wide, rows), lambda j, i, marks: (j, 0))
    run = share // parts
    near = parts.bit_length() - 1
    specs, shapes = divided([order], levels, run, height, wide, width)
    halves = pl.pallas_call(
        functools.partial(outer_kernel, run, levels, near, [order], right_dim),
        grid_spec=pltpu.PrefetchScalarGridSpec(
            num_scalar_prefetch=1,
            grid=(width // wide, height // high),
            in_specs=[pl.BlockSpec((rows, high), lambda j, i, marks: (0, i)), right_spec],
            out_specs=specs,
        ),
        out_shape=shapes,
        compiler_params=pltpu.CompilerParams(vmem_limit_bytes=VMEM),
        cost_estimate=pl.CostEstimate(
            flops=2 * rows * height * width, bytes_accessed=1 << 25, transcendentals=0
        ),
        name="outer",
    )(marks, left, right)
    return [item.reshape(height // 2, width) for item in halves]


def mixed_kernel(
    run, levels, near, orders, first_far, marks, d_own, d_far, normed, normed_far, w, *outs
):
    *halves, bias, sums = outs
    step = pl.program_id(1)
    total = dot(d_own[...], normed[...], 1, 0)
    bias[...] = jnp.sum(d_own[...].astype(f32), axis=1, keepdims=True)

    @pl.when(step == 0)
    def _():
        sums[...] = jnp.zeros(sums.shape, f32)

    def finish(value):
        divide(value, run, levels, near, marks, orders, halves)
        weights = w[...].astype(f32).T
        sums[0:1, :] += column_sum(weights * value)
        sums[1:2, :] += column_sum(weights * bias[...])

    @pl.when(step < first_far)
    def _():
        finish(total)

    @pl.when(step >= first_far)
    def _():
        bias[...] += jnp.sum(d_far[...].astype(f32), axis=1, keepdims=True)
        finish(total + dot(d_far[...], normed_far[...], 1, 0))


def mixed_halves(marks, d_own, d_far, normed, normed_far, w, cores, parts, orders):
    height, rows = d_own.shape
    far = d_far.shape[1]
    width = normed.shape[1]
    share = height // cores
    pairs = max(1, 768 // (2 * share))
    levels = pairs.bit_length() - 1
    high = 2 * share * pairs
    first_far = width // high
    run = share // parts
    near = parts.bit_length() - 1

    def fixed(shape):
        return pl.BlockSpec(shape, lambda j, i, marks: (0, 0), pipeline_mode=pl.Buffered(1))

    specs, shapes = divided(orders, levels, run, height, width, width)
    *halves, bias, sums = pl.pallas_call(
        functools.partial(mixed_kernel, run, levels, near, orders, first_far),
        grid_spec=pltpu.PrefetchScalarGridSpec(
            num_scalar_prefetch=1,
            grid=(1, height // high),
            in_specs=[
                pl.BlockSpec((high, rows), lambda j, i, marks: (i, 0)),
                pl.BlockSpec((high, far), lambda j, i, marks: (jnp.maximum(i, first_far), 0)),
                fixed(normed.shape),
                fixed(normed_far.shape),
                pl.BlockSpec((width, high), lambda j, i, marks: (0, i)),
            ],
            out_specs=specs
            + [
                pl.BlockSpec((high, 1), lambda j, i, marks: (i, 0)),
                pl.BlockSpec((2, width), lambda j, i, marks: (0, 0)),
            ],
        ),
        out_shape=shapes
        + [
            jax.ShapeDtypeStruct((height, 1), f32),
            jax.ShapeDtypeStruct((2, width), f32),
        ],
        compiler_params=pltpu.CompilerParams(vmem_limit_bytes=VMEM),
        cost_estimate=pl.CostEstimate(
            flops=2 * (rows + far) * height * width, bytes_accessed=1 << 25, transcendentals=0
        ),
        name="mixed",
    )(marks, d_own, d_far, normed, normed_far, w)
    halves = [item.reshape(-1, width) for item in halves]
    return [halves[i : i + 2] for i in range(0, len(halves), 2)], bias, sums


def bit_of(axis, position):
    return (lax.axis_index(axis) >> position) & 1


def swap(values, axis, position):
    size = lax.axis_size(axis)
    return lax.ppermute(values, axis, [(i, i ^ (1 << position)) for i in range(size)])


class Halving:
    def __init__(self, halves, order):
        self.order = list(order)
        kept, given = halves
        self.terms = [kept, swap(given, "wide", 0)]

    def send(self, array, away):
        self.terms = [array, swap(away, *self.order.pop(0))]


class Adding:
    def __init__(self, array, order):
        self.order = list(order)
        self.terms = [array, swap(array, *self.order.pop(0))]

    def send(self, total):
        self.terms = [total, swap(total, *self.order.pop(0))]


def halve_kernel(count, *refs):
    ins, outs = refs[: 4 * count + 2], refs[4 * count + 2 :]
    for i in range(count):
        one, two = ins[4 * i : 4 * i + 2], ins[4 * i + 2 : 4 * i + 4]
        for half in range(2):
            total = one[half][0].astype(f32) + two[half][0].astype(f32)
            outs[2 * i + half][...] = total.astype(bf16)
    outs[-1][...] = ins[-2][...] + ins[-1][...]


def halve(sums, small):
    heights = [item.terms[0].shape[0] // 2 for item in sums]
    grid = 4 if all(height % 64 == 0 for height in heights) else 1
    operands, in_specs, out_specs, out_shape = [], [], [], []
    for item, height in zip(sums, heights):
        width = item.terms[0].shape[1]
        block = (height // grid, width)
        for term in item.terms:
            for half in range(2):
                operands.append(term.reshape(2, height, width))
                in_specs.append(pl.BlockSpec((1, *block), lambda i, half=half: (half, i, 0)))
        out_specs += [pl.BlockSpec(block, lambda i: (i, 0))] * 2
        out_shape += [jax.ShapeDtypeStruct((height, width), bf16)] * 2
    whole_small = pl.BlockSpec(small.terms[0].shape, lambda i: (0, 0))
    return pl.pallas_call(
        functools.partial(halve_kernel, len(sums)),
        grid=(grid,),
        in_specs=in_specs + [whole_small] * 2,
        out_specs=out_specs + [whole_small],
        out_shape=out_shape + [jax.ShapeDtypeStruct(small.terms[0].shape, f32)],
        compiler_params=pltpu.CompilerParams(vmem_limit_bytes=VMEM),
        name="halve",
    )(*operands, *small.terms)


def launch(lead, sums, small, *others):
    lead, others, halves = lax.optimization_barrier((lead, others, halve(sums, small)))
    for i, item in enumerate(sums):
        item.send(halves[2 * i], halves[2 * i + 1])
    small.send(halves[-1])
    return (lead, *others)


def settle(lead, sums, small):
    everything = sums + [small]
    lead, terms = lax.optimization_barrier((lead, [item.terms for item in everything]))
    for item, arrays in zip(everything, terms):
        item.terms = list(arrays)
    return lead


def collect_kernel(groups, *refs):
    at = 0
    for out, count in zip(refs[-len(groups) :], groups):
        parts = [
            refs[at + 2 * i][...].astype(f32) + refs[at + 2 * i + 1][...].astype(f32)
            for i in range(count)
        ]
        at += 2 * count
        height = parts[0].shape[0]
        for i, part in enumerate(parts):
            out[i * height : (i + 1) * height, :] = part


def collect(groups):
    operands = [term for group in groups for item in group for term in item.terms]
    return pl.pallas_call(
        functools.partial(collect_kernel, [len(group) for group in groups]),
        out_shape=[
            jax.ShapeDtypeStruct(
                (sum(item.terms[0].shape[0] for item in group), group[0].terms[0].shape[1]), f32
            )
            for group in groups
        ],
        compiler_params=pltpu.CompilerParams(vmem_limit_bytes=VMEM),
        name="collect",
    )(*operands)


def angles(positions):
    half = HEAD_DIM // 2
    freqs = jnp.power(10000.0, -jnp.arange(half, dtype=f32) / half)
    theta = freqs[:, None] * positions.astype(f32)[None, :]
    return jnp.cos(theta), jnp.sin(theta)


def axis_bits(axis):
    return [(axis, position) for position in range(lax.axis_size(axis).bit_length() - 1)]


def body(
    inputs,
    cotangent,
    lengths,
    w_qkv,
    b_qkv,
    w_out,
    b_out,
    w_up,
    b_up,
    w_down,
    b_down,
    gain_one,
    shift_one,
    gain_two,
    shift_two,
    gain_three,
    shift_three,
    gain_four,
    shift_four,
):
    group = inputs.shape[3]
    width = inputs.shape[4]
    parts = lax.axis_size("narrow")
    place = lax.axis_index("narrow")
    cores = lax.axis_size("wide")
    others = parts - 1
    rows = 2 * group
    offsets = jnp.arange(group, dtype=jnp.int32)

    def row(vector):
        return vector[None, :]

    def positions(owners):
        starts = jnp.stack([owners, 2 * parts - 1 - owners], axis=1).reshape(-1) * group
        return (starts[:, None] + offsets[None]).reshape(-1)

    def joined(items):
        return jnp.concatenate(items, axis=0) if len(items) > 1 else items[0]

    tokens = inputs.reshape(rows, width)
    far_tokens = joined(
        [
            lax.ppermute(tokens, "narrow", [((n + shift) % parts, n) for n in range(parts)])
            for shift in range(1, parts)
        ]
    )
    other = (place + 1 + jnp.arange(others, dtype=jnp.int32)) % parts
    early_at = place * group
    late_at = (2 * parts - 1 - place) * group
    info = jnp.stack([place, lengths[0], early_at, late_at]).astype(jnp.int32)
    marks = jnp.stack([lax.axis_index("wide"), place]).astype(jnp.int32)
    turns = angles(positions(place[None]))
    turns_far = angles(positions(other))

    norm_one = [row(gain_one), row(shift_one)]
    normed, qT, kT, vT = project(tokens, w_qkv, row(b_qkv), *norm_one, *turns, (0, 1, 2))
    state = attend_local(info, qT, kT, vT, group)
    normed_far, kT_far, vT_far = project(
        far_tokens, w_qkv, row(b_qkv), *norm_one, *turns_far, (1, 2)
    )
    oT, lse = attend_remote(info, qT, kT_far, vT_far, state, group, parts)

    blocks = block_call(
        oT,
        tokens,
        cotangent.reshape(rows, width),
        [w_out, w_up, w_down],
        [row(item) for item in (b_out, b_up, b_down)]
        + [row(item) for item in (gain_two, shift_two, gain_three, shift_three)]
        + [row(item) for item in (gain_four, shift_four)],
    )
    result, d_middle, hidden, d_outer, normed_two, d_inner, d_branch, doT, small, small_up = blocks

    wide_bits = axis_bits("wide")
    narrow_bits = axis_bits("narrow")
    first_order = wide_bits[1:2] + narrow_bits + wide_bits[2:]
    second_order = narrow_bits + wide_bits[1:]
    third_order = narrow_bits + wide_bits[2:3] + wide_bits[1:2] + wide_bits[3:]
    fourth_order = wide_bits[2:3] + wide_bits[1:2] + narrow_bits + wide_bits[3:]
    small_order = wide_bits[:1] + first_order

    def outer(left, right, right_dim, order):
        return Halving(outer_halves(marks, left, right, right_dim, cores, parts, order), order)

    sum_up = outer(d_inner, normed_two, 0, first_order)
    sum_down = outer(d_outer, hidden, 0, second_order)
    sum_out = outer(d_branch, oT, 1, first_order)
    flat = jnp.concatenate([small.reshape(-1), small_up.reshape(-1)])
    early = Adding(flat.reshape(-1, PAIR), small_order)
    sums = [sum_down, sum_up, sum_out]

    heads = width // PAIR
    portions = 2 if heads % 2 == 0 else 1
    count = heads // portions
    far = []
    for portion in range(portions):
        (doT,) = launch(doT, sums, early)
        far = back_remote(
            info,
            [qT, doT, oT, lse],
            turns_far,
            [kT_far, vT_far],
            group,
            parts,
            portion * count,
            count,
            far,
        )
    dq_far, d_far = far
    d_back = unproject(d_far, w_qkv, (1, 2), 0, others * rows)
    d_mixed = []
    for portion in range(portions):
        doT, d_back = launch(doT, sums, early, d_back)
        if not portion:
            returned = [
                lax.ppermute(
                    d_back[j * rows : (j + 1) * rows] if others > 1 else d_back,
                    "narrow",
                    [(n, (n + j + 1) % parts) for n in range(parts)],
                )
                for j in range(others)
            ]
        d_mixed = [
            back_local(
                info,
                [qT, doT, oT, lse],
                turns,
                [kT, vT],
                dq_far,
                group,
                portion * count,
                count,
                d_mixed,
            )
        ]
    d_mixed = d_mixed[0]
    while early.order:
        (d_mixed,) = launch(d_mixed, sums, early)
    d_mixed = settle(d_mixed, sums, early)
    d_mixed, returned = lax.optimization_barrier((d_mixed, returned))
    if others > 1:
        returned = [functools.reduce(jnp.add, [item.astype(f32) for item in returned])]

    orders = [first_order, third_order, fourth_order]
    pieces, bias, weighted = mixed_halves(
        marks,
        d_mixed.reshape(3 * width, rows),
        d_far.reshape(3 * width, -1),
        normed,
        normed_far,
        w_qkv,
        cores,
        parts,
        orders,
    )
    pieces = [Halving(halves, order) for halves, order in zip(pieces, orders)]
    part_shift = weighted[1]
    part_gain = (weighted[0] - shift_one * part_shift) / gain_one
    flat = jnp.concatenate([bias.reshape(-1), part_gain, part_shift])
    late = Adding(flat.reshape(-1, PAIR), small_order)
    sum_w_down, sum_w_up, sum_w_out = collect([[item] for item in sums])
    (d_mixed,) = launch(d_mixed, pieces, late)
    d_tokens = []
    for i in range(2):
        finish = (returned[0], tokens, d_middle, row(gain_one))
        d_tokens = [
            unproject(d_mixed, w_qkv, (0, 1, 2), i * group, group, finish, d_tokens)
        ]
        if late.order:
            d_mixed, d_tokens[0] = launch(d_mixed, pieces, late, d_tokens[0])
    while late.order:
        (d_tokens[0],) = launch(d_tokens[0], pieces, late)

    (sum_w_qkv,) = collect([pieces])
    early_small = (early.terms[0] + early.terms[1]).reshape(-1)
    small = early_small[: 8 * width].reshape(8, width)
    small_up = early_small[8 * width :]
    late_small = (late.terms[0] + late.terms[1]).reshape(-1)
    shape = inputs.shape
    return (
        result.reshape(shape),
        d_tokens[0].reshape(shape),
        sum_w_qkv.T,
        sum_w_out.T,
        sum_w_up.T,
        sum_w_down.T,
        late_small[: 3 * width],
        small[7],
        small_up,
        small[2],
        late_small[3 * width : 4 * width],
        late_small[4 * width :],
        small[5],
        small[6],
        small[3],
        small[4],
        small[0],
        small[1],
    )


def solution(mesh):
    tokens = P("wide", None, "narrow", None, None)
    columns = P(None, ("wide", "narrow"))
    in_specs = (tokens, tokens, P("wide")) + (P(),) * 16
    out_specs = (tokens, tokens) + (columns,) * 4 + (P(),) * 12
    return jax.shard_map(body, mesh=mesh, in_specs=in_specs, out_specs=out_specs, check_vma=False)
```

```python
import functools

import jax
import jax.numpy as jnp
from jax import lax
from jax.experimental import pallas as pl
from jax.experimental.pallas import tpu as pltpu
from jax.sharding import PartitionSpec as P

HEAD_DIM = 64
PAIR = 2 * HEAD_DIM
EPS = 1e-05
LOG2E = 1.4426950408889634
LN2 = 0.6931471805599453
NEG = -1e30
REACH = 60.0
VMEM = 62 * 1024 * 1024
SPAN = 1024

f32 = jnp.float32
bf16 = jnp.bfloat16


def dot(left, right, left_dim, right_dim):
    return lax.dot_general(
        left, right, (((left_dim,), (right_dim,)), ((), ())), preferred_element_type=f32
    )


def bounded(qT, kT):
    worst = None
    for h in range(2):
        rows = slice(HEAD_DIM * h, HEAD_DIM * (h + 1))
        norms = []
        for item in (qT, kT):
            values = item[rows, :].astype(f32)
            norms.append(jnp.max(jnp.sum(values * values, axis=0, keepdims=True)))
        both = norms[0] * norms[1]
        worst = both if worst is None else jnp.maximum(worst, both)
    return worst <= REACH * REACH


def fwd_chunk(fast, q0, k0, q_n, k_n, limit, store, qT, kT, vT, m_ref, l_ref, acc):
    queries = pl.ds(q0, q_n)
    strip = min(256, k_n)
    for h in range(2):
        rows = slice(HEAD_DIM * h, HEAD_DIM * (h + 1))
        old = m_ref[h : h + 1, queries]
        new = jnp.zeros_like(old) if fast else old
        strips = []
        for j in range(k_n // strip):
            keys = pl.ds(k0 + j * strip, strip)
            scores = dot(kT[rows, keys], qT[rows, queries], 0, 0)
            if limit is not None:
                key_at = lax.broadcasted_iota(jnp.int32, (strip, q_n), 0)
                scores = jnp.where(key_at < limit - j * strip, scores, NEG)
            strips.append(scores)
            if not fast:
                new = jnp.maximum(new, jnp.max(scores, axis=0, keepdims=True))
        factor = jnp.exp2(old - new)
        total = l_ref[h : h + 1, queries] * factor
        value = acc[rows, queries] * factor
        for j in range(k_n // strip):
            keys = pl.ds(k0 + j * strip, strip)
            weights = jnp.exp2(strips[j] if fast else strips[j] - new)
            total = total + jnp.sum(weights, axis=0, keepdims=True)
            weights = weights.astype(bf16)
            if fast:
                store(h, j, weights)
            value = value + dot(vT[rows, keys], weights, 1, 0)
        m_ref[h : h + 1, queries] = new
        l_ref[h : h + 1, queries] = total
        acc[rows, queries] = value


def pad_left(values, count):
    if not count:
        return values
    return jnp.concatenate([jnp.zeros((values.shape[0], count), f32), values], axis=1)


def pad_right(values, count):
    if not count:
        return values
    return jnp.concatenate([values, jnp.zeros((values.shape[0], count), f32)], axis=1)


def fwd_diagonal(fast, base, group, limit, store, qT, kT, vT, m_ref, l_ref, acc):
    strip = min(256, group)
    count = group // strip
    for h in range(2):
        rows = slice(HEAD_DIM * h, HEAD_DIM * (h + 1))
        strips = []
        for j in range(count):
            wide = group - j * strip
            keys, queries = pl.ds(base + j * strip, strip), pl.ds(base + j * strip, wide)
            scores = dot(kT[rows, keys], qT[rows, queries], 0, 0)
            key_at = lax.broadcasted_iota(jnp.int32, scores.shape, 0)
            query_at = lax.broadcasted_iota(jnp.int32, scores.shape, 1)
            scores = jnp.where(key_at <= query_at, scores, NEG)
            if limit is not None:
                scores = jnp.where(key_at < limit - j * strip, scores, NEG)
            strips.append(scores)
        peaks = []
        for g in range(0 if fast else count):
            peak = None
            for j in range(g + 1):
                part = strips[j][:, (g - j) * strip : (g - j + 1) * strip]
                part = jnp.max(part, axis=0, keepdims=True)
                peak = part if peak is None else jnp.maximum(peak, part)
            peaks.append(peak)
        if fast:
            peak = jnp.zeros((1, group), f32)
        else:
            peak = jnp.concatenate(peaks, axis=1) if count > 1 else peaks[0]
        total, value = None, None
        for j in range(count):
            keys = pl.ds(base + j * strip, strip)
            weights = jnp.exp2(strips[j] if fast else strips[j] - peak[:, j * strip :])
            part = pad_left(jnp.sum(weights, axis=0, keepdims=True), j * strip)
            weights = weights.astype(bf16)
            if fast:
                store(h, j, weights)
            term = pad_left(dot(vT[rows, keys], weights, 1, 0), j * strip)
            total = part if total is None else total + part
            value = term if value is None else value + term
        queries = pl.ds(base, group)
        m_ref[h : h + 1, queries] = peak
        l_ref[h : h + 1, queries] = total
        acc[rows, queries] = value


def triangle_slot(i, j, group):
    strip = min(256, group)
    count = group // strip
    row = jnp.where(i == 0, j, count - j) * strip
    column = jnp.where(i == 0, j * strip, 0)
    wide = group - j * strip
    return (
        pl.ds(pl.multiple_of(row, strip), strip),
        pl.ds(pl.multiple_of(column, strip), wide),
    )


def square_slot(j, group):
    strip = min(256, group)
    return pl.ds(group + strip + j * strip, strip), slice(None)


def fwd_local_kernel(group, info, qT, kT, vT, acc, m_ref, l_ref, kept, flags):
    length = info[1]
    m_ref[...] = jnp.full(m_ref.shape, NEG, f32)
    l_ref[...] = jnp.zeros(l_ref.shape, f32)
    acc[...] = jnp.zeros(acc.shape, f32)
    refs = (qT, kT, vT, m_ref.at[0], l_ref.at[0], acc)

    def walk(fast):
        def own(i, carry):
            base = pl.multiple_of(i * group, group)
            start = info[2 + i]

            def store(h, j, weights):
                rows, columns = triangle_slot(i, j, group)
                kept[h, rows, columns] = weights

            @pl.when(start + group <= length)
            def _():
                fwd_diagonal(fast, base, group, None, store, *refs)

            @pl.when((start < length) & (start + group > length))
            def _():
                fwd_diagonal(fast, base, group, length - start, store, *refs)

            return carry

        lax.fori_loop(0, 2, own, 0)
        early = info[2]

        def store(h, j, weights):
            rows, columns = square_slot(j, group)
            kept[h, rows, columns] = weights

        @pl.when(early + group <= length)
        def _():
            fwd_chunk(fast, group, 0, group, group, None, store, *refs)

        @pl.when((early < length) & (early + group > length))
        def _():
            fwd_chunk(fast, group, 0, group, group, length - early, store, *refs)

    small = bounded(qT, kT)
    flags[pl.program_id(0)] = small.astype(jnp.int32)
    pl.when(small)(functools.partial(walk, True))
    pl.when(jnp.logical_not(small))(functools.partial(walk, False))


def remote_steps(group, parts, info, full, partial):
    place, length = info[0], info[1]

    def visit(i, carry):
        j, turn_at = i // 3, lax.rem(i, 3)
        other = lax.rem(place + 1 + j, parts)
        late_key = turn_at == 2
        block = jnp.where(late_key, 2 * parts - 1 - other, other)
        before = (other < place).astype(jnp.int32)
        wanted = jnp.where(turn_at == 0, before, jnp.where(late_key, 1 - before, 1)) == 1
        q0 = pl.multiple_of(jnp.where(turn_at == 0, 0, group), group)
        k0 = pl.multiple_of((2 * j + jnp.where(late_key, 1, 0)) * group, group)
        slot = pl.multiple_of((2 * j + turn_at - (1 - before)) * group, group)
        start = block * group

        @pl.when(wanted & (start + group <= length))
        def _():
            full(q0, k0, slot)

        @pl.when(wanted & (start < length) & (start + group > length))
        def _():
            partial(q0, k0, slot, length - start)

        return carry

    lax.fori_loop(0, 3 * (parts - 1), visit, 0)


def fwd_remote_kernel(
    group, parts, info, qT, kT, vT, acc_in, m_in, l_in, out, lse, kept, flags, acc, m_ref, l_ref
):
    acc[...] = acc_in[...]
    m_ref[...] = m_in[0]
    l_ref[...] = l_in[0]
    refs = (qT, kT, vT, m_ref, l_ref, acc)
    strip = min(256, group)

    def walk(fast):
        def partial(q0, k0, slot, limit):
            def store(h, j, weights):
                kept[h, pl.ds(pl.multiple_of(slot + j * strip, strip), strip), :] = weights

            fwd_chunk(fast, q0, k0, group, group, limit, store, *refs)

        def full(q0, k0, slot):
            partial(q0, k0, slot, None)

        remote_steps(group, parts, info, full, partial)

    small = bounded(qT, kT) & (jnp.max(m_in[...]) <= 0.0)
    flags[pl.program_id(0)] = small.astype(jnp.int32)
    pl.when(small)(functools.partial(walk, True))
    pl.when(jnp.logical_not(small))(functools.partial(walk, False))
    for h in range(2):
        rows = slice(HEAD_DIM * h, HEAD_DIM * (h + 1))
        total = l_ref[h : h + 1, :]
        out[rows, :] = (acc[rows, :] / total).astype(bf16)
        lse[0, h : h + 1, :] = m_ref[h : h + 1, :] + jnp.log2(total)


def split_three(values):
    high = values.astype(bf16).astype(f32)
    rest = values - high
    middle = rest.astype(bf16).astype(f32)
    low = (rest - middle).astype(bf16).astype(f32)
    return [high, middle, low]


def bwd_prepare(qT, kT, vT, doT, oT, lse, qa, da, ka, va):
    n_q, n_k = qT.shape[1], ka.shape[2]
    extra = qa.shape[1] - HEAD_DIM
    pad = jnp.zeros((extra - 3, n_q), f32)
    row_at = lax.broadcasted_iota(jnp.int32, (extra, n_k), 0)
    tail = jnp.where(row_at < 3, 1.0, 0.0).astype(bf16)
    for h in range(2):
        rows = slice(HEAD_DIM * h, HEAD_DIM * (h + 1))
        grad = doT[rows, :].astype(f32)
        delta = jnp.sum(grad * oT[rows, :].astype(f32), axis=0, keepdims=True)
        qa[h, :HEAD_DIM, :] = qT[rows, :]
        parts = split_three(-lse[0, h : h + 1, :]) + [pad]
        qa[h, HEAD_DIM:, :] = jnp.concatenate(parts, axis=0).astype(bf16)
        da[h, :HEAD_DIM, :] = doT[rows, :]
        parts = split_three(-delta) + [pad]
        da[h, HEAD_DIM:, :] = jnp.concatenate(parts, axis=0).astype(bf16)
        ka[h, :HEAD_DIM, :] = kT[rows, :]
        va[h, :HEAD_DIM, :] = vT[rows, :]
        ka[h, HEAD_DIM:, :] = tail
        va[h, HEAD_DIM:, :] = tail


def bwd_chunk(q0, k0, q_n, k_n, limit, qT, doT, qa, da, ka, va, dq, dk, dv):
    queries, keys = pl.ds(q0, q_n), pl.ds(k0, k_n)
    for h in range(2):
        rows = slice(HEAD_DIM * h, HEAD_DIM * (h + 1))
        probs = jnp.exp2(dot(qa[h, :, queries], ka[h, :, keys], 0, 0))
        if limit is not None:
            key_at = lax.broadcasted_iota(jnp.int32, (q_n, k_n), 1)
            probs = jnp.where(key_at < limit, probs, 0.0)
        d_probs = dot(da[h, :, queries], va[h, :, keys], 0, 0)
        d_scores = (probs * d_probs).astype(bf16)
        dv[rows, keys] += dot(doT[rows, queries], probs.astype(bf16), 1, 0)
        dk[rows, keys] += dot(qT[rows, queries], d_scores, 1, 0)
        dq[rows, queries] += dot(ka[h, :HEAD_DIM, keys], d_scores, 1, 1)


def bwd_diagonal(base, group, limit, qT, doT, qa, da, ka, va, dq, dk, dv):
    strip = min(256, group)
    count = group // strip
    for h in range(2):
        rows = slice(HEAD_DIM * h, HEAD_DIM * (h + 1))
        d_keys, d_values, d_queries = None, None, []
        for j in range(count):
            wide = (j + 1) * strip
            queries, keys = pl.ds(base + j * strip, strip), pl.ds(base, wide)
            probs = jnp.exp2(dot(qa[h, :, queries], ka[h, :, keys], 0, 0))
            query_at = lax.broadcasted_iota(jnp.int32, probs.shape, 0)
            key_at = lax.broadcasted_iota(jnp.int32, probs.shape, 1)
            probs = jnp.where(key_at <= query_at + j * strip, probs, 0.0)
            if limit is not None:
                probs = jnp.where(key_at < limit, probs, 0.0)
            d_probs = dot(da[h, :, queries], va[h, :, keys], 0, 0)
            d_scores = (probs * d_probs).astype(bf16)
            value = pad_right(dot(doT[rows, queries], probs.astype(bf16), 1, 0), group - wide)
            key = pad_right(dot(qT[rows, queries], d_scores, 1, 0), group - wide)
            d_values = value if d_values is None else d_values + value
            d_keys = key if d_keys is None else d_keys + key
            d_queries.append(dot(ka[h, :HEAD_DIM, keys], d_scores, 1, 1))
        here = pl.ds(base, group)
        dq[rows, here] += jnp.concatenate(d_queries, axis=1) if count > 1 else d_queries[0]
        dk[rows, here] += d_keys
        dv[rows, here] += d_values


def stored_prepare(doT, oT, lse, scaled, delta):
    for h in range(2):
        rows = slice(HEAD_DIM * h, HEAD_DIM * (h + 1))
        grad = (doT[rows, :].astype(f32) * jnp.exp2(-lse[0, h : h + 1, :])).astype(bf16)
        scaled[rows, :] = grad
        delta[h : h + 1, :] = column_sum(grad.astype(f32) * oT[rows, :].astype(f32))


def stored_chunk(h, weights, queries, keys, qT, kT, vT, scaled, delta, dq, dk, dv):
    rows = slice(HEAD_DIM * h, HEAD_DIM * (h + 1))
    d_probs = dot(vT[rows, keys], scaled[rows, queries], 0, 0)
    d_scores = weights.astype(f32) * (d_probs - delta[h : h + 1, queries])
    d_scores = d_scores.astype(bf16)
    dv[rows, keys] += dot(scaled[rows, queries], weights, 1, 1)
    dk[rows, keys] += dot(qT[rows, queries], d_scores, 1, 1)
    dq[rows, queries] += dot(kT[rows, keys], d_scores, 1, 0)


def turn_back(values, cosine, sine):
    half = HEAD_DIM // 2
    first, second = values[:half], values[half:]
    return jnp.concatenate(
        [first * cosine + second * sine, second * cosine - first * sine], axis=0
    )


def bwd_remote_kernel(
    group, parts, first, info, flags, qT, doT, oT, lse, cosine, sine, kT, vT, kept, *rest
):
    dq, dkv, qa, da, ka, va, dk, dv, scaled, delta = rest[-10:]
    dq[...] = jnp.zeros(dq.shape, f32)
    dk[...] = jnp.zeros(dk.shape, f32)
    dv[...] = jnp.zeros(dv.shape, f32)
    fast = flags[first + pl.program_id(0)] == 1

    @pl.when(fast)
    def _():
        stored_prepare(doT, oT, lse, scaled, delta)

        def full(q0, k0, slot):
            for h in range(2):
                weights = kept[h, pl.ds(slot, group), :]
                queries, keys = pl.ds(q0, group), pl.ds(k0, group)
                stored_chunk(h, weights, queries, keys, qT, kT, vT, scaled, delta, dq, dk, dv)

        def partial(q0, k0, slot, limit):
            full(q0, k0, slot)

        remote_steps(group, parts, info, full, partial)

    @pl.when(jnp.logical_not(fast))
    def _():
        bwd_prepare(qT, kT, vT, doT, oT, lse, qa, da, ka, va)
        refs = (qT, doT, qa, da, ka, va, dq, dk, dv)

        def full(q0, k0, slot):
            bwd_chunk(q0, k0, group, group, None, *refs)

        def partial(q0, k0, slot, limit):
            bwd_chunk(q0, k0, group, group, limit, *refs)

        remote_steps(group, parts, info, full, partial)

    for h in range(2):
        rows = slice(HEAD_DIM * h, HEAD_DIM * (h + 1))
        dkv[1, rows, :] = turn_back(dk[rows, :] * LN2, cosine[...], sine[...]).astype(bf16)
    dkv[0] = jnp.zeros(dv.shape, bf16)
    dkv[2] = dv[...].astype(bf16)


def bwd_local_kernel(
    group, first, info, flags, qT, doT, oT, lse, cosine, sine, kT, vT, dq_in, kept, *rest
):
    dqkv, qa, da, ka, va, dk, dv, scaled, delta, dq = rest[-10:]
    length = info[1]
    dq[...] = dq_in[...]
    dk[...] = jnp.zeros(dk.shape, f32)
    dv[...] = jnp.zeros(dv.shape, f32)
    early = info[2]
    strip = min(256, group)
    fast = flags[first + pl.program_id(0)] == 1

    @pl.when(fast)
    def _():
        stored_prepare(doT, oT, lse, scaled, delta)
        refs = (qT, kT, vT, scaled, delta, dq, dk, dv)

        def own(i, carry):
            base = pl.multiple_of(i * group, group)

            @pl.when(info[2 + i] < length)
            def _():
                for h in range(2):
                    for j in range(group // strip):
                        rows, columns = triangle_slot(i, j, group)
                        queries = pl.ds(base + j * strip, group - j * strip)
                        keys = pl.ds(base + j * strip, strip)
                        stored_chunk(h, kept[h, rows, columns], queries, keys, *refs)

            return carry

        lax.fori_loop(0, 2, own, 0)

        @pl.when(early < length)
        def _():
            for h in range(2):
                weights = kept[h, group + strip :, :]
                stored_chunk(h, weights, pl.ds(group, group), pl.ds(0, group), *refs)

    @pl.when(jnp.logical_not(fast))
    def _():
        bwd_prepare(qT, kT, vT, doT, oT, lse, qa, da, ka, va)
        refs = (qT, doT, qa, da, ka, va, dq, dk, dv)

        def own(i, carry):
            base = pl.multiple_of(i * group, group)
            start = info[2 + i]

            @pl.when(start < length)
            def _():
                bwd_diagonal(base, group, length - start, *refs)

            return carry

        lax.fori_loop(0, 2, own, 0)

        @pl.when(early < length)
        def _():
            bwd_chunk(group, 0, group, group, length - early, *refs)

    for h in range(2):
        rows = slice(HEAD_DIM * h, HEAD_DIM * (h + 1))
        d_query = dq[rows, :] * 0.125
        dqkv[0, rows, :] = turn_back(d_query, cosine[...], sine[...]).astype(bf16)
        dqkv[1, rows, :] = turn_back(dk[rows, :] * LN2, cosine[...], sine[...]).astype(bf16)
    dqkv[2] = dv[...].astype(bf16)


def rows_of(count, first=0):
    return pl.BlockSpec((PAIR, count), lambda i, *info: (first + i, 0))


def stats_of(count, first=0):
    return pl.BlockSpec((1, 2, count), lambda i, *info: (first + i, 0, 0))


def planes_of(planes, count, first=0):
    return pl.BlockSpec((planes, PAIR, count), lambda i, *info: (0, first + i, 0))


def kept_of(rows, group, first=0):
    return pl.BlockSpec((2, rows, group), lambda i, *info: (first + i, 0, 0))


def scalars():
    return pl.BlockSpec(memory_space=pltpu.SMEM)


def whole(shape):
    return pl.BlockSpec(shape, lambda i, *info: (0,) * len(shape))


def attention_call(kernel, pairs, in_specs, out_specs, out_shape, scratch, flops, name, alias={}, prefetch=1):
    return pl.pallas_call(
        kernel,
        grid_spec=pltpu.PrefetchScalarGridSpec(
            num_scalar_prefetch=prefetch,
            grid=(pairs,),
            in_specs=in_specs,
            out_specs=out_specs,
            scratch_shapes=scratch,
        ),
        out_shape=out_shape,
        input_output_aliases=alias,
        compiler_params=pltpu.CompilerParams(vmem_limit_bytes=VMEM),
        cost_estimate=pl.CostEstimate(
            flops=int(flops), bytes_accessed=1 << 25, transcendentals=0
        ),
        name=name,
    )


def attend_local(info, qT, kT, vT, group):
    width, n_q = qT.shape
    pairs = width // PAIR
    kept_rows = 2 * group + min(256, group)
    call = attention_call(
        functools.partial(fwd_local_kernel, group),
        pairs,
        [rows_of(n_q)] * 3,
        [rows_of(n_q), stats_of(n_q), stats_of(n_q), kept_of(kept_rows, group), scalars()],
        [
            jax.ShapeDtypeStruct((width, n_q), f32),
            jax.ShapeDtypeStruct((pairs, 2, n_q), f32),
            jax.ShapeDtypeStruct((pairs, 2, n_q), f32),
            jax.ShapeDtypeStruct((2 * pairs, kept_rows, group), bf16),
            jax.ShapeDtypeStruct((pairs,), jnp.int32),
        ],
        [],
        4 * width * 2 * group * group * 4,
        "attend_local",
    )
    *state, kept, flags = call(info, qT, kT, vT)
    return state, kept, flags


def attend_remote(info, qT, kT, vT, state, group, parts):
    width, n_q = qT.shape
    n_k = kT.shape[1]
    pairs = width // PAIR
    call = attention_call(
        functools.partial(fwd_remote_kernel, group, parts),
        pairs,
        [rows_of(n_q), rows_of(n_k), rows_of(n_k), rows_of(n_q), stats_of(n_q), stats_of(n_q)],
        [rows_of(n_q), stats_of(n_q), kept_of(n_k, group), scalars()],
        [
            jax.ShapeDtypeStruct((width, n_q), bf16),
            jax.ShapeDtypeStruct((pairs, 2, n_q), f32),
            jax.ShapeDtypeStruct((2 * pairs, n_k, group), bf16),
            jax.ShapeDtypeStruct((pairs,), jnp.int32),
        ],
        [pltpu.VMEM((PAIR, n_q), f32)] + [pltpu.VMEM((2, n_q), f32)] * 2,
        4 * width * 2 * group * group * 4,
        "attend_remote",
    )
    return call(info, qT, kT, vT, *state)


def back_scratch(n_q, n_k):
    rows = HEAD_DIM + 16
    return (
        [pltpu.VMEM((2, rows, n_q), bf16)] * 2
        + [pltpu.VMEM((2, rows, n_k), bf16)] * 2
        + [pltpu.VMEM((PAIR, n_k), f32)] * 2
        + [pltpu.VMEM((PAIR, n_q), bf16), pltpu.VMEM((2, n_q), f32)]
    )


def back_remote(info, flags, operands, turns, keys, kept, group, parts, first, count, before):
    width, n_q = operands[0].shape
    n_k = keys[0].shape[1]
    half = HEAD_DIM // 2
    n_in = 2 + len(operands) + len(turns) + len(keys) + 1
    call = attention_call(
        functools.partial(bwd_remote_kernel, group, parts, first),
        count,
        [rows_of(n_q, first)] * 3
        + [stats_of(n_q, first)]
        + [whole((half, n_k))] * 2
        + [rows_of(n_k, first)] * 2
        + [kept_of(kept.shape[1], group, first)]
        + [pl.BlockSpec(memory_space=pl.ANY)] * len(before),
        [rows_of(n_q, first), planes_of(3, n_k, first)],
        [
            jax.ShapeDtypeStruct((width, n_q), f32),
            jax.ShapeDtypeStruct((3, width, n_k), bf16),
        ],
        back_scratch(n_q, n_k),
        10 * count * PAIR * 2 * group * group * 4,
        "back_remote",
        {n_in + i: i for i in range(len(before))},
        2,
    )
    return call(info, flags, *operands, *turns, *keys, kept, *before)


def back_local(info, flags, operands, turns, keys, dq, kept, group, first, count, before):
    width, n_q = operands[0].shape
    half = HEAD_DIM // 2
    n_in = 2 + len(operands) + len(turns) + len(keys) + 2
    call = attention_call(
        functools.partial(bwd_local_kernel, group, first),
        count,
        [rows_of(n_q, first)] * 3
        + [stats_of(n_q, first)]
        + [whole((half, n_q))] * 2
        + [rows_of(n_q, first)] * 3
        + [kept_of(kept.shape[1], group, first)]
        + [pl.BlockSpec(memory_space=pl.ANY)] * len(before),
        planes_of(3, n_q, first),
        jax.ShapeDtypeStruct((3, width, n_q), bf16),
        back_scratch(n_q, n_q) + [pltpu.VMEM((PAIR, n_q), f32)],
        10 * count * PAIR * 2 * group * group * 4,
        "back_local",
        {n_in + i: i for i in range(len(before))},
        2,
    )
    return call(info, flags, *operands, *turns, *keys, dq, kept, *before)


def normalize(values):
    centre = values - jnp.mean(values, axis=-1, keepdims=True)
    spread = jnp.mean(centre * centre, axis=-1, keepdims=True)
    rate = lax.rsqrt(spread + EPS)
    return centre * rate, rate


def norm_back(grad, unit, rate, gain):
    scaled = grad * gain
    first = jnp.mean(scaled, axis=-1, keepdims=True)
    second = jnp.mean(scaled * unit, axis=-1, keepdims=True)
    return rate * (scaled - first - unit * second)


GELU_A = 0.7978845608028654
GELU_B = 0.044715


def column_sum(values):
    return jnp.sum(values, axis=0, keepdims=True)


def block_kernel(
    span,
    oT,
    tokens,
    cotangent,
    w_out,
    w_up,
    w_down,
    b_out,
    b_up,
    b_down,
    gain_two,
    shift_two,
    gain_three,
    shift_three,
    gain_four,
    shift_four,
    result,
    d_middle_out,
    hidden_out,
    d_outer_out,
    normed_out,
    d_inner_out,
    d_branch_out,
    doT,
    small,
    small_up,
    slope,
):
    step = pl.program_id(0)

    @pl.when(step == 0)
    def _():
        small[...] = jnp.zeros(small.shape, f32)
        small_up[...] = jnp.zeros(small_up.shape, f32)

    wide = w_up.shape[1]
    branch = dot(oT[...], w_out[...], 0, 0) + b_out[...]
    unit_two, rate_two = normalize(branch)
    middle = tokens[...].astype(f32) + (unit_two * gain_two[...] + shift_two[...])
    unit_three, rate_three = normalize(middle)
    normed = (unit_three * gain_three[...] + shift_three[...]).astype(bf16)
    normed_out[...] = normed
    outer = None
    for c in range(wide // span):
        columns = slice(c * span, (c + 1) * span)
        inner = dot(normed, w_up[:, columns], 1, 0) + b_up[:, columns]
        square = inner * inner
        bend = jnp.tanh(inner * (GELU_A + (GELU_A * GELU_B) * square))
        half = 0.5 + 0.5 * bend
        hidden = (inner * half).astype(bf16)
        hidden_out[:, columns] = hidden
        slope[:, columns] = half + inner * (1.0 - bend * bend) * (
            0.5 * GELU_A + (1.5 * GELU_A * GELU_B) * square
        )
        term = dot(hidden, w_down[columns, :], 1, 0)
        outer = term if outer is None else outer + term
    unit_four, rate_four = normalize(outer + b_down[...])
    result[...] = (middle + (unit_four * gain_four[...] + shift_four[...])).astype(bf16)

    grad = cotangent[...].astype(f32)
    d_outer = norm_back(grad, unit_four, rate_four, gain_four[...]).astype(bf16)
    d_outer_out[...] = d_outer
    small[0:1, :] += column_sum(grad * unit_four)
    small[1:2, :] += column_sum(grad)
    small[2:3, :] += column_sum(d_outer.astype(f32))
    d_normed = None
    for c in range(wide // span):
        columns = slice(c * span, (c + 1) * span)
        d_hidden = dot(d_outer, w_down[columns, :], 1, 1)
        d_inner = (d_hidden * slope[:, columns]).astype(bf16)
        d_inner_out[:, columns] = d_inner
        small_up[:, columns] += column_sum(d_inner.astype(f32))
        term = dot(d_inner, w_up[:, columns], 1, 1)
        d_normed = term if d_normed is None else d_normed + term
    small[3:4, :] += column_sum(d_normed * unit_three)
    small[4:5, :] += column_sum(d_normed)
    d_middle = grad + norm_back(d_normed, unit_three, rate_three, gain_three[...])
    d_middle_out[...] = d_middle
    small[5:6, :] += column_sum(d_middle * unit_two)
    small[6:7, :] += column_sum(d_middle)
    d_branch = norm_back(d_middle, unit_two, rate_two, gain_two[...]).astype(bf16)
    d_branch_out[...] = d_branch
    small[7:8, :] += column_sum(d_branch.astype(f32))
    doT[...] = dot(w_out[...], d_branch, 1, 1).astype(bf16)


def block_call(oT, tokens, cotangent, weights, vectors):
    width, rows = oT.shape
    wide = weights[1].shape[1]
    step = min(256, rows)
    span = min(SPAN, wide)

    def lines(count):
        return pl.BlockSpec((step, count), lambda i: (i, 0))

    def fixed(shape):
        return pl.BlockSpec(shape, lambda i: (0, 0), pipeline_mode=pl.Buffered(1))

    def total(shape):
        return pl.BlockSpec(shape, lambda i: (0, 0))

    features = pl.BlockSpec((width, step), lambda i: (0, i))
    sizes = [width, width, wide, width, width, wide, width]
    kinds = [bf16, f32, bf16, bf16, bf16, bf16, bf16]
    return pl.pallas_call(
        functools.partial(block_kernel, span),
        grid=(rows // step,),
        in_specs=[features, lines(width), lines(width)]
        + [fixed(item.shape) for item in weights]
        + [fixed(item.shape) for item in vectors],
        out_specs=[lines(size) for size in sizes]
        + [features, total((8, width)), total((1, wide))],
        out_shape=[jax.ShapeDtypeStruct((rows, size), kind) for size, kind in zip(sizes, kinds)]
        + [
            jax.ShapeDtypeStruct((width, rows), bf16),
            jax.ShapeDtypeStruct((8, width), f32),
            jax.ShapeDtypeStruct((1, wide), f32),
        ],
        scratch_shapes=[pltpu.VMEM((step, wide), f32)],
        compiler_params=pltpu.CompilerParams(vmem_limit_bytes=VMEM),
        cost_estimate=pl.CostEstimate(
            flops=2 * 2 * rows * (width * width + 2 * width * wide),
            bytes_accessed=1 << 26,
            transcendentals=rows * wide,
        ),
        name="block",
    )(oT, tokens, cotangent, *weights, *vectors)


def turn(values, cosine, sine):
    half = HEAD_DIM // 2
    first, second = values[:half], values[half:]
    return jnp.concatenate(
        [first * cosine - second * sine, second * cosine + first * sine], axis=0
    )


def project_kernel(sections, tokens, w, b, gain, shift, cosine, sine, normed_out, *outs):
    unit, rate = normalize(tokens[...].astype(f32))
    normed = (unit * gain[...] + shift[...]).astype(bf16)
    normed_out[...] = normed
    width = tokens.shape[1]
    chunk = min(256, width)
    for section, out in zip(sections, outs):
        for c in range(width // chunk):
            at = section * width + c * chunk
            mixed = dot(w[:, at : at + chunk], normed, 0, 1) + b[:, at : at + chunk].T
            for h in range(chunk // HEAD_DIM):
                rows = slice(h * HEAD_DIM, (h + 1) * HEAD_DIM)
                place = slice(c * chunk + h * HEAD_DIM, c * chunk + (h + 1) * HEAD_DIM)
                value = mixed[rows]
                if section < 2:
                    value = turn(value, cosine[...], sine[...])
                if section == 0:
                    value = value * (0.125 * LOG2E)
                out[place, :] = value.astype(bf16)


def project(tokens, w, b, gain, shift, cosine, sine, sections):
    rows, width = tokens.shape
    step = min(512, rows)
    half = HEAD_DIM // 2

    def fixed(shape):
        return pl.BlockSpec(shape, lambda i: (0, 0), pipeline_mode=pl.Buffered(1))

    lines = pl.BlockSpec((step, width), lambda i: (i, 0))
    features = pl.BlockSpec((width, step), lambda i: (0, i))
    turns = pl.BlockSpec((half, step), lambda i: (0, i))
    return pl.pallas_call(
        functools.partial(project_kernel, sections),
        grid=(rows // step,),
        in_specs=[lines, fixed(w.shape), fixed(b.shape), fixed(gain.shape), fixed(shift.shape)]
        + [turns] * 2,
        out_specs=[lines] + [features] * len(sections),
        out_shape=[jax.ShapeDtypeStruct((rows, width), bf16)]
        + [jax.ShapeDtypeStruct((width, rows), bf16)] * len(sections),
        compiler_params=pltpu.CompilerParams(vmem_limit_bytes=VMEM),
        cost_estimate=pl.CostEstimate(
            flops=2 * rows * width * width * len(sections),
            bytes_accessed=1 << 24,
            transcendentals=0,
        ),
        name="project",
    )(tokens, w, b, gain, shift, cosine, sine)


def unproject_kernel(planes, finish, *refs):
    d_mixed, w, out = refs[: len(planes)], refs[len(planes)], refs[-1]
    width = w.shape[0]
    total = None
    for plane, ref in zip(planes, d_mixed):
        term = dot(ref[0], w[:, plane * width : (plane + 1) * width], 0, 1)
        total = term if total is None else total + term
    if not finish:
        out[...] = total.astype(bf16)
        return
    returned, tokens, d_middle, gain = refs[len(planes) + 1 : len(planes) + 5]
    total = total + returned[...].astype(f32)
    unit, rate = normalize(tokens[...].astype(f32))
    out[...] = (d_middle[...] + norm_back(total, unit, rate, gain[...])).astype(bf16)


def unproject(d_mixed, w, planes, start, count, finish=(), before=()):
    _, width, total = d_mixed.shape
    step = min(256, count)
    first = start // step

    def fixed(shape):
        return pl.BlockSpec(shape, lambda i: (0, 0), pipeline_mode=pl.Buffered(1))

    def plane_of(plane):
        return pl.BlockSpec((1, width, step), lambda i: (plane, 0, first + i))

    lines = pl.BlockSpec((step, width), lambda i: (i, 0))
    later = pl.BlockSpec((step, width), lambda i: (first + i, 0))
    specs = [later] * 3 + [fixed(finish[-1].shape)] if finish else []
    n_in = len(planes) + 1 + len(finish)
    return pl.pallas_call(
        functools.partial(unproject_kernel, planes, bool(finish)),
        grid=(count // step,),
        in_specs=[plane_of(plane) for plane in planes]
        + [fixed(w.shape)]
        + specs
        + [pl.BlockSpec(memory_space=pl.ANY)] * len(before),
        out_specs=later if finish else lines,
        out_shape=jax.ShapeDtypeStruct((total if finish else count, width), bf16),
        input_output_aliases={n_in + i: i for i in range(len(before))},
        compiler_params=pltpu.CompilerParams(vmem_limit_bytes=VMEM),
        cost_estimate=pl.CostEstimate(
            flops=2 * count * width * width * len(planes),
            bytes_accessed=1 << 24,
            transcendentals=0,
        ),
        name="unproject",
    )(*[d_mixed] * len(planes), w, *finish, *before)


def divide(total, run, levels, near, marks, orders, outs):
    bits = [("narrow", i) for i in range(near)] + [("wide", i) for i in range(levels + 1)]
    cut = run // len(orders)

    def write(core):
        for at in range(0, total.shape[0], run):
            number = at // run
            value = {}
            for place, (axis, position) in enumerate(bits):
                mine = (marks[1 if axis == "narrow" else 0] >> position) & 1
                value[axis, position] = mine ^ ((number >> place) & 1)
            other = core ^ ((number >> near) & 1)
            for i, order in enumerate(orders):
                index = tuple(value.get(bit, 0) for bit in order)
                part = total[at + i * cut : at + (i + 1) * cut]
                outs[2 * i + other][index] = part.astype(bf16)

    pl.when((marks[0] & 1) == 0)(functools.partial(write, 0))
    pl.when((marks[0] & 1) == 1)(functools.partial(write, 1))


def divided(orders, levels, run, height, wide, width):
    cut = run // len(orders)
    specs, shapes = [], []
    for order in orders:

        def held(bit):
            return bit[0] == "narrow" or bit[1] <= levels

        def index(j, i, marks, order=order):
            relative = i ^ (marks[0] >> (levels + 1))
            at = [0 if held(bit) else (relative >> (bit[1] - 1 - levels)) & 1 for bit in order]
            return (*at, 0, j)

        block = tuple(2 if held(bit) else 1 for bit in order) + (cut, wide)
        specs += [pl.BlockSpec(block, index)] * 2
        shapes += [jax.ShapeDtypeStruct((2,) * len(order) + (cut, width), bf16)] * 2
    return specs, shapes


def outer_kernel(run, levels, near, orders, right_dim, marks, left, right, *outs):
    divide(dot(left[...], right[...], 0, right_dim), run, levels, near, marks, orders, outs)


def outer_halves(marks, left, right, right_dim, cores, parts, order):
    rows, height = left.shape
    width = right.shape[1 - right_dim]
    share = height // cores
    high = max(2 * share, min(1024, height))
    levels = (high // (2 * share)).bit_length() - 1
    wide = min(1024, width)
    if right_dim == 0:
        right_spec = pl.BlockSpec((rows, wide), lambda j, i, marks: (0, j))
    else:
        right_spec = pl.BlockSpec((wide, rows), lambda j, i, marks: (j, 0))
    run = share // parts
    near = parts.bit_length() - 1
    specs, shapes = divided([order], levels, run, height, wide, width)
    halves = pl.pallas_call(
        functools.partial(outer_kernel, run, levels, near, [order], right_dim),
        grid_spec=pltpu.PrefetchScalarGridSpec(
            num_scalar_prefetch=1,
            grid=(width // wide, height // high),
            in_specs=[pl.BlockSpec((rows, high), lambda j, i, marks: (0, i)), right_spec],
            out_specs=specs,
        ),
        out_shape=shapes,
        compiler_params=pltpu.CompilerParams(vmem_limit_bytes=VMEM),
        cost_estimate=pl.CostEstimate(
            flops=2 * rows * height * width, bytes_accessed=1 << 25, transcendentals=0
        ),
        name="outer",
    )(marks, left, right)
    return [item.reshape(height // 2, width) for item in halves]


def mixed_kernel(
    run, levels, near, orders, first_far, marks, d_own, d_far, normed, normed_far, w, *outs
):
    *halves, bias, sums = outs
    step = pl.program_id(1)
    total = dot(d_own[...], normed[...], 1, 0)
    bias[...] = jnp.sum(d_own[...].astype(f32), axis=1, keepdims=True)

    @pl.when(step == 0)
    def _():
        sums[...] = jnp.zeros(sums.shape, f32)

    def finish(value):
        divide(value, run, levels, near, marks, orders, halves)
        weights = w[...].astype(f32).T
        sums[0:1, :] += column_sum(weights * value)
        sums[1:2, :] += column_sum(weights * bias[...])

    @pl.when(step < first_far)
    def _():
        finish(total)

    @pl.when(step >= first_far)
    def _():
        bias[...] += jnp.sum(d_far[...].astype(f32), axis=1, keepdims=True)
        finish(total + dot(d_far[...], normed_far[...], 1, 0))


def mixed_halves(marks, d_own, d_far, normed, normed_far, w, cores, parts, orders):
    height, rows = d_own.shape
    far = d_far.shape[1]
    width = normed.shape[1]
    share = height // cores
    pairs = max(1, 768 // (2 * share))
    levels = pairs.bit_length() - 1
    high = 2 * share * pairs
    first_far = width // high
    run = share // parts
    near = parts.bit_length() - 1

    def fixed(shape):
        return pl.BlockSpec(shape, lambda j, i, marks: (0, 0), pipeline_mode=pl.Buffered(1))

    specs, shapes = divided(orders, levels, run, height, width, width)
    *halves, bias, sums = pl.pallas_call(
        functools.partial(mixed_kernel, run, levels, near, orders, first_far),
        grid_spec=pltpu.PrefetchScalarGridSpec(
            num_scalar_prefetch=1,
            grid=(1, height // high),
            in_specs=[
                pl.BlockSpec((high, rows), lambda j, i, marks: (i, 0)),
                pl.BlockSpec((high, far), lambda j, i, marks: (jnp.maximum(i, first_far), 0)),
                fixed(normed.shape),
                fixed(normed_far.shape),
                pl.BlockSpec((width, high), lambda j, i, marks: (0, i)),
            ],
            out_specs=specs
            + [
                pl.BlockSpec((high, 1), lambda j, i, marks: (i, 0)),
                pl.BlockSpec((2, width), lambda j, i, marks: (0, 0)),
            ],
        ),
        out_shape=shapes
        + [
            jax.ShapeDtypeStruct((height, 1), f32),
            jax.ShapeDtypeStruct((2, width), f32),
        ],
        compiler_params=pltpu.CompilerParams(vmem_limit_bytes=VMEM),
        cost_estimate=pl.CostEstimate(
            flops=2 * (rows + far) * height * width, bytes_accessed=1 << 25, transcendentals=0
        ),
        name="mixed",
    )(marks, d_own, d_far, normed, normed_far, w)
    halves = [item.reshape(-1, width) for item in halves]
    return [halves[i : i + 2] for i in range(0, len(halves), 2)], bias, sums


def bit_of(axis, position):
    return (lax.axis_index(axis) >> position) & 1


def swap(values, axis, position):
    size = lax.axis_size(axis)
    return lax.ppermute(values, axis, [(i, i ^ (1 << position)) for i in range(size)])


class Halving:
    def __init__(self, halves, order):
        self.order = list(order)
        kept, given = halves
        self.terms = [kept, swap(given, "wide", 0)]

    def send(self, array, away):
        self.terms = [array, swap(away, *self.order.pop(0))]


class Adding:
    def __init__(self, array, order):
        self.order = list(order)
        self.terms = [array, swap(array, *self.order.pop(0))]

    def send(self, total):
        self.terms = [total, swap(total, *self.order.pop(0))]


def halve_kernel(count, *refs):
    ins, outs = refs[: 4 * count + 2], refs[4 * count + 2 :]
    for i in range(count):
        one, two = ins[4 * i : 4 * i + 2], ins[4 * i + 2 : 4 * i + 4]
        for half in range(2):
            total = one[half][0].astype(f32) + two[half][0].astype(f32)
            outs[2 * i + half][...] = total.astype(bf16)
    outs[-1][...] = ins[-2][...] + ins[-1][...]


def halve(sums, small):
    heights = [item.terms[0].shape[0] // 2 for item in sums]
    grid = 4 if all(height % 64 == 0 for height in heights) else 1
    operands, in_specs, out_specs, out_shape = [], [], [], []
    for item, height in zip(sums, heights):
        width = item.terms[0].shape[1]
        block = (height // grid, width)
        for term in item.terms:
            for half in range(2):
                operands.append(term.reshape(2, height, width))
                in_specs.append(pl.BlockSpec((1, *block), lambda i, half=half: (half, i, 0)))
        out_specs += [pl.BlockSpec(block, lambda i: (i, 0))] * 2
        out_shape += [jax.ShapeDtypeStruct((height, width), bf16)] * 2
    whole_small = pl.BlockSpec(small.terms[0].shape, lambda i: (0, 0))
    return pl.pallas_call(
        functools.partial(halve_kernel, len(sums)),
        grid=(grid,),
        in_specs=in_specs + [whole_small] * 2,
        out_specs=out_specs + [whole_small],
        out_shape=out_shape + [jax.ShapeDtypeStruct(small.terms[0].shape, f32)],
        compiler_params=pltpu.CompilerParams(vmem_limit_bytes=VMEM),
        name="halve",
    )(*operands, *small.terms)


def launch(lead, sums, small, *others):
    lead, others, halves = lax.optimization_barrier((lead, others, halve(sums, small)))
    for i, item in enumerate(sums):
        item.send(halves[2 * i], halves[2 * i + 1])
    small.send(halves[-1])
    return (lead, *others)


def settle(lead, sums, small):
    everything = sums + [small]
    lead, terms = lax.optimization_barrier((lead, [item.terms for item in everything]))
    for item, arrays in zip(everything, terms):
        item.terms = list(arrays)
    return lead


def collect_kernel(groups, *refs):
    at = 0
    for out, count in zip(refs[-len(groups) :], groups):
        parts = [
            refs[at + 2 * i][...].astype(f32) + refs[at + 2 * i + 1][...].astype(f32)
            for i in range(count)
        ]
        at += 2 * count
        height = parts[0].shape[0]
        for i, part in enumerate(parts):
            out[i * height : (i + 1) * height, :] = part


def collect(groups):
    operands = [term for group in groups for item in group for term in item.terms]
    return pl.pallas_call(
        functools.partial(collect_kernel, [len(group) for group in groups]),
        out_shape=[
            jax.ShapeDtypeStruct(
                (sum(item.terms[0].shape[0] for item in group), group[0].terms[0].shape[1]), f32
            )
            for group in groups
        ],
        compiler_params=pltpu.CompilerParams(vmem_limit_bytes=VMEM),
        name="collect",
    )(*operands)


def read_small(ref, at, rows):
    parts = [ref[at + i * rows : at + (i + 1) * rows, :].astype(f32) for i in range(3)]
    return parts[0] + parts[1] + parts[2]


def joint_kernel(plan, last, *refs):
    count, buffers, from_at, small_from, to_at, small_to, rows = plan
    arrays, refs = refs[:count], refs[count:]
    received, refs = refs[:buffers], refs[buffers:]
    small, refs = refs[0], refs[1:]
    if small_from is None:
        total = small[...] + refs[0][...]
        refs = refs[1:]
    else:
        total = small[...] + read_small(received[small_from[0]], small_from[1], rows)
    if last:
        out, small_out = refs
        for i in range(count):
            which, at = from_at[i]
            height = arrays[i].shape[0]
            part = received[which][at : at + height, :].astype(f32)
            out[i * height : (i + 1) * height, :] = arrays[i][...].astype(f32) + part
        small_out[...] = total
        return
    outs, sent, small_out = refs[:count], refs[count:-1], refs[-1]
    for i in range(count):
        which, at = from_at[i]
        height = arrays[i].shape[0] // 2
        for half in range(2):
            here = slice(half * height, (half + 1) * height)
            there = slice(at + half * height, at + (half + 1) * height)
            part = arrays[i][here, :].astype(f32) + received[which][there, :].astype(f32)
            if half:
                which_out, at_out = to_at[i]
                sent[which_out][at_out : at_out + height, :] = part.astype(bf16)
            else:
                outs[i][...] = part.astype(bf16)
    small_out[...] = total
    which_out, at_out = small_to
    for part in split_three(total):
        sent[which_out][at_out : at_out + rows, :] = part.astype(bf16)
        at_out += rows


class Joint:
    def __init__(self, halves, orders, small):
        self.arrays = [kept for kept, _ in halves]
        self.received = [swap(given, "wide", 0) for _, given in halves]
        self.from_at = [(i, 0) for i in range(len(halves))]
        self.orders = [list(order) for order in orders]
        self.small, self.small_from = small, None
        self.extra = [swap(small, "wide", 0)]

    def call(self, plan, last, shapes):
        return pl.pallas_call(
            functools.partial(joint_kernel, plan, last),
            out_shape=shapes,
            compiler_params=pltpu.CompilerParams(vmem_limit_bytes=VMEM),
            name="joint",
        )(*self.arrays, *self.received, self.small, *self.extra)

    def plan(self, to_at, small_to):
        buffers, rows = len(self.received), self.small.shape[0]
        count = len(self.arrays)
        return count, buffers, self.from_at, self.small_from, to_at, small_to, rows

    def step(self, lead, *others):
        bits, heights, to_at = [], [], []
        width = self.arrays[0].shape[1]
        for array, order in zip(self.arrays, self.orders):
            bit = order.pop(0)
            if bit not in bits:
                bits.append(bit)
                heights.append(0)
            which = bits.index(bit)
            to_at.append((which, heights[which]))
            heights[which] += array.shape[0] // 2
        small_to = (0, heights[0])
        heights[0] += 3 * self.small.shape[0]
        shapes = [
            jax.ShapeDtypeStruct((array.shape[0] // 2, width), bf16) for array in self.arrays
        ]
        shapes += [jax.ShapeDtypeStruct((height, width), bf16) for height in heights]
        shapes += [jax.ShapeDtypeStruct(self.small.shape, f32)]
        outs = self.call(self.plan(to_at, small_to), False, shapes)
        lead, others, outs = lax.optimization_barrier((lead, others, outs))
        count = len(self.arrays)
        self.arrays, sent, self.small = outs[:count], outs[count:-1], outs[-1]
        self.received = [swap(item, *bit) for item, bit in zip(sent, bits)]
        self.from_at, self.small_from, self.extra = to_at, small_to, []
        return (lead, *others)

    def result(self):
        height = sum(array.shape[0] for array in self.arrays)
        shapes = [
            jax.ShapeDtypeStruct((height, self.arrays[0].shape[1]), f32),
            jax.ShapeDtypeStruct(self.small.shape, f32),
        ]
        return self.call(self.plan([], None), True, shapes)


def angles(positions):
    half = HEAD_DIM // 2
    freqs = jnp.power(10000.0, -jnp.arange(half, dtype=f32) / half)
    theta = freqs[:, None] * positions.astype(f32)[None, :]
    return jnp.cos(theta), jnp.sin(theta)


def axis_bits(axis):
    return [(axis, position) for position in range(lax.axis_size(axis).bit_length() - 1)]


def body(
    inputs,
    cotangent,
    lengths,
    w_qkv,
    b_qkv,
    w_out,
    b_out,
    w_up,
    b_up,
    w_down,
    b_down,
    gain_one,
    shift_one,
    gain_two,
    shift_two,
    gain_three,
    shift_three,
    gain_four,
    shift_four,
):
    group = inputs.shape[3]
    width = inputs.shape[4]
    parts = lax.axis_size("narrow")
    place = lax.axis_index("narrow")
    cores = lax.axis_size("wide")
    others = parts - 1
    rows = 2 * group
    offsets = jnp.arange(group, dtype=jnp.int32)

    def row(vector):
        return vector[None, :]

    def positions(owners):
        starts = jnp.stack([owners, 2 * parts - 1 - owners], axis=1).reshape(-1) * group
        return (starts[:, None] + offsets[None]).reshape(-1)

    def joined(items):
        return jnp.concatenate(items, axis=0) if len(items) > 1 else items[0]

    tokens = inputs.reshape(rows, width)
    far_tokens = joined(
        [
            lax.ppermute(tokens, "narrow", [((n + shift) % parts, n) for n in range(parts)])
            for shift in range(1, parts)
        ]
    )
    other = (place + 1 + jnp.arange(others, dtype=jnp.int32)) % parts
    early_at = place * group
    late_at = (2 * parts - 1 - place) * group
    info = jnp.stack([place, lengths[0], early_at, late_at]).astype(jnp.int32)
    marks = jnp.stack([lax.axis_index("wide"), place]).astype(jnp.int32)
    turns = angles(positions(place[None]))
    turns_far = angles(positions(other))

    norm_one = [row(gain_one), row(shift_one)]
    normed, qT, kT, vT = project(tokens, w_qkv, row(b_qkv), *norm_one, *turns, (0, 1, 2))
    state, kept_own, flags_own = attend_local(info, qT, kT, vT, group)
    normed_far, kT_far, vT_far = project(
        far_tokens, w_qkv, row(b_qkv), *norm_one, *turns_far, (1, 2)
    )
    oT, lse, kept_far, flags_far = attend_remote(
        info, qT, kT_far, vT_far, state, group, parts
    )

    blocks = block_call(
        oT,
        tokens,
        cotangent.reshape(rows, width),
        [w_out, w_up, w_down],
        [row(item) for item in (b_out, b_up, b_down)]
        + [row(item) for item in (gain_two, shift_two, gain_three, shift_three)]
        + [row(item) for item in (gain_four, shift_four)],
    )
    result, d_middle, hidden, d_outer, normed_two, d_inner, d_branch, doT, small, small_up = blocks

    wide_bits = axis_bits("wide")
    narrow_bits = axis_bits("narrow")
    first_order = wide_bits[1:2] + narrow_bits + wide_bits[2:]
    second_order = narrow_bits + wide_bits[1:]
    third_order = narrow_bits + wide_bits[2:3] + wide_bits[1:2] + wide_bits[3:]
    fourth_order = wide_bits[2:3] + wide_bits[1:2] + narrow_bits + wide_bits[3:]
    small_order = wide_bits[:1] + first_order

    def outer(left, right, right_dim, order):
        return Halving(outer_halves(marks, left, right, right_dim, cores, parts, order), order)

    sum_up = outer(d_inner, normed_two, 0, first_order)
    sum_down = outer(d_outer, hidden, 0, second_order)
    sum_out = outer(d_branch, oT, 1, first_order)
    flat = jnp.concatenate([small.reshape(-1), small_up.reshape(-1)])
    early = Adding(flat.reshape(-1, PAIR), small_order)
    sums = [sum_down, sum_up, sum_out]

    heads = width // PAIR
    portions = 2 if heads % 2 == 0 else 1
    count = heads // portions
    far = []
    for portion in range(portions):
        (doT,) = launch(doT, sums, early)
        far = back_remote(
            info,
            flags_far,
            [qT, doT, oT, lse],
            turns_far,
            [kT_far, vT_far],
            kept_far,
            group,
            parts,
            portion * count,
            count,
            far,
        )
    dq_far, d_far = far
    d_back = unproject(d_far, w_qkv, (1, 2), 0, others * rows)
    d_mixed = []
    for portion in range(portions):
        doT, d_back = launch(doT, sums, early, d_back)
        if not portion:
            returned = [
                lax.ppermute(
                    d_back[j * rows : (j + 1) * rows] if others > 1 else d_back,
                    "narrow",
                    [(n, (n + j + 1) % parts) for n in range(parts)],
                )
                for j in range(others)
            ]
        d_mixed = [
            back_local(
                info,
                flags_own,
                [qT, doT, oT, lse],
                turns,
                [kT, vT],
                dq_far,
                kept_own,
                group,
                portion * count,
                count,
                d_mixed,
            )
        ]
    d_mixed = d_mixed[0]
    while early.order:
        (d_mixed,) = launch(d_mixed, sums, early)
    d_mixed = settle(d_mixed, sums, early)
    d_mixed, returned = lax.optimization_barrier((d_mixed, returned))
    if others > 1:
        returned = [functools.reduce(jnp.add, [item.astype(f32) for item in returned])]

    orders = [first_order, third_order, fourth_order]
    pieces, bias, weighted = mixed_halves(
        marks,
        d_mixed.reshape(3 * width, rows),
        d_far.reshape(3 * width, -1),
        normed,
        normed_far,
        w_qkv,
        cores,
        parts,
        orders,
    )
    part_shift = weighted[1]
    part_gain = (weighted[0] - shift_one * part_shift) / gain_one
    flat = jnp.concatenate(
        [bias.reshape(-1), part_gain, part_shift, jnp.zeros((11 * width,), f32)]
    )
    tail = Joint(pieces, orders, flat.reshape(16, width))
    (d_mixed,) = tail.step(d_mixed)
    d_tokens = []
    for i in range(2):
        finish = (returned[0], tokens, d_middle, row(gain_one))
        d_tokens = [
            unproject(d_mixed, w_qkv, (0, 1, 2), i * group, group, finish, d_tokens)
        ]
        if tail.orders[0]:
            d_mixed, d_tokens[0] = tail.step(d_mixed, d_tokens[0])
    while tail.orders[0]:
        d_tokens[0], *terms = tail.step(d_tokens[0], *[item.terms for item in sums])
        for item, arrays in zip(sums, terms):
            item.terms = list(arrays)

    sum_w_down, sum_w_up, sum_w_out = collect([[item] for item in sums])
    sum_w_qkv, late_small = tail.result()
    late_small = late_small.reshape(-1)[: 5 * width]
    early_small = (early.terms[0] + early.terms[1]).reshape(-1)
    small = early_small[: 8 * width].reshape(8, width)
    small_up = early_small[8 * width :]
    shape = inputs.shape
    return (
        result.reshape(shape),
        d_tokens[0].reshape(shape),
        sum_w_qkv.T,
        sum_w_out.T,
        sum_w_up.T,
        sum_w_down.T,
        late_small[: 3 * width],
        small[7],
        small_up,
        small[2],
        late_small[3 * width : 4 * width],
        late_small[4 * width :],
        small[5],
        small[6],
        small[3],
        small[4],
        small[0],
        small[1],
    )


def solution(mesh):
    tokens = P("wide", None, "narrow", None, None)
    columns = P(None, ("wide", "narrow"))
    in_specs = (tokens, tokens, P("wide")) + (P(),) * 16
    out_specs = (tokens, tokens) + (columns,) * 4 + (P(),) * 12
    return jax.shard_map(body, mesh=mesh, in_specs=in_specs, out_specs=out_specs, check_vma=False)
```

```python
import functools

import jax
import jax.numpy as jnp
from jax import lax
from jax.experimental import pallas as pl
from jax.experimental.pallas import tpu as pltpu
from jax.sharding import PartitionSpec as P

HEAD_DIM = 64
PAIR = 2 * HEAD_DIM
EPS = 1e-05
LOG2E = 1.4426950408889634
LN2 = 0.6931471805599453
NEG = -1e30
REACH = 60.0
VMEM = 62 * 1024 * 1024
SPAN = 1024

f32 = jnp.float32
bf16 = jnp.bfloat16


def dot(left, right, left_dim, right_dim):
    return lax.dot_general(
        left, right, (((left_dim,), (right_dim,)), ((), ())), preferred_element_type=f32
    )


def bounded(qT, kT):
    worst = None
    for h in range(2):
        rows = slice(HEAD_DIM * h, HEAD_DIM * (h + 1))
        norms = []
        for item in (qT, kT):
            values = item[rows, :].astype(f32)
            norms.append(jnp.max(jnp.sum(values * values, axis=0, keepdims=True)))
        both = norms[0] * norms[1]
        worst = both if worst is None else jnp.maximum(worst, both)
    return worst <= REACH * REACH


def fwd_chunk(fast, q0, k0, q_n, k_n, limit, store, qT, kT, vT, m_ref, l_ref, acc):
    queries = pl.ds(q0, q_n)
    strip = min(256, k_n)
    for h in range(2):
        rows = slice(HEAD_DIM * h, HEAD_DIM * (h + 1))
        old = m_ref[h : h + 1, queries]
        new = jnp.zeros_like(old) if fast else old
        strips = []
        for j in range(k_n // strip):
            keys = pl.ds(k0 + j * strip, strip)
            scores = dot(kT[rows, keys], qT[rows, queries], 0, 0)
            if limit is not None:
                key_at = lax.broadcasted_iota(jnp.int32, (strip, q_n), 0)
                scores = jnp.where(key_at < limit - j * strip, scores, NEG)
            strips.append(scores)
            if not fast:
                new = jnp.maximum(new, jnp.max(scores, axis=0, keepdims=True))
        factor = jnp.exp2(old - new)
        total = l_ref[h : h + 1, queries] * factor
        value = acc[rows, queries] * factor
        for j in range(k_n // strip):
            keys = pl.ds(k0 + j * strip, strip)
            weights = jnp.exp2(strips[j] if fast else strips[j] - new)
            total = total + jnp.sum(weights, axis=0, keepdims=True)
            weights = weights.astype(bf16)
            if fast:
                store(h, j, weights)
            value = value + dot(vT[rows, keys], weights, 1, 0)
        m_ref[h : h + 1, queries] = new
        l_ref[h : h + 1, queries] = total
        acc[rows, queries] = value


def pad_left(values, count):
    if not count:
        return values
    return jnp.concatenate([jnp.zeros((values.shape[0], count), f32), values], axis=1)


def pad_right(values, count):
    if not count:
        return values
    return jnp.concatenate([values, jnp.zeros((values.shape[0], count), f32)], axis=1)


def fwd_diagonal(fast, base, group, limit, store, qT, kT, vT, m_ref, l_ref, acc):
    strip = min(256, group)
    count = group // strip
    for h in range(2):
        rows = slice(HEAD_DIM * h, HEAD_DIM * (h + 1))
        strips = []
        for j in range(count):
            wide = group - j * strip
            keys, queries = pl.ds(base + j * strip, strip), pl.ds(base + j * strip, wide)
            scores = dot(kT[rows, keys], qT[rows, queries], 0, 0)
            key_at = lax.broadcasted_iota(jnp.int32, scores.shape, 0)
            query_at = lax.broadcasted_iota(jnp.int32, scores.shape, 1)
            scores = jnp.where(key_at <= query_at, scores, NEG)
            if limit is not None:
                scores = jnp.where(key_at < limit - j * strip, scores, NEG)
            strips.append(scores)
        peaks = []
        for g in range(0 if fast else count):
            peak = None
            for j in range(g + 1):
                part = strips[j][:, (g - j) * strip : (g - j + 1) * strip]
                part = jnp.max(part, axis=0, keepdims=True)
                peak = part if peak is None else jnp.maximum(peak, part)
            peaks.append(peak)
        if fast:
            peak = jnp.zeros((1, group), f32)
        else:
            peak = jnp.concatenate(peaks, axis=1) if count > 1 else peaks[0]
        total, value = None, None
        for j in range(count):
            keys = pl.ds(base + j * strip, strip)
            weights = jnp.exp2(strips[j] if fast else strips[j] - peak[:, j * strip :])
            part = pad_left(jnp.sum(weights, axis=0, keepdims=True), j * strip)
            weights = weights.astype(bf16)
            if fast:
                store(h, j, weights)
            term = pad_left(dot(vT[rows, keys], weights, 1, 0), j * strip)
            total = part if total is None else total + part
            value = term if value is None else value + term
        queries = pl.ds(base, group)
        m_ref[h : h + 1, queries] = peak
        l_ref[h : h + 1, queries] = total
        acc[rows, queries] = value


def triangle_slot(i, j, group):
    strip = min(256, group)
    count = group // strip
    row = jnp.where(i == 0, j, count - j) * strip
    column = jnp.where(i == 0, j * strip, 0)
    wide = group - j * strip
    return (
        pl.ds(pl.multiple_of(row, strip), strip),
        pl.ds(pl.multiple_of(column, strip), wide),
    )


def square_slot(j, group):
    strip = min(256, group)
    return pl.ds(group + strip + j * strip, strip), slice(None)


def fwd_local_kernel(group, info, qT, kT, vT, acc, m_ref, l_ref, kept, flags):
    length = info[1]
    m_ref[...] = jnp.full(m_ref.shape, NEG, f32)
    l_ref[...] = jnp.zeros(l_ref.shape, f32)
    acc[...] = jnp.zeros(acc.shape, f32)
    refs = (qT, kT, vT, m_ref.at[0], l_ref.at[0], acc)

    def walk(fast):
        def own(i, carry):
            base = pl.multiple_of(i * group, group)
            start = info[2 + i]

            def store(h, j, weights):
                rows, columns = triangle_slot(i, j, group)
                kept[h, rows, columns] = weights

            @pl.when(start + group <= length)
            def _():
                fwd_diagonal(fast, base, group, None, store, *refs)

            @pl.when((start < length) & (start + group > length))
            def _():
                fwd_diagonal(fast, base, group, length - start, store, *refs)

            return carry

        lax.fori_loop(0, 2, own, 0)
        early = info[2]

        def store(h, j, weights):
            rows, columns = square_slot(j, group)
            kept[h, rows, columns] = weights

        @pl.when(early + group <= length)
        def _():
            fwd_chunk(fast, group, 0, group, group, None, store, *refs)

        @pl.when((early < length) & (early + group > length))
        def _():
            fwd_chunk(fast, group, 0, group, group, length - early, store, *refs)

    small = bounded(qT, kT)
    flags[pl.program_id(0)] = small.astype(jnp.int32)
    pl.when(small)(functools.partial(walk, True))
    pl.when(jnp.logical_not(small))(functools.partial(walk, False))


def remote_steps(group, parts, info, full, partial):
    place, length = info[0], info[1]

    def visit(i, carry):
        j, turn_at = i // 3, lax.rem(i, 3)
        other = lax.rem(place + 1 + j, parts)
        late_key = turn_at == 2
        block = jnp.where(late_key, 2 * parts - 1 - other, other)
        before = (other < place).astype(jnp.int32)
        wanted = jnp.where(turn_at == 0, before, jnp.where(late_key, 1 - before, 1)) == 1
        q0 = pl.multiple_of(jnp.where(turn_at == 0, 0, group), group)
        k0 = pl.multiple_of((2 * j + jnp.where(late_key, 1, 0)) * group, group)
        slot = pl.multiple_of((2 * j + turn_at - (1 - before)) * group, group)
        start = block * group

        @pl.when(wanted & (start + group <= length))
        def _():
            full(q0, k0, slot)

        @pl.when(wanted & (start < length) & (start + group > length))
        def _():
            partial(q0, k0, slot, length - start)

        return carry

    lax.fori_loop(0, 3 * (parts - 1), visit, 0)


def fwd_remote_kernel(
    group, parts, info, qT, kT, vT, acc_in, m_in, l_in, out, lse, kept, flags, acc, m_ref, l_ref
):
    acc[...] = acc_in[...]
    m_ref[...] = m_in[0]
    l_ref[...] = l_in[0]
    refs = (qT, kT, vT, m_ref, l_ref, acc)
    strip = min(256, group)

    def walk(fast):
        def partial(q0, k0, slot, limit):
            def store(h, j, weights):
                kept[h, pl.ds(pl.multiple_of(slot + j * strip, strip), strip), :] = weights

            fwd_chunk(fast, q0, k0, group, group, limit, store, *refs)

        def full(q0, k0, slot):
            partial(q0, k0, slot, None)

        remote_steps(group, parts, info, full, partial)

    small = bounded(qT, kT) & (jnp.max(m_in[...]) <= 0.0)
    flags[pl.program_id(0)] = small.astype(jnp.int32)
    pl.when(small)(functools.partial(walk, True))
    pl.when(jnp.logical_not(small))(functools.partial(walk, False))
    for h in range(2):
        rows = slice(HEAD_DIM * h, HEAD_DIM * (h + 1))
        total = l_ref[h : h + 1, :]
        out[rows, :] = (acc[rows, :] / total).astype(bf16)
        lse[0, h : h + 1, :] = m_ref[h : h + 1, :] + jnp.log2(total)


def split_three(values):
    high = values.astype(bf16).astype(f32)
    rest = values - high
    middle = rest.astype(bf16).astype(f32)
    low = (rest - middle).astype(bf16).astype(f32)
    return [high, middle, low]


def bwd_prepare(qT, kT, vT, doT, oT, lse, qa, da, ka, va):
    n_q, n_k = qT.shape[1], ka.shape[2]
    extra = qa.shape[1] - HEAD_DIM
    pad = jnp.zeros((extra - 3, n_q), f32)
    row_at = lax.broadcasted_iota(jnp.int32, (extra, n_k), 0)
    tail = jnp.where(row_at < 3, 1.0, 0.0).astype(bf16)
    for h in range(2):
        rows = slice(HEAD_DIM * h, HEAD_DIM * (h + 1))
        grad = doT[rows, :].astype(f32)
        delta = jnp.sum(grad * oT[rows, :].astype(f32), axis=0, keepdims=True)
        qa[h, :HEAD_DIM, :] = qT[rows, :]
        parts = split_three(-lse[0, h : h + 1, :]) + [pad]
        qa[h, HEAD_DIM:, :] = jnp.concatenate(parts, axis=0).astype(bf16)
        da[h, :HEAD_DIM, :] = doT[rows, :]
        parts = split_three(-delta) + [pad]
        da[h, HEAD_DIM:, :] = jnp.concatenate(parts, axis=0).astype(bf16)
        ka[h, :HEAD_DIM, :] = kT[rows, :]
        va[h, :HEAD_DIM, :] = vT[rows, :]
        ka[h, HEAD_DIM:, :] = tail
        va[h, HEAD_DIM:, :] = tail


def bwd_chunk(q0, k0, q_n, k_n, limit, qT, doT, qa, da, ka, va, dq, dk, dv):
    queries, keys = pl.ds(q0, q_n), pl.ds(k0, k_n)
    for h in range(2):
        rows = slice(HEAD_DIM * h, HEAD_DIM * (h + 1))
        probs = jnp.exp2(dot(qa[h, :, queries], ka[h, :, keys], 0, 0))
        if limit is not None:
            key_at = lax.broadcasted_iota(jnp.int32, (q_n, k_n), 1)
            probs = jnp.where(key_at < limit, probs, 0.0)
        d_probs = dot(da[h, :, queries], va[h, :, keys], 0, 0)
        d_scores = (probs * d_probs).astype(bf16)
        dv[rows, keys] += dot(doT[rows, queries], probs.astype(bf16), 1, 0)
        dk[rows, keys] += dot(qT[rows, queries], d_scores, 1, 0)
        dq[rows, queries] += dot(ka[h, :HEAD_DIM, keys], d_scores, 1, 1)


def bwd_diagonal(base, group, limit, qT, doT, qa, da, ka, va, dq, dk, dv):
    strip = min(256, group)
    count = group // strip
    for h in range(2):
        rows = slice(HEAD_DIM * h, HEAD_DIM * (h + 1))
        d_keys, d_values, d_queries = None, None, []
        for j in range(count):
            wide = (j + 1) * strip
            queries, keys = pl.ds(base + j * strip, strip), pl.ds(base, wide)
            probs = jnp.exp2(dot(qa[h, :, queries], ka[h, :, keys], 0, 0))
            query_at = lax.broadcasted_iota(jnp.int32, probs.shape, 0)
            key_at = lax.broadcasted_iota(jnp.int32, probs.shape, 1)
            probs = jnp.where(key_at <= query_at + j * strip, probs, 0.0)
            if limit is not None:
                probs = jnp.where(key_at < limit, probs, 0.0)
            d_probs = dot(da[h, :, queries], va[h, :, keys], 0, 0)
            d_scores = (probs * d_probs).astype(bf16)
            value = pad_right(dot(doT[rows, queries], probs.astype(bf16), 1, 0), group - wide)
            key = pad_right(dot(qT[rows, queries], d_scores, 1, 0), group - wide)
            d_values = value if d_values is None else d_values + value
            d_keys = key if d_keys is None else d_keys + key
            d_queries.append(dot(ka[h, :HEAD_DIM, keys], d_scores, 1, 1))
        here = pl.ds(base, group)
        dq[rows, here] += jnp.concatenate(d_queries, axis=1) if count > 1 else d_queries[0]
        dk[rows, here] += d_keys
        dv[rows, here] += d_values


def stored_prepare(doT, oT, lse, scaled, delta):
    for h in range(2):
        rows = slice(HEAD_DIM * h, HEAD_DIM * (h + 1))
        grad = (doT[rows, :].astype(f32) * jnp.exp2(-lse[0, h : h + 1, :])).astype(bf16)
        scaled[rows, :] = grad
        delta[h : h + 1, :] = column_sum(grad.astype(f32) * oT[rows, :].astype(f32))


def stored_chunk(h, weights, queries, keys, qT, kT, vT, scaled, delta, dq, dk, dv):
    rows = slice(HEAD_DIM * h, HEAD_DIM * (h + 1))
    d_probs = dot(vT[rows, keys], scaled[rows, queries], 0, 0)
    d_scores = weights.astype(f32) * (d_probs - delta[h : h + 1, queries])
    d_scores = d_scores.astype(bf16)
    dv[rows, keys] += dot(scaled[rows, queries], weights, 1, 1)
    dk[rows, keys] += dot(qT[rows, queries], d_scores, 1, 1)
    dq[rows, queries] += dot(kT[rows, keys], d_scores, 1, 0)


def turn_back(values, cosine, sine):
    half = HEAD_DIM // 2
    first, second = values[:half], values[half:]
    return jnp.concatenate(
        [first * cosine + second * sine, second * cosine - first * sine], axis=0
    )


def bwd_remote_kernel(
    group, parts, first, info, flags, qT, doT, oT, lse, cosine, sine, kT, vT, kept, *rest
):
    dq, dkv, qa, da, ka, va, dk, dv, scaled, delta = rest[-10:]
    dq[...] = jnp.zeros(dq.shape, f32)
    dk[...] = jnp.zeros(dk.shape, f32)
    dv[...] = jnp.zeros(dv.shape, f32)
    fast = flags[first + pl.program_id(0)] == 1

    @pl.when(fast)
    def _():
        stored_prepare(doT, oT, lse, scaled, delta)

        def full(q0, k0, slot):
            for h in range(2):
                weights = kept[h, pl.ds(slot, group), :]
                queries, keys = pl.ds(q0, group), pl.ds(k0, group)
                stored_chunk(h, weights, queries, keys, qT, kT, vT, scaled, delta, dq, dk, dv)

        def partial(q0, k0, slot, limit):
            full(q0, k0, slot)

        remote_steps(group, parts, info, full, partial)

    @pl.when(jnp.logical_not(fast))
    def _():
        bwd_prepare(qT, kT, vT, doT, oT, lse, qa, da, ka, va)
        refs = (qT, doT, qa, da, ka, va, dq, dk, dv)

        def full(q0, k0, slot):
            bwd_chunk(q0, k0, group, group, None, *refs)

        def partial(q0, k0, slot, limit):
            bwd_chunk(q0, k0, group, group, limit, *refs)

        remote_steps(group, parts, info, full, partial)

    for h in range(2):
        rows = slice(HEAD_DIM * h, HEAD_DIM * (h + 1))
        dkv[1, rows, :] = turn_back(dk[rows, :] * LN2, cosine[...], sine[...]).astype(bf16)
    dkv[0] = jnp.zeros(dv.shape, bf16)
    dkv[2] = dv[...].astype(bf16)


def bwd_local_kernel(
    group, first, info, flags, qT, doT, oT, lse, cosine, sine, kT, vT, dq_in, kept, *rest
):
    dqkv, qa, da, ka, va, dk, dv, scaled, delta, dq = rest[-10:]
    length = info[1]
    dq[...] = dq_in[...]
    dk[...] = jnp.zeros(dk.shape, f32)
    dv[...] = jnp.zeros(dv.shape, f32)
    early = info[2]
    strip = min(256, group)
    fast = flags[first + pl.program_id(0)] == 1

    @pl.when(fast)
    def _():
        stored_prepare(doT, oT, lse, scaled, delta)
        refs = (qT, kT, vT, scaled, delta, dq, dk, dv)

        def own(i, carry):
            base = pl.multiple_of(i * group, group)

            @pl.when(info[2 + i] < length)
            def _():
                for h in range(2):
                    for j in range(group // strip):
                        rows, columns = triangle_slot(i, j, group)
                        queries = pl.ds(base + j * strip, group - j * strip)
                        keys = pl.ds(base + j * strip, strip)
                        stored_chunk(h, kept[h, rows, columns], queries, keys, *refs)

            return carry

        lax.fori_loop(0, 2, own, 0)

        @pl.when(early < length)
        def _():
            for h in range(2):
                weights = kept[h, group + strip :, :]
                stored_chunk(h, weights, pl.ds(group, group), pl.ds(0, group), *refs)

    @pl.when(jnp.logical_not(fast))
    def _():
        bwd_prepare(qT, kT, vT, doT, oT, lse, qa, da, ka, va)
        refs = (qT, doT, qa, da, ka, va, dq, dk, dv)

        def own(i, carry):
            base = pl.multiple_of(i * group, group)
            start = info[2 + i]

            @pl.when(start < length)
            def _():
                bwd_diagonal(base, group, length - start, *refs)

            return carry

        lax.fori_loop(0, 2, own, 0)

        @pl.when(early < length)
        def _():
            bwd_chunk(group, 0, group, group, length - early, *refs)

    for h in range(2):
        rows = slice(HEAD_DIM * h, HEAD_DIM * (h + 1))
        d_query = dq[rows, :] * 0.125
        dqkv[0, rows, :] = turn_back(d_query, cosine[...], sine[...]).astype(bf16)
        dqkv[1, rows, :] = turn_back(dk[rows, :] * LN2, cosine[...], sine[...]).astype(bf16)
    dqkv[2] = dv[...].astype(bf16)


def rows_of(count, first=0):
    return pl.BlockSpec((PAIR, count), lambda i, *info: (first + i, 0))


def stats_of(count, first=0):
    return pl.BlockSpec((1, 2, count), lambda i, *info: (first + i, 0, 0))


def planes_of(planes, count, first=0):
    return pl.BlockSpec((planes, PAIR, count), lambda i, *info: (0, first + i, 0))


def kept_of(rows, group, first=0):
    return pl.BlockSpec((2, rows, group), lambda i, *info: (first + i, 0, 0))


def scalars():
    return pl.BlockSpec(memory_space=pltpu.SMEM)


def whole(shape):
    return pl.BlockSpec(shape, lambda i, *info: (0,) * len(shape))


def attention_call(kernel, pairs, in_specs, out_specs, out_shape, scratch, flops, name, alias={}, prefetch=1):
    return pl.pallas_call(
        kernel,
        grid_spec=pltpu.PrefetchScalarGridSpec(
            num_scalar_prefetch=prefetch,
            grid=(pairs,),
            in_specs=in_specs,
            out_specs=out_specs,
            scratch_shapes=scratch,
        ),
        out_shape=out_shape,
        input_output_aliases=alias,
        compiler_params=pltpu.CompilerParams(vmem_limit_bytes=VMEM),
        cost_estimate=pl.CostEstimate(
            flops=int(flops), bytes_accessed=1 << 25, transcendentals=0
        ),
        name=name,
    )


def attend_local(info, qT, kT, vT, group):
    width, n_q = qT.shape
    pairs = width // PAIR
    kept_rows = 2 * group + min(256, group)
    call = attention_call(
        functools.partial(fwd_local_kernel, group),
        pairs,
        [rows_of(n_q)] * 3,
        [rows_of(n_q), stats_of(n_q), stats_of(n_q), kept_of(kept_rows, group), scalars()],
        [
            jax.ShapeDtypeStruct((width, n_q), f32),
            jax.ShapeDtypeStruct((pairs, 2, n_q), f32),
            jax.ShapeDtypeStruct((pairs, 2, n_q), f32),
            jax.ShapeDtypeStruct((2 * pairs, kept_rows, group), bf16),
            jax.ShapeDtypeStruct((pairs,), jnp.int32),
        ],
        [],
        4 * width * 2 * group * group * 4,
        "attend_local",
    )
    *state, kept, flags = call(info, qT, kT, vT)
    return state, kept, flags


def attend_remote(info, qT, kT, vT, state, group, parts):
    width, n_q = qT.shape
    n_k = kT.shape[1]
    pairs = width // PAIR
    call = attention_call(
        functools.partial(fwd_remote_kernel, group, parts),
        pairs,
        [rows_of(n_q), rows_of(n_k), rows_of(n_k), rows_of(n_q), stats_of(n_q), stats_of(n_q)],
        [rows_of(n_q), stats_of(n_q), kept_of(n_k, group), scalars()],
        [
            jax.ShapeDtypeStruct((width, n_q), bf16),
            jax.ShapeDtypeStruct((pairs, 2, n_q), f32),
            jax.ShapeDtypeStruct((2 * pairs, n_k, group), bf16),
            jax.ShapeDtypeStruct((pairs,), jnp.int32),
        ],
        [pltpu.VMEM((PAIR, n_q), f32)] + [pltpu.VMEM((2, n_q), f32)] * 2,
        4 * width * 2 * group * group * 4,
        "attend_remote",
    )
    return call(info, qT, kT, vT, *state)


def back_scratch(n_q, n_k):
    rows = HEAD_DIM + 16
    return (
        [pltpu.VMEM((2, rows, n_q), bf16)] * 2
        + [pltpu.VMEM((2, rows, n_k), bf16)] * 2
        + [pltpu.VMEM((PAIR, n_k), f32)] * 2
        + [pltpu.VMEM((PAIR, n_q), bf16), pltpu.VMEM((2, n_q), f32)]
    )


def back_remote(info, flags, operands, turns, keys, kept, group, parts, first, count, before):
    width, n_q = operands[0].shape
    n_k = keys[0].shape[1]
    half = HEAD_DIM // 2
    n_in = 2 + len(operands) + len(turns) + len(keys) + 1
    call = attention_call(
        functools.partial(bwd_remote_kernel, group, parts, first),
        count,
        [rows_of(n_q, first)] * 3
        + [stats_of(n_q, first)]
        + [whole((half, n_k))] * 2
        + [rows_of(n_k, first)] * 2
        + [kept_of(kept.shape[1], group, first)]
        + [pl.BlockSpec(memory_space=pl.ANY)] * len(before),
        [rows_of(n_q, first), planes_of(3, n_k, first)],
        [
            jax.ShapeDtypeStruct((width, n_q), f32),
            jax.ShapeDtypeStruct((3, width, n_k), bf16),
        ],
        back_scratch(n_q, n_k),
        10 * count * PAIR * 2 * group * group * 4,
        "back_remote",
        {n_in + i: i for i in range(len(before))},
        2,
    )
    return call(info, flags, *operands, *turns, *keys, kept, *before)


def back_local(info, flags, operands, turns, keys, dq, kept, group, first, count, before):
    width, n_q = operands[0].shape
    half = HEAD_DIM // 2
    n_in = 2 + len(operands) + len(turns) + len(keys) + 2
    call = attention_call(
        functools.partial(bwd_local_kernel, group, first),
        count,
        [rows_of(n_q, first)] * 3
        + [stats_of(n_q, first)]
        + [whole((half, n_q))] * 2
        + [rows_of(n_q, first)] * 3
        + [kept_of(kept.shape[1], group, first)]
        + [pl.BlockSpec(memory_space=pl.ANY)] * len(before),
        planes_of(3, n_q, first),
        jax.ShapeDtypeStruct((3, width, n_q), bf16),
        back_scratch(n_q, n_q) + [pltpu.VMEM((PAIR, n_q), f32)],
        10 * count * PAIR * 2 * group * group * 4,
        "back_local",
        {n_in + i: i for i in range(len(before))},
        2,
    )
    return call(info, flags, *operands, *turns, *keys, dq, kept, *before)


def normalize(values):
    centre = values - jnp.mean(values, axis=-1, keepdims=True)
    spread = jnp.mean(centre * centre, axis=-1, keepdims=True)
    rate = lax.rsqrt(spread + EPS)
    return centre * rate, rate


def norm_back(grad, unit, rate, gain):
    scaled = grad * gain
    first = jnp.mean(scaled, axis=-1, keepdims=True)
    second = jnp.mean(scaled * unit, axis=-1, keepdims=True)
    return rate * (scaled - first - unit * second)


GELU_A = 0.7978845608028654
GELU_B = 0.044715


def column_sum(values):
    return jnp.sum(values, axis=0, keepdims=True)


def block_kernel(
    span,
    oT,
    tokens,
    cotangent,
    w_out,
    w_up,
    w_down,
    b_out,
    b_up,
    b_down,
    gain_two,
    shift_two,
    gain_three,
    shift_three,
    gain_four,
    shift_four,
    result,
    d_middle_out,
    hidden_out,
    d_outer_out,
    normed_out,
    d_inner_out,
    d_branch_out,
    doT,
    small,
    small_up,
    slope,
):
    step = pl.program_id(0)

    @pl.when(step == 0)
    def _():
        small[...] = jnp.zeros(small.shape, f32)
        small_up[...] = jnp.zeros(small_up.shape, f32)

    wide = w_up.shape[1]
    branch = dot(oT[...], w_out[...], 0, 0) + b_out[...]
    unit_two, rate_two = normalize(branch)
    middle = tokens[...].astype(f32) + (unit_two * gain_two[...] + shift_two[...])
    unit_three, rate_three = normalize(middle)
    normed = (unit_three * gain_three[...] + shift_three[...]).astype(bf16)
    normed_out[...] = normed
    outer = None
    for c in range(wide // span):
        columns = slice(c * span, (c + 1) * span)
        inner = dot(normed, w_up[:, columns], 1, 0) + b_up[:, columns]
        square = inner * inner
        bend = jnp.tanh(inner * (GELU_A + (GELU_A * GELU_B) * square))
        half = 0.5 + 0.5 * bend
        hidden = (inner * half).astype(bf16)
        hidden_out[:, columns] = hidden
        slope[:, columns] = half + inner * (1.0 - bend * bend) * (
            0.5 * GELU_A + (1.5 * GELU_A * GELU_B) * square
        )
        term = dot(hidden, w_down[columns, :], 1, 0)
        outer = term if outer is None else outer + term
    unit_four, rate_four = normalize(outer + b_down[...])
    result[...] = (middle + (unit_four * gain_four[...] + shift_four[...])).astype(bf16)

    grad = cotangent[...].astype(f32)
    d_outer = norm_back(grad, unit_four, rate_four, gain_four[...]).astype(bf16)
    d_outer_out[...] = d_outer
    small[0:1, :] += column_sum(grad * unit_four)
    small[1:2, :] += column_sum(grad)
    small[2:3, :] += column_sum(d_outer.astype(f32))
    d_normed = None
    for c in range(wide // span):
        columns = slice(c * span, (c + 1) * span)
        d_hidden = dot(d_outer, w_down[columns, :], 1, 1)
        d_inner = (d_hidden * slope[:, columns]).astype(bf16)
        d_inner_out[:, columns] = d_inner
        small_up[:, columns] += column_sum(d_inner.astype(f32))
        term = dot(d_inner, w_up[:, columns], 1, 1)
        d_normed = term if d_normed is None else d_normed + term
    small[3:4, :] += column_sum(d_normed * unit_three)
    small[4:5, :] += column_sum(d_normed)
    d_middle = grad + norm_back(d_normed, unit_three, rate_three, gain_three[...])
    d_middle_out[...] = d_middle
    small[5:6, :] += column_sum(d_middle * unit_two)
    small[6:7, :] += column_sum(d_middle)
    d_branch = norm_back(d_middle, unit_two, rate_two, gain_two[...]).astype(bf16)
    d_branch_out[...] = d_branch
    small[7:8, :] += column_sum(d_branch.astype(f32))
    doT[...] = dot(w_out[...], d_branch, 1, 1).astype(bf16)


def block_call(oT, tokens, cotangent, weights, vectors):
    width, rows = oT.shape
    wide = weights[1].shape[1]
    step = min(256, rows)
    span = min(SPAN, wide)

    def lines(count):
        return pl.BlockSpec((step, count), lambda i: (i, 0))

    def fixed(shape):
        return pl.BlockSpec(shape, lambda i: (0, 0), pipeline_mode=pl.Buffered(1))

    def total(shape):
        return pl.BlockSpec(shape, lambda i: (0, 0))

    features = pl.BlockSpec((width, step), lambda i: (0, i))
    sizes = [width, width, wide, width, width, wide, width]
    kinds = [bf16, f32, bf16, bf16, bf16, bf16, bf16]
    return pl.pallas_call(
        functools.partial(block_kernel, span),
        grid=(rows // step,),
        in_specs=[features, lines(width), lines(width)]
        + [fixed(item.shape) for item in weights]
        + [fixed(item.shape) for item in vectors],
        out_specs=[lines(size) for size in sizes]
        + [features, total((8, width)), total((1, wide))],
        out_shape=[jax.ShapeDtypeStruct((rows, size), kind) for size, kind in zip(sizes, kinds)]
        + [
            jax.ShapeDtypeStruct((width, rows), bf16),
            jax.ShapeDtypeStruct((8, width), f32),
            jax.ShapeDtypeStruct((1, wide), f32),
        ],
        scratch_shapes=[pltpu.VMEM((step, wide), f32)],
        compiler_params=pltpu.CompilerParams(vmem_limit_bytes=VMEM),
        cost_estimate=pl.CostEstimate(
            flops=2 * 2 * rows * (width * width + 2 * width * wide),
            bytes_accessed=1 << 26,
            transcendentals=rows * wide,
        ),
        name="block",
    )(oT, tokens, cotangent, *weights, *vectors)


def turn(values, cosine, sine):
    half = HEAD_DIM // 2
    first, second = values[:half], values[half:]
    return jnp.concatenate(
        [first * cosine - second * sine, second * cosine + first * sine], axis=0
    )


def project_kernel(sections, tokens, w, b, gain, shift, cosine, sine, normed_out, *outs):
    unit, rate = normalize(tokens[...].astype(f32))
    normed = (unit * gain[...] + shift[...]).astype(bf16)
    normed_out[...] = normed
    width = tokens.shape[1]
    chunk = min(256, width)
    for section, out in zip(sections, outs):
        for c in range(width // chunk):
            at = section * width + c * chunk
            mixed = (dot(normed, w[:, at : at + chunk], 1, 0) + b[:, at : at + chunk]).T
            for h in range(chunk // HEAD_DIM):
                rows = slice(h * HEAD_DIM, (h + 1) * HEAD_DIM)
                place = slice(c * chunk + h * HEAD_DIM, c * chunk + (h + 1) * HEAD_DIM)
                value = mixed[rows]
                if section < 2:
                    value = turn(value, cosine[...], sine[...])
                if section == 0:
                    value = value * (0.125 * LOG2E)
                out[place, :] = value.astype(bf16)


def project(tokens, w, b, gain, shift, cosine, sine, sections):
    rows, width = tokens.shape
    step = min(512, rows)
    half = HEAD_DIM // 2

    def fixed(shape):
        return pl.BlockSpec(shape, lambda i: (0, 0), pipeline_mode=pl.Buffered(1))

    lines = pl.BlockSpec((step, width), lambda i: (i, 0))
    features = pl.BlockSpec((width, step), lambda i: (0, i))
    turns = pl.BlockSpec((half, step), lambda i: (0, i))
    return pl.pallas_call(
        functools.partial(project_kernel, sections),
        grid=(rows // step,),
        in_specs=[lines, fixed(w.shape), fixed(b.shape), fixed(gain.shape), fixed(shift.shape)]
        + [turns] * 2,
        out_specs=[lines] + [features] * len(sections),
        out_shape=[jax.ShapeDtypeStruct((rows, width), bf16)]
        + [jax.ShapeDtypeStruct((width, rows), bf16)] * len(sections),
        compiler_params=pltpu.CompilerParams(vmem_limit_bytes=VMEM),
        cost_estimate=pl.CostEstimate(
            flops=2 * rows * width * width * len(sections),
            bytes_accessed=1 << 24,
            transcendentals=0,
        ),
        name="project",
    )(tokens, w, b, gain, shift, cosine, sine)


def unproject_kernel(planes, finish, *refs):
    d_mixed, w, out = refs[: len(planes)], refs[len(planes)], refs[-1]
    width = w.shape[0]
    total = None
    for plane, ref in zip(planes, d_mixed):
        term = dot(ref[0], w[:, plane * width : (plane + 1) * width], 0, 1)
        total = term if total is None else total + term
    if not finish:
        out[...] = total.astype(bf16)
        return
    returned, tokens, d_middle, gain = refs[len(planes) + 1 : len(planes) + 5]
    total = total + returned[...].astype(f32)
    unit, rate = normalize(tokens[...].astype(f32))
    out[...] = (d_middle[...] + norm_back(total, unit, rate, gain[...])).astype(bf16)


def unproject(d_mixed, w, planes, start, count, finish=(), before=()):
    _, width, total = d_mixed.shape
    step = min(256, count)
    first = start // step

    def fixed(shape):
        return pl.BlockSpec(shape, lambda i: (0, 0), pipeline_mode=pl.Buffered(1))

    def plane_of(plane):
        return pl.BlockSpec((1, width, step), lambda i: (plane, 0, first + i))

    lines = pl.BlockSpec((step, width), lambda i: (i, 0))
    later = pl.BlockSpec((step, width), lambda i: (first + i, 0))
    specs = [later] * 3 + [fixed(finish[-1].shape)] if finish else []
    n_in = len(planes) + 1 + len(finish)
    return pl.pallas_call(
        functools.partial(unproject_kernel, planes, bool(finish)),
        grid=(count // step,),
        in_specs=[plane_of(plane) for plane in planes]
        + [fixed(w.shape)]
        + specs
        + [pl.BlockSpec(memory_space=pl.ANY)] * len(before),
        out_specs=later if finish else lines,
        out_shape=jax.ShapeDtypeStruct((total if finish else count, width), bf16),
        input_output_aliases={n_in + i: i for i in range(len(before))},
        compiler_params=pltpu.CompilerParams(vmem_limit_bytes=VMEM),
        cost_estimate=pl.CostEstimate(
            flops=2 * count * width * width * len(planes),
            bytes_accessed=1 << 24,
            transcendentals=0,
        ),
        name="unproject",
    )(*[d_mixed] * len(planes), w, *finish, *before)


def divide(total, run, levels, near, marks, orders, outs):
    bits = [("narrow", i) for i in range(near)] + [("wide", i) for i in range(levels + 1)]
    cut = run // len(orders)

    def write(core):
        for at in range(0, total.shape[0], run):
            number = at // run
            value = {}
            for place, (axis, position) in enumerate(bits):
                mine = (marks[1 if axis == "narrow" else 0] >> position) & 1
                value[axis, position] = mine ^ ((number >> place) & 1)
            other = core ^ ((number >> near) & 1)
            for i, order in enumerate(orders):
                index = tuple(value.get(bit, 0) for bit in order)
                part = total[at + i * cut : at + (i + 1) * cut]
                outs[2 * i + other][index] = part.astype(bf16)

    pl.when((marks[0] & 1) == 0)(functools.partial(write, 0))
    pl.when((marks[0] & 1) == 1)(functools.partial(write, 1))


def divided(orders, levels, run, height, wide, width):
    cut = run // len(orders)
    specs, shapes = [], []
    for order in orders:

        def held(bit):
            return bit[0] == "narrow" or bit[1] <= levels

        def index(j, i, marks, order=order):
            relative = i ^ (marks[0] >> (levels + 1))
            at = [0 if held(bit) else (relative >> (bit[1] - 1 - levels)) & 1 for bit in order]
            return (*at, 0, j)

        block = tuple(2 if held(bit) else 1 for bit in order) + (cut, wide)
        specs += [pl.BlockSpec(block, index)] * 2
        shapes += [jax.ShapeDtypeStruct((2,) * len(order) + (cut, width), bf16)] * 2
    return specs, shapes


def outer_kernel(run, levels, near, orders, right_dim, marks, left, right, *outs):
    divide(dot(left[...], right[...], 0, right_dim), run, levels, near, marks, orders, outs)


def outer_halves(marks, left, right, right_dim, cores, parts, order):
    rows, height = left.shape
    width = right.shape[1 - right_dim]
    share = height // cores
    high = max(2 * share, min(1024, height))
    levels = (high // (2 * share)).bit_length() - 1
    wide = min(1024, width)
    if right_dim == 0:
        right_spec = pl.BlockSpec((rows, wide), lambda j, i, marks: (0, j))
    else:
        right_spec = pl.BlockSpec((wide, rows), lambda j, i, marks: (j, 0))
    run = share // parts
    near = parts.bit_length() - 1
    specs, shapes = divided([order], levels, run, height, wide, width)
    halves = pl.pallas_call(
        functools.partial(outer_kernel, run, levels, near, [order], right_dim),
        grid_spec=pltpu.PrefetchScalarGridSpec(
            num_scalar_prefetch=1,
            grid=(width // wide, height // high),
            in_specs=[pl.BlockSpec((rows, high), lambda j, i, marks: (0, i)), right_spec],
            out_specs=specs,
        ),
        out_shape=shapes,
        compiler_params=pltpu.CompilerParams(vmem_limit_bytes=VMEM),
        cost_estimate=pl.CostEstimate(
            flops=2 * rows * height * width, bytes_accessed=1 << 25, transcendentals=0
        ),
        name="outer",
    )(marks, left, right)
    return [item.reshape(height // 2, width) for item in halves]


def mixed_kernel(
    run,
    levels,
    near,
    orders,
    first_far,
    marks,
    d_own,
    d_far,
    normed,
    normed_far,
    w,
    gain,
    shift,
    *outs,
):
    *halves, small, sums, bias = outs
    step, last = pl.program_id(1), pl.num_programs(1) - 1
    total = dot(d_own[...], normed[...], 1, 0)
    bias[...] = jnp.sum(d_own[...].astype(f32), axis=1, keepdims=True)

    @pl.when(step == 0)
    def _():
        sums[...] = jnp.zeros(sums.shape, f32)
        small[...] = jnp.zeros(small.shape, f32)

    def finish(value):
        divide(value, run, levels, near, marks, orders, halves)
        weights = w[...].astype(f32).T
        sums[0:1, :] += column_sum(weights * value)
        sums[1:2, :] += column_sum(weights * bias[...])
        wide = jnp.broadcast_to(bias[...], (bias.shape[0], PAIR)).T
        small[pl.ds(step, 1), : bias.shape[0]] = wide[0:1, :]

    @pl.when(step < first_far)
    def _():
        finish(total)

    @pl.when(step >= first_far)
    def _():
        bias[...] += jnp.sum(d_far[...].astype(f32), axis=1, keepdims=True)
        finish(total + dot(d_far[...], normed_far[...], 1, 0))

    @pl.when(step == last)
    def _():
        small[pl.ds(last + 1, 1), :] = (sums[0:1, :] - shift[...] * sums[1:2, :]) / gain[...]
        small[pl.ds(last + 2, 1), :] = sums[1:2, :]


def mixed_halves(marks, d_own, d_far, normed, normed_far, w, gain, shift, cores, parts, orders):
    height, rows = d_own.shape
    far = d_far.shape[1]
    width = normed.shape[1]
    share = height // cores
    pairs = max(1, 768 // (2 * share))
    levels = pairs.bit_length() - 1
    high = 2 * share * pairs
    first_far = width // high
    run = share // parts
    near = parts.bit_length() - 1
    steps = height // high

    def fixed(shape):
        return pl.BlockSpec(shape, lambda j, i, marks: (0, 0), pipeline_mode=pl.Buffered(1))

    specs, shapes = divided(orders, levels, run, height, width, width)
    *halves, small = pl.pallas_call(
        functools.partial(mixed_kernel, run, levels, near, orders, first_far),
        grid_spec=pltpu.PrefetchScalarGridSpec(
            num_scalar_prefetch=1,
            grid=(1, steps),
            in_specs=[
                pl.BlockSpec((high, rows), lambda j, i, marks: (i, 0)),
                pl.BlockSpec((high, far), lambda j, i, marks: (jnp.maximum(i, first_far), 0)),
                fixed(normed.shape),
                fixed(normed_far.shape),
                pl.BlockSpec((width, high), lambda j, i, marks: (0, i)),
                fixed(gain.shape),
                fixed(shift.shape),
            ],
            out_specs=specs + [pl.BlockSpec((16, width), lambda j, i, marks: (0, 0))],
            scratch_shapes=[pltpu.VMEM((2, width), f32), pltpu.VMEM((high, 1), f32)],
        ),
        out_shape=shapes + [jax.ShapeDtypeStruct((16, width), f32)],
        compiler_params=pltpu.CompilerParams(vmem_limit_bytes=VMEM),
        cost_estimate=pl.CostEstimate(
            flops=2 * (rows + far) * height * width, bytes_accessed=1 << 25, transcendentals=0
        ),
        name="mixed",
    )(marks, d_own, d_far, normed, normed_far, w, gain, shift)
    halves = [item.reshape(-1, width) for item in halves]
    return [halves[i : i + 2] for i in range(0, len(halves), 2)], small, steps


def bit_of(axis, position):
    return (lax.axis_index(axis) >> position) & 1


def swap(values, axis, position):
    size = lax.axis_size(axis)
    return lax.ppermute(values, axis, [(i, i ^ (1 << position)) for i in range(size)])


class Halving:
    def __init__(self, halves, order):
        self.order = list(order)
        kept, given = halves
        self.height = kept.shape[0]
        self.terms = [kept, swap(given, "wide", 0)]

    def send(self, away):
        self.terms = self.terms + [swap(away, *self.order.pop(0))]
        self.height //= 2

    def blocks(self, height, grid, which):
        width = self.terms[0].shape[1]
        spec = pl.BlockSpec((1, height // grid, width), lambda i: (which, i, 0))
        return [term.reshape(-1, height, width) for term in self.terms], [spec] * len(self.terms)


class Adding:
    def __init__(self, array, order):
        self.order = list(order)
        self.terms = [array, swap(array, *self.order.pop(0))]

    def send(self, total):
        self.terms = [total, swap(total, *self.order.pop(0))]


def halve_kernel(counts, *refs):
    ins, outs = refs[: sum(counts) + 2], refs[sum(counts) + 2 :]
    at = 0
    for count, out in zip(counts, outs):
        parts = [ref[0].astype(f32) for ref in ins[at : at + count]]
        out[...] = functools.reduce(jnp.add, parts).astype(bf16)
        at += count
    outs[-1][...] = ins[-2][...] + ins[-1][...]


def halve(sums, small):
    heights = [item.height // 2 for item in sums]
    grid = 4 if all(height % 64 == 0 for height in heights) else 1
    operands, in_specs, out_specs, out_shape = [], [], [], []
    for item, height in zip(sums, heights):
        arrays, specs = item.blocks(height, grid, 1)
        operands += arrays
        in_specs += specs
        width = arrays[0].shape[2]
        out_specs.append(pl.BlockSpec((height // grid, width), lambda i: (i, 0)))
        out_shape.append(jax.ShapeDtypeStruct((height, width), bf16))
    whole_small = pl.BlockSpec(small.terms[0].shape, lambda i: (0, 0))
    return pl.pallas_call(
        functools.partial(halve_kernel, [len(item.terms) for item in sums]),
        grid=(grid,),
        in_specs=in_specs + [whole_small] * 2,
        out_specs=out_specs + [whole_small],
        out_shape=out_shape + [jax.ShapeDtypeStruct(small.terms[0].shape, f32)],
        compiler_params=pltpu.CompilerParams(vmem_limit_bytes=VMEM),
        name="halve",
    )(*operands, *small.terms)


def launch(lead, sums, small, *others):
    lead, others, halves = lax.optimization_barrier((lead, others, halve(sums, small)))
    for item, away in zip(sums, halves):
        item.send(away)
    small.send(halves[-1])
    return (lead, *others)


def settle(lead, sums, small):
    everything = sums + [small]
    lead, terms = lax.optimization_barrier((lead, [item.terms for item in everything]))
    for item, arrays in zip(everything, terms):
        item.terms = list(arrays)
    return lead


def collect_kernel(counts, *refs):
    at = 0
    for count, out in zip(counts, refs[sum(counts) :]):
        out[...] = functools.reduce(jnp.add, [ref[0].astype(f32) for ref in refs[at : at + count]])
        at += count


def collect(sums):
    operands, in_specs, out_specs, out_shape = [], [], [], []
    for item in sums:
        arrays, specs = item.blocks(item.height, 1, 0)
        operands += arrays
        in_specs += specs
        shape = arrays[0].shape[1:]
        out_specs.append(pl.BlockSpec(shape, lambda i: (0, 0)))
        out_shape.append(jax.ShapeDtypeStruct(shape, f32))
    return pl.pallas_call(
        functools.partial(collect_kernel, [len(item.terms) for item in sums]),
        grid=(1,),
        in_specs=in_specs,
        out_specs=out_specs,
        out_shape=out_shape,
        compiler_params=pltpu.CompilerParams(vmem_limit_bytes=VMEM),
        name="collect",
    )(*operands)


def read_small(ref, at, rows):
    parts = [ref[at + i * rows : at + (i + 1) * rows, :].astype(f32) for i in range(3)]
    return parts[0] + parts[1] + parts[2]


def joint_kernel(plan, last, *refs):
    count, buffers, from_at, small_from, to_at, small_to, rows = plan
    arrays, refs = refs[:count], refs[count:]
    received, refs = refs[:buffers], refs[buffers:]
    small, refs = refs[0], refs[1:]
    if small_from is None:
        total = small[...] + refs[0][...]
        refs = refs[1:]
    else:
        total = small[...] + read_small(received[small_from[0]], small_from[1], rows)
    if last:
        out, small_out = refs
        for i in range(count):
            which, at = from_at[i]
            height = arrays[i].shape[0]
            part = received[which][at : at + height, :].astype(f32)
            out[i * height : (i + 1) * height, :] = arrays[i][...].astype(f32) + part
        small_out[...] = total
        return
    outs, sent, small_out = refs[:count], refs[count:-1], refs[-1]
    for i in range(count):
        which, at = from_at[i]
        height = arrays[i].shape[0] // 2
        for half in range(2):
            here = slice(half * height, (half + 1) * height)
            there = slice(at + half * height, at + (half + 1) * height)
            part = arrays[i][here, :].astype(f32) + received[which][there, :].astype(f32)
            if half:
                which_out, at_out = to_at[i]
                sent[which_out][at_out : at_out + height, :] = part.astype(bf16)
            else:
                outs[i][...] = part.astype(bf16)
    small_out[...] = total
    which_out, at_out = small_to
    for part in split_three(total):
        sent[which_out][at_out : at_out + rows, :] = part.astype(bf16)
        at_out += rows


class Joint:
    def __init__(self, halves, orders, small):
        self.arrays = [kept for kept, _ in halves]
        self.received = [swap(given, "wide", 0) for _, given in halves]
        self.from_at = [(i, 0) for i in range(len(halves))]
        self.orders = [list(order) for order in orders]
        self.small, self.small_from = small, None
        self.extra = [swap(small, "wide", 0)]

    def call(self, plan, last, shapes):
        return pl.pallas_call(
            functools.partial(joint_kernel, plan, last),
            out_shape=shapes,
            compiler_params=pltpu.CompilerParams(vmem_limit_bytes=VMEM),
            name="joint",
        )(*self.arrays, *self.received, self.small, *self.extra)

    def plan(self, to_at, small_to):
        buffers, rows = len(self.received), self.small.shape[0]
        count = len(self.arrays)
        return count, buffers, self.from_at, self.small_from, to_at, small_to, rows

    def step(self, lead, *others):
        bits, heights, to_at = [], [], []
        width = self.arrays[0].shape[1]
        for array, order in zip(self.arrays, self.orders):
            bit = order.pop(0)
            if bit not in bits:
                bits.append(bit)
                heights.append(0)
            which = bits.index(bit)
            to_at.append((which, heights[which]))
            heights[which] += array.shape[0] // 2
        small_to = (0, heights[0])
        heights[0] += 3 * self.small.shape[0]
        shapes = [
            jax.ShapeDtypeStruct((array.shape[0] // 2, width), bf16) for array in self.arrays
        ]
        shapes += [jax.ShapeDtypeStruct((height, width), bf16) for height in heights]
        shapes += [jax.ShapeDtypeStruct(self.small.shape, f32)]
        outs = self.call(self.plan(to_at, small_to), False, shapes)
        lead, others, outs = lax.optimization_barrier((lead, others, outs))
        count = len(self.arrays)
        self.arrays, sent, self.small = outs[:count], outs[count:-1], outs[-1]
        self.received = [swap(item, *bit) for item, bit in zip(sent, bits)]
        self.from_at, self.small_from, self.extra = to_at, small_to, []
        return (lead, *others)

    def result(self):
        height = sum(array.shape[0] for array in self.arrays)
        shapes = [
            jax.ShapeDtypeStruct((height, self.arrays[0].shape[1]), f32),
            jax.ShapeDtypeStruct(self.small.shape, f32),
        ]
        return self.call(self.plan([], None), True, shapes)


def angles(positions):
    half = HEAD_DIM // 2
    freqs = jnp.power(10000.0, -jnp.arange(half, dtype=f32) / half)
    theta = freqs[:, None] * positions.astype(f32)[None, :]
    return jnp.cos(theta), jnp.sin(theta)


def axis_bits(axis):
    return [(axis, position) for position in range(lax.axis_size(axis).bit_length() - 1)]


def body(
    inputs,
    cotangent,
    lengths,
    w_qkv,
    b_qkv,
    w_out,
    b_out,
    w_up,
    b_up,
    w_down,
    b_down,
    gain_one,
    shift_one,
    gain_two,
    shift_two,
    gain_three,
    shift_three,
    gain_four,
    shift_four,
):
    group = inputs.shape[3]
    width = inputs.shape[4]
    parts = lax.axis_size("narrow")
    place = lax.axis_index("narrow")
    cores = lax.axis_size("wide")
    others = parts - 1
    rows = 2 * group
    offsets = jnp.arange(group, dtype=jnp.int32)

    def row(vector):
        return vector[None, :]

    def positions(owners):
        starts = jnp.stack([owners, 2 * parts - 1 - owners], axis=1).reshape(-1) * group
        return (starts[:, None] + offsets[None]).reshape(-1)

    def joined(items):
        return jnp.concatenate(items, axis=0) if len(items) > 1 else items[0]

    tokens = inputs.reshape(rows, width)
    far_tokens = joined(
        [
            lax.ppermute(tokens, "narrow", [((n + shift) % parts, n) for n in range(parts)])
            for shift in range(1, parts)
        ]
    )
    other = (place + 1 + jnp.arange(others, dtype=jnp.int32)) % parts
    early_at = place * group
    late_at = (2 * parts - 1 - place) * group
    info = jnp.stack([place, lengths[0], early_at, late_at]).astype(jnp.int32)
    marks = jnp.stack([lax.axis_index("wide"), place]).astype(jnp.int32)
    turns = angles(positions(place[None]))
    turns_far = angles(positions(other))

    norm_one = [row(gain_one), row(shift_one)]
    normed, qT, kT, vT = project(tokens, w_qkv, row(b_qkv), *norm_one, *turns, (0, 1, 2))
    state, kept_own, flags_own = attend_local(info, qT, kT, vT, group)
    normed_far, kT_far, vT_far = project(
        far_tokens, w_qkv, row(b_qkv), *norm_one, *turns_far, (1, 2)
    )
    oT, lse, kept_far, flags_far = attend_remote(
        info, qT, kT_far, vT_far, state, group, parts
    )

    blocks = block_call(
        oT,
        tokens,
        cotangent.reshape(rows, width),
        [w_out, w_up, w_down],
        [row(item) for item in (b_out, b_up, b_down)]
        + [row(item) for item in (gain_two, shift_two, gain_three, shift_three)]
        + [row(item) for item in (gain_four, shift_four)],
    )
    result, d_middle, hidden, d_outer, normed_two, d_inner, d_branch, doT, small, small_up = blocks

    wide_bits = axis_bits("wide")
    narrow_bits = axis_bits("narrow")
    first_order = wide_bits[1:2] + narrow_bits + wide_bits[2:]
    second_order = narrow_bits + wide_bits[1:]
    third_order = narrow_bits + wide_bits[2:3] + wide_bits[1:2] + wide_bits[3:]
    fourth_order = wide_bits[2:3] + wide_bits[1:2] + narrow_bits + wide_bits[3:]
    small_order = wide_bits[:1] + first_order

    def outer(left, right, right_dim, order):
        return Halving(outer_halves(marks, left, right, right_dim, cores, parts, order), order)

    sum_up = outer(d_inner, normed_two, 0, first_order)
    sum_down = outer(d_outer, hidden, 0, second_order)
    sum_out = outer(d_branch, oT, 1, fourth_order)
    flat = jnp.concatenate([small.reshape(-1), small_up.reshape(-1)])
    early = Adding(flat.reshape(-1, PAIR), small_order)
    sums = [sum_down, sum_up, sum_out]

    heads = width // PAIR
    portions = 2 if heads % 2 == 0 else 1
    count = heads // portions
    far = []
    for portion in range(portions):
        (doT,) = launch(doT, sums, early)
        far = back_remote(
            info,
            flags_far,
            [qT, doT, oT, lse],
            turns_far,
            [kT_far, vT_far],
            kept_far,
            group,
            parts,
            portion * count,
            count,
            far,
        )
    dq_far, d_far = far
    d_back = unproject(d_far, w_qkv, (1, 2), 0, others * rows)
    d_mixed = []
    for portion in range(portions):
        doT, d_back = launch(doT, sums, early, d_back)
        if not portion:
            returned = [
                lax.ppermute(
                    d_back[j * rows : (j + 1) * rows] if others > 1 else d_back,
                    "narrow",
                    [(n, (n + j + 1) % parts) for n in range(parts)],
                )
                for j in range(others)
            ]
        d_mixed = [
            back_local(
                info,
                flags_own,
                [qT, doT, oT, lse],
                turns,
                [kT, vT],
                dq_far,
                kept_own,
                group,
                portion * count,
                count,
                d_mixed,
            )
        ]
    d_mixed = d_mixed[0]
    while early.order:
        (d_mixed,) = launch(d_mixed, sums, early)
    d_mixed = settle(d_mixed, sums, early)
    d_mixed, returned = lax.optimization_barrier((d_mixed, returned))
    if others > 1:
        returned = [functools.reduce(jnp.add, [item.astype(f32) for item in returned])]

    orders = [first_order, third_order, fourth_order]
    pieces, late, steps = mixed_halves(
        marks,
        d_mixed.reshape(3 * width, rows),
        d_far.reshape(3 * width, -1),
        normed,
        normed_far,
        w_qkv,
        *norm_one,
        cores,
        parts,
        orders,
    )
    tail = Joint(pieces, orders, late)
    (d_mixed,) = tail.step(d_mixed)
    d_tokens = []
    for i in range(2):
        finish = (returned[0], tokens, d_middle, row(gain_one))
        d_tokens = [
            unproject(d_mixed, w_qkv, (0, 1, 2), i * group, group, finish, d_tokens)
        ]
        if tail.orders[0]:
            d_mixed, d_tokens[0] = tail.step(d_mixed, d_tokens[0])
    while tail.orders[0]:
        d_tokens[0], *terms = tail.step(d_tokens[0], *[item.terms for item in sums])
        for item, arrays in zip(sums, terms):
            item.terms = list(arrays)

    sum_w_down, sum_w_up, sum_w_out = collect(sums)
    sum_w_qkv, late_small = tail.result()
    grad_b_qkv = late_small[:steps, : 3 * width // steps].reshape(-1)
    early_small = (early.terms[0] + early.terms[1]).reshape(-1)
    small = early_small[: 8 * width].reshape(8, width)
    small_up = early_small[8 * width :]
    shape = inputs.shape
    return (
        result.reshape(shape),
        d_tokens[0].reshape(shape),
        sum_w_qkv.T,
        sum_w_out.T,
        sum_w_up.T,
        sum_w_down.T,
        grad_b_qkv,
        small[7],
        small_up,
        small[2],
        late_small[steps],
        late_small[steps + 1],
        small[5],
        small[6],
        small[3],
        small[4],
        small[0],
        small[1],
    )


def solution(mesh):
    tokens = P("wide", None, "narrow", None, None)
    columns = P(None, ("wide", "narrow"))
    in_specs = (tokens, tokens, P("wide")) + (P(),) * 16
    out_specs = (tokens, tokens) + (columns,) * 4 + (P(),) * 12
    return jax.shard_map(body, mesh=mesh, in_specs=in_specs, out_specs=out_specs, check_vma=False)
```

```python
import functools

import jax
import jax.numpy as jnp
from jax import lax
from jax.experimental import pallas as pl
from jax.experimental.pallas import tpu as pltpu
from jax.sharding import PartitionSpec as P

HEAD_DIM = 64
PAIR = 2 * HEAD_DIM
EPS = 1e-05
LOG2E = 1.4426950408889634
LN2 = 0.6931471805599453
NEG = -1e30
REACH = 60.0
VMEM = 62 * 1024 * 1024
SPAN = 1024

f32 = jnp.float32
bf16 = jnp.bfloat16


def dot(left, right, left_dim, right_dim):
    return lax.dot_general(
        left, right, (((left_dim,), (right_dim,)), ((), ())), preferred_element_type=f32
    )


def bounded(qT, kT):
    worst = None
    for h in range(2):
        rows = slice(HEAD_DIM * h, HEAD_DIM * (h + 1))
        norms = []
        for item in (qT, kT):
            values = item[rows, :].astype(f32)
            norms.append(jnp.max(jnp.sum(values * values, axis=0, keepdims=True)))
        both = norms[0] * norms[1]
        worst = both if worst is None else jnp.maximum(worst, both)
    return worst <= REACH * REACH


def fwd_chunk(fast, q0, k0, q_n, k_n, limit, store, qT, kT, vT, m_ref, l_ref, acc):
    queries = pl.ds(q0, q_n)
    strip = min(256, k_n)
    for h in range(2):
        rows = slice(HEAD_DIM * h, HEAD_DIM * (h + 1))
        old = m_ref[h : h + 1, queries]
        new = jnp.zeros_like(old) if fast else old
        strips = []
        for j in range(k_n // strip):
            keys = pl.ds(k0 + j * strip, strip)
            scores = dot(kT[rows, keys], qT[rows, queries], 0, 0)
            if limit is not None:
                key_at = lax.broadcasted_iota(jnp.int32, (strip, q_n), 0)
                scores = jnp.where(key_at < limit - j * strip, scores, NEG)
            strips.append(scores)
            if not fast:
                new = jnp.maximum(new, jnp.max(scores, axis=0, keepdims=True))
        factor = jnp.exp2(old - new)
        total = l_ref[h : h + 1, queries] * factor
        value = acc[rows, queries] * factor
        for j in range(k_n // strip):
            keys = pl.ds(k0 + j * strip, strip)
            weights = jnp.exp2(strips[j] if fast else strips[j] - new)
            total = total + jnp.sum(weights, axis=0, keepdims=True)
            weights = weights.astype(bf16)
            if fast:
                store(h, j, weights)
            value = value + dot(vT[rows, keys], weights, 1, 0)
        m_ref[h : h + 1, queries] = new
        l_ref[h : h + 1, queries] = total
        acc[rows, queries] = value


def pad_left(values, count):
    if not count:
        return values
    return jnp.concatenate([jnp.zeros((values.shape[0], count), f32), values], axis=1)


def pad_right(values, count):
    if not count:
        return values
    return jnp.concatenate([values, jnp.zeros((values.shape[0], count), f32)], axis=1)


def fwd_diagonal(fast, base, group, limit, store, qT, kT, vT, m_ref, l_ref, acc):
    strip = min(256, group)
    count = group // strip
    for h in range(2):
        rows = slice(HEAD_DIM * h, HEAD_DIM * (h + 1))
        strips = []
        for j in range(count):
            wide = group - j * strip
            keys, queries = pl.ds(base + j * strip, strip), pl.ds(base + j * strip, wide)
            scores = dot(kT[rows, keys], qT[rows, queries], 0, 0)
            key_at = lax.broadcasted_iota(jnp.int32, scores.shape, 0)
            query_at = lax.broadcasted_iota(jnp.int32, scores.shape, 1)
            scores = jnp.where(key_at <= query_at, scores, NEG)
            if limit is not None:
                scores = jnp.where(key_at < limit - j * strip, scores, NEG)
            strips.append(scores)
        peaks = []
        for g in range(0 if fast else count):
            peak = None
            for j in range(g + 1):
                part = strips[j][:, (g - j) * strip : (g - j + 1) * strip]
                part = jnp.max(part, axis=0, keepdims=True)
                peak = part if peak is None else jnp.maximum(peak, part)
            peaks.append(peak)
        if fast:
            peak = jnp.zeros((1, group), f32)
        else:
            peak = jnp.concatenate(peaks, axis=1) if count > 1 else peaks[0]
        total, value = None, None
        for j in range(count):
            keys = pl.ds(base + j * strip, strip)
            weights = jnp.exp2(strips[j] if fast else strips[j] - peak[:, j * strip :])
            part = pad_left(jnp.sum(weights, axis=0, keepdims=True), j * strip)
            weights = weights.astype(bf16)
            if fast:
                store(h, j, weights)
            term = pad_left(dot(vT[rows, keys], weights, 1, 0), j * strip)
            total = part if total is None else total + part
            value = term if value is None else value + term
        queries = pl.ds(base, group)
        m_ref[h : h + 1, queries] = peak
        l_ref[h : h + 1, queries] = total
        acc[rows, queries] = value


def triangle_slot(i, j, group):
    strip = min(256, group)
    count = group // strip
    row = jnp.where(i == 0, j, count - j) * strip
    column = jnp.where(i == 0, j * strip, 0)
    wide = group - j * strip
    return (
        pl.ds(pl.multiple_of(row, strip), strip),
        pl.ds(pl.multiple_of(column, strip), wide),
    )


def square_slot(j, group):
    strip = min(256, group)
    return pl.ds(group + strip + j * strip, strip), slice(None)


def fwd_local_kernel(group, info, qT, kT, vT, acc, m_ref, l_ref, kept, flags):
    length = info[1]
    m_ref[...] = jnp.full(m_ref.shape, NEG, f32)
    l_ref[...] = jnp.zeros(l_ref.shape, f32)
    acc[...] = jnp.zeros(acc.shape, f32)
    refs = (qT, kT, vT, m_ref.at[0], l_ref.at[0], acc)

    def walk(fast):
        def own(i, carry):
            base = pl.multiple_of(i * group, group)
            start = info[2 + i]

            def store(h, j, weights):
                rows, columns = triangle_slot(i, j, group)
                kept[h, rows, columns] = weights

            @pl.when(start + group <= length)
            def _():
                fwd_diagonal(fast, base, group, None, store, *refs)

            @pl.when((start < length) & (start + group > length))
            def _():
                fwd_diagonal(fast, base, group, length - start, store, *refs)

            return carry

        lax.fori_loop(0, 2, own, 0)
        early = info[2]

        def store(h, j, weights):
            rows, columns = square_slot(j, group)
            kept[h, rows, columns] = weights

        @pl.when(early + group <= length)
        def _():
            fwd_chunk(fast, group, 0, group, group, None, store, *refs)

        @pl.when((early < length) & (early + group > length))
        def _():
            fwd_chunk(fast, group, 0, group, group, length - early, store, *refs)

    small = bounded(qT, kT)
    flags[pl.program_id(0)] = small.astype(jnp.int32)
    pl.when(small)(functools.partial(walk, True))
    pl.when(jnp.logical_not(small))(functools.partial(walk, False))


def remote_steps(group, parts, info, full, partial):
    place, length = info[0], info[1]

    def visit(i, carry):
        j, turn_at = i // 3, lax.rem(i, 3)
        other = lax.rem(place + 1 + j, parts)
        late_key = turn_at == 2
        block = jnp.where(late_key, 2 * parts - 1 - other, other)
        before = (other < place).astype(jnp.int32)
        wanted = jnp.where(turn_at == 0, before, jnp.where(late_key, 1 - before, 1)) == 1
        q0 = pl.multiple_of(jnp.where(turn_at == 0, 0, group), group)
        k0 = pl.multiple_of((2 * j + jnp.where(late_key, 1, 0)) * group, group)
        slot = pl.multiple_of((2 * j + turn_at - (1 - before)) * group, group)
        start = block * group

        @pl.when(wanted & (start + group <= length))
        def _():
            full(q0, k0, slot)

        @pl.when(wanted & (start < length) & (start + group > length))
        def _():
            partial(q0, k0, slot, length - start)

        return carry

    lax.fori_loop(0, 3 * (parts - 1), visit, 0)


def fwd_remote_kernel(
    group, parts, info, qT, kT, vT, acc_in, m_in, l_in, out, lse, kept, flags, acc, m_ref, l_ref
):
    acc[...] = acc_in[...]
    m_ref[...] = m_in[0]
    l_ref[...] = l_in[0]
    refs = (qT, kT, vT, m_ref, l_ref, acc)
    strip = min(256, group)

    def walk(fast):
        def partial(q0, k0, slot, limit):
            def store(h, j, weights):
                kept[h, pl.ds(pl.multiple_of(slot + j * strip, strip), strip), :] = weights

            fwd_chunk(fast, q0, k0, group, group, limit, store, *refs)

        def full(q0, k0, slot):
            partial(q0, k0, slot, None)

        remote_steps(group, parts, info, full, partial)

    small = bounded(qT, kT) & (jnp.max(m_in[...]) <= 0.0)
    flags[pl.program_id(0)] = small.astype(jnp.int32)
    pl.when(small)(functools.partial(walk, True))
    pl.when(jnp.logical_not(small))(functools.partial(walk, False))
    for h in range(2):
        rows = slice(HEAD_DIM * h, HEAD_DIM * (h + 1))
        total = l_ref[h : h + 1, :]
        out[rows, :] = (acc[rows, :] / total).astype(bf16)
        lse[0, h : h + 1, :] = m_ref[h : h + 1, :] + jnp.log2(total)


def split_three(values):
    high = values.astype(bf16).astype(f32)
    rest = values - high
    middle = rest.astype(bf16).astype(f32)
    low = (rest - middle).astype(bf16).astype(f32)
    return [high, middle, low]


def bwd_prepare(qT, kT, vT, doT, oT, lse, qa, da, ka, va):
    n_q, n_k = qT.shape[1], ka.shape[2]
    extra = qa.shape[1] - HEAD_DIM
    pad = jnp.zeros((extra - 3, n_q), f32)
    row_at = lax.broadcasted_iota(jnp.int32, (extra, n_k), 0)
    tail = jnp.where(row_at < 3, 1.0, 0.0).astype(bf16)
    for h in range(2):
        rows = slice(HEAD_DIM * h, HEAD_DIM * (h + 1))
        grad = doT[rows, :].astype(f32)
        delta = jnp.sum(grad * oT[rows, :].astype(f32), axis=0, keepdims=True)
        qa[h, :HEAD_DIM, :] = qT[rows, :]
        parts = split_three(-lse[0, h : h + 1, :]) + [pad]
        qa[h, HEAD_DIM:, :] = jnp.concatenate(parts, axis=0).astype(bf16)
        da[h, :HEAD_DIM, :] = doT[rows, :]
        parts = split_three(-delta) + [pad]
        da[h, HEAD_DIM:, :] = jnp.concatenate(parts, axis=0).astype(bf16)
        ka[h, :HEAD_DIM, :] = kT[rows, :]
        va[h, :HEAD_DIM, :] = vT[rows, :]
        ka[h, HEAD_DIM:, :] = tail
        va[h, HEAD_DIM:, :] = tail


def bwd_chunk(q0, k0, q_n, k_n, limit, qT, doT, qa, da, ka, va, dq, dk, dv):
    queries, keys = pl.ds(q0, q_n), pl.ds(k0, k_n)
    for h in range(2):
        rows = slice(HEAD_DIM * h, HEAD_DIM * (h + 1))
        probs = jnp.exp2(dot(qa[h, :, queries], ka[h, :, keys], 0, 0))
        if limit is not None:
            key_at = lax.broadcasted_iota(jnp.int32, (q_n, k_n), 1)
            probs = jnp.where(key_at < limit, probs, 0.0)
        d_probs = dot(da[h, :, queries], va[h, :, keys], 0, 0)
        d_scores = (probs * d_probs).astype(bf16)
        dv[rows, keys] += dot(doT[rows, queries], probs.astype(bf16), 1, 0)
        dk[rows, keys] += dot(qT[rows, queries], d_scores, 1, 0)
        dq[rows, queries] += dot(ka[h, :HEAD_DIM, keys], d_scores, 1, 1)


def bwd_diagonal(base, group, limit, qT, doT, qa, da, ka, va, dq, dk, dv):
    strip = min(256, group)
    count = group // strip
    for h in range(2):
        rows = slice(HEAD_DIM * h, HEAD_DIM * (h + 1))
        d_keys, d_values, d_queries = None, None, []
        for j in range(count):
            wide = (j + 1) * strip
            queries, keys = pl.ds(base + j * strip, strip), pl.ds(base, wide)
            probs = jnp.exp2(dot(qa[h, :, queries], ka[h, :, keys], 0, 0))
            query_at = lax.broadcasted_iota(jnp.int32, probs.shape, 0)
            key_at = lax.broadcasted_iota(jnp.int32, probs.shape, 1)
            probs = jnp.where(key_at <= query_at + j * strip, probs, 0.0)
            if limit is not None:
                probs = jnp.where(key_at < limit, probs, 0.0)
            d_probs = dot(da[h, :, queries], va[h, :, keys], 0, 0)
            d_scores = (probs * d_probs).astype(bf16)
            value = pad_right(dot(doT[rows, queries], probs.astype(bf16), 1, 0), group - wide)
            key = pad_right(dot(qT[rows, queries], d_scores, 1, 0), group - wide)
            d_values = value if d_values is None else d_values + value
            d_keys = key if d_keys is None else d_keys + key
            d_queries.append(dot(ka[h, :HEAD_DIM, keys], d_scores, 1, 1))
        here = pl.ds(base, group)
        dq[rows, here] += jnp.concatenate(d_queries, axis=1) if count > 1 else d_queries[0]
        dk[rows, here] += d_keys
        dv[rows, here] += d_values


def stored_chunk(h, weights, queries, keys, qT, kT, vT, scaled, delta, dq, dk, dv):
    rows = slice(HEAD_DIM * h, HEAD_DIM * (h + 1))
    d_probs = dot(vT[rows, keys], scaled[rows, queries], 0, 0)
    d_scores = weights.astype(f32) * (d_probs - delta[0, h : h + 1, queries])
    d_scores = d_scores.astype(bf16)
    dv[rows, keys] += dot(scaled[rows, queries], weights, 1, 1)
    dk[rows, keys] += dot(qT[rows, queries], d_scores, 1, 1)
    dq[rows, queries] += dot(kT[rows, keys], d_scores, 1, 0)


def turn_back(values, cosine, sine):
    half = HEAD_DIM // 2
    first, second = values[:half], values[half:]
    return jnp.concatenate(
        [first * cosine + second * sine, second * cosine - first * sine], axis=0
    )


def bwd_remote_kernel(
    group,
    parts,
    first,
    info,
    flags,
    qT,
    doT,
    oT,
    lse,
    scaled,
    delta,
    cosine,
    sine,
    kT,
    vT,
    kept,
    *rest,
):
    dq, dkv, qa, da, ka, va, dk, dv = rest[-8:]
    dq[...] = jnp.zeros(dq.shape, f32)
    dk[...] = jnp.zeros(dk.shape, f32)
    dv[...] = jnp.zeros(dv.shape, f32)
    fast = flags[first + pl.program_id(0)] == 1

    @pl.when(fast)
    def _():
        def full(q0, k0, slot):
            for h in range(2):
                weights = kept[h, pl.ds(slot, group), :]
                queries, keys = pl.ds(q0, group), pl.ds(k0, group)
                stored_chunk(h, weights, queries, keys, qT, kT, vT, scaled, delta, dq, dk, dv)

        def partial(q0, k0, slot, limit):
            full(q0, k0, slot)

        remote_steps(group, parts, info, full, partial)

    @pl.when(jnp.logical_not(fast))
    def _():
        bwd_prepare(qT, kT, vT, doT, oT, lse, qa, da, ka, va)
        refs = (qT, doT, qa, da, ka, va, dq, dk, dv)

        def full(q0, k0, slot):
            bwd_chunk(q0, k0, group, group, None, *refs)

        def partial(q0, k0, slot, limit):
            bwd_chunk(q0, k0, group, group, limit, *refs)

        remote_steps(group, parts, info, full, partial)

    for h in range(2):
        rows = slice(HEAD_DIM * h, HEAD_DIM * (h + 1))
        dkv[1, rows, :] = turn_back(dk[rows, :] * LN2, cosine[...], sine[...]).astype(bf16)
    dkv[0] = jnp.zeros(dv.shape, bf16)
    dkv[2] = dv[...].astype(bf16)


def bwd_local_kernel(
    group,
    first,
    info,
    flags,
    qT,
    doT,
    oT,
    lse,
    scaled,
    delta,
    cosine,
    sine,
    kT,
    vT,
    dq_in,
    kept,
    *rest,
):
    dqkv, qa, da, ka, va, dk, dv, dq = rest[-8:]
    length = info[1]
    dq[...] = dq_in[...]
    dk[...] = jnp.zeros(dk.shape, f32)
    dv[...] = jnp.zeros(dv.shape, f32)
    early = info[2]
    strip = min(256, group)
    fast = flags[first + pl.program_id(0)] == 1

    @pl.when(fast)
    def _():
        refs = (qT, kT, vT, scaled, delta, dq, dk, dv)

        def own(i, carry):
            base = pl.multiple_of(i * group, group)

            @pl.when(info[2 + i] < length)
            def _():
                for h in range(2):
                    for j in range(group // strip):
                        rows, columns = triangle_slot(i, j, group)
                        queries = pl.ds(base + j * strip, group - j * strip)
                        keys = pl.ds(base + j * strip, strip)
                        stored_chunk(h, kept[h, rows, columns], queries, keys, *refs)

            return carry

        lax.fori_loop(0, 2, own, 0)

        @pl.when(early < length)
        def _():
            for h in range(2):
                weights = kept[h, group + strip :, :]
                stored_chunk(h, weights, pl.ds(group, group), pl.ds(0, group), *refs)

    @pl.when(jnp.logical_not(fast))
    def _():
        bwd_prepare(qT, kT, vT, doT, oT, lse, qa, da, ka, va)
        refs = (qT, doT, qa, da, ka, va, dq, dk, dv)

        def own(i, carry):
            base = pl.multiple_of(i * group, group)
            start = info[2 + i]

            @pl.when(start < length)
            def _():
                bwd_diagonal(base, group, length - start, *refs)

            return carry

        lax.fori_loop(0, 2, own, 0)

        @pl.when(early < length)
        def _():
            bwd_chunk(group, 0, group, group, length - early, *refs)

    for h in range(2):
        rows = slice(HEAD_DIM * h, HEAD_DIM * (h + 1))
        d_query = dq[rows, :] * 0.125
        dqkv[0, rows, :] = turn_back(d_query, cosine[...], sine[...]).astype(bf16)
        dqkv[1, rows, :] = turn_back(dk[rows, :] * LN2, cosine[...], sine[...]).astype(bf16)
    dqkv[2] = dv[...].astype(bf16)


def rows_of(count, first=0):
    return pl.BlockSpec((PAIR, count), lambda i, *info: (first + i, 0))


def stats_of(count, first=0):
    return pl.BlockSpec((1, 2, count), lambda i, *info: (first + i, 0, 0))


def planes_of(planes, count, first=0):
    return pl.BlockSpec((planes, PAIR, count), lambda i, *info: (0, first + i, 0))


def kept_of(rows, group, first=0):
    return pl.BlockSpec((2, rows, group), lambda i, *info: (first + i, 0, 0))


def scalars():
    return pl.BlockSpec(memory_space=pltpu.SMEM)


def whole(shape):
    return pl.BlockSpec(shape, lambda i, *info: (0,) * len(shape))


def attention_call(kernel, pairs, in_specs, out_specs, out_shape, scratch, flops, name, alias={}, prefetch=1):
    return pl.pallas_call(
        kernel,
        grid_spec=pltpu.PrefetchScalarGridSpec(
            num_scalar_prefetch=prefetch,
            grid=(pairs,),
            in_specs=in_specs,
            out_specs=out_specs,
            scratch_shapes=scratch,
        ),
        out_shape=out_shape,
        input_output_aliases=alias,
        compiler_params=pltpu.CompilerParams(vmem_limit_bytes=VMEM),
        cost_estimate=pl.CostEstimate(
            flops=int(flops), bytes_accessed=1 << 25, transcendentals=0
        ),
        name=name,
    )


def attend_local(info, qT, kT, vT, group):
    width, n_q = qT.shape
    pairs = width // PAIR
    kept_rows = 2 * group + min(256, group)
    call = attention_call(
        functools.partial(fwd_local_kernel, group),
        pairs,
        [rows_of(n_q)] * 3,
        [rows_of(n_q), stats_of(n_q), stats_of(n_q), kept_of(kept_rows, group), scalars()],
        [
            jax.ShapeDtypeStruct((width, n_q), f32),
            jax.ShapeDtypeStruct((pairs, 2, n_q), f32),
            jax.ShapeDtypeStruct((pairs, 2, n_q), f32),
            jax.ShapeDtypeStruct((2 * pairs, kept_rows, group), bf16),
            jax.ShapeDtypeStruct((pairs,), jnp.int32),
        ],
        [],
        4 * width * 2 * group * group * 4,
        "attend_local",
    )
    *state, kept, flags = call(info, qT, kT, vT)
    return state, kept, flags


def attend_remote(info, qT, kT, vT, state, group, parts):
    width, n_q = qT.shape
    n_k = kT.shape[1]
    pairs = width // PAIR
    call = attention_call(
        functools.partial(fwd_remote_kernel, group, parts),
        pairs,
        [rows_of(n_q), rows_of(n_k), rows_of(n_k), rows_of(n_q), stats_of(n_q), stats_of(n_q)],
        [rows_of(n_q), stats_of(n_q), kept_of(n_k, group), scalars()],
        [
            jax.ShapeDtypeStruct((width, n_q), bf16),
            jax.ShapeDtypeStruct((pairs, 2, n_q), f32),
            jax.ShapeDtypeStruct((2 * pairs, n_k, group), bf16),
            jax.ShapeDtypeStruct((pairs,), jnp.int32),
        ],
        [pltpu.VMEM((PAIR, n_q), f32)] + [pltpu.VMEM((2, n_q), f32)] * 2,
        4 * width * 2 * group * group * 4,
        "attend_remote",
    )
    return call(info, qT, kT, vT, *state)


def back_scratch(n_q, n_k):
    rows = HEAD_DIM + 16
    return (
        [pltpu.VMEM((2, rows, n_q), bf16)] * 2
        + [pltpu.VMEM((2, rows, n_k), bf16)] * 2
        + [pltpu.VMEM((PAIR, n_k), f32)] * 2
    )


def back_remote(info, flags, operands, turns, keys, kept, group, parts, first, count, before):
    width, n_q = operands[0].shape
    n_k = keys[0].shape[1]
    half = HEAD_DIM // 2
    n_in = 2 + len(operands) + len(turns) + len(keys) + 1
    call = attention_call(
        functools.partial(bwd_remote_kernel, group, parts, first),
        count,
        [rows_of(n_q, first)] * 3
        + [stats_of(n_q, first), rows_of(n_q, first), stats_of(n_q, first)]
        + [whole((half, n_k))] * 2
        + [rows_of(n_k, first)] * 2
        + [kept_of(kept.shape[1], group, first)]
        + [pl.BlockSpec(memory_space=pl.ANY)] * len(before),
        [rows_of(n_q, first), planes_of(3, n_k, first)],
        [
            jax.ShapeDtypeStruct((width, n_q), f32),
            jax.ShapeDtypeStruct((3, width, n_k), bf16),
        ],
        back_scratch(n_q, n_k),
        10 * count * PAIR * 2 * group * group * 4,
        "back_remote",
        {n_in + i: i for i in range(len(before))},
        2,
    )
    return call(info, flags, *operands, *turns, *keys, kept, *before)


def back_local(info, flags, operands, turns, keys, dq, kept, group, first, count, before):
    width, n_q = operands[0].shape
    half = HEAD_DIM // 2
    n_in = 2 + len(operands) + len(turns) + len(keys) + 2
    call = attention_call(
        functools.partial(bwd_local_kernel, group, first),
        count,
        [rows_of(n_q, first)] * 3
        + [stats_of(n_q, first), rows_of(n_q, first), stats_of(n_q, first)]
        + [whole((half, n_q))] * 2
        + [rows_of(n_q, first)] * 3
        + [kept_of(kept.shape[1], group, first)]
        + [pl.BlockSpec(memory_space=pl.ANY)] * len(before),
        planes_of(3, n_q, first),
        jax.ShapeDtypeStruct((3, width, n_q), bf16),
        back_scratch(n_q, n_q) + [pltpu.VMEM((PAIR, n_q), f32)],
        10 * count * PAIR * 2 * group * group * 4,
        "back_local",
        {n_in + i: i for i in range(len(before))},
        2,
    )
    return call(info, flags, *operands, *turns, *keys, dq, kept, *before)


def normalize(values):
    centre = values - jnp.mean(values, axis=-1, keepdims=True)
    spread = jnp.mean(centre * centre, axis=-1, keepdims=True)
    rate = lax.rsqrt(spread + EPS)
    return centre * rate, rate


def norm_back(grad, unit, rate, gain):
    scaled = grad * gain
    first = jnp.mean(scaled, axis=-1, keepdims=True)
    second = jnp.mean(scaled * unit, axis=-1, keepdims=True)
    return rate * (scaled - first - unit * second)


GELU_A = 0.7978845608028654
GELU_B = 0.044715


def column_sum(values):
    return jnp.sum(values, axis=0, keepdims=True)


def block_kernel(
    span,
    oT,
    lse,
    tokens,
    cotangent,
    w_out,
    w_up,
    w_down,
    b_out,
    b_up,
    b_down,
    gain_two,
    shift_two,
    gain_three,
    shift_three,
    gain_four,
    shift_four,
    result,
    d_middle_out,
    hidden_out,
    d_outer_out,
    normed_out,
    d_inner_out,
    d_branch_out,
    doT,
    scaled,
    delta,
    small,
    small_up,
    slope,
):
    step = pl.program_id(0)

    @pl.when(step == 0)
    def _():
        small[...] = jnp.zeros(small.shape, f32)
        small_up[...] = jnp.zeros(small_up.shape, f32)

    wide = w_up.shape[1]
    branch = dot(oT[...], w_out[...], 0, 0) + b_out[...]
    unit_two, rate_two = normalize(branch)
    middle = tokens[...].astype(f32) + (unit_two * gain_two[...] + shift_two[...])
    unit_three, rate_three = normalize(middle)
    normed = (unit_three * gain_three[...] + shift_three[...]).astype(bf16)
    normed_out[...] = normed
    outer = None
    for c in range(wide // span):
        columns = slice(c * span, (c + 1) * span)
        inner = dot(normed, w_up[:, columns], 1, 0) + b_up[:, columns]
        square = inner * inner
        bend = jnp.tanh(inner * (GELU_A + (GELU_A * GELU_B) * square))
        half = 0.5 + 0.5 * bend
        hidden = (inner * half).astype(bf16)
        hidden_out[:, columns] = hidden
        slope[:, columns] = half + inner * (1.0 - bend * bend) * (
            0.5 * GELU_A + (1.5 * GELU_A * GELU_B) * square
        )
        term = dot(hidden, w_down[columns, :], 1, 0)
        outer = term if outer is None else outer + term
    unit_four, rate_four = normalize(outer + b_down[...])
    result[...] = (middle + (unit_four * gain_four[...] + shift_four[...])).astype(bf16)

    grad = cotangent[...].astype(f32)
    d_outer = norm_back(grad, unit_four, rate_four, gain_four[...]).astype(bf16)
    d_outer_out[...] = d_outer
    small[0:1, :] += column_sum(grad * unit_four)
    small[1:2, :] += column_sum(grad)
    small[2:3, :] += column_sum(d_outer.astype(f32))
    d_normed = None
    for c in range(wide // span):
        columns = slice(c * span, (c + 1) * span)
        d_hidden = dot(d_outer, w_down[columns, :], 1, 1)
        d_inner = (d_hidden * slope[:, columns]).astype(bf16)
        d_inner_out[:, columns] = d_inner
        small_up[:, columns] += column_sum(d_inner.astype(f32))
        term = dot(d_inner, w_up[:, columns], 1, 1)
        d_normed = term if d_normed is None else d_normed + term
    small[3:4, :] += column_sum(d_normed * unit_three)
    small[4:5, :] += column_sum(d_normed)
    d_middle = grad + norm_back(d_normed, unit_three, rate_three, gain_three[...])
    d_middle_out[...] = d_middle
    small[5:6, :] += column_sum(d_middle * unit_two)
    small[6:7, :] += column_sum(d_middle)
    d_branch = norm_back(d_middle, unit_two, rate_two, gain_two[...]).astype(bf16)
    d_branch_out[...] = d_branch
    small[7:8, :] += column_sum(d_branch.astype(f32))
    d_attended = dot(w_out[...], d_branch, 1, 1).astype(bf16)
    doT[...] = d_attended
    for h in range(oT.shape[0] // HEAD_DIM):
        rows = slice(HEAD_DIM * h, HEAD_DIM * (h + 1))
        at = slice(h % 2, h % 2 + 1)
        part = (d_attended[rows].astype(f32) * jnp.exp2(-lse[h // 2, at, :])).astype(bf16)
        scaled[rows, :] = part
        delta[h // 2, at, :] = column_sum(part.astype(f32) * oT[rows, :].astype(f32))


def block_call(oT, lse, tokens, cotangent, weights, vectors):
    width, rows = oT.shape
    wide = weights[1].shape[1]
    step = min(256, rows)
    span = min(SPAN, wide)

    def lines(count):
        return pl.BlockSpec((step, count), lambda i: (i, 0))

    def fixed(shape):
        return pl.BlockSpec(shape, lambda i: (0, 0), pipeline_mode=pl.Buffered(1))

    def total(shape):
        return pl.BlockSpec(shape, lambda i: (0, 0))

    features = pl.BlockSpec((width, step), lambda i: (0, i))
    stats = pl.BlockSpec((*lse.shape[:2], step), lambda i: (0, 0, i))
    sizes = [width, width, wide, width, width, wide, width]
    kinds = [bf16, f32, bf16, bf16, bf16, bf16, bf16]
    return pl.pallas_call(
        functools.partial(block_kernel, span),
        grid=(rows // step,),
        in_specs=[features, stats, lines(width), lines(width)]
        + [fixed(item.shape) for item in weights]
        + [fixed(item.shape) for item in vectors],
        out_specs=[lines(size) for size in sizes]
        + [features, features, stats, total((8, width)), total((1, wide))],
        out_shape=[jax.ShapeDtypeStruct((rows, size), kind) for size, kind in zip(sizes, kinds)]
        + [
            jax.ShapeDtypeStruct((width, rows), bf16),
            jax.ShapeDtypeStruct((width, rows), bf16),
            jax.ShapeDtypeStruct(lse.shape, f32),
            jax.ShapeDtypeStruct((8, width), f32),
            jax.ShapeDtypeStruct((1, wide), f32),
        ],
        scratch_shapes=[pltpu.VMEM((step, wide), f32)],
        compiler_params=pltpu.CompilerParams(vmem_limit_bytes=VMEM),
        cost_estimate=pl.CostEstimate(
            flops=2 * 2 * rows * (width * width + 2 * width * wide),
            bytes_accessed=1 << 26,
            transcendentals=rows * wide,
        ),
        name="block",
    )(oT, lse, tokens, cotangent, *weights, *vectors)


def turn(values, cosine, sine):
    half = HEAD_DIM // 2
    first, second = values[:half], values[half:]
    return jnp.concatenate(
        [first * cosine - second * sine, second * cosine + first * sine], axis=0
    )


def project_kernel(sections, tokens, w, b, gain, shift, cosine, sine, normed_out, *outs):
    unit, rate = normalize(tokens[...].astype(f32))
    normed = (unit * gain[...] + shift[...]).astype(bf16)
    normed_out[...] = normed
    width = tokens.shape[1]
    chunk = min(256, width)
    for section, out in zip(sections, outs):
        for c in range(width // chunk):
            at = section * width + c * chunk
            mixed = (dot(normed, w[:, at : at + chunk], 1, 0) + b[:, at : at + chunk]).T
            for h in range(chunk // HEAD_DIM):
                rows = slice(h * HEAD_DIM, (h + 1) * HEAD_DIM)
                place = slice(c * chunk + h * HEAD_DIM, c * chunk + (h + 1) * HEAD_DIM)
                value = mixed[rows]
                if section < 2:
                    value = turn(value, cosine[...], sine[...])
                if section == 0:
                    value = value * (0.125 * LOG2E)
                out[place, :] = value.astype(bf16)


def project(tokens, w, b, gain, shift, cosine, sine, sections):
    rows, width = tokens.shape
    step = min(512, rows)
    half = HEAD_DIM // 2

    def fixed(shape):
        return pl.BlockSpec(shape, lambda i: (0, 0), pipeline_mode=pl.Buffered(1))

    lines = pl.BlockSpec((step, width), lambda i: (i, 0))
    features = pl.BlockSpec((width, step), lambda i: (0, i))
    turns = pl.BlockSpec((half, step), lambda i: (0, i))
    return pl.pallas_call(
        functools.partial(project_kernel, sections),
        grid=(rows // step,),
        in_specs=[lines, fixed(w.shape), fixed(b.shape), fixed(gain.shape), fixed(shift.shape)]
        + [turns] * 2,
        out_specs=[lines] + [features] * len(sections),
        out_shape=[jax.ShapeDtypeStruct((rows, width), bf16)]
        + [jax.ShapeDtypeStruct((width, rows), bf16)] * len(sections),
        compiler_params=pltpu.CompilerParams(vmem_limit_bytes=VMEM),
        cost_estimate=pl.CostEstimate(
            flops=2 * rows * width * width * len(sections),
            bytes_accessed=1 << 24,
            transcendentals=0,
        ),
        name="project",
    )(tokens, w, b, gain, shift, cosine, sine)


def unproject_kernel(planes, finish, *refs):
    d_mixed, w, out = refs[: len(planes)], refs[len(planes)], refs[-1]
    width = w.shape[0]
    total = None
    for plane, ref in zip(planes, d_mixed):
        term = dot(ref[0], w[:, plane * width : (plane + 1) * width], 0, 1)
        total = term if total is None else total + term
    if not finish:
        out[...] = total.astype(bf16)
        return
    returned, tokens, d_middle, gain = refs[len(planes) + 1 : len(planes) + 5]
    total = total + returned[...].astype(f32)
    unit, rate = normalize(tokens[...].astype(f32))
    out[...] = (d_middle[...] + norm_back(total, unit, rate, gain[...])).astype(bf16)


def unproject(d_mixed, w, planes, start, count, finish=(), before=()):
    _, width, total = d_mixed.shape
    step = min(256, count)
    first = start // step

    def fixed(shape):
        return pl.BlockSpec(shape, lambda i: (0, 0), pipeline_mode=pl.Buffered(1))

    def plane_of(plane):
        return pl.BlockSpec((1, width, step), lambda i: (plane, 0, first + i))

    lines = pl.BlockSpec((step, width), lambda i: (i, 0))
    later = pl.BlockSpec((step, width), lambda i: (first + i, 0))
    specs = [later] * 3 + [fixed(finish[-1].shape)] if finish else []
    n_in = len(planes) + 1 + len(finish)
    return pl.pallas_call(
        functools.partial(unproject_kernel, planes, bool(finish)),
        grid=(count // step,),
        in_specs=[plane_of(plane) for plane in planes]
        + [fixed(w.shape)]
        + specs
        + [pl.BlockSpec(memory_space=pl.ANY)] * len(before),
        out_specs=later if finish else lines,
        out_shape=jax.ShapeDtypeStruct((total if finish else count, width), bf16),
        input_output_aliases={n_in + i: i for i in range(len(before))},
        compiler_params=pltpu.CompilerParams(vmem_limit_bytes=VMEM),
        cost_estimate=pl.CostEstimate(
            flops=2 * count * width * width * len(planes),
            bytes_accessed=1 << 24,
            transcendentals=0,
        ),
        name="unproject",
    )(*[d_mixed] * len(planes), w, *finish, *before)


def divide(total, run, levels, near, marks, orders, outs):
    bits = [("narrow", i) for i in range(near)] + [("wide", i) for i in range(levels + 1)]
    cut = run // len(orders)

    def write(core):
        for at in range(0, total.shape[0], run):
            number = at // run
            value = {}
            for place, (axis, position) in enumerate(bits):
                mine = (marks[1 if axis == "narrow" else 0] >> position) & 1
                value[axis, position] = mine ^ ((number >> place) & 1)
            other = core ^ ((number >> near) & 1)
            for i, order in enumerate(orders):
                index = tuple(value.get(bit, 0) for bit in order)
                part = total[at + i * cut : at + (i + 1) * cut]
                outs[2 * i + other][index] = part.astype(bf16)

    pl.when((marks[0] & 1) == 0)(functools.partial(write, 0))
    pl.when((marks[0] & 1) == 1)(functools.partial(write, 1))


def divided(orders, levels, run, height, wide, width):
    cut = run // len(orders)
    specs, shapes = [], []
    for order in orders:

        def held(bit):
            return bit[0] == "narrow" or bit[1] <= levels

        def index(j, i, marks, order=order):
            relative = i ^ (marks[0] >> (levels + 1))
            at = [0 if held(bit) else (relative >> (bit[1] - 1 - levels)) & 1 for bit in order]
            return (*at, 0, j)

        block = tuple(2 if held(bit) else 1 for bit in order) + (cut, wide)
        specs += [pl.BlockSpec(block, index)] * 2
        shapes += [jax.ShapeDtypeStruct((2,) * len(order) + (cut, width), bf16)] * 2
    return specs, shapes


def outer_kernel(run, levels, near, orders, right_dim, marks, left, right, *outs):
    divide(dot(left[...], right[...], 0, right_dim), run, levels, near, marks, orders, outs)


def outer_halves(marks, left, right, right_dim, cores, parts, order):
    rows, height = left.shape
    width = right.shape[1 - right_dim]
    share = height // cores
    high = max(2 * share, min(1024, height))
    levels = (high // (2 * share)).bit_length() - 1
    wide = min(1024, width)
    if right_dim == 0:
        right_spec = pl.BlockSpec((rows, wide), lambda j, i, marks: (0, j))
    else:
        right_spec = pl.BlockSpec((wide, rows), lambda j, i, marks: (j, 0))
    run = share // parts
    near = parts.bit_length() - 1
    specs, shapes = divided([order], levels, run, height, wide, width)
    halves = pl.pallas_call(
        functools.partial(outer_kernel, run, levels, near, [order], right_dim),
        grid_spec=pltpu.PrefetchScalarGridSpec(
            num_scalar_prefetch=1,
            grid=(width // wide, height // high),
            in_specs=[pl.BlockSpec((rows, high), lambda j, i, marks: (0, i)), right_spec],
            out_specs=specs,
        ),
        out_shape=shapes,
        compiler_params=pltpu.CompilerParams(vmem_limit_bytes=VMEM),
        cost_estimate=pl.CostEstimate(
            flops=2 * rows * height * width, bytes_accessed=1 << 25, transcendentals=0
        ),
        name="outer",
    )(marks, left, right)
    return [item.reshape(height // 2, width) for item in halves]


def mixed_kernel(
    run,
    levels,
    near,
    orders,
    first_far,
    marks,
    d_own,
    d_far,
    normed,
    normed_far,
    w,
    gain,
    shift,
    *outs,
):
    *halves, small, sums, bias = outs
    step, last = pl.program_id(1), pl.num_programs(1) - 1
    total = dot(d_own[...], normed[...], 1, 0)
    bias[...] = jnp.sum(d_own[...].astype(f32), axis=1, keepdims=True)

    @pl.when(step == 0)
    def _():
        sums[...] = jnp.zeros(sums.shape, f32)
        small[...] = jnp.zeros(small.shape, f32)

    def finish(value):
        divide(value, run, levels, near, marks, orders, halves)
        weights = w[...].astype(f32).T
        sums[0:1, :] += column_sum(weights * value)
        sums[1:2, :] += column_sum(weights * bias[...])
        wide = jnp.broadcast_to(bias[...], (bias.shape[0], PAIR)).T
        small[pl.ds(step, 1), : bias.shape[0]] = wide[0:1, :]

    @pl.when(step < first_far)
    def _():
        finish(total)

    @pl.when(step >= first_far)
    def _():
        bias[...] += jnp.sum(d_far[...].astype(f32), axis=1, keepdims=True)
        finish(total + dot(d_far[...], normed_far[...], 1, 0))

    @pl.when(step == last)
    def _():
        small[pl.ds(last + 1, 1), :] = (sums[0:1, :] - shift[...] * sums[1:2, :]) / gain[...]
        small[pl.ds(last + 2, 1), :] = sums[1:2, :]


def mixed_halves(marks, d_own, d_far, normed, normed_far, w, gain, shift, cores, parts, orders):
    height, rows = d_own.shape
    far = d_far.shape[1]
    width = normed.shape[1]
    share = height // cores
    pairs = max(1, 768 // (2 * share))
    levels = pairs.bit_length() - 1
    high = 2 * share * pairs
    first_far = width // high
    run = share // parts
    near = parts.bit_length() - 1
    steps = height // high

    def fixed(shape):
        return pl.BlockSpec(shape, lambda j, i, marks: (0, 0), pipeline_mode=pl.Buffered(1))

    specs, shapes = divided(orders, levels, run, height, width, width)
    *halves, small = pl.pallas_call(
        functools.partial(mixed_kernel, run, levels, near, orders, first_far),
        grid_spec=pltpu.PrefetchScalarGridSpec(
            num_scalar_prefetch=1,
            grid=(1, steps),
            in_specs=[
                pl.BlockSpec((high, rows), lambda j, i, marks: (i, 0)),
                pl.BlockSpec((high, far), lambda j, i, marks: (jnp.maximum(i, first_far), 0)),
                fixed(normed.shape),
                fixed(normed_far.shape),
                pl.BlockSpec((width, high), lambda j, i, marks: (0, i)),
                fixed(gain.shape),
                fixed(shift.shape),
            ],
            out_specs=specs + [pl.BlockSpec((16, width), lambda j, i, marks: (0, 0))],
            scratch_shapes=[pltpu.VMEM((2, width), f32), pltpu.VMEM((high, 1), f32)],
        ),
        out_shape=shapes + [jax.ShapeDtypeStruct((16, width), f32)],
        compiler_params=pltpu.CompilerParams(vmem_limit_bytes=VMEM),
        cost_estimate=pl.CostEstimate(
            flops=2 * (rows + far) * height * width, bytes_accessed=1 << 25, transcendentals=0
        ),
        name="mixed",
    )(marks, d_own, d_far, normed, normed_far, w, gain, shift)
    halves = [item.reshape(-1, width) for item in halves]
    return [halves[i : i + 2] for i in range(0, len(halves), 2)], small, steps


def bit_of(axis, position):
    return (lax.axis_index(axis) >> position) & 1


def swap(values, axis, position):
    size = lax.axis_size(axis)
    return lax.ppermute(values, axis, [(i, i ^ (1 << position)) for i in range(size)])


class Halving:
    def __init__(self, halves, order):
        self.order = list(order)
        kept, given = halves
        self.height = kept.shape[0]
        self.terms = [kept, swap(given, "wide", 0)]

    def send(self, away):
        self.terms = self.terms + [swap(away, *self.order.pop(0))]
        self.height //= 2

    def blocks(self, height, grid, which):
        width = self.terms[0].shape[1]
        spec = pl.BlockSpec((1, height // grid, width), lambda i: (which, i, 0))
        return [term.reshape(-1, height, width) for term in self.terms], [spec] * len(self.terms)


class Adding:
    def __init__(self, array, order):
        self.order = list(order)
        self.terms = [array, swap(array, *self.order.pop(0))]

    def send(self, total):
        self.terms = [total, swap(total, *self.order.pop(0))]


def halve_kernel(counts, *refs):
    ins, outs = refs[: sum(counts) + 2], refs[sum(counts) + 2 :]
    at = 0
    for count, out in zip(counts, outs):
        parts = [ref[0].astype(f32) for ref in ins[at : at + count]]
        out[...] = functools.reduce(jnp.add, parts).astype(bf16)
        at += count
    outs[-1][...] = ins[-2][...] + ins[-1][...]


def halve(sums, small):
    heights = [item.height // 2 for item in sums]
    grid = 4 if all(height % 64 == 0 for height in heights) else 1
    operands, in_specs, out_specs, out_shape = [], [], [], []
    for item, height in zip(sums, heights):
        arrays, specs = item.blocks(height, grid, 1)
        operands += arrays
        in_specs += specs
        width = arrays[0].shape[2]
        out_specs.append(pl.BlockSpec((height // grid, width), lambda i: (i, 0)))
        out_shape.append(jax.ShapeDtypeStruct((height, width), bf16))
    whole_small = pl.BlockSpec(small.terms[0].shape, lambda i: (0, 0))
    return pl.pallas_call(
        functools.partial(halve_kernel, [len(item.terms) for item in sums]),
        grid=(grid,),
        in_specs=in_specs + [whole_small] * 2,
        out_specs=out_specs + [whole_small],
        out_shape=out_shape + [jax.ShapeDtypeStruct(small.terms[0].shape, f32)],
        compiler_params=pltpu.CompilerParams(vmem_limit_bytes=VMEM),
        name="halve",
    )(*operands, *small.terms)


def launch(lead, sums, small, *others):
    lead, others, halves = lax.optimization_barrier((lead, others, halve(sums, small)))
    for item, away in zip(sums, halves):
        item.send(away)
    small.send(halves[-1])
    return (lead, *others)


def settle(lead, sums, small):
    everything = sums + [small]
    lead, terms = lax.optimization_barrier((lead, [item.terms for item in everything]))
    for item, arrays in zip(everything, terms):
        item.terms = list(arrays)
    return lead


def collect_kernel(counts, *refs):
    at = 0
    for count, out in zip(counts, refs[sum(counts) :]):
        out[...] = functools.reduce(jnp.add, [ref[0].astype(f32) for ref in refs[at : at + count]])
        at += count


def collect(sums):
    operands, in_specs, out_specs, out_shape = [], [], [], []
    for item in sums:
        arrays, specs = item.blocks(item.height, 1, 0)
        operands += arrays
        in_specs += specs
        shape = arrays[0].shape[1:]
        out_specs.append(pl.BlockSpec(shape, lambda i: (0, 0)))
        out_shape.append(jax.ShapeDtypeStruct(shape, f32))
    return pl.pallas_call(
        functools.partial(collect_kernel, [len(item.terms) for item in sums]),
        grid=(1,),
        in_specs=in_specs,
        out_specs=out_specs,
        out_shape=out_shape,
        compiler_params=pltpu.CompilerParams(vmem_limit_bytes=VMEM),
        name="collect",
    )(*operands)


def read_small(ref, at, rows):
    parts = [ref[at + i * rows : at + (i + 1) * rows, :].astype(f32) for i in range(3)]
    return parts[0] + parts[1] + parts[2]


def joint_kernel(plan, last, *refs):
    count, buffers, from_at, small_from, to_at, small_to, rows = plan
    arrays, refs = refs[:count], refs[count:]
    received, refs = refs[:buffers], refs[buffers:]
    small, refs = refs[0], refs[1:]
    if small_from is None:
        total = small[...] + refs[0][...]
        refs = refs[1:]
    else:
        total = small[...] + read_small(received[small_from[0]], small_from[1], rows)
    if last:
        out, small_out = refs
        for i in range(count):
            which, at = from_at[i]
            height = arrays[i].shape[0]
            part = received[which][at : at + height, :].astype(f32)
            out[i * height : (i + 1) * height, :] = arrays[i][...].astype(f32) + part
        small_out[...] = total
        return
    outs, sent, small_out = refs[:count], refs[count:-1], refs[-1]
    for i in range(count):
        which, at = from_at[i]
        height = arrays[i].shape[0] // 2
        for half in range(2):
            here = slice(half * height, (half + 1) * height)
            there = slice(at + half * height, at + (half + 1) * height)
            part = arrays[i][here, :].astype(f32) + received[which][there, :].astype(f32)
            if half:
                which_out, at_out = to_at[i]
                sent[which_out][at_out : at_out + height, :] = part.astype(bf16)
            else:
                outs[i][...] = part.astype(bf16)
    small_out[...] = total
    which_out, at_out = small_to
    for part in split_three(total):
        sent[which_out][at_out : at_out + rows, :] = part.astype(bf16)
        at_out += rows


class Joint:
    def __init__(self, halves, orders, small):
        self.arrays = [kept for kept, _ in halves]
        self.received = [swap(given, "wide", 0) for _, given in halves]
        self.from_at = [(i, 0) for i in range(len(halves))]
        self.orders = [list(order) for order in orders]
        self.small, self.small_from = small, None
        self.extra = [swap(small, "wide", 0)]

    def call(self, plan, last, shapes):
        return pl.pallas_call(
            functools.partial(joint_kernel, plan, last),
            out_shape=shapes,
            compiler_params=pltpu.CompilerParams(vmem_limit_bytes=VMEM),
            name="joint",
        )(*self.arrays, *self.received, self.small, *self.extra)

    def plan(self, to_at, small_to):
        buffers, rows = len(self.received), self.small.shape[0]
        count = len(self.arrays)
        return count, buffers, self.from_at, self.small_from, to_at, small_to, rows

    def step(self, lead, *others):
        bits, heights, to_at = [], [], []
        width = self.arrays[0].shape[1]
        for array, order in zip(self.arrays, self.orders):
            bit = order.pop(0)
            if bit not in bits:
                bits.append(bit)
                heights.append(0)
            which = bits.index(bit)
            to_at.append((which, heights[which]))
            heights[which] += array.shape[0] // 2
        small_to = (0, heights[0])
        heights[0] += 3 * self.small.shape[0]
        shapes = [
            jax.ShapeDtypeStruct((array.shape[0] // 2, width), bf16) for array in self.arrays
        ]
        shapes += [jax.ShapeDtypeStruct((height, width), bf16) for height in heights]
        shapes += [jax.ShapeDtypeStruct(self.small.shape, f32)]
        outs = self.call(self.plan(to_at, small_to), False, shapes)
        lead, others, outs = lax.optimization_barrier((lead, others, outs))
        count = len(self.arrays)
        self.arrays, sent, self.small = outs[:count], outs[count:-1], outs[-1]
        self.received = [swap(item, *bit) for item, bit in zip(sent, bits)]
        self.from_at, self.small_from, self.extra = to_at, small_to, []
        return (lead, *others)

    def result(self):
        height = sum(array.shape[0] for array in self.arrays)
        shapes = [
            jax.ShapeDtypeStruct((height, self.arrays[0].shape[1]), f32),
            jax.ShapeDtypeStruct(self.small.shape, f32),
        ]
        return self.call(self.plan([], None), True, shapes)


def angles(positions):
    half = HEAD_DIM // 2
    freqs = jnp.power(10000.0, -jnp.arange(half, dtype=f32) / half)
    theta = freqs[:, None] * positions.astype(f32)[None, :]
    return jnp.cos(theta), jnp.sin(theta)


def axis_bits(axis):
    return [(axis, position) for position in range(lax.axis_size(axis).bit_length() - 1)]


def body(
    inputs,
    cotangent,
    lengths,
    w_qkv,
    b_qkv,
    w_out,
    b_out,
    w_up,
    b_up,
    w_down,
    b_down,
    gain_one,
    shift_one,
    gain_two,
    shift_two,
    gain_three,
    shift_three,
    gain_four,
    shift_four,
):
    group = inputs.shape[3]
    width = inputs.shape[4]
    parts = lax.axis_size("narrow")
    place = lax.axis_index("narrow")
    cores = lax.axis_size("wide")
    others = parts - 1
    rows = 2 * group
    offsets = jnp.arange(group, dtype=jnp.int32)

    def row(vector):
        return vector[None, :]

    def positions(owners):
        starts = jnp.stack([owners, 2 * parts - 1 - owners], axis=1).reshape(-1) * group
        return (starts[:, None] + offsets[None]).reshape(-1)

    def joined(items):
        return jnp.concatenate(items, axis=0) if len(items) > 1 else items[0]

    tokens = inputs.reshape(rows, width)
    far_tokens = joined(
        [
            lax.ppermute(tokens, "narrow", [((n + shift) % parts, n) for n in range(parts)])
            for shift in range(1, parts)
        ]
    )
    other = (place + 1 + jnp.arange(others, dtype=jnp.int32)) % parts
    early_at = place * group
    late_at = (2 * parts - 1 - place) * group
    info = jnp.stack([place, lengths[0], early_at, late_at]).astype(jnp.int32)
    marks = jnp.stack([lax.axis_index("wide"), place]).astype(jnp.int32)
    turns = angles(positions(place[None]))
    turns_far = angles(positions(other))

    norm_one = [row(gain_one), row(shift_one)]
    normed, qT, kT, vT = project(tokens, w_qkv, row(b_qkv), *norm_one, *turns, (0, 1, 2))
    state, kept_own, flags_own = attend_local(info, qT, kT, vT, group)
    normed_far, kT_far, vT_far = project(
        far_tokens, w_qkv, row(b_qkv), *norm_one, *turns_far, (1, 2)
    )
    oT, lse, kept_far, flags_far = attend_remote(
        info, qT, kT_far, vT_far, state, group, parts
    )

    blocks = block_call(
        oT,
        lse,
        tokens,
        cotangent.reshape(rows, width),
        [w_out, w_up, w_down],
        [row(item) for item in (b_out, b_up, b_down)]
        + [row(item) for item in (gain_two, shift_two, gain_three, shift_three)]
        + [row(item) for item in (gain_four, shift_four)],
    )
    result, d_middle, hidden, d_outer, normed_two, d_inner, d_branch = blocks[:7]
    doT, scaled, delta, small, small_up = blocks[7:]

    wide_bits = axis_bits("wide")
    narrow_bits = axis_bits("narrow")
    first_order = wide_bits[1:2] + narrow_bits + wide_bits[2:]
    second_order = narrow_bits + wide_bits[1:]
    third_order = narrow_bits + wide_bits[2:3] + wide_bits[1:2] + wide_bits[3:]
    fourth_order = wide_bits[2:3] + wide_bits[1:2] + narrow_bits + wide_bits[3:]
    small_order = wide_bits[:1] + first_order

    def outer(left, right, right_dim, order):
        return Halving(outer_halves(marks, left, right, right_dim, cores, parts, order), order)

    sum_up = outer(d_inner, normed_two, 0, first_order)
    sum_down = outer(d_outer, hidden, 0, second_order)
    sum_out = outer(d_branch, oT, 1, fourth_order)
    flat = jnp.concatenate([small.reshape(-1), small_up.reshape(-1)])
    early = Adding(flat.reshape(-1, PAIR), small_order)
    sums = [sum_down, sum_up, sum_out]

    heads = width // PAIR
    portions = 2 if heads % 2 == 0 else 1
    count = heads // portions
    (doT,) = launch(doT, sums, early)
    dq_far, d_far = back_remote(
        info,
        flags_far,
        [qT, doT, oT, lse, scaled, delta],
        turns_far,
        [kT_far, vT_far],
        kept_far,
        group,
        parts,
        0,
        heads,
        [],
    )
    d_back = unproject(d_far, w_qkv, (1, 2), 0, others * rows)
    d_mixed = []
    for portion in range(portions):
        doT, d_back = launch(doT, sums, early, d_back)
        if not portion:
            returned = [
                lax.ppermute(
                    d_back[j * rows : (j + 1) * rows] if others > 1 else d_back,
                    "narrow",
                    [(n, (n + j + 1) % parts) for n in range(parts)],
                )
                for j in range(others)
            ]
        d_mixed = [
            back_local(
                info,
                flags_own,
                [qT, doT, oT, lse, scaled, delta],
                turns,
                [kT, vT],
                dq_far,
                kept_own,
                group,
                portion * count,
                count,
                d_mixed,
            )
        ]
    d_mixed = d_mixed[0]
    while early.order:
        (d_mixed,) = launch(d_mixed, sums, early)
    d_mixed, returned = lax.optimization_barrier((d_mixed, returned))
    if others > 1:
        returned = [functools.reduce(jnp.add, [item.astype(f32) for item in returned])]

    orders = [first_order, third_order, fourth_order]
    pieces, late, steps = mixed_halves(
        marks,
        d_mixed.reshape(3 * width, rows),
        d_far.reshape(3 * width, -1),
        normed,
        normed_far,
        w_qkv,
        *norm_one,
        cores,
        parts,
        orders,
    )
    late, pieces = settle((late, pieces), sums, early)
    tail = Joint(pieces, orders, late)
    (d_mixed,) = tail.step(d_mixed)
    d_tokens = []
    for i in range(2):
        finish = (returned[0], tokens, d_middle, row(gain_one))
        d_tokens = [
            unproject(d_mixed, w_qkv, (0, 1, 2), i * group, group, finish, d_tokens)
        ]
        if tail.orders[0]:
            d_mixed, d_tokens[0] = tail.step(d_mixed, d_tokens[0])
    while tail.orders[0]:
        d_tokens[0], *terms = tail.step(d_tokens[0], *[item.terms for item in sums])
        for item, arrays in zip(sums, terms):
            item.terms = list(arrays)

    sum_w_down, sum_w_up, sum_w_out = collect(sums)
    sum_w_qkv, late_small = tail.result()
    grad_b_qkv = late_small[:steps, : 3 * width // steps].reshape(-1)
    early_small = (early.terms[0] + early.terms[1]).reshape(-1)
    small = early_small[: 8 * width].reshape(8, width)
    small_up = early_small[8 * width :]
    shape = inputs.shape
    return (
        result.reshape(shape),
        d_tokens[0].reshape(shape),
        sum_w_qkv.T,
        sum_w_out.T,
        sum_w_up.T,
        sum_w_down.T,
        grad_b_qkv,
        small[7],
        small_up,
        small[2],
        late_small[steps],
        late_small[steps + 1],
        small[5],
        small[6],
        small[3],
        small[4],
        small[0],
        small[1],
    )


def solution(mesh):
    tokens = P("wide", None, "narrow", None, None)
    columns = P(None, ("wide", "narrow"))
    in_specs = (tokens, tokens, P("wide")) + (P(),) * 16
    out_specs = (tokens, tokens) + (columns,) * 4 + (P(),) * 12
    return jax.shard_map(body, mesh=mesh, in_specs=in_specs, out_specs=out_specs, check_vma=False)
```

```python
import functools

import jax
import jax.numpy as jnp
from jax import lax
from jax.experimental import pallas as pl
from jax.experimental.pallas import tpu as pltpu
from jax.sharding import PartitionSpec as P

HEAD_DIM = 64
PAIR = 2 * HEAD_DIM
EPS = 1e-05
LOG2E = 1.4426950408889634
LN2 = 0.6931471805599453
NEG = -1e30
REACH = 60.0
VMEM = 62 * 1024 * 1024
SPAN = 1024

f32 = jnp.float32
bf16 = jnp.bfloat16


def dot(left, right, left_dim, right_dim):
    return lax.dot_general(
        left, right, (((left_dim,), (right_dim,)), ((), ())), preferred_element_type=f32
    )


def bounded(qT, kT):
    worst = None
    for h in range(2):
        rows = slice(HEAD_DIM * h, HEAD_DIM * (h + 1))
        norms = []
        for item in (qT, kT):
            values = item[rows, :].astype(f32)
            norms.append(jnp.max(jnp.sum(values * values, axis=0, keepdims=True)))
        both = norms[0] * norms[1]
        worst = both if worst is None else jnp.maximum(worst, both)
    return worst <= REACH * REACH


def fwd_chunk(fast, q0, k0, q_n, k_n, limit, store, qT, kT, vT, m_ref, l_ref, acc):
    queries = pl.ds(q0, q_n)
    strip = min(256, k_n)
    for h in range(2):
        rows = slice(HEAD_DIM * h, HEAD_DIM * (h + 1))
        old = m_ref[h : h + 1, queries]
        new = jnp.zeros_like(old) if fast else old
        strips = []
        for j in range(k_n // strip):
            keys = pl.ds(k0 + j * strip, strip)
            scores = dot(kT[rows, keys], qT[rows, queries], 0, 0)
            if limit is not None:
                key_at = lax.broadcasted_iota(jnp.int32, (strip, q_n), 0)
                scores = jnp.where(key_at < limit - j * strip, scores, NEG)
            strips.append(scores)
            if not fast:
                new = jnp.maximum(new, jnp.max(scores, axis=0, keepdims=True))
        factor = jnp.exp2(old - new)
        total = l_ref[h : h + 1, queries] * factor
        value = acc[rows, queries] * factor
        for j in range(k_n // strip):
            keys = pl.ds(k0 + j * strip, strip)
            weights = jnp.exp2(strips[j] if fast else strips[j] - new)
            total = total + jnp.sum(weights, axis=0, keepdims=True)
            weights = weights.astype(bf16)
            if fast:
                store(h, j, weights)
            value = value + dot(vT[rows, keys], weights, 1, 0)
        m_ref[h : h + 1, queries] = new
        l_ref[h : h + 1, queries] = total
        acc[rows, queries] = value


def pad_left(values, count):
    if not count:
        return values
    return jnp.concatenate([jnp.zeros((values.shape[0], count), f32), values], axis=1)


def pad_right(values, count):
    if not count:
        return values
    return jnp.concatenate([values, jnp.zeros((values.shape[0], count), f32)], axis=1)


def fwd_diagonal(fast, base, group, limit, store, qT, kT, vT, m_ref, l_ref, acc):
    strip = min(256, group)
    count = group // strip
    for h in range(2):
        rows = slice(HEAD_DIM * h, HEAD_DIM * (h + 1))
        strips = []
        for j in range(count):
            wide = group - j * strip
            keys, queries = pl.ds(base + j * strip, strip), pl.ds(base + j * strip, wide)
            scores = dot(kT[rows, keys], qT[rows, queries], 0, 0)
            key_at = lax.broadcasted_iota(jnp.int32, scores.shape, 0)
            query_at = lax.broadcasted_iota(jnp.int32, scores.shape, 1)
            scores = jnp.where(key_at <= query_at, scores, NEG)
            if limit is not None:
                scores = jnp.where(key_at < limit - j * strip, scores, NEG)
            strips.append(scores)
        peaks = []
        for g in range(0 if fast else count):
            peak = None
            for j in range(g + 1):
                part = strips[j][:, (g - j) * strip : (g - j + 1) * strip]
                part = jnp.max(part, axis=0, keepdims=True)
                peak = part if peak is None else jnp.maximum(peak, part)
            peaks.append(peak)
        if fast:
            peak = jnp.zeros((1, group), f32)
        else:
            peak = jnp.concatenate(peaks, axis=1) if count > 1 else peaks[0]
        total, value = None, None
        for j in range(count):
            keys = pl.ds(base + j * strip, strip)
            weights = jnp.exp2(strips[j] if fast else strips[j] - peak[:, j * strip :])
            part = pad_left(jnp.sum(weights, axis=0, keepdims=True), j * strip)
            weights = weights.astype(bf16)
            if fast:
                store(h, j, weights)
            term = pad_left(dot(vT[rows, keys], weights, 1, 0), j * strip)
            total = part if total is None else total + part
            value = term if value is None else value + term
        queries = pl.ds(base, group)
        m_ref[h : h + 1, queries] = peak
        l_ref[h : h + 1, queries] = total
        acc[rows, queries] = value


def triangle_slot(i, j, group):
    strip = min(256, group)
    count = group // strip
    row = jnp.where(i == 0, j, count - j) * strip
    column = jnp.where(i == 0, j * strip, 0)
    wide = group - j * strip
    return (
        pl.ds(pl.multiple_of(row, strip), strip),
        pl.ds(pl.multiple_of(column, strip), wide),
    )


def square_slot(j, group):
    strip = min(256, group)
    return pl.ds(group + strip + j * strip, strip), slice(None)


def fwd_local_kernel(group, info, qT, kT, vT, acc, m_ref, l_ref, kept, flags):
    length = info[1]
    m_ref[...] = jnp.full(m_ref.shape, NEG, f32)
    l_ref[...] = jnp.zeros(l_ref.shape, f32)
    acc[...] = jnp.zeros(acc.shape, f32)
    refs = (qT, kT, vT, m_ref.at[0], l_ref.at[0], acc)

    def walk(fast):
        def own(i, carry):
            base = pl.multiple_of(i * group, group)
            start = info[2 + i]

            def store(h, j, weights):
                rows, columns = triangle_slot(i, j, group)
                kept[h, rows, columns] = weights

            @pl.when(start + group <= length)
            def _():
                fwd_diagonal(fast, base, group, None, store, *refs)

            @pl.when((start < length) & (start + group > length))
            def _():
                fwd_diagonal(fast, base, group, length - start, store, *refs)

            return carry

        lax.fori_loop(0, 2, own, 0)
        early = info[2]

        def store(h, j, weights):
            rows, columns = square_slot(j, group)
            kept[h, rows, columns] = weights

        @pl.when(early + group <= length)
        def _():
            fwd_chunk(fast, group, 0, group, group, None, store, *refs)

        @pl.when((early < length) & (early + group > length))
        def _():
            fwd_chunk(fast, group, 0, group, group, length - early, store, *refs)

    small = bounded(qT, kT)
    flags[pl.program_id(0)] = small.astype(jnp.int32)
    pl.when(small)(functools.partial(walk, True))
    pl.when(jnp.logical_not(small))(functools.partial(walk, False))


def remote_steps(group, parts, info, full, partial):
    place, length = info[0], info[1]

    def visit(i, carry):
        j, turn_at = i // 3, lax.rem(i, 3)
        other = lax.rem(place + 1 + j, parts)
        late_key = turn_at == 2
        block = jnp.where(late_key, 2 * parts - 1 - other, other)
        before = (other < place).astype(jnp.int32)
        wanted = jnp.where(turn_at == 0, before, jnp.where(late_key, 1 - before, 1)) == 1
        q0 = pl.multiple_of(jnp.where(turn_at == 0, 0, group), group)
        k0 = pl.multiple_of((2 * j + jnp.where(late_key, 1, 0)) * group, group)
        slot = pl.multiple_of((2 * j + turn_at - (1 - before)) * group, group)
        start = block * group

        @pl.when(wanted & (start + group <= length))
        def _():
            full(q0, k0, slot)

        @pl.when(wanted & (start < length) & (start + group > length))
        def _():
            partial(q0, k0, slot, length - start)

        return carry

    lax.fori_loop(0, 3 * (parts - 1), visit, 0)


def fwd_remote_kernel(
    group, parts, info, qT, kT, vT, acc_in, m_in, l_in, out, lse, kept, flags, acc, m_ref, l_ref
):
    acc[...] = acc_in[...]
    m_ref[...] = m_in[0]
    l_ref[...] = l_in[0]
    refs = (qT, kT, vT, m_ref, l_ref, acc)
    strip = min(256, group)

    def walk(fast):
        def partial(q0, k0, slot, limit):
            def store(h, j, weights):
                kept[h, pl.ds(pl.multiple_of(slot + j * strip, strip), strip), :] = weights

            fwd_chunk(fast, q0, k0, group, group, limit, store, *refs)

        def full(q0, k0, slot):
            partial(q0, k0, slot, None)

        remote_steps(group, parts, info, full, partial)

    small = bounded(qT, kT) & (jnp.max(m_in[...]) <= 0.0)
    flags[pl.program_id(0)] = small.astype(jnp.int32)
    pl.when(small)(functools.partial(walk, True))
    pl.when(jnp.logical_not(small))(functools.partial(walk, False))
    for h in range(2):
        rows = slice(HEAD_DIM * h, HEAD_DIM * (h + 1))
        total = l_ref[h : h + 1, :]
        out[rows, :] = (acc[rows, :] / total).astype(bf16)
        lse[0, h : h + 1, :] = m_ref[h : h + 1, :] + jnp.log2(total)


def split_three(values):
    high = values.astype(bf16).astype(f32)
    rest = values - high
    middle = rest.astype(bf16).astype(f32)
    low = (rest - middle).astype(bf16).astype(f32)
    return [high, middle, low]


def bwd_prepare(qT, kT, vT, doT, oT, lse, qa, da, ka, va):
    n_q, n_k = qT.shape[1], ka.shape[2]
    extra = qa.shape[1] - HEAD_DIM
    pad = jnp.zeros((extra - 3, n_q), f32)
    row_at = lax.broadcasted_iota(jnp.int32, (extra, n_k), 0)
    tail = jnp.where(row_at < 3, 1.0, 0.0).astype(bf16)
    for h in range(2):
        rows = slice(HEAD_DIM * h, HEAD_DIM * (h + 1))
        grad = doT[rows, :].astype(f32)
        delta = jnp.sum(grad * oT[rows, :].astype(f32), axis=0, keepdims=True)
        qa[h, :HEAD_DIM, :] = qT[rows, :]
        parts = split_three(-lse[0, h : h + 1, :]) + [pad]
        qa[h, HEAD_DIM:, :] = jnp.concatenate(parts, axis=0).astype(bf16)
        da[h, :HEAD_DIM, :] = doT[rows, :]
        parts = split_three(-delta) + [pad]
        da[h, HEAD_DIM:, :] = jnp.concatenate(parts, axis=0).astype(bf16)
        ka[h, :HEAD_DIM, :] = kT[rows, :]
        va[h, :HEAD_DIM, :] = vT[rows, :]
        ka[h, HEAD_DIM:, :] = tail
        va[h, HEAD_DIM:, :] = tail


def bwd_chunk(q0, k0, q_n, k_n, limit, qT, doT, qa, da, ka, va, dq, dk, dv):
    queries, keys = pl.ds(q0, q_n), pl.ds(k0, k_n)
    for h in range(2):
        rows = slice(HEAD_DIM * h, HEAD_DIM * (h + 1))
        probs = jnp.exp2(dot(qa[h, :, queries], ka[h, :, keys], 0, 0))
        if limit is not None:
            key_at = lax.broadcasted_iota(jnp.int32, (q_n, k_n), 1)
            probs = jnp.where(key_at < limit, probs, 0.0)
        d_probs = dot(da[h, :, queries], va[h, :, keys], 0, 0)
        d_scores = (probs * d_probs).astype(bf16)
        dv[rows, keys] += dot(doT[rows, queries], probs.astype(bf16), 1, 0)
        dk[rows, keys] += dot(qT[rows, queries], d_scores, 1, 0)
        dq[rows, queries] += dot(ka[h, :HEAD_DIM, keys], d_scores, 1, 1)


def bwd_diagonal(base, group, limit, qT, doT, qa, da, ka, va, dq, dk, dv):
    strip = min(256, group)
    count = group // strip
    for h in range(2):
        rows = slice(HEAD_DIM * h, HEAD_DIM * (h + 1))
        d_keys, d_values, d_queries = None, None, []
        for j in range(count):
            wide = (j + 1) * strip
            queries, keys = pl.ds(base + j * strip, strip), pl.ds(base, wide)
            probs = jnp.exp2(dot(qa[h, :, queries], ka[h, :, keys], 0, 0))
            query_at = lax.broadcasted_iota(jnp.int32, probs.shape, 0)
            key_at = lax.broadcasted_iota(jnp.int32, probs.shape, 1)
            probs = jnp.where(key_at <= query_at + j * strip, probs, 0.0)
            if limit is not None:
                probs = jnp.where(key_at < limit, probs, 0.0)
            d_probs = dot(da[h, :, queries], va[h, :, keys], 0, 0)
            d_scores = (probs * d_probs).astype(bf16)
            value = pad_right(dot(doT[rows, queries], probs.astype(bf16), 1, 0), group - wide)
            key = pad_right(dot(qT[rows, queries], d_scores, 1, 0), group - wide)
            d_values = value if d_values is None else d_values + value
            d_keys = key if d_keys is None else d_keys + key
            d_queries.append(dot(ka[h, :HEAD_DIM, keys], d_scores, 1, 1))
        here = pl.ds(base, group)
        dq[rows, here] += jnp.concatenate(d_queries, axis=1) if count > 1 else d_queries[0]
        dk[rows, here] += d_keys
        dv[rows, here] += d_values


def stored_chunk(h, weights, queries, keys, qT, kT, vT, scaled, delta, dq, dk, dv):
    rows = slice(HEAD_DIM * h, HEAD_DIM * (h + 1))
    d_probs = dot(vT[rows, keys], scaled[rows, queries], 0, 0)
    d_scores = weights.astype(f32) * (d_probs - delta[0, h : h + 1, queries])
    d_scores = d_scores.astype(bf16)
    dv[rows, keys] += dot(scaled[rows, queries], weights, 1, 1)
    dk[rows, keys] += dot(qT[rows, queries], d_scores, 1, 1)
    dq[rows, queries] += dot(kT[rows, keys], d_scores, 1, 0)


def turn_back(values, cosine, sine):
    half = HEAD_DIM // 2
    first, second = values[:half], values[half:]
    return jnp.concatenate(
        [first * cosine + second * sine, second * cosine - first * sine], axis=0
    )


def bwd_remote_kernel(
    group,
    parts,
    first,
    info,
    flags,
    qT,
    doT,
    oT,
    lse,
    scaled,
    delta,
    cosine,
    sine,
    kT,
    vT,
    kept,
    *rest,
):
    dq, dkv, qa, da, ka, va, dk, dv = rest[-8:]
    dq[...] = jnp.zeros(dq.shape, f32)
    dk[...] = jnp.zeros(dk.shape, f32)
    dv[...] = jnp.zeros(dv.shape, f32)
    fast = flags[first + pl.program_id(0)] == 1

    @pl.when(fast)
    def _():
        def full(q0, k0, slot):
            for h in range(2):
                weights = kept[h, pl.ds(slot, group), :]
                queries, keys = pl.ds(q0, group), pl.ds(k0, group)
                stored_chunk(h, weights, queries, keys, qT, kT, vT, scaled, delta, dq, dk, dv)

        def partial(q0, k0, slot, limit):
            full(q0, k0, slot)

        remote_steps(group, parts, info, full, partial)

    @pl.when(jnp.logical_not(fast))
    def _():
        bwd_prepare(qT, kT, vT, doT, oT, lse, qa, da, ka, va)
        refs = (qT, doT, qa, da, ka, va, dq, dk, dv)

        def full(q0, k0, slot):
            bwd_chunk(q0, k0, group, group, None, *refs)

        def partial(q0, k0, slot, limit):
            bwd_chunk(q0, k0, group, group, limit, *refs)

        remote_steps(group, parts, info, full, partial)

    for h in range(2):
        rows = slice(HEAD_DIM * h, HEAD_DIM * (h + 1))
        dkv[1, rows, :] = turn_back(dk[rows, :] * LN2, cosine[...], sine[...]).astype(bf16)
    dkv[0] = jnp.zeros(dv.shape, bf16)
    dkv[2] = dv[...].astype(bf16)


def bwd_local_kernel(
    group,
    first,
    info,
    flags,
    qT,
    doT,
    oT,
    lse,
    scaled,
    delta,
    cosine,
    sine,
    kT,
    vT,
    dq_in,
    kept,
    *rest,
):
    dqkv, qa, da, ka, va, dk, dv, dq = rest[-8:]
    length = info[1]
    dq[...] = dq_in[...]
    dk[...] = jnp.zeros(dk.shape, f32)
    dv[...] = jnp.zeros(dv.shape, f32)
    early = info[2]
    strip = min(256, group)
    fast = flags[first + pl.program_id(0)] == 1

    @pl.when(fast)
    def _():
        refs = (qT, kT, vT, scaled, delta, dq, dk, dv)

        def own(i, carry):
            base = pl.multiple_of(i * group, group)

            @pl.when(info[2 + i] < length)
            def _():
                for h in range(2):
                    for j in range(group // strip):
                        rows, columns = triangle_slot(i, j, group)
                        queries = pl.ds(base + j * strip, group - j * strip)
                        keys = pl.ds(base + j * strip, strip)
                        stored_chunk(h, kept[h, rows, columns], queries, keys, *refs)

            return carry

        lax.fori_loop(0, 2, own, 0)

        @pl.when(early < length)
        def _():
            for h in range(2):
                weights = kept[h, group + strip :, :]
                stored_chunk(h, weights, pl.ds(group, group), pl.ds(0, group), *refs)

    @pl.when(jnp.logical_not(fast))
    def _():
        bwd_prepare(qT, kT, vT, doT, oT, lse, qa, da, ka, va)
        refs = (qT, doT, qa, da, ka, va, dq, dk, dv)

        def own(i, carry):
            base = pl.multiple_of(i * group, group)
            start = info[2 + i]

            @pl.when(start < length)
            def _():
                bwd_diagonal(base, group, length - start, *refs)

            return carry

        lax.fori_loop(0, 2, own, 0)

        @pl.when(early < length)
        def _():
            bwd_chunk(group, 0, group, group, length - early, *refs)

    for h in range(2):
        rows = slice(HEAD_DIM * h, HEAD_DIM * (h + 1))
        d_query = dq[rows, :] * 0.125
        dqkv[0, rows, :] = turn_back(d_query, cosine[...], sine[...]).astype(bf16)
        dqkv[1, rows, :] = turn_back(dk[rows, :] * LN2, cosine[...], sine[...]).astype(bf16)
    dqkv[2] = dv[...].astype(bf16)


def rows_of(count, first=0):
    return pl.BlockSpec((PAIR, count), lambda i, *info: (first + i, 0))


def stats_of(count, first=0):
    return pl.BlockSpec((1, 2, count), lambda i, *info: (first + i, 0, 0))


def planes_of(planes, count, first=0):
    return pl.BlockSpec((planes, PAIR, count), lambda i, *info: (0, first + i, 0))


def kept_of(rows, group, first=0):
    return pl.BlockSpec((2, rows, group), lambda i, *info: (first + i, 0, 0))


def scalars():
    return pl.BlockSpec(memory_space=pltpu.SMEM)


def whole(shape):
    return pl.BlockSpec(shape, lambda i, *info: (0,) * len(shape))


def attention_call(kernel, pairs, in_specs, out_specs, out_shape, scratch, flops, name, alias={}, prefetch=1):
    return pl.pallas_call(
        kernel,
        grid_spec=pltpu.PrefetchScalarGridSpec(
            num_scalar_prefetch=prefetch,
            grid=(pairs,),
            in_specs=in_specs,
            out_specs=out_specs,
            scratch_shapes=scratch,
        ),
        out_shape=out_shape,
        input_output_aliases=alias,
        compiler_params=pltpu.CompilerParams(vmem_limit_bytes=VMEM),
        cost_estimate=pl.CostEstimate(
            flops=int(flops), bytes_accessed=1 << 25, transcendentals=0
        ),
        name=name,
    )


def attend_local(info, qT, kT, vT, group):
    width, n_q = qT.shape
    pairs = width // PAIR
    kept_rows = 2 * group + min(256, group)
    call = attention_call(
        functools.partial(fwd_local_kernel, group),
        pairs,
        [rows_of(n_q)] * 3,
        [rows_of(n_q), stats_of(n_q), stats_of(n_q), kept_of(kept_rows, group), scalars()],
        [
            jax.ShapeDtypeStruct((width, n_q), f32),
            jax.ShapeDtypeStruct((pairs, 2, n_q), f32),
            jax.ShapeDtypeStruct((pairs, 2, n_q), f32),
            jax.ShapeDtypeStruct((2 * pairs, kept_rows, group), bf16),
            jax.ShapeDtypeStruct((pairs,), jnp.int32),
        ],
        [],
        4 * width * 2 * group * group * 4,
        "attend_local",
    )
    *state, kept, flags = call(info, qT, kT, vT)
    return state, kept, flags


def attend_remote(info, qT, kT, vT, state, group, parts):
    width, n_q = qT.shape
    n_k = kT.shape[1]
    pairs = width // PAIR
    call = attention_call(
        functools.partial(fwd_remote_kernel, group, parts),
        pairs,
        [rows_of(n_q), rows_of(n_k), rows_of(n_k), rows_of(n_q), stats_of(n_q), stats_of(n_q)],
        [rows_of(n_q), stats_of(n_q), kept_of(n_k, group), scalars()],
        [
            jax.ShapeDtypeStruct((width, n_q), bf16),
            jax.ShapeDtypeStruct((pairs, 2, n_q), f32),
            jax.ShapeDtypeStruct((2 * pairs, n_k, group), bf16),
            jax.ShapeDtypeStruct((pairs,), jnp.int32),
        ],
        [pltpu.VMEM((PAIR, n_q), f32)] + [pltpu.VMEM((2, n_q), f32)] * 2,
        4 * width * 2 * group * group * 4,
        "attend_remote",
    )
    return call(info, qT, kT, vT, *state)


def back_scratch(n_q, n_k):
    rows = HEAD_DIM + 16
    return (
        [pltpu.VMEM((2, rows, n_q), bf16)] * 2
        + [pltpu.VMEM((2, rows, n_k), bf16)] * 2
        + [pltpu.VMEM((PAIR, n_k), f32)] * 2
    )


def back_remote(info, flags, operands, turns, keys, kept, group, parts, first, count, before):
    width, n_q = operands[0].shape
    n_k = keys[0].shape[1]
    half = HEAD_DIM // 2
    n_in = 2 + len(operands) + len(turns) + len(keys) + 1
    call = attention_call(
        functools.partial(bwd_remote_kernel, group, parts, first),
        count,
        [rows_of(n_q, first)] * 3
        + [stats_of(n_q, first), rows_of(n_q, first), stats_of(n_q, first)]
        + [whole((half, n_k))] * 2
        + [rows_of(n_k, first)] * 2
        + [kept_of(kept.shape[1], group, first)]
        + [pl.BlockSpec(memory_space=pl.ANY)] * len(before),
        [rows_of(n_q, first), planes_of(3, n_k, first)],
        [
            jax.ShapeDtypeStruct((width, n_q), f32),
            jax.ShapeDtypeStruct((3, width, n_k), bf16),
        ],
        back_scratch(n_q, n_k),
        10 * count * PAIR * 2 * group * group * 4,
        "back_remote",
        {n_in + i: i for i in range(len(before))},
        2,
    )
    return call(info, flags, *operands, *turns, *keys, kept, *before)


def back_local(info, flags, operands, turns, keys, dq, kept, group, first, count, before):
    width, n_q = operands[0].shape
    half = HEAD_DIM // 2
    n_in = 2 + len(operands) + len(turns) + len(keys) + 2
    call = attention_call(
        functools.partial(bwd_local_kernel, group, first),
        count,
        [rows_of(n_q, first)] * 3
        + [stats_of(n_q, first), rows_of(n_q, first), stats_of(n_q, first)]
        + [whole((half, n_q))] * 2
        + [rows_of(n_q, first)] * 3
        + [kept_of(kept.shape[1], group, first)]
        + [pl.BlockSpec(memory_space=pl.ANY)] * len(before),
        planes_of(3, n_q, first),
        jax.ShapeDtypeStruct((3, width, n_q), bf16),
        back_scratch(n_q, n_q) + [pltpu.VMEM((PAIR, n_q), f32)],
        10 * count * PAIR * 2 * group * group * 4,
        "back_local",
        {n_in + i: i for i in range(len(before))},
        2,
    )
    return call(info, flags, *operands, *turns, *keys, dq, kept, *before)


def normalize(values):
    centre = values - jnp.mean(values, axis=-1, keepdims=True)
    spread = jnp.mean(centre * centre, axis=-1, keepdims=True)
    rate = lax.rsqrt(spread + EPS)
    return centre * rate, rate


def norm_back(grad, unit, rate, gain):
    scaled = grad * gain
    first = jnp.mean(scaled, axis=-1, keepdims=True)
    second = jnp.mean(scaled * unit, axis=-1, keepdims=True)
    return rate * (scaled - first - unit * second)


GELU_A = 0.7978845608028654
GELU_B = 0.044715


def column_sum(values):
    return jnp.sum(values, axis=0, keepdims=True)


def block_kernel(
    span,
    oT,
    lse,
    tokens,
    cotangent,
    w_out,
    w_up,
    w_down,
    b_out,
    b_up,
    b_down,
    gain_two,
    shift_two,
    gain_three,
    shift_three,
    gain_four,
    shift_four,
    result,
    d_middle_out,
    hidden_out,
    d_outer_out,
    normed_out,
    d_inner_out,
    d_branch_out,
    doT,
    scaled,
    delta,
    small,
    small_up,
    slope,
):
    step = pl.program_id(0)

    @pl.when(step == 0)
    def _():
        small[...] = jnp.zeros(small.shape, f32)
        small_up[...] = jnp.zeros(small_up.shape, f32)

    wide = w_up.shape[1]
    branch = dot(oT[...], w_out[...], 0, 0) + b_out[...]
    unit_two, rate_two = normalize(branch)
    middle = tokens[...].astype(f32) + (unit_two * gain_two[...] + shift_two[...])
    unit_three, rate_three = normalize(middle)
    normed = (unit_three * gain_three[...] + shift_three[...]).astype(bf16)
    normed_out[...] = normed
    outer = None
    for c in range(wide // span):
        columns = slice(c * span, (c + 1) * span)
        inner = dot(normed, w_up[:, columns], 1, 0) + b_up[:, columns]
        square = inner * inner
        bend = jnp.tanh(inner * (GELU_A + (GELU_A * GELU_B) * square))
        half = 0.5 + 0.5 * bend
        hidden = (inner * half).astype(bf16)
        hidden_out[:, columns] = hidden
        slope[:, columns] = half + inner * (1.0 - bend * bend) * (
            0.5 * GELU_A + (1.5 * GELU_A * GELU_B) * square
        )
        term = dot(hidden, w_down[columns, :], 1, 0)
        outer = term if outer is None else outer + term
    unit_four, rate_four = normalize(outer + b_down[...])
    result[...] = (middle + (unit_four * gain_four[...] + shift_four[...])).astype(bf16)

    grad = cotangent[...].astype(f32)
    d_outer = norm_back(grad, unit_four, rate_four, gain_four[...]).astype(bf16)
    d_outer_out[...] = d_outer
    small[0:1, :] += column_sum(grad * unit_four)
    small[1:2, :] += column_sum(grad)
    small[2:3, :] += column_sum(d_outer.astype(f32))
    d_normed = None
    for c in range(wide // span):
        columns = slice(c * span, (c + 1) * span)
        d_hidden = dot(d_outer, w_down[columns, :], 1, 1)
        d_inner = (d_hidden * slope[:, columns]).astype(bf16)
        d_inner_out[:, columns] = d_inner
        small_up[:, columns] += column_sum(d_inner.astype(f32))
        term = dot(d_inner, w_up[:, columns], 1, 1)
        d_normed = term if d_normed is None else d_normed + term
    small[3:4, :] += column_sum(d_normed * unit_three)
    small[4:5, :] += column_sum(d_normed)
    d_middle = grad + norm_back(d_normed, unit_three, rate_three, gain_three[...])
    d_middle_out[...] = d_middle
    small[5:6, :] += column_sum(d_middle * unit_two)
    small[6:7, :] += column_sum(d_middle)
    d_branch = norm_back(d_middle, unit_two, rate_two, gain_two[...]).astype(bf16)
    d_branch_out[...] = d_branch
    small[7:8, :] += column_sum(d_branch.astype(f32))
    d_attended = dot(w_out[...], d_branch, 1, 1).astype(bf16)
    doT[...] = d_attended
    for h in range(oT.shape[0] // HEAD_DIM):
        rows = slice(HEAD_DIM * h, HEAD_DIM * (h + 1))
        at = slice(h % 2, h % 2 + 1)
        part = (d_attended[rows].astype(f32) * jnp.exp2(-lse[h // 2, at, :])).astype(bf16)
        scaled[rows, :] = part
        delta[h // 2, at, :] = column_sum(part.astype(f32) * oT[rows, :].astype(f32))


def block_call(oT, lse, tokens, cotangent, weights, vectors):
    width, rows = oT.shape
    wide = weights[1].shape[1]
    step = min(256, rows)
    span = min(SPAN, wide)

    def lines(count):
        return pl.BlockSpec((step, count), lambda i: (i, 0))

    def fixed(shape):
        return pl.BlockSpec(shape, lambda i: (0, 0), pipeline_mode=pl.Buffered(1))

    def total(shape):
        return pl.BlockSpec(shape, lambda i: (0, 0))

    features = pl.BlockSpec((width, step), lambda i: (0, i))
    stats = pl.BlockSpec((*lse.shape[:2], step), lambda i: (0, 0, i))
    sizes = [width, width, wide, width, width, wide, width]
    kinds = [bf16, f32, bf16, bf16, bf16, bf16, bf16]
    return pl.pallas_call(
        functools.partial(block_kernel, span),
        grid=(rows // step,),
        in_specs=[features, stats, lines(width), lines(width)]
        + [fixed(item.shape) for item in weights]
        + [fixed(item.shape) for item in vectors],
        out_specs=[lines(size) for size in sizes]
        + [features, features, stats, total((8, width)), total((1, wide))],
        out_shape=[jax.ShapeDtypeStruct((rows, size), kind) for size, kind in zip(sizes, kinds)]
        + [
            jax.ShapeDtypeStruct((width, rows), bf16),
            jax.ShapeDtypeStruct((width, rows), bf16),
            jax.ShapeDtypeStruct(lse.shape, f32),
            jax.ShapeDtypeStruct((8, width), f32),
            jax.ShapeDtypeStruct((1, wide), f32),
        ],
        scratch_shapes=[pltpu.VMEM((step, wide), f32)],
        compiler_params=pltpu.CompilerParams(vmem_limit_bytes=VMEM),
        cost_estimate=pl.CostEstimate(
            flops=2 * 2 * rows * (width * width + 2 * width * wide),
            bytes_accessed=1 << 26,
            transcendentals=rows * wide,
        ),
        name="block",
    )(oT, lse, tokens, cotangent, *weights, *vectors)


def turn(values, cosine, sine):
    half = HEAD_DIM // 2
    first, second = values[:half], values[half:]
    return jnp.concatenate(
        [first * cosine - second * sine, second * cosine + first * sine], axis=0
    )


def project_kernel(sections, tokens, w, b, gain, shift, cosine, sine, normed_out, *outs):
    unit, rate = normalize(tokens[...].astype(f32))
    normed = (unit * gain[...] + shift[...]).astype(bf16)
    normed_out[...] = normed
    width = tokens.shape[1]
    chunk = min(256, width)
    for section, out in zip(sections, outs):
        for c in range(width // chunk):
            at = section * width + c * chunk
            mixed = (dot(normed, w[:, at : at + chunk], 1, 0) + b[:, at : at + chunk]).T
            for h in range(chunk // HEAD_DIM):
                rows = slice(h * HEAD_DIM, (h + 1) * HEAD_DIM)
                place = slice(c * chunk + h * HEAD_DIM, c * chunk + (h + 1) * HEAD_DIM)
                value = mixed[rows]
                if section < 2:
                    value = turn(value, cosine[...], sine[...])
                if section == 0:
                    value = value * (0.125 * LOG2E)
                out[place, :] = value.astype(bf16)


def project(tokens, w, b, gain, shift, cosine, sine, sections):
    rows, width = tokens.shape
    step = min(512, rows)
    half = HEAD_DIM // 2

    def fixed(shape):
        return pl.BlockSpec(shape, lambda i: (0, 0), pipeline_mode=pl.Buffered(1))

    lines = pl.BlockSpec((step, width), lambda i: (i, 0))
    features = pl.BlockSpec((width, step), lambda i: (0, i))
    turns = pl.BlockSpec((half, step), lambda i: (0, i))
    return pl.pallas_call(
        functools.partial(project_kernel, sections),
        grid=(rows // step,),
        in_specs=[lines, fixed(w.shape), fixed(b.shape), fixed(gain.shape), fixed(shift.shape)]
        + [turns] * 2,
        out_specs=[lines] + [features] * len(sections),
        out_shape=[jax.ShapeDtypeStruct((rows, width), bf16)]
        + [jax.ShapeDtypeStruct((width, rows), bf16)] * len(sections),
        compiler_params=pltpu.CompilerParams(vmem_limit_bytes=VMEM),
        cost_estimate=pl.CostEstimate(
            flops=2 * rows * width * width * len(sections),
            bytes_accessed=1 << 24,
            transcendentals=0,
        ),
        name="project",
    )(tokens, w, b, gain, shift, cosine, sine)


def unproject_kernel(planes, finish, *refs):
    d_mixed, w, out = refs[: len(planes)], refs[len(planes)], refs[-1]
    width = w.shape[0]
    total = None
    for plane, ref in zip(planes, d_mixed):
        term = dot(ref[0], w[:, plane * width : (plane + 1) * width], 0, 1)
        total = term if total is None else total + term
    if not finish:
        out[...] = total.astype(bf16)
        return
    returned, tokens, d_middle, gain = refs[len(planes) + 1 : len(planes) + 5]
    total = total + returned[...].astype(f32)
    unit, rate = normalize(tokens[...].astype(f32))
    out[...] = (d_middle[...] + norm_back(total, unit, rate, gain[...])).astype(bf16)


def unproject(d_mixed, w, planes, start, count, finish=(), before=()):
    _, width, total = d_mixed.shape
    step = min(256, count)
    first = start // step

    def fixed(shape):
        return pl.BlockSpec(shape, lambda i: (0, 0), pipeline_mode=pl.Buffered(1))

    def plane_of(plane):
        return pl.BlockSpec((1, width, step), lambda i: (plane, 0, first + i))

    lines = pl.BlockSpec((step, width), lambda i: (i, 0))
    later = pl.BlockSpec((step, width), lambda i: (first + i, 0))
    specs = [later] * 3 + [fixed(finish[-1].shape)] if finish else []
    n_in = len(planes) + 1 + len(finish)
    return pl.pallas_call(
        functools.partial(unproject_kernel, planes, bool(finish)),
        grid=(count // step,),
        in_specs=[plane_of(plane) for plane in planes]
        + [fixed(w.shape)]
        + specs
        + [pl.BlockSpec(memory_space=pl.ANY)] * len(before),
        out_specs=later if finish else lines,
        out_shape=jax.ShapeDtypeStruct((total if finish else count, width), bf16),
        input_output_aliases={n_in + i: i for i in range(len(before))},
        compiler_params=pltpu.CompilerParams(vmem_limit_bytes=VMEM),
        cost_estimate=pl.CostEstimate(
            flops=2 * count * width * width * len(planes),
            bytes_accessed=1 << 24,
            transcendentals=0,
        ),
        name="unproject",
    )(*[d_mixed] * len(planes), w, *finish, *before)


def divide(total, run, levels, near, marks, orders, outs):
    bits = [("narrow", i) for i in range(near)] + [("wide", i) for i in range(levels + 1)]
    cut = run // len(orders)

    def write(core):
        for at in range(0, total.shape[0], run):
            number = at // run
            value = {}
            for place, (axis, position) in enumerate(bits):
                mine = (marks[1 if axis == "narrow" else 0] >> position) & 1
                value[axis, position] = mine ^ ((number >> place) & 1)
            other = core ^ ((number >> near) & 1)
            for i, order in enumerate(orders):
                index = tuple(value.get(bit, 0) for bit in order)
                part = total[at + i * cut : at + (i + 1) * cut]
                outs[2 * i + other][index] = part.astype(bf16)

    pl.when((marks[0] & 1) == 0)(functools.partial(write, 0))
    pl.when((marks[0] & 1) == 1)(functools.partial(write, 1))


def divided(orders, levels, run, height, wide, width):
    cut = run // len(orders)
    specs, shapes = [], []
    for order in orders:

        def held(bit):
            return bit[0] == "narrow" or bit[1] <= levels

        def index(j, i, marks, order=order):
            relative = i ^ (marks[0] >> (levels + 1))
            at = [0 if held(bit) else (relative >> (bit[1] - 1 - levels)) & 1 for bit in order]
            return (*at, 0, j)

        block = tuple(2 if held(bit) else 1 for bit in order) + (cut, wide)
        specs += [pl.BlockSpec(block, index)] * 2
        shapes += [jax.ShapeDtypeStruct((2,) * len(order) + (cut, width), bf16)] * 2
    return specs, shapes


def outer_kernel(run, levels, near, orders, right_dim, marks, left, right, *outs):
    divide(dot(left[...], right[...], 0, right_dim), run, levels, near, marks, orders, outs)


def outer_halves(marks, left, right, right_dim, cores, parts, order):
    rows, height = left.shape
    width = right.shape[1 - right_dim]
    share = height // cores
    high = max(2 * share, min(512 if right_dim else 1024, height))
    levels = (high // (2 * share)).bit_length() - 1
    wide = min(1024, width)
    if right_dim == 0:
        right_spec = pl.BlockSpec((rows, wide), lambda j, i, marks: (0, j))
    else:
        right_spec = pl.BlockSpec((wide, rows), lambda j, i, marks: (j, 0))
    run = share // parts
    near = parts.bit_length() - 1
    specs, shapes = divided([order], levels, run, height, wide, width)
    halves = pl.pallas_call(
        functools.partial(outer_kernel, run, levels, near, [order], right_dim),
        grid_spec=pltpu.PrefetchScalarGridSpec(
            num_scalar_prefetch=1,
            grid=(width // wide, height // high),
            in_specs=[pl.BlockSpec((rows, high), lambda j, i, marks: (0, i)), right_spec],
            out_specs=specs,
        ),
        out_shape=shapes,
        compiler_params=pltpu.CompilerParams(vmem_limit_bytes=VMEM),
        cost_estimate=pl.CostEstimate(
            flops=2 * rows * height * width, bytes_accessed=1 << 25, transcendentals=0
        ),
        name="outer",
    )(marks, left, right)
    return [item.reshape(height // 2, width) for item in halves]


def mixed_kernel(
    run,
    levels,
    near,
    orders,
    first_far,
    marks,
    d_own,
    d_far,
    normed,
    normed_far,
    w,
    gain,
    shift,
    *outs,
):
    *halves, small, sums, bias = outs
    step, last = pl.program_id(1), pl.num_programs(1) - 1
    total = dot(d_own[...], normed[...], 1, 0)
    bias[...] = jnp.sum(d_own[...].astype(f32), axis=1, keepdims=True)

    @pl.when(step == 0)
    def _():
        sums[...] = jnp.zeros(sums.shape, f32)
        small[...] = jnp.zeros(small.shape, f32)

    def finish(value):
        divide(value, run, levels, near, marks, orders, halves)
        weights = w[...].astype(f32).T
        sums[0:1, :] += column_sum(weights * value)
        sums[1:2, :] += column_sum(weights * bias[...])
        wide = jnp.broadcast_to(bias[...], (bias.shape[0], PAIR)).T
        small[pl.ds(step, 1), : bias.shape[0]] = wide[0:1, :]

    @pl.when(step < first_far)
    def _():
        finish(total)

    @pl.when(step >= first_far)
    def _():
        bias[...] += jnp.sum(d_far[...].astype(f32), axis=1, keepdims=True)
        finish(total + dot(d_far[...], normed_far[...], 1, 0))

    @pl.when(step == last)
    def _():
        small[pl.ds(last + 1, 1), :] = (sums[0:1, :] - shift[...] * sums[1:2, :]) / gain[...]
        small[pl.ds(last + 2, 1), :] = sums[1:2, :]


def mixed_halves(marks, d_own, d_far, normed, normed_far, w, gain, shift, cores, parts, orders):
    height, rows = d_own.shape
    far = d_far.shape[1]
    width = normed.shape[1]
    share = height // cores
    pairs = max(1, 768 // (2 * share))
    levels = pairs.bit_length() - 1
    high = 2 * share * pairs
    first_far = width // high
    run = share // parts
    near = parts.bit_length() - 1
    steps = height // high

    def fixed(shape):
        return pl.BlockSpec(shape, lambda j, i, marks: (0, 0), pipeline_mode=pl.Buffered(1))

    specs, shapes = divided(orders, levels, run, height, width, width)
    *halves, small = pl.pallas_call(
        functools.partial(mixed_kernel, run, levels, near, orders, first_far),
        grid_spec=pltpu.PrefetchScalarGridSpec(
            num_scalar_prefetch=1,
            grid=(1, steps),
            in_specs=[
                pl.BlockSpec((high, rows), lambda j, i, marks: (i, 0)),
                pl.BlockSpec((high, far), lambda j, i, marks: (jnp.maximum(i, first_far), 0)),
                fixed(normed.shape),
                fixed(normed_far.shape),
                pl.BlockSpec((width, high), lambda j, i, marks: (0, i)),
                fixed(gain.shape),
                fixed(shift.shape),
            ],
            out_specs=specs + [pl.BlockSpec((16, width), lambda j, i, marks: (0, 0))],
            scratch_shapes=[pltpu.VMEM((2, width), f32), pltpu.VMEM((high, 1), f32)],
        ),
        out_shape=shapes + [jax.ShapeDtypeStruct((16, width), f32)],
        compiler_params=pltpu.CompilerParams(vmem_limit_bytes=VMEM),
        cost_estimate=pl.CostEstimate(
            flops=2 * (rows + far) * height * width, bytes_accessed=1 << 25, transcendentals=0
        ),
        name="mixed",
    )(marks, d_own, d_far, normed, normed_far, w, gain, shift)
    halves = [item.reshape(-1, width) for item in halves]
    return [halves[i : i + 2] for i in range(0, len(halves), 2)], small, steps


def bit_of(axis, position):
    return (lax.axis_index(axis) >> position) & 1


def swap(values, axis, position):
    size = lax.axis_size(axis)
    return lax.ppermute(values, axis, [(i, i ^ (1 << position)) for i in range(size)])


class Halving:
    def __init__(self, halves, order):
        self.order = list(order)
        kept, given = halves
        self.height = kept.shape[0]
        self.terms = [kept, swap(given, "wide", 0)]

    def send(self, away):
        self.terms = self.terms + [swap(away, *self.order.pop(0))]
        self.height //= 2

    def blocks(self, height, grid, which):
        width = self.terms[0].shape[1]
        spec = pl.BlockSpec((1, height // grid, width), lambda i: (which, i, 0))
        return [term.reshape(-1, height, width) for term in self.terms], [spec] * len(self.terms)


class Adding:
    def __init__(self, array, order):
        self.order = list(order)
        self.terms = [array, swap(array, *self.order.pop(0))]

    def send(self, total):
        self.terms = [total, swap(total, *self.order.pop(0))]


def halve_kernel(counts, *refs):
    ins, outs = refs[: sum(counts) + 2], refs[sum(counts) + 2 :]
    at = 0
    for count, out in zip(counts, outs):
        parts = [ref[0].astype(f32) for ref in ins[at : at + count]]
        out[...] = functools.reduce(jnp.add, parts).astype(bf16)
        at += count
    outs[-1][...] = ins[-2][...] + ins[-1][...]


def halve(sums, small):
    heights = [item.height // 2 for item in sums]
    grid = 4 if all(height % 64 == 0 for height in heights) else 1
    operands, in_specs, out_specs, out_shape = [], [], [], []
    for item, height in zip(sums, heights):
        arrays, specs = item.blocks(height, grid, 1)
        operands += arrays
        in_specs += specs
        width = arrays[0].shape[2]
        out_specs.append(pl.BlockSpec((height // grid, width), lambda i: (i, 0)))
        out_shape.append(jax.ShapeDtypeStruct((height, width), bf16))
    whole_small = pl.BlockSpec(small.terms[0].shape, lambda i: (0, 0))
    return pl.pallas_call(
        functools.partial(halve_kernel, [len(item.terms) for item in sums]),
        grid=(grid,),
        in_specs=in_specs + [whole_small] * 2,
        out_specs=out_specs + [whole_small],
        out_shape=out_shape + [jax.ShapeDtypeStruct(small.terms[0].shape, f32)],
        compiler_params=pltpu.CompilerParams(vmem_limit_bytes=VMEM),
        name="halve",
    )(*operands, *small.terms)


def launch(lead, sums, small, *others):
    lead, others, halves = lax.optimization_barrier((lead, others, halve(sums, small)))
    for item, away in zip(sums, halves):
        item.send(away)
    small.send(halves[-1])
    return (lead, *others)


def settle(lead, sums, small):
    everything = sums + [small]
    lead, terms = lax.optimization_barrier((lead, [item.terms for item in everything]))
    for item, arrays in zip(everything, terms):
        item.terms = list(arrays)
    return lead


def collect_kernel(counts, *refs):
    at = 0
    for count, out in zip(counts, refs[sum(counts) :]):
        out[...] = functools.reduce(jnp.add, [ref[0].astype(f32) for ref in refs[at : at + count]])
        at += count


def collect(sums):
    operands, in_specs, out_specs, out_shape = [], [], [], []
    for item in sums:
        arrays, specs = item.blocks(item.height, 1, 0)
        operands += arrays
        in_specs += specs
        shape = arrays[0].shape[1:]
        out_specs.append(pl.BlockSpec(shape, lambda i: (0, 0)))
        out_shape.append(jax.ShapeDtypeStruct(shape, f32))
    return pl.pallas_call(
        functools.partial(collect_kernel, [len(item.terms) for item in sums]),
        grid=(1,),
        in_specs=in_specs,
        out_specs=out_specs,
        out_shape=out_shape,
        compiler_params=pltpu.CompilerParams(vmem_limit_bytes=VMEM),
        name="collect",
    )(*operands)


def read_small(ref, at, rows):
    parts = [ref[at + i * rows : at + (i + 1) * rows, :].astype(f32) for i in range(3)]
    return parts[0] + parts[1] + parts[2]


def joint_kernel(plan, last, *refs):
    count, buffers, from_at, small_from, to_at, small_to, rows = plan
    arrays, refs = refs[:count], refs[count:]
    received, refs = refs[:buffers], refs[buffers:]
    small, refs = refs[0], refs[1:]
    if small_from is None:
        total = small[...] + refs[0][...]
        refs = refs[1:]
    else:
        total = small[...] + read_small(received[small_from[0]], small_from[1], rows)
    if last:
        out, small_out = refs
        for i in range(count):
            which, at = from_at[i]
            height = arrays[i].shape[0]
            part = received[which][at : at + height, :].astype(f32)
            out[i * height : (i + 1) * height, :] = arrays[i][...].astype(f32) + part
        small_out[...] = total
        return
    outs, sent, small_out = refs[:count], refs[count:-1], refs[-1]
    for i in range(count):
        which, at = from_at[i]
        height = arrays[i].shape[0] // 2
        for half in range(2):
            here = slice(half * height, (half + 1) * height)
            there = slice(at + half * height, at + (half + 1) * height)
            part = arrays[i][here, :].astype(f32) + received[which][there, :].astype(f32)
            if half:
                which_out, at_out = to_at[i]
                sent[which_out][at_out : at_out + height, :] = part.astype(bf16)
            else:
                outs[i][...] = part.astype(bf16)
    small_out[...] = total
    which_out, at_out = small_to
    for part in split_three(total):
        sent[which_out][at_out : at_out + rows, :] = part.astype(bf16)
        at_out += rows


class Joint:
    def __init__(self, halves, orders, small):
        self.arrays = [kept for kept, _ in halves]
        self.received = [swap(given, "wide", 0) for _, given in halves]
        self.from_at = [(i, 0) for i in range(len(halves))]
        self.orders = [list(order) for order in orders]
        self.small, self.small_from = small, None
        self.extra = [swap(small, "wide", 0)]

    def call(self, plan, last, shapes):
        return pl.pallas_call(
            functools.partial(joint_kernel, plan, last),
            out_shape=shapes,
            compiler_params=pltpu.CompilerParams(vmem_limit_bytes=VMEM),
            name="joint",
        )(*self.arrays, *self.received, self.small, *self.extra)

    def plan(self, to_at, small_to):
        buffers, rows = len(self.received), self.small.shape[0]
        count = len(self.arrays)
        return count, buffers, self.from_at, self.small_from, to_at, small_to, rows

    def step(self, lead, *others):
        bits, heights, to_at = [], [], []
        width = self.arrays[0].shape[1]
        for array, order in zip(self.arrays, self.orders):
            bit = order.pop(0)
            if bit not in bits:
                bits.append(bit)
                heights.append(0)
            which = bits.index(bit)
            to_at.append((which, heights[which]))
            heights[which] += array.shape[0] // 2
        small_to = (0, heights[0])
        heights[0] += 3 * self.small.shape[0]
        shapes = [
            jax.ShapeDtypeStruct((array.shape[0] // 2, width), bf16) for array in self.arrays
        ]
        shapes += [jax.ShapeDtypeStruct((height, width), bf16) for height in heights]
        shapes += [jax.ShapeDtypeStruct(self.small.shape, f32)]
        outs = self.call(self.plan(to_at, small_to), False, shapes)
        lead, others, outs = lax.optimization_barrier((lead, others, outs))
        count = len(self.arrays)
        self.arrays, sent, self.small = outs[:count], outs[count:-1], outs[-1]
        self.received = [swap(item, *bit) for item, bit in zip(sent, bits)]
        self.from_at, self.small_from, self.extra = to_at, small_to, []
        return (lead, *others)

    def result(self):
        height = sum(array.shape[0] for array in self.arrays)
        shapes = [
            jax.ShapeDtypeStruct((height, self.arrays[0].shape[1]), f32),
            jax.ShapeDtypeStruct(self.small.shape, f32),
        ]
        return self.call(self.plan([], None), True, shapes)


def angles(positions):
    half = HEAD_DIM // 2
    freqs = jnp.power(10000.0, -jnp.arange(half, dtype=f32) / half)
    theta = freqs[:, None] * positions.astype(f32)[None, :]
    return jnp.cos(theta), jnp.sin(theta)


def axis_bits(axis):
    return [(axis, position) for position in range(lax.axis_size(axis).bit_length() - 1)]


def body(
    inputs,
    cotangent,
    lengths,
    w_qkv,
    b_qkv,
    w_out,
    b_out,
    w_up,
    b_up,
    w_down,
    b_down,
    gain_one,
    shift_one,
    gain_two,
    shift_two,
    gain_three,
    shift_three,
    gain_four,
    shift_four,
):
    group = inputs.shape[3]
    width = inputs.shape[4]
    parts = lax.axis_size("narrow")
    place = lax.axis_index("narrow")
    cores = lax.axis_size("wide")
    others = parts - 1
    rows = 2 * group
    offsets = jnp.arange(group, dtype=jnp.int32)

    def row(vector):
        return vector[None, :]

    def positions(owners):
        starts = jnp.stack([owners, 2 * parts - 1 - owners], axis=1).reshape(-1) * group
        return (starts[:, None] + offsets[None]).reshape(-1)

    def joined(items):
        return jnp.concatenate(items, axis=0) if len(items) > 1 else items[0]

    tokens = inputs.reshape(rows, width)
    far_tokens = joined(
        [
            lax.ppermute(tokens, "narrow", [((n + shift) % parts, n) for n in range(parts)])
            for shift in range(1, parts)
        ]
    )
    other = (place + 1 + jnp.arange(others, dtype=jnp.int32)) % parts
    early_at = place * group
    late_at = (2 * parts - 1 - place) * group
    info = jnp.stack([place, lengths[0], early_at, late_at]).astype(jnp.int32)
    marks = jnp.stack([lax.axis_index("wide"), place]).astype(jnp.int32)
    turns = angles(positions(place[None]))
    turns_far = angles(positions(other))

    norm_one = [row(gain_one), row(shift_one)]
    normed, qT, kT, vT = project(tokens, w_qkv, row(b_qkv), *norm_one, *turns, (0, 1, 2))
    state, kept_own, flags_own = attend_local(info, qT, kT, vT, group)
    normed_far, kT_far, vT_far = project(
        far_tokens, w_qkv, row(b_qkv), *norm_one, *turns_far, (1, 2)
    )
    oT, lse, kept_far, flags_far = attend_remote(
        info, qT, kT_far, vT_far, state, group, parts
    )

    blocks = block_call(
        oT,
        lse,
        tokens,
        cotangent.reshape(rows, width),
        [w_out, w_up, w_down],
        [row(item) for item in (b_out, b_up, b_down)]
        + [row(item) for item in (gain_two, shift_two, gain_three, shift_three)]
        + [row(item) for item in (gain_four, shift_four)],
    )
    result, d_middle, hidden, d_outer, normed_two, d_inner, d_branch = blocks[:7]
    doT, scaled, delta, small, small_up = blocks[7:]

    wide_bits = axis_bits("wide")
    narrow_bits = axis_bits("narrow")
    first_order = wide_bits[1:2] + narrow_bits + wide_bits[2:]
    second_order = narrow_bits + wide_bits[1:]
    third_order = narrow_bits + wide_bits[2:3] + wide_bits[1:2] + wide_bits[3:]
    fourth_order = wide_bits[2:3] + wide_bits[1:2] + narrow_bits + wide_bits[3:]
    fifth_order = wide_bits[2:3] + narrow_bits + wide_bits[1:2] + wide_bits[3:]
    small_order = wide_bits[:1] + first_order

    def outer(left, right, right_dim, order):
        return Halving(outer_halves(marks, left, right, right_dim, cores, parts, order), order)

    sum_up = outer(d_inner, normed_two, 0, first_order)
    sum_down = outer(d_outer, hidden, 0, second_order)
    sum_out = outer(d_branch, oT, 1, fifth_order)
    flat = jnp.concatenate([small.reshape(-1), small_up.reshape(-1)])
    early = Adding(flat.reshape(-1, PAIR), small_order)
    sums = [sum_down, sum_up, sum_out]

    heads = width // PAIR
    portions = 2 if heads % 2 == 0 else 1
    count = heads // portions
    (doT,) = launch(doT, sums, early)
    dq_far, d_far = back_remote(
        info,
        flags_far,
        [qT, doT, oT, lse, scaled, delta],
        turns_far,
        [kT_far, vT_far],
        kept_far,
        group,
        parts,
        0,
        heads,
        [],
    )
    d_back = unproject(d_far, w_qkv, (1, 2), 0, others * rows)
    d_mixed = []
    for portion in range(portions):
        doT, d_back = launch(doT, sums, early, d_back)
        if not portion:
            returned = [
                lax.ppermute(
                    d_back[j * rows : (j + 1) * rows] if others > 1 else d_back,
                    "narrow",
                    [(n, (n + j + 1) % parts) for n in range(parts)],
                )
                for j in range(others)
            ]
        d_mixed = [
            back_local(
                info,
                flags_own,
                [qT, doT, oT, lse, scaled, delta],
                turns,
                [kT, vT],
                dq_far,
                kept_own,
                group,
                portion * count,
                count,
                d_mixed,
            )
        ]
    d_mixed = d_mixed[0]
    while early.order:
        (d_mixed,) = launch(d_mixed, sums, early)
    d_mixed, returned = lax.optimization_barrier((d_mixed, returned))
    if others > 1:
        returned = [functools.reduce(jnp.add, [item.astype(f32) for item in returned])]

    orders = [first_order, third_order, fourth_order]
    pieces, late, steps = mixed_halves(
        marks,
        d_mixed.reshape(3 * width, rows),
        d_far.reshape(3 * width, -1),
        normed,
        normed_far,
        w_qkv,
        *norm_one,
        cores,
        parts,
        orders,
    )
    late, pieces = settle((late, pieces), sums, early)
    tail = Joint(pieces, orders, late)
    (d_mixed,) = tail.step(d_mixed)
    d_tokens = []
    for i in range(2):
        finish = (returned[0], tokens, d_middle, row(gain_one))
        d_tokens = [
            unproject(d_mixed, w_qkv, (0, 1, 2), i * group, group, finish, d_tokens)
        ]
        if tail.orders[0]:
            d_mixed, d_tokens[0] = tail.step(d_mixed, d_tokens[0])
    while tail.orders[0]:
        d_tokens[0], *terms = tail.step(d_tokens[0], *[item.terms for item in sums])
        for item, arrays in zip(sums, terms):
            item.terms = list(arrays)

    sum_w_down, sum_w_up, sum_w_out = collect(sums)
    sum_w_qkv, late_small = tail.result()
    grad_b_qkv = late_small[:steps, : 3 * width // steps].reshape(-1)
    early_small = (early.terms[0] + early.terms[1]).reshape(-1)
    small = early_small[: 8 * width].reshape(8, width)
    small_up = early_small[8 * width :]
    shape = inputs.shape
    return (
        result.reshape(shape),
        d_tokens[0].reshape(shape),
        sum_w_qkv.T,
        sum_w_out.T,
        sum_w_up.T,
        sum_w_down.T,
        grad_b_qkv,
        small[7],
        small_up,
        small[2],
        late_small[steps],
        late_small[steps + 1],
        small[5],
        small[6],
        small[3],
        small[4],
        small[0],
        small[1],
    )


def solution(mesh):
    tokens = P("wide", None, "narrow", None, None)
    columns = P(None, ("wide", "narrow"))
    in_specs = (tokens, tokens, P("wide")) + (P(),) * 16
    out_specs = (tokens, tokens) + (columns,) * 4 + (P(),) * 12
    return jax.shard_map(body, mesh=mesh, in_specs=in_specs, out_specs=out_specs, check_vma=False)
```

```python
import functools

import jax
import jax.numpy as jnp
from jax import lax
from jax.experimental import pallas as pl
from jax.experimental.pallas import tpu as pltpu
from jax.sharding import PartitionSpec as P

HEAD_DIM = 64
PAIR = 2 * HEAD_DIM
EPS = 1e-05
LOG2E = 1.4426950408889634
LN2 = 0.6931471805599453
NEG = -1e30
REACH = 60.0
VMEM = 62 * 1024 * 1024
SPAN = 1024

f32 = jnp.float32
bf16 = jnp.bfloat16


def dot(left, right, left_dim, right_dim):
    return lax.dot_general(
        left, right, (((left_dim,), (right_dim,)), ((), ())), preferred_element_type=f32
    )


def bounded(qT, kT):
    worst = None
    for h in range(2):
        rows = slice(HEAD_DIM * h, HEAD_DIM * (h + 1))
        norms = []
        for item in (qT, kT):
            values = item[rows, :].astype(f32)
            norms.append(jnp.max(jnp.sum(values * values, axis=0, keepdims=True)))
        both = norms[0] * norms[1]
        worst = both if worst is None else jnp.maximum(worst, both)
    return worst <= REACH * REACH


def fwd_chunk(fast, q0, k0, q_n, k_n, limit, store, qT, kT, vT, m_ref, l_ref, acc):
    queries = pl.ds(q0, q_n)
    strip = min(256, k_n)
    for h in range(2):
        rows = slice(HEAD_DIM * h, HEAD_DIM * (h + 1))
        old = m_ref[h : h + 1, queries]
        new = jnp.zeros_like(old) if fast else old
        strips = []
        for j in range(k_n // strip):
            keys = pl.ds(k0 + j * strip, strip)
            scores = dot(kT[rows, keys], qT[rows, queries], 0, 0)
            if limit is not None:
                key_at = lax.broadcasted_iota(jnp.int32, (strip, q_n), 0)
                scores = jnp.where(key_at < limit - j * strip, scores, NEG)
            strips.append(scores)
            if not fast:
                new = jnp.maximum(new, jnp.max(scores, axis=0, keepdims=True))
        factor = jnp.exp2(old - new)
        total = l_ref[h : h + 1, queries] * factor
        value = acc[rows, queries] * factor
        for j in range(k_n // strip):
            keys = pl.ds(k0 + j * strip, strip)
            weights = jnp.exp2(strips[j] if fast else strips[j] - new)
            total = total + jnp.sum(weights, axis=0, keepdims=True)
            weights = weights.astype(bf16)
            if fast:
                store(h, j, weights)
            value = value + dot(vT[rows, keys], weights, 1, 0)
        m_ref[h : h + 1, queries] = new
        l_ref[h : h + 1, queries] = total
        acc[rows, queries] = value


def pad_left(values, count):
    if not count:
        return values
    return jnp.concatenate([jnp.zeros((values.shape[0], count), f32), values], axis=1)


def pad_right(values, count):
    if not count:
        return values
    return jnp.concatenate([values, jnp.zeros((values.shape[0], count), f32)], axis=1)


def fwd_diagonal(fast, base, group, limit, store, qT, kT, vT, m_ref, l_ref, acc):
    strip = min(256, group)
    count = group // strip
    for h in range(2):
        rows = slice(HEAD_DIM * h, HEAD_DIM * (h + 1))
        strips = []
        for j in range(count):
            wide = group - j * strip
            keys, queries = pl.ds(base + j * strip, strip), pl.ds(base + j * strip, wide)
            scores = dot(kT[rows, keys], qT[rows, queries], 0, 0)
            key_at = lax.broadcasted_iota(jnp.int32, scores.shape, 0)
            query_at = lax.broadcasted_iota(jnp.int32, scores.shape, 1)
            scores = jnp.where(key_at <= query_at, scores, NEG)
            if limit is not None:
                scores = jnp.where(key_at < limit - j * strip, scores, NEG)
            strips.append(scores)
        peaks = []
        for g in range(0 if fast else count):
            peak = None
            for j in range(g + 1):
                part = strips[j][:, (g - j) * strip : (g - j + 1) * strip]
                part = jnp.max(part, axis=0, keepdims=True)
                peak = part if peak is None else jnp.maximum(peak, part)
            peaks.append(peak)
        if fast:
            peak = jnp.zeros((1, group), f32)
        else:
            peak = jnp.concatenate(peaks, axis=1) if count > 1 else peaks[0]
        total, value = None, None
        for j in range(count):
            keys = pl.ds(base + j * strip, strip)
            weights = jnp.exp2(strips[j] if fast else strips[j] - peak[:, j * strip :])
            part = pad_left(jnp.sum(weights, axis=0, keepdims=True), j * strip)
            weights = weights.astype(bf16)
            if fast:
                store(h, j, weights)
            term = pad_left(dot(vT[rows, keys], weights, 1, 0), j * strip)
            total = part if total is None else total + part
            value = term if value is None else value + term
        queries = pl.ds(base, group)
        m_ref[h : h + 1, queries] = peak
        l_ref[h : h + 1, queries] = total
        acc[rows, queries] = value


def triangle_slot(i, j, group):
    strip = min(256, group)
    count = group // strip
    row = jnp.where(i == 0, j, count - j) * strip
    column = jnp.where(i == 0, j * strip, 0)
    wide = group - j * strip
    return (
        pl.ds(pl.multiple_of(row, strip), strip),
        pl.ds(pl.multiple_of(column, strip), wide),
    )


def square_slot(j, group):
    strip = min(256, group)
    return pl.ds(group + strip + j * strip, strip), slice(None)


def fwd_local_kernel(group, info, qT, kT, vT, acc, m_ref, l_ref, kept, flags):
    length = info[1]
    m_ref[...] = jnp.full(m_ref.shape, NEG, f32)
    l_ref[...] = jnp.zeros(l_ref.shape, f32)
    acc[...] = jnp.zeros(acc.shape, f32)
    refs = (qT, kT, vT, m_ref.at[0], l_ref.at[0], acc)

    def walk(fast):
        def own(i, carry):
            base = pl.multiple_of(i * group, group)
            start = info[2 + i]

            def store(h, j, weights):
                rows, columns = triangle_slot(i, j, group)
                kept[h, rows, columns] = weights

            @pl.when(start + group <= length)
            def _():
                fwd_diagonal(fast, base, group, None, store, *refs)

            @pl.when((start < length) & (start + group > length))
            def _():
                fwd_diagonal(fast, base, group, length - start, store, *refs)

            return carry

        lax.fori_loop(0, 2, own, 0)
        early = info[2]

        def store(h, j, weights):
            rows, columns = square_slot(j, group)
            kept[h, rows, columns] = weights

        @pl.when(early + group <= length)
        def _():
            fwd_chunk(fast, group, 0, group, group, None, store, *refs)

        @pl.when((early < length) & (early + group > length))
        def _():
            fwd_chunk(fast, group, 0, group, group, length - early, store, *refs)

    small = bounded(qT, kT)
    flags[pl.program_id(0)] = small.astype(jnp.int32)
    pl.when(small)(functools.partial(walk, True))
    pl.when(jnp.logical_not(small))(functools.partial(walk, False))


def remote_steps(group, parts, info, full, partial):
    place, length = info[0], info[1]

    def visit(i, carry):
        j, turn_at = i // 3, lax.rem(i, 3)
        other = lax.rem(place + 1 + j, parts)
        late_key = turn_at == 2
        block = jnp.where(late_key, 2 * parts - 1 - other, other)
        before = (other < place).astype(jnp.int32)
        wanted = jnp.where(turn_at == 0, before, jnp.where(late_key, 1 - before, 1)) == 1
        q0 = pl.multiple_of(jnp.where(turn_at == 0, 0, group), group)
        k0 = pl.multiple_of((2 * j + jnp.where(late_key, 1, 0)) * group, group)
        slot = pl.multiple_of((2 * j + turn_at - (1 - before)) * group, group)
        start = block * group

        @pl.when(wanted & (start + group <= length))
        def _():
            full(q0, k0, slot)

        @pl.when(wanted & (start < length) & (start + group > length))
        def _():
            partial(q0, k0, slot, length - start)

        return carry

    lax.fori_loop(0, 3 * (parts - 1), visit, 0)


def fwd_remote_kernel(
    group, parts, info, qT, kT, vT, acc_in, m_in, l_in, out, lse, kept, flags, acc, m_ref, l_ref
):
    acc[...] = acc_in[...]
    m_ref[...] = m_in[0]
    l_ref[...] = l_in[0]
    refs = (qT, kT, vT, m_ref, l_ref, acc)
    strip = min(256, group)

    def walk(fast):
        def partial(q0, k0, slot, limit):
            def store(h, j, weights):
                kept[h, pl.ds(pl.multiple_of(slot + j * strip, strip), strip), :] = weights

            fwd_chunk(fast, q0, k0, group, group, limit, store, *refs)

        def full(q0, k0, slot):
            partial(q0, k0, slot, None)

        remote_steps(group, parts, info, full, partial)

    small = bounded(qT, kT) & (jnp.max(m_in[...]) <= 0.0)
    flags[pl.program_id(0)] = small.astype(jnp.int32)
    pl.when(small)(functools.partial(walk, True))
    pl.when(jnp.logical_not(small))(functools.partial(walk, False))
    for h in range(2):
        rows = slice(HEAD_DIM * h, HEAD_DIM * (h + 1))
        total = l_ref[h : h + 1, :]
        out[rows, :] = (acc[rows, :] / total).astype(bf16)
        lse[0, h : h + 1, :] = m_ref[h : h + 1, :] + jnp.log2(total)


def split_three(values):
    high = values.astype(bf16).astype(f32)
    rest = values - high
    middle = rest.astype(bf16).astype(f32)
    low = (rest - middle).astype(bf16).astype(f32)
    return [high, middle, low]


def bwd_prepare(qT, kT, vT, doT, oT, lse, qa, da, ka, va):
    n_q, n_k = qT.shape[1], ka.shape[2]
    extra = qa.shape[1] - HEAD_DIM
    pad = jnp.zeros((extra - 3, n_q), f32)
    row_at = lax.broadcasted_iota(jnp.int32, (extra, n_k), 0)
    tail = jnp.where(row_at < 3, 1.0, 0.0).astype(bf16)
    for h in range(2):
        rows = slice(HEAD_DIM * h, HEAD_DIM * (h + 1))
        grad = doT[rows, :].astype(f32)
        delta = jnp.sum(grad * oT[rows, :].astype(f32), axis=0, keepdims=True)
        qa[h, :HEAD_DIM, :] = qT[rows, :]
        parts = split_three(-lse[0, h : h + 1, :]) + [pad]
        qa[h, HEAD_DIM:, :] = jnp.concatenate(parts, axis=0).astype(bf16)
        da[h, :HEAD_DIM, :] = doT[rows, :]
        parts = split_three(-delta) + [pad]
        da[h, HEAD_DIM:, :] = jnp.concatenate(parts, axis=0).astype(bf16)
        ka[h, :HEAD_DIM, :] = kT[rows, :]
        va[h, :HEAD_DIM, :] = vT[rows, :]
        ka[h, HEAD_DIM:, :] = tail
        va[h, HEAD_DIM:, :] = tail


def bwd_chunk(q0, k0, q_n, k_n, limit, qT, doT, qa, da, ka, va, dq, dk, dv):
    queries, keys = pl.ds(q0, q_n), pl.ds(k0, k_n)
    for h in range(2):
        rows = slice(HEAD_DIM * h, HEAD_DIM * (h + 1))
        probs = jnp.exp2(dot(qa[h, :, queries], ka[h, :, keys], 0, 0))
        if limit is not None:
            key_at = lax.broadcasted_iota(jnp.int32, (q_n, k_n), 1)
            probs = jnp.where(key_at < limit, probs, 0.0)
        d_probs = dot(da[h, :, queries], va[h, :, keys], 0, 0)
        d_scores = (probs * d_probs).astype(bf16)
        dv[rows, keys] += dot(doT[rows, queries], probs.astype(bf16), 1, 0)
        dk[rows, keys] += dot(qT[rows, queries], d_scores, 1, 0)
        dq[rows, queries] += dot(ka[h, :HEAD_DIM, keys], d_scores, 1, 1)


def bwd_diagonal(base, group, limit, qT, doT, qa, da, ka, va, dq, dk, dv):
    strip = min(256, group)
    count = group // strip
    for h in range(2):
        rows = slice(HEAD_DIM * h, HEAD_DIM * (h + 1))
        d_keys, d_values, d_queries = None, None, []
        for j in range(count):
            wide = (j + 1) * strip
            queries, keys = pl.ds(base + j * strip, strip), pl.ds(base, wide)
            probs = jnp.exp2(dot(qa[h, :, queries], ka[h, :, keys], 0, 0))
            query_at = lax.broadcasted_iota(jnp.int32, probs.shape, 0)
            key_at = lax.broadcasted_iota(jnp.int32, probs.shape, 1)
            probs = jnp.where(key_at <= query_at + j * strip, probs, 0.0)
            if limit is not None:
                probs = jnp.where(key_at < limit, probs, 0.0)
            d_probs = dot(da[h, :, queries], va[h, :, keys], 0, 0)
            d_scores = (probs * d_probs).astype(bf16)
            value = pad_right(dot(doT[rows, queries], probs.astype(bf16), 1, 0), group - wide)
            key = pad_right(dot(qT[rows, queries], d_scores, 1, 0), group - wide)
            d_values = value if d_values is None else d_values + value
            d_keys = key if d_keys is None else d_keys + key
            d_queries.append(dot(ka[h, :HEAD_DIM, keys], d_scores, 1, 1))
        here = pl.ds(base, group)
        dq[rows, here] += jnp.concatenate(d_queries, axis=1) if count > 1 else d_queries[0]
        dk[rows, here] += d_keys
        dv[rows, here] += d_values


def stored_chunk(h, weights, queries, keys, qT, kT, vT, scaled, delta, dq, dk, dv):
    rows = slice(HEAD_DIM * h, HEAD_DIM * (h + 1))
    d_probs = dot(vT[rows, keys], scaled[rows, queries], 0, 0)
    d_scores = weights.astype(f32) * (d_probs - delta[0, h : h + 1, queries])
    d_scores = d_scores.astype(bf16)
    dv[rows, keys] += dot(scaled[rows, queries], weights, 1, 1)
    dk[rows, keys] += dot(qT[rows, queries], d_scores, 1, 1)
    dq[rows, queries] += dot(kT[rows, keys], d_scores, 1, 0)


def turn_back(values, cosine, sine):
    half = HEAD_DIM // 2
    first, second = values[:half], values[half:]
    return jnp.concatenate(
        [first * cosine + second * sine, second * cosine - first * sine], axis=0
    )


def bwd_remote_kernel(
    group,
    parts,
    first,
    info,
    flags,
    qT,
    doT,
    oT,
    lse,
    scaled,
    delta,
    cosine,
    sine,
    kT,
    vT,
    kept,
    *rest,
):
    dq, dkv, qa, da, ka, va, dk, dv = rest[-8:]
    dq[...] = jnp.zeros(dq.shape, f32)
    dk[...] = jnp.zeros(dk.shape, f32)
    dv[...] = jnp.zeros(dv.shape, f32)
    fast = flags[first + pl.program_id(0)] == 1

    @pl.when(fast)
    def _():
        def full(q0, k0, slot):
            for h in range(2):
                weights = kept[h, pl.ds(slot, group), :]
                queries, keys = pl.ds(q0, group), pl.ds(k0, group)
                stored_chunk(h, weights, queries, keys, qT, kT, vT, scaled, delta, dq, dk, dv)

        def partial(q0, k0, slot, limit):
            full(q0, k0, slot)

        remote_steps(group, parts, info, full, partial)

    @pl.when(jnp.logical_not(fast))
    def _():
        bwd_prepare(qT, kT, vT, doT, oT, lse, qa, da, ka, va)
        refs = (qT, doT, qa, da, ka, va, dq, dk, dv)

        def full(q0, k0, slot):
            bwd_chunk(q0, k0, group, group, None, *refs)

        def partial(q0, k0, slot, limit):
            bwd_chunk(q0, k0, group, group, limit, *refs)

        remote_steps(group, parts, info, full, partial)

    for h in range(2):
        rows = slice(HEAD_DIM * h, HEAD_DIM * (h + 1))
        dkv[1, rows, :] = turn_back(dk[rows, :] * LN2, cosine[...], sine[...]).astype(bf16)
    dkv[0] = jnp.zeros(dv.shape, bf16)
    dkv[2] = dv[...].astype(bf16)


def bwd_local_kernel(
    group,
    first,
    info,
    flags,
    qT,
    doT,
    oT,
    lse,
    scaled,
    delta,
    cosine,
    sine,
    kT,
    vT,
    dq_in,
    kept,
    *rest,
):
    dqkv, qa, da, ka, va, dk, dv, dq = rest[-8:]
    length = info[1]
    dq[...] = dq_in[...]
    dk[...] = jnp.zeros(dk.shape, f32)
    dv[...] = jnp.zeros(dv.shape, f32)
    early = info[2]
    strip = min(256, group)
    fast = flags[first + pl.program_id(0)] == 1

    @pl.when(fast)
    def _():
        refs = (qT, kT, vT, scaled, delta, dq, dk, dv)

        def own(i, carry):
            base = pl.multiple_of(i * group, group)

            @pl.when(info[2 + i] < length)
            def _():
                for h in range(2):
                    for j in range(group // strip):
                        rows, columns = triangle_slot(i, j, group)
                        queries = pl.ds(base + j * strip, group - j * strip)
                        keys = pl.ds(base + j * strip, strip)
                        stored_chunk(h, kept[h, rows, columns], queries, keys, *refs)

            return carry

        lax.fori_loop(0, 2, own, 0)

        @pl.when(early < length)
        def _():
            for h in range(2):
                weights = kept[h, group + strip :, :]
                stored_chunk(h, weights, pl.ds(group, group), pl.ds(0, group), *refs)

    @pl.when(jnp.logical_not(fast))
    def _():
        bwd_prepare(qT, kT, vT, doT, oT, lse, qa, da, ka, va)
        refs = (qT, doT, qa, da, ka, va, dq, dk, dv)

        def own(i, carry):
            base = pl.multiple_of(i * group, group)
            start = info[2 + i]

            @pl.when(start < length)
            def _():
                bwd_diagonal(base, group, length - start, *refs)

            return carry

        lax.fori_loop(0, 2, own, 0)

        @pl.when(early < length)
        def _():
            bwd_chunk(group, 0, group, group, length - early, *refs)

    for h in range(2):
        rows = slice(HEAD_DIM * h, HEAD_DIM * (h + 1))
        d_query = dq[rows, :] * 0.125
        dqkv[0, rows, :] = turn_back(d_query, cosine[...], sine[...]).astype(bf16)
        dqkv[1, rows, :] = turn_back(dk[rows, :] * LN2, cosine[...], sine[...]).astype(bf16)
    dqkv[2] = dv[...].astype(bf16)


def rows_of(count, first=0):
    return pl.BlockSpec((PAIR, count), lambda i, *info: (first + i, 0))


def stats_of(count, first=0):
    return pl.BlockSpec((1, 2, count), lambda i, *info: (first + i, 0, 0))


def planes_of(planes, count, first=0):
    return pl.BlockSpec((planes, PAIR, count), lambda i, *info: (0, first + i, 0))


def kept_of(rows, group, first=0):
    return pl.BlockSpec((2, rows, group), lambda i, *info: (first + i, 0, 0))


def scalars():
    return pl.BlockSpec(memory_space=pltpu.SMEM)


def whole(shape):
    return pl.BlockSpec(shape, lambda i, *info: (0,) * len(shape))


def attention_call(kernel, pairs, in_specs, out_specs, out_shape, scratch, flops, name, alias={}, prefetch=1):
    return pl.pallas_call(
        kernel,
        grid_spec=pltpu.PrefetchScalarGridSpec(
            num_scalar_prefetch=prefetch,
            grid=(pairs,),
            in_specs=in_specs,
            out_specs=out_specs,
            scratch_shapes=scratch,
        ),
        out_shape=out_shape,
        input_output_aliases=alias,
        compiler_params=pltpu.CompilerParams(vmem_limit_bytes=VMEM),
        cost_estimate=pl.CostEstimate(
            flops=int(flops), bytes_accessed=1 << 25, transcendentals=0
        ),
        name=name,
    )


def attend_local(info, qT, kT, vT, group):
    width, n_q = qT.shape
    pairs = width // PAIR
    kept_rows = 2 * group + min(256, group)
    call = attention_call(
        functools.partial(fwd_local_kernel, group),
        pairs,
        [rows_of(n_q)] * 3,
        [rows_of(n_q), stats_of(n_q), stats_of(n_q), kept_of(kept_rows, group), scalars()],
        [
            jax.ShapeDtypeStruct((width, n_q), f32),
            jax.ShapeDtypeStruct((pairs, 2, n_q), f32),
            jax.ShapeDtypeStruct((pairs, 2, n_q), f32),
            jax.ShapeDtypeStruct((2 * pairs, kept_rows, group), bf16),
            jax.ShapeDtypeStruct((pairs,), jnp.int32),
        ],
        [],
        4 * width * 2 * group * group * 4,
        "attend_local",
    )
    *state, kept, flags = call(info, qT, kT, vT)
    return state, kept, flags


def attend_remote(info, qT, kT, vT, state, group, parts):
    width, n_q = qT.shape
    n_k = kT.shape[1]
    pairs = width // PAIR
    call = attention_call(
        functools.partial(fwd_remote_kernel, group, parts),
        pairs,
        [rows_of(n_q), rows_of(n_k), rows_of(n_k), rows_of(n_q), stats_of(n_q), stats_of(n_q)],
        [rows_of(n_q), stats_of(n_q), kept_of(n_k, group), scalars()],
        [
            jax.ShapeDtypeStruct((width, n_q), bf16),
            jax.ShapeDtypeStruct((pairs, 2, n_q), f32),
            jax.ShapeDtypeStruct((2 * pairs, n_k, group), bf16),
            jax.ShapeDtypeStruct((pairs,), jnp.int32),
        ],
        [pltpu.VMEM((PAIR, n_q), f32)] + [pltpu.VMEM((2, n_q), f32)] * 2,
        4 * width * 2 * group * group * 4,
        "attend_remote",
    )
    return call(info, qT, kT, vT, *state)


def back_scratch(n_q, n_k):
    rows = HEAD_DIM + 16
    return (
        [pltpu.VMEM((2, rows, n_q), bf16)] * 2
        + [pltpu.VMEM((2, rows, n_k), bf16)] * 2
        + [pltpu.VMEM((PAIR, n_k), f32)] * 2
    )


def back_remote(info, flags, operands, turns, keys, kept, group, parts, first, count, before):
    width, n_q = operands[0].shape
    n_k = keys[0].shape[1]
    half = HEAD_DIM // 2
    n_in = 2 + len(operands) + len(turns) + len(keys) + 1
    call = attention_call(
        functools.partial(bwd_remote_kernel, group, parts, first),
        count,
        [rows_of(n_q, first)] * 3
        + [stats_of(n_q, first), rows_of(n_q, first), stats_of(n_q, first)]
        + [whole((half, n_k))] * 2
        + [rows_of(n_k, first)] * 2
        + [kept_of(kept.shape[1], group, first)]
        + [pl.BlockSpec(memory_space=pl.ANY)] * len(before),
        [rows_of(n_q, first), planes_of(3, n_k, first)],
        [
            jax.ShapeDtypeStruct((width, n_q), f32),
            jax.ShapeDtypeStruct((3, width, n_k), bf16),
        ],
        back_scratch(n_q, n_k),
        10 * count * PAIR * 2 * group * group * 4,
        "back_remote",
        {n_in + i: i for i in range(len(before))},
        2,
    )
    return call(info, flags, *operands, *turns, *keys, kept, *before)


def back_local(info, flags, operands, turns, keys, dq, kept, group, first, count, before):
    width, n_q = operands[0].shape
    half = HEAD_DIM // 2
    n_in = 2 + len(operands) + len(turns) + len(keys) + 2
    call = attention_call(
        functools.partial(bwd_local_kernel, group, first),
        count,
        [rows_of(n_q, first)] * 3
        + [stats_of(n_q, first), rows_of(n_q, first), stats_of(n_q, first)]
        + [whole((half, n_q))] * 2
        + [rows_of(n_q, first)] * 3
        + [kept_of(kept.shape[1], group, first)]
        + [pl.BlockSpec(memory_space=pl.ANY)] * len(before),
        planes_of(3, n_q, first),
        jax.ShapeDtypeStruct((3, width, n_q), bf16),
        back_scratch(n_q, n_q) + [pltpu.VMEM((PAIR, n_q), f32)],
        10 * count * PAIR * 2 * group * group * 4,
        "back_local",
        {n_in + i: i for i in range(len(before))},
        2,
    )
    return call(info, flags, *operands, *turns, *keys, dq, kept, *before)


def normalize(values):
    centre = values - jnp.mean(values, axis=-1, keepdims=True)
    spread = jnp.mean(centre * centre, axis=-1, keepdims=True)
    rate = lax.rsqrt(spread + EPS)
    return centre * rate, rate


def norm_back(grad, unit, rate, gain):
    scaled = grad * gain
    first = jnp.mean(scaled, axis=-1, keepdims=True)
    second = jnp.mean(scaled * unit, axis=-1, keepdims=True)
    return rate * (scaled - first - unit * second)


GELU_A = 0.7978845608028654
GELU_B = 0.044715


def column_sum(values):
    return jnp.sum(values, axis=0, keepdims=True)


def block_kernel(
    span,
    oT,
    lse,
    tokens,
    cotangent,
    w_out,
    w_up,
    w_down,
    b_out,
    b_up,
    b_down,
    gain_two,
    shift_two,
    gain_three,
    shift_three,
    gain_four,
    shift_four,
    result,
    d_middle_out,
    hidden_out,
    d_outer_out,
    normed_out,
    d_inner_out,
    d_branch_out,
    doT,
    scaled,
    delta,
    small,
    small_up,
    slope,
):
    step = pl.program_id(0)

    @pl.when(step == 0)
    def _():
        small[...] = jnp.zeros(small.shape, f32)
        small_up[...] = jnp.zeros(small_up.shape, f32)

    wide = w_up.shape[1]
    branch = dot(oT[...], w_out[...], 0, 0) + b_out[...]
    unit_two, rate_two = normalize(branch)
    middle = tokens[...].astype(f32) + (unit_two * gain_two[...] + shift_two[...])
    unit_three, rate_three = normalize(middle)
    normed = (unit_three * gain_three[...] + shift_three[...]).astype(bf16)
    normed_out[...] = normed
    outer = None
    for c in range(wide // span):
        columns = slice(c * span, (c + 1) * span)
        inner = dot(normed, w_up[:, columns], 1, 0) + b_up[:, columns]
        square = inner * inner
        bend = jnp.tanh(inner * (GELU_A + (GELU_A * GELU_B) * square))
        half = 0.5 + 0.5 * bend
        hidden = (inner * half).astype(bf16)
        hidden_out[:, columns] = hidden
        slope[:, columns] = half + inner * (1.0 - bend * bend) * (
            0.5 * GELU_A + (1.5 * GELU_A * GELU_B) * square
        )
        term = dot(hidden, w_down[columns, :], 1, 0)
        outer = term if outer is None else outer + term
    unit_four, rate_four = normalize(outer + b_down[...])
    result[...] = (middle + (unit_four * gain_four[...] + shift_four[...])).astype(bf16)

    grad = cotangent[...].astype(f32)
    d_outer = norm_back(grad, unit_four, rate_four, gain_four[...]).astype(bf16)
    d_outer_out[...] = d_outer
    small[0:1, :] += column_sum(grad * unit_four)
    small[1:2, :] += column_sum(grad)
    small[2:3, :] += column_sum(d_outer.astype(f32))
    d_normed = None
    for c in range(wide // span):
        columns = slice(c * span, (c + 1) * span)
        d_hidden = dot(d_outer, w_down[columns, :], 1, 1)
        d_inner = (d_hidden * slope[:, columns]).astype(bf16)
        d_inner_out[:, columns] = d_inner
        small_up[:, columns] += column_sum(d_inner.astype(f32))
        term = dot(d_inner, w_up[:, columns], 1, 1)
        d_normed = term if d_normed is None else d_normed + term
    small[3:4, :] += column_sum(d_normed * unit_three)
    small[4:5, :] += column_sum(d_normed)
    d_middle = grad + norm_back(d_normed, unit_three, rate_three, gain_three[...])
    d_middle_out[...] = d_middle
    small[5:6, :] += column_sum(d_middle * unit_two)
    small[6:7, :] += column_sum(d_middle)
    d_branch = norm_back(d_middle, unit_two, rate_two, gain_two[...]).astype(bf16)
    d_branch_out[...] = d_branch
    small[7:8, :] += column_sum(d_branch.astype(f32))
    d_attended = dot(w_out[...], d_branch, 1, 1).astype(bf16)
    doT[...] = d_attended
    for h in range(oT.shape[0] // HEAD_DIM):
        rows = slice(HEAD_DIM * h, HEAD_DIM * (h + 1))
        at = slice(h % 2, h % 2 + 1)
        part = (d_attended[rows].astype(f32) * jnp.exp2(-lse[h // 2, at, :])).astype(bf16)
        scaled[rows, :] = part
        delta[h // 2, at, :] = column_sum(part.astype(f32) * oT[rows, :].astype(f32))


def block_call(oT, lse, tokens, cotangent, weights, vectors):
    width, rows = oT.shape
    wide = weights[1].shape[1]
    step = min(256, rows)
    span = min(SPAN, wide)

    def lines(count):
        return pl.BlockSpec((step, count), lambda i: (i, 0))

    def fixed(shape):
        return pl.BlockSpec(shape, lambda i: (0, 0), pipeline_mode=pl.Buffered(1))

    def total(shape):
        return pl.BlockSpec(shape, lambda i: (0, 0))

    features = pl.BlockSpec((width, step), lambda i: (0, i))
    stats = pl.BlockSpec((*lse.shape[:2], step), lambda i: (0, 0, i))
    sizes = [width, width, wide, width, width, wide, width]
    kinds = [bf16, f32, bf16, bf16, bf16, bf16, bf16]
    return pl.pallas_call(
        functools.partial(block_kernel, span),
        grid=(rows // step,),
        in_specs=[features, stats, lines(width), lines(width)]
        + [fixed(item.shape) for item in weights]
        + [fixed(item.shape) for item in vectors],
        out_specs=[lines(size) for size in sizes]
        + [features, features, stats, total((8, width)), total((1, wide))],
        out_shape=[jax.ShapeDtypeStruct((rows, size), kind) for size, kind in zip(sizes, kinds)]
        + [
            jax.ShapeDtypeStruct((width, rows), bf16),
            jax.ShapeDtypeStruct((width, rows), bf16),
            jax.ShapeDtypeStruct(lse.shape, f32),
            jax.ShapeDtypeStruct((8, width), f32),
            jax.ShapeDtypeStruct((1, wide), f32),
        ],
        scratch_shapes=[pltpu.VMEM((step, wide), f32)],
        compiler_params=pltpu.CompilerParams(vmem_limit_bytes=VMEM),
        cost_estimate=pl.CostEstimate(
            flops=2 * 2 * rows * (width * width + 2 * width * wide),
            bytes_accessed=1 << 26,
            transcendentals=rows * wide,
        ),
        name="block",
    )(oT, lse, tokens, cotangent, *weights, *vectors)


def turn(values, cosine, sine):
    half = HEAD_DIM // 2
    first, second = values[:half], values[half:]
    return jnp.concatenate(
        [first * cosine - second * sine, second * cosine + first * sine], axis=0
    )


def project_kernel(sections, tokens, w, b, gain, shift, cosine, sine, normed_out, *outs):
    unit, rate = normalize(tokens[...].astype(f32))
    normed = (unit * gain[...] + shift[...]).astype(bf16)
    normed_out[...] = normed
    width = tokens.shape[1]
    chunk = min(256, width)
    for section, out in zip(sections, outs):
        for c in range(width // chunk):
            at = section * width + c * chunk
            mixed = (dot(normed, w[:, at : at + chunk], 1, 0) + b[:, at : at + chunk]).T
            for h in range(chunk // HEAD_DIM):
                rows = slice(h * HEAD_DIM, (h + 1) * HEAD_DIM)
                place = slice(c * chunk + h * HEAD_DIM, c * chunk + (h + 1) * HEAD_DIM)
                value = mixed[rows]
                if section < 2:
                    value = turn(value, cosine[...], sine[...])
                if section == 0:
                    value = value * (0.125 * LOG2E)
                out[place, :] = value.astype(bf16)


def project(tokens, w, b, gain, shift, cosine, sine, sections):
    rows, width = tokens.shape
    step = min(512, rows)
    half = HEAD_DIM // 2

    def fixed(shape):
        return pl.BlockSpec(shape, lambda i: (0, 0), pipeline_mode=pl.Buffered(1))

    lines = pl.BlockSpec((step, width), lambda i: (i, 0))
    features = pl.BlockSpec((width, step), lambda i: (0, i))
    turns = pl.BlockSpec((half, step), lambda i: (0, i))
    return pl.pallas_call(
        functools.partial(project_kernel, sections),
        grid=(rows // step,),
        in_specs=[lines, fixed(w.shape), fixed(b.shape), fixed(gain.shape), fixed(shift.shape)]
        + [turns] * 2,
        out_specs=[lines] + [features] * len(sections),
        out_shape=[jax.ShapeDtypeStruct((rows, width), bf16)]
        + [jax.ShapeDtypeStruct((width, rows), bf16)] * len(sections),
        compiler_params=pltpu.CompilerParams(vmem_limit_bytes=VMEM),
        cost_estimate=pl.CostEstimate(
            flops=2 * rows * width * width * len(sections),
            bytes_accessed=1 << 24,
            transcendentals=0,
        ),
        name="project",
    )(tokens, w, b, gain, shift, cosine, sine)


def unproject_kernel(planes, finish, *refs):
    d_mixed, w, out = refs[: len(planes)], refs[len(planes)], refs[-1]
    width = w.shape[0]
    total = None
    for plane, ref in zip(planes, d_mixed):
        term = dot(ref[0], w[:, plane * width : (plane + 1) * width], 0, 1)
        total = term if total is None else total + term
    if not finish:
        out[...] = total.astype(bf16)
        return
    returned, tokens, d_middle, gain = refs[len(planes) + 1 : len(planes) + 5]
    total = total + returned[...].astype(f32)
    unit, rate = normalize(tokens[...].astype(f32))
    out[...] = (d_middle[...] + norm_back(total, unit, rate, gain[...])).astype(bf16)


def unproject(d_mixed, w, planes, start, count, finish=(), before=()):
    _, width, total = d_mixed.shape
    step = min(256 if finish else 512, count)
    first = start // step

    def fixed(shape):
        return pl.BlockSpec(shape, lambda i: (0, 0), pipeline_mode=pl.Buffered(1))

    def plane_of(plane):
        return pl.BlockSpec((1, width, step), lambda i: (plane, 0, first + i))

    lines = pl.BlockSpec((step, width), lambda i: (i, 0))
    later = pl.BlockSpec((step, width), lambda i: (first + i, 0))
    specs = [later] * 3 + [fixed(finish[-1].shape)] if finish else []
    n_in = len(planes) + 1 + len(finish)
    return pl.pallas_call(
        functools.partial(unproject_kernel, planes, bool(finish)),
        grid=(count // step,),
        in_specs=[plane_of(plane) for plane in planes]
        + [fixed(w.shape)]
        + specs
        + [pl.BlockSpec(memory_space=pl.ANY)] * len(before),
        out_specs=later if finish else lines,
        out_shape=jax.ShapeDtypeStruct((total if finish else count, width), bf16),
        input_output_aliases={n_in + i: i for i in range(len(before))},
        compiler_params=pltpu.CompilerParams(vmem_limit_bytes=VMEM),
        cost_estimate=pl.CostEstimate(
            flops=2 * count * width * width * len(planes),
            bytes_accessed=1 << 24,
            transcendentals=0,
        ),
        name="unproject",
    )(*[d_mixed] * len(planes), w, *finish, *before)


def divide(total, run, levels, near, marks, orders, outs):
    bits = [("narrow", i) for i in range(near)] + [("wide", i) for i in range(levels + 1)]
    cut = run // len(orders)

    def write(core):
        for at in range(0, total.shape[0], run):
            number = at // run
            value = {}
            for place, (axis, position) in enumerate(bits):
                mine = (marks[1 if axis == "narrow" else 0] >> position) & 1
                value[axis, position] = mine ^ ((number >> place) & 1)
            other = core ^ ((number >> near) & 1)
            for i, order in enumerate(orders):
                index = tuple(value.get(bit, 0) for bit in order)
                part = total[at + i * cut : at + (i + 1) * cut]
                outs[2 * i + other][index] = part.astype(bf16)

    pl.when((marks[0] & 1) == 0)(functools.partial(write, 0))
    pl.when((marks[0] & 1) == 1)(functools.partial(write, 1))


def divided(orders, levels, run, height, wide, width):
    cut = run // len(orders)
    specs, shapes = [], []
    for order in orders:

        def held(bit):
            return bit[0] == "narrow" or bit[1] <= levels

        def index(j, i, marks, order=order):
            relative = i ^ (marks[0] >> (levels + 1))
            at = [0 if held(bit) else (relative >> (bit[1] - 1 - levels)) & 1 for bit in order]
            return (*at, 0, j)

        block = tuple(2 if held(bit) else 1 for bit in order) + (cut, wide)
        specs += [pl.BlockSpec(block, index)] * 2
        shapes += [jax.ShapeDtypeStruct((2,) * len(order) + (cut, width), bf16)] * 2
    return specs, shapes


def outer_kernel(run, levels, near, orders, right_dim, marks, left, right, *outs):
    divide(dot(left[...], right[...], 0, right_dim), run, levels, near, marks, orders, outs)


def outer_halves(marks, left, right, right_dim, cores, parts, order):
    rows, height = left.shape
    width = right.shape[1 - right_dim]
    share = height // cores
    high = max(2 * share, min(512 if right_dim else 1024, height))
    levels = (high // (2 * share)).bit_length() - 1
    wide = min(1024, width)
    if right_dim == 0:
        right_spec = pl.BlockSpec((rows, wide), lambda j, i, marks: (0, j))
    else:
        right_spec = pl.BlockSpec((wide, rows), lambda j, i, marks: (j, 0))
    run = share // parts
    near = parts.bit_length() - 1
    specs, shapes = divided([order], levels, run, height, wide, width)
    halves = pl.pallas_call(
        functools.partial(outer_kernel, run, levels, near, [order], right_dim),
        grid_spec=pltpu.PrefetchScalarGridSpec(
            num_scalar_prefetch=1,
            grid=(width // wide, height // high),
            in_specs=[pl.BlockSpec((rows, high), lambda j, i, marks: (0, i)), right_spec],
            out_specs=specs,
        ),
        out_shape=shapes,
        compiler_params=pltpu.CompilerParams(vmem_limit_bytes=VMEM),
        cost_estimate=pl.CostEstimate(
            flops=2 * rows * height * width, bytes_accessed=1 << 25, transcendentals=0
        ),
        name="outer",
    )(marks, left, right)
    return [item.reshape(height // 2, width) for item in halves]


def mixed_kernel(
    run,
    levels,
    near,
    orders,
    first_far,
    marks,
    d_own,
    d_far,
    normed,
    normed_far,
    w,
    gain,
    shift,
    *outs,
):
    *halves, small, sums, bias = outs
    step, last = pl.program_id(1), pl.num_programs(1) - 1
    total = dot(d_own[...], normed[...], 1, 0)
    bias[...] = jnp.sum(d_own[...].astype(f32), axis=1, keepdims=True)

    @pl.when(step == 0)
    def _():
        sums[...] = jnp.zeros(sums.shape, f32)
        small[...] = jnp.zeros(small.shape, f32)

    def finish(value):
        divide(value, run, levels, near, marks, orders, halves)
        weights = w[...].astype(f32).T
        sums[0:1, :] += column_sum(weights * value)
        sums[1:2, :] += column_sum(weights * bias[...])
        wide = jnp.broadcast_to(bias[...], (bias.shape[0], PAIR)).T
        small[pl.ds(step, 1), : bias.shape[0]] = wide[0:1, :]

    @pl.when(step < first_far)
    def _():
        finish(total)

    @pl.when(step >= first_far)
    def _():
        bias[...] += jnp.sum(d_far[...].astype(f32), axis=1, keepdims=True)
        finish(total + dot(d_far[...], normed_far[...], 1, 0))

    @pl.when(step == last)
    def _():
        small[pl.ds(last + 1, 1), :] = (sums[0:1, :] - shift[...] * sums[1:2, :]) / gain[...]
        small[pl.ds(last + 2, 1), :] = sums[1:2, :]


def mixed_halves(marks, d_own, d_far, normed, normed_far, w, gain, shift, cores, parts, orders):
    height, rows = d_own.shape
    far = d_far.shape[1]
    width = normed.shape[1]
    share = height // cores
    pairs = max(1, 768 // (2 * share))
    levels = pairs.bit_length() - 1
    high = 2 * share * pairs
    first_far = width // high
    run = share // parts
    near = parts.bit_length() - 1
    steps = height // high

    def fixed(shape):
        return pl.BlockSpec(shape, lambda j, i, marks: (0, 0), pipeline_mode=pl.Buffered(1))

    specs, shapes = divided(orders, levels, run, height, width, width)
    *halves, small = pl.pallas_call(
        functools.partial(mixed_kernel, run, levels, near, orders, first_far),
        grid_spec=pltpu.PrefetchScalarGridSpec(
            num_scalar_prefetch=1,
            grid=(1, steps),
            in_specs=[
                pl.BlockSpec((high, rows), lambda j, i, marks: (i, 0)),
                pl.BlockSpec((high, far), lambda j, i, marks: (jnp.maximum(i, first_far), 0)),
                fixed(normed.shape),
                fixed(normed_far.shape),
                pl.BlockSpec((width, high), lambda j, i, marks: (0, i)),
                fixed(gain.shape),
                fixed(shift.shape),
            ],
            out_specs=specs + [pl.BlockSpec((16, width), lambda j, i, marks: (0, 0))],
            scratch_shapes=[pltpu.VMEM((2, width), f32), pltpu.VMEM((high, 1), f32)],
        ),
        out_shape=shapes + [jax.ShapeDtypeStruct((16, width), f32)],
        compiler_params=pltpu.CompilerParams(vmem_limit_bytes=VMEM),
        cost_estimate=pl.CostEstimate(
            flops=2 * (rows + far) * height * width, bytes_accessed=1 << 25, transcendentals=0
        ),
        name="mixed",
    )(marks, d_own, d_far, normed, normed_far, w, gain, shift)
    halves = [item.reshape(-1, width) for item in halves]
    return [halves[i : i + 2] for i in range(0, len(halves), 2)], small, steps


def bit_of(axis, position):
    return (lax.axis_index(axis) >> position) & 1


def swap(values, axis, position):
    size = lax.axis_size(axis)
    return lax.ppermute(values, axis, [(i, i ^ (1 << position)) for i in range(size)])


class Halving:
    def __init__(self, halves, order):
        self.order = list(order)
        kept, given = halves
        self.height = kept.shape[0]
        self.terms = [kept, swap(given, "wide", 0)]

    def send(self, away):
        self.terms = self.terms + [swap(away, *self.order.pop(0))]
        self.height //= 2

    def blocks(self, height, grid, which):
        width = self.terms[0].shape[1]
        spec = pl.BlockSpec((1, height // grid, width), lambda i: (which, i, 0))
        return [term.reshape(-1, height, width) for term in self.terms], [spec] * len(self.terms)


class Adding:
    def __init__(self, array, order):
        self.order = list(order)
        self.terms = [array, swap(array, *self.order.pop(0))]

    def send(self, total):
        self.terms = [total, swap(total, *self.order.pop(0))]


def halve_kernel(counts, *refs):
    ins, outs = refs[: sum(counts) + 2], refs[sum(counts) + 2 :]
    at = 0
    for count, out in zip(counts, outs):
        parts = [ref[0].astype(f32) for ref in ins[at : at + count]]
        out[...] = functools.reduce(jnp.add, parts).astype(bf16)
        at += count
    outs[-1][...] = ins[-2][...] + ins[-1][...]


def halve(sums, small):
    heights = [item.height // 2 for item in sums]
    grid = max(n for n in (1, 4, 8) if n == 1 or all(item % (16 * n) == 0 for item in heights))
    operands, in_specs, out_specs, out_shape = [], [], [], []
    for item, height in zip(sums, heights):
        arrays, specs = item.blocks(height, grid, 1)
        operands += arrays
        in_specs += specs
        width = arrays[0].shape[2]
        out_specs.append(pl.BlockSpec((height // grid, width), lambda i: (i, 0)))
        out_shape.append(jax.ShapeDtypeStruct((height, width), bf16))
    whole_small = pl.BlockSpec(small.terms[0].shape, lambda i: (0, 0))
    return pl.pallas_call(
        functools.partial(halve_kernel, [len(item.terms) for item in sums]),
        grid=(grid,),
        in_specs=in_specs + [whole_small] * 2,
        out_specs=out_specs + [whole_small],
        out_shape=out_shape + [jax.ShapeDtypeStruct(small.terms[0].shape, f32)],
        compiler_params=pltpu.CompilerParams(vmem_limit_bytes=VMEM),
        name="halve",
    )(*operands, *small.terms)


def launch(lead, sums, small, *others):
    lead, others, halves = lax.optimization_barrier((lead, others, halve(sums, small)))
    for item, away in zip(sums, halves):
        item.send(away)
    small.send(halves[-1])
    return (lead, *others)


def settle(lead, sums, small):
    everything = sums + [small]
    lead, terms = lax.optimization_barrier((lead, [item.terms for item in everything]))
    for item, arrays in zip(everything, terms):
        item.terms = list(arrays)
    return lead


def collect_kernel(counts, *refs):
    at = 0
    for count, out in zip(counts, refs[sum(counts) :]):
        out[...] = functools.reduce(jnp.add, [ref[0].astype(f32) for ref in refs[at : at + count]])
        at += count


def collect(sums):
    operands, in_specs, out_specs, out_shape = [], [], [], []
    for item in sums:
        arrays, specs = item.blocks(item.height, 1, 0)
        operands += arrays
        in_specs += specs
        shape = arrays[0].shape[1:]
        out_specs.append(pl.BlockSpec(shape, lambda i: (0, 0)))
        out_shape.append(jax.ShapeDtypeStruct(shape, f32))
    return pl.pallas_call(
        functools.partial(collect_kernel, [len(item.terms) for item in sums]),
        grid=(1,),
        in_specs=in_specs,
        out_specs=out_specs,
        out_shape=out_shape,
        compiler_params=pltpu.CompilerParams(vmem_limit_bytes=VMEM),
        name="collect",
    )(*operands)


def read_small(ref, at, rows):
    parts = [ref[at + i * rows : at + (i + 1) * rows, :].astype(f32) for i in range(3)]
    return parts[0] + parts[1] + parts[2]


def joint_kernel(plan, last, *refs):
    count, buffers, from_at, small_from, to_at, small_to, rows = plan
    arrays, refs = refs[:count], refs[count:]
    received, refs = refs[:buffers], refs[buffers:]
    small, refs = refs[0], refs[1:]
    if small_from is None:
        total = small[...] + refs[0][...]
        refs = refs[1:]
    else:
        total = small[...] + read_small(received[small_from[0]], small_from[1], rows)
    if last:
        out, small_out = refs
        for i in range(count):
            which, at = from_at[i]
            height = arrays[i].shape[0]
            part = received[which][at : at + height, :].astype(f32)
            out[i * height : (i + 1) * height, :] = arrays[i][...].astype(f32) + part
        small_out[...] = total
        return
    outs, sent, small_out = refs[:count], refs[count:-1], refs[-1]
    for i in range(count):
        which, at = from_at[i]
        height = arrays[i].shape[0] // 2
        for half in range(2):
            here = slice(half * height, (half + 1) * height)
            there = slice(at + half * height, at + (half + 1) * height)
            part = arrays[i][here, :].astype(f32) + received[which][there, :].astype(f32)
            if half:
                which_out, at_out = to_at[i]
                sent[which_out][at_out : at_out + height, :] = part.astype(bf16)
            else:
                outs[i][...] = part.astype(bf16)
    small_out[...] = total
    which_out, at_out = small_to
    for part in split_three(total):
        sent[which_out][at_out : at_out + rows, :] = part.astype(bf16)
        at_out += rows


class Joint:
    def __init__(self, halves, orders, small):
        self.arrays = [kept for kept, _ in halves]
        self.received = [swap(given, "wide", 0) for _, given in halves]
        self.from_at = [(i, 0) for i in range(len(halves))]
        self.orders = [list(order) for order in orders]
        self.small, self.small_from = small, None
        self.extra = [swap(small, "wide", 0)]

    def call(self, plan, last, shapes):
        return pl.pallas_call(
            functools.partial(joint_kernel, plan, last),
            out_shape=shapes,
            compiler_params=pltpu.CompilerParams(vmem_limit_bytes=VMEM),
            name="joint",
        )(*self.arrays, *self.received, self.small, *self.extra)

    def plan(self, to_at, small_to):
        buffers, rows = len(self.received), self.small.shape[0]
        count = len(self.arrays)
        return count, buffers, self.from_at, self.small_from, to_at, small_to, rows

    def step(self, lead, *others):
        bits, heights, to_at = [], [], []
        width = self.arrays[0].shape[1]
        for array, order in zip(self.arrays, self.orders):
            bit = order.pop(0)
            if bit not in bits:
                bits.append(bit)
                heights.append(0)
            which = bits.index(bit)
            to_at.append((which, heights[which]))
            heights[which] += array.shape[0] // 2
        small_to = (0, heights[0])
        heights[0] += 3 * self.small.shape[0]
        shapes = [
            jax.ShapeDtypeStruct((array.shape[0] // 2, width), bf16) for array in self.arrays
        ]
        shapes += [jax.ShapeDtypeStruct((height, width), bf16) for height in heights]
        shapes += [jax.ShapeDtypeStruct(self.small.shape, f32)]
        outs = self.call(self.plan(to_at, small_to), False, shapes)
        lead, others, outs = lax.optimization_barrier((lead, others, outs))
        count = len(self.arrays)
        self.arrays, sent, self.small = outs[:count], outs[count:-1], outs[-1]
        self.received = [swap(item, *bit) for item, bit in zip(sent, bits)]
        self.from_at, self.small_from, self.extra = to_at, small_to, []
        return (lead, *others)

    def result(self):
        height = sum(array.shape[0] for array in self.arrays)
        shapes = [
            jax.ShapeDtypeStruct((height, self.arrays[0].shape[1]), f32),
            jax.ShapeDtypeStruct(self.small.shape, f32),
        ]
        return self.call(self.plan([], None), True, shapes)


def angles(positions):
    half = HEAD_DIM // 2
    freqs = jnp.power(10000.0, -jnp.arange(half, dtype=f32) / half)
    theta = freqs[:, None] * positions.astype(f32)[None, :]
    return jnp.cos(theta), jnp.sin(theta)


def axis_bits(axis):
    return [(axis, position) for position in range(lax.axis_size(axis).bit_length() - 1)]


def body(
    inputs,
    cotangent,
    lengths,
    w_qkv,
    b_qkv,
    w_out,
    b_out,
    w_up,
    b_up,
    w_down,
    b_down,
    gain_one,
    shift_one,
    gain_two,
    shift_two,
    gain_three,
    shift_three,
    gain_four,
    shift_four,
):
    group = inputs.shape[3]
    width = inputs.shape[4]
    parts = lax.axis_size("narrow")
    place = lax.axis_index("narrow")
    cores = lax.axis_size("wide")
    others = parts - 1
    rows = 2 * group
    offsets = jnp.arange(group, dtype=jnp.int32)

    def row(vector):
        return vector[None, :]

    def positions(owners):
        starts = jnp.stack([owners, 2 * parts - 1 - owners], axis=1).reshape(-1) * group
        return (starts[:, None] + offsets[None]).reshape(-1)

    def joined(items):
        return jnp.concatenate(items, axis=0) if len(items) > 1 else items[0]

    tokens = inputs.reshape(rows, width)
    far_tokens = joined(
        [
            lax.ppermute(tokens, "narrow", [((n + shift) % parts, n) for n in range(parts)])
            for shift in range(1, parts)
        ]
    )
    other = (place + 1 + jnp.arange(others, dtype=jnp.int32)) % parts
    early_at = place * group
    late_at = (2 * parts - 1 - place) * group
    info = jnp.stack([place, lengths[0], early_at, late_at]).astype(jnp.int32)
    marks = jnp.stack([lax.axis_index("wide"), place]).astype(jnp.int32)
    turns = angles(positions(place[None]))
    turns_far = angles(positions(other))

    norm_one = [row(gain_one), row(shift_one)]
    normed, qT, kT, vT = project(tokens, w_qkv, row(b_qkv), *norm_one, *turns, (0, 1, 2))
    state, kept_own, flags_own = attend_local(info, qT, kT, vT, group)
    normed_far, kT_far, vT_far = project(
        far_tokens, w_qkv, row(b_qkv), *norm_one, *turns_far, (1, 2)
    )
    oT, lse, kept_far, flags_far = attend_remote(
        info, qT, kT_far, vT_far, state, group, parts
    )

    blocks = block_call(
        oT,
        lse,
        tokens,
        cotangent.reshape(rows, width),
        [w_out, w_up, w_down],
        [row(item) for item in (b_out, b_up, b_down)]
        + [row(item) for item in (gain_two, shift_two, gain_three, shift_three)]
        + [row(item) for item in (gain_four, shift_four)],
    )
    result, d_middle, hidden, d_outer, normed_two, d_inner, d_branch = blocks[:7]
    doT, scaled, delta, small, small_up = blocks[7:]

    wide_bits = axis_bits("wide")
    narrow_bits = axis_bits("narrow")
    first_order = wide_bits[1:2] + narrow_bits + wide_bits[2:]
    second_order = narrow_bits + wide_bits[1:]
    third_order = narrow_bits + wide_bits[2:3] + wide_bits[1:2] + wide_bits[3:]
    fourth_order = wide_bits[2:3] + wide_bits[1:2] + narrow_bits + wide_bits[3:]
    fifth_order = wide_bits[2:3] + narrow_bits + wide_bits[1:2] + wide_bits[3:]
    small_order = wide_bits[:1] + first_order

    def outer(left, right, right_dim, order):
        return Halving(outer_halves(marks, left, right, right_dim, cores, parts, order), order)

    sum_up = outer(d_inner, normed_two, 0, first_order)
    sum_down = outer(d_outer, hidden, 0, second_order)
    sum_out = outer(d_branch, oT, 1, fifth_order)
    flat = jnp.concatenate([small.reshape(-1), small_up.reshape(-1)])
    early = Adding(flat.reshape(-1, PAIR), small_order)
    sums = [sum_down, sum_up, sum_out]

    heads = width // PAIR
    portions = 2 if heads % 2 == 0 else 1
    count = heads // portions
    (doT,) = launch(doT, sums, early)
    dq_far, d_far = back_remote(
        info,
        flags_far,
        [qT, doT, oT, lse, scaled, delta],
        turns_far,
        [kT_far, vT_far],
        kept_far,
        group,
        parts,
        0,
        heads,
        [],
    )
    d_back = unproject(d_far, w_qkv, (1, 2), 0, others * rows)
    d_mixed = []
    for portion in range(portions):
        doT, d_back = launch(doT, sums, early, d_back)
        if not portion:
            returned = [
                lax.ppermute(
                    d_back[j * rows : (j + 1) * rows] if others > 1 else d_back,
                    "narrow",
                    [(n, (n + j + 1) % parts) for n in range(parts)],
                )
                for j in range(others)
            ]
        d_mixed = [
            back_local(
                info,
                flags_own,
                [qT, doT, oT, lse, scaled, delta],
                turns,
                [kT, vT],
                dq_far,
                kept_own,
                group,
                portion * count,
                count,
                d_mixed,
            )
        ]
    d_mixed = d_mixed[0]
    while early.order:
        (d_mixed,) = launch(d_mixed, sums, early)
    d_mixed, returned = lax.optimization_barrier((d_mixed, returned))
    if others > 1:
        returned = [functools.reduce(jnp.add, [item.astype(f32) for item in returned])]

    orders = [first_order, third_order, fourth_order]
    pieces, late, steps = mixed_halves(
        marks,
        d_mixed.reshape(3 * width, rows),
        d_far.reshape(3 * width, -1),
        normed,
        normed_far,
        w_qkv,
        *norm_one,
        cores,
        parts,
        orders,
    )
    late, pieces = settle((late, pieces), sums, early)
    tail = Joint(pieces, orders, late)
    (d_mixed,) = tail.step(d_mixed)
    d_tokens = []
    for i in range(2):
        finish = (returned[0], tokens, d_middle, row(gain_one))
        d_tokens = [
            unproject(d_mixed, w_qkv, (0, 1, 2), i * group, group, finish, d_tokens)
        ]
        if tail.orders[0]:
            d_mixed, d_tokens[0] = tail.step(d_mixed, d_tokens[0])
    while tail.orders[0]:
        d_tokens[0], *terms = tail.step(d_tokens[0], *[item.terms for item in sums])
        for item, arrays in zip(sums, terms):
            item.terms = list(arrays)

    sum_w_down, sum_w_up, sum_w_out = collect(sums)
    sum_w_qkv, late_small = tail.result()
    grad_b_qkv = late_small[:steps, : 3 * width // steps].reshape(-1)
    early_small = (early.terms[0] + early.terms[1]).reshape(-1)
    small = early_small[: 8 * width].reshape(8, width)
    small_up = early_small[8 * width :]
    shape = inputs.shape
    return (
        result.reshape(shape),
        d_tokens[0].reshape(shape),
        sum_w_qkv.T,
        sum_w_out.T,
        sum_w_up.T,
        sum_w_down.T,
        grad_b_qkv,
        small[7],
        small_up,
        small[2],
        late_small[steps],
        late_small[steps + 1],
        small[5],
        small[6],
        small[3],
        small[4],
        small[0],
        small[1],
    )


def solution(mesh):
    tokens = P("wide", None, "narrow", None, None)
    columns = P(None, ("wide", "narrow"))
    in_specs = (tokens, tokens, P("wide")) + (P(),) * 16
    out_specs = (tokens, tokens) + (columns,) * 4 + (P(),) * 12
    return jax.shard_map(body, mesh=mesh, in_specs=in_specs, out_specs=out_specs, check_vma=False)
```
